128 devices in a mesh: rep: 16 (over x, z_lo, core), grp: 8 (over y, z_hi).
Axes of the slice: x: 4, y: 4, z: 4 (z_hi: 2, z_lo: 2; z = z_hi * 2 + z_lo), core: 2. Of those that a mesh axis runs over, the one named last changes fastest.
Arguments:
- tokens: bfloat16 [16, 1024, 1600], P('rep', 'grp'), may hold values from -6 to 6
- ln1_gain: bfloat16 [1600], P('grp'), may hold values from 0.25 to 1.75
- ln1_bias: bfloat16 [1600], P('grp'), may hold values from -1.5 to 1.5
- w_qkv: bfloat16 [1600, 4800], P('grp'), may hold values from -0.15625 to 0.15625
- bias_q: bfloat16 [1600], P('grp'), may hold values from -1.5 to 1.5
- bias_v: bfloat16 [1600], P('grp'), may hold values from -1.5 to 1.5
- w_out: bfloat16 [1600, 1600], P('grp'), may hold values from -1.25 to 1.25
- bias_out: bfloat16 [1600], P('grp'), may hold values from -1.5 to 1.5
- ln2_gain: bfloat16 [1600], P('grp'), may hold values from 0.25 to 1.75
- ln2_bias: bfloat16 [1600], P('grp'), may hold values from -1.5 to 1.5
- w_fc: bfloat16 [1600, 6400], P('grp'), may hold values from -0.15625 to 0.15625
- bias_fc: bfloat16 [6400], P('grp'), may hold values from -2.5 to 2.5
- w_proj: bfloat16 [6400, 1600], P('grp'), may hold values from -0.078125 to 0.078125
- bias_proj: bfloat16 [1600], P('grp'), may hold values from -1.5 to 1.5
- cotangent: bfloat16 [16, 1024, 1600], P('rep', 'grp'), may hold values from -6 to 6
Outputs:
- output: bfloat16 [16, 1024, 1600], P('rep', 'grp')
- grad_tokens: float32 [16, 1024, 1600], P('rep', 'grp')
- grad_ln1_gain: float32 [1600], P('grp')
- grad_ln1_bias: float32 [1600], P('grp')
- grad_w_qkv: float32 [1600, 4800], P('grp')
- grad_bias_q: float32 [1600], P('grp')
- grad_bias_v: float32 [1600], P('grp')
- grad_w_out: float32 [1600, 1600], P('grp')
- grad_bias_out: float32 [1600], P('grp')
- grad_ln2_gain: float32 [1600], P('grp')
- grad_ln2_bias: float32 [1600], P('grp')
- grad_w_fc: float32 [1600, 6400], P('grp')
- grad_bias_fc: float32 [6400], P('grp')
- grad_w_proj: float32 [6400, 1600], P('grp')
- grad_bias_proj: float32 [1600], P('grp')
The draws below stay inside these ranges and needn't reach their ends.
All inputs are finite; a program needn't handle non-finite values.
Results may differ from the reference program's by a relative error of at most 0.02.
Values may be sent and summed in bfloat16 or wider, within the bound.
No kernel may reach another device: no remote copies, remote signals or barrier semaphores. Data moves between devices by JAX's collectives and lax.ppermute only.
A program may use at most 256 MiB of HBM per device.

```python
import math
import jax
import jax.numpy as jnp
from jax import lax

D = 1600
HEADS = 25
HEAD_DIM = 64
FF = 6400
SEQ_LEN = 1024
BATCH = 16


def block_levels(key, dims, split, least, largest):
    loudness = 1.0
    for dim, shards_of in split:
        draws = jax.random.uniform(jax.random.fold_in(jax.random.fold_in(key, 6), dim), (shards_of,), jnp.float32, least / len(split), largest / len(split))
        loudness = loudness * jnp.repeat(jnp.exp(draws), dims[dim] // shards_of).reshape((-1,) + (1,) * (len(dims) - 1 - dim))
    return loudness


def noise(rng, dims, scale, reach, pieces=(), dtype=jnp.bfloat16):
    entries = scale * jax.random.normal(rng, dims, jnp.float32)
    if pieces:
        entries = entries * block_levels(rng, dims, pieces, -0.22, 0.18)
    return jnp.clip(entries, -reach, reach).astype(dtype)


def setup_inputs(seed: int = 0) -> dict:
    arg_keys = jax.random.split(jax.random.key(seed), 16)
    return {
        "tokens": noise(arg_keys[0], (BATCH, SEQ_LEN, D), 1.0, 6.0, ((0, 16), (1, 8))),
        "ln1_gain": jnp.clip(1.0 + 0.15 * jax.random.normal(arg_keys[1], (D,), jnp.float32), 0.25, 1.75).astype(jnp.bfloat16),
        "ln1_bias": noise(arg_keys[2], (D,), 0.3, 1.5, ((0, 8),)),
        "w_qkv": noise(arg_keys[3], (D, 3 * D), D ** -0.5, 0.15625, ((0, 8),)),
        "bias_q": noise(arg_keys[4], (D,), 0.3, 1.5, ((0, 8),)),
        "bias_v": noise(arg_keys[5], (D,), 0.3, 1.5, ((0, 8),)),
        "w_out": noise(arg_keys[6], (D, D), (D * 16 // SEQ_LEN) ** -0.5, 1.25, ((0, 8),)),
        "bias_out": noise(arg_keys[7], (D,), 0.3, 1.5, ((0, 8),)),
        "ln2_gain": jnp.clip(1.0 + 0.15 * jax.random.normal(arg_keys[8], (D,), jnp.float32), 0.25, 1.75).astype(jnp.bfloat16),
        "ln2_bias": noise(arg_keys[9], (D,), 0.3, 1.5, ((0, 8),)),
        "w_fc": noise(arg_keys[10], (D, FF), D ** -0.5, 0.15625, ((0, 8),)),
        "bias_fc": noise(arg_keys[11], (FF,), 0.5, 2.5, ((0, 8),)),
        "w_proj": noise(arg_keys[12], (FF, D), FF ** -0.5, 0.078125, ((0, 8),)),
        "bias_proj": noise(arg_keys[13], (D,), 0.3, 1.5, ((0, 8),)),
        "cotangent": noise(arg_keys[14], (BATCH, SEQ_LEN, D), 1.0, 6.0, ((0, 16), (1, 8))),
    }


@jax.custom_vjp
def low(v):
    return lax.optimization_barrier(v.astype(jnp.bfloat16)).astype(jnp.float32)

@jax.custom_vjp
def low_back(v):
    return v

def low_keep(v):
    return (low(v), None)

def low_pass(kept, grad):
    return (grad,)

def back_keep(v):
    return (v, None)

def back_low(kept, grad):
    return (low(grad),)
low.defvjp(low_keep, low_pass)
low_back.defvjp(back_keep, back_low)

def rounded_both(value):
    return low_back(low(value))

def product(left, right):
    return jnp.dot(left, right, precision=lax.Precision.HIGHEST, preferred_element_type=jnp.float32)

def layer_norm(value, gain, shift):
    center = value - lax.optimization_barrier(jnp.mean(value, axis=-1, keepdims=True))
    spread = lax.optimization_barrier(jnp.mean(center * center, axis=-1, keepdims=True))
    return center * lax.rsqrt(spread + 1e-05) * gain + shift

def gelu_tanh(value):
    return 0.5 * value * (1.0 + jnp.tanh(0.7978845608028654 * (value + 0.044715 * value * value * value)))

def residual_block(inputs, params):
    ln1_gain, ln1_bias, w_qkv, bias_q, bias_v, w_out, bias_out, ln2_gain, ln2_bias, w_fc, bias_fc, w_proj, bias_proj = params
    seq_length = inputs.shape[0]
    first = low(layer_norm(inputs, ln1_gain, ln1_bias))
    mixed = product(first, w_qkv)
    query = rounded_both(mixed[:, :D] + bias_q)
    keys_all = rounded_both(mixed[:, D:2 * D])
    values_all = rounded_both(mixed[:, 2 * D:] + bias_v)
    query_heads = query.reshape(seq_length, HEADS, HEAD_DIM)
    key_heads = keys_all.reshape(seq_length, HEADS, HEAD_DIM)
    value_heads = values_all.reshape(seq_length, HEADS, HEAD_DIM)
    scores = jnp.einsum('qhd,khd->hqk', query_heads, key_heads, precision=lax.Precision.HIGHEST)
    scores = low_back(scores * (1.0 / math.sqrt(HEAD_DIM)))
    row_pos = lax.broadcasted_iota(jnp.int32, (seq_length, seq_length), 0)
    col_pos = lax.broadcasted_iota(jnp.int32, (seq_length, seq_length), 1)
    scores = jnp.where(col_pos <= row_pos, scores, -1e+30)
    probs = jax.nn.softmax(scores, axis=-1)
    probs_low = low(probs)
    attended = jnp.einsum('hqk,khd->qhd', probs_low, value_heads, precision=lax.Precision.HIGHEST)
    attended = rounded_both(attended.reshape(seq_length, D))
    branch = low_back(product(attended, w_out) + bias_out)
    middle = inputs + branch
    second = low(layer_norm(middle, ln2_gain, ln2_bias))
    before = low_back(product(second, w_fc) + bias_fc)
    active = low(gelu_tanh(before))
    down_branch = low_back(product(active, w_proj) + bias_proj)
    return middle + down_branch

def reference(tokens, ln1_gain, ln1_bias, w_qkv, bias_q, bias_v, w_out, bias_out, ln2_gain, ln2_bias, w_fc, bias_fc, w_proj, bias_proj, cotangent):
    params = (ln1_gain, ln1_bias, w_qkv, bias_q, bias_v, w_out, bias_out, ln2_gain, ln2_bias, w_fc, bias_fc, w_proj, bias_proj)
    params_full = tuple((p.astype(jnp.float32) for p in params))
    inputs = tokens.astype(jnp.float32)
    cot_full = cotangent.astype(jnp.float32)
    zeros_init = tuple((jnp.zeros_like(p) for p in params_full))

    def one_sequence(totals, item):
        sequence, seq_cot = item
        result, pull = jax.vjp(residual_block, sequence, params_full)
        grad_input, grad_params = pull(seq_cot)
        totals = tuple((a + b for a, b in zip(totals, grad_params)))
        return (totals, (result.astype(jnp.bfloat16), grad_input))
    totals, (results, grad_inputs) = lax.scan(one_sequence, zeros_init, (inputs, cot_full))
    return (results, grad_inputs, totals[0], totals[1], totals[2], totals[3], totals[4], totals[5], totals[6], totals[7], totals[8], totals[9], totals[10], totals[11], totals[12])
```

```python
import math

import jax
import jax.numpy as jnp
from jax import lax
from jax.experimental import pallas as pl
from jax.experimental.pallas import tpu as pltpu
from jax.sharding import PartitionSpec as P

HEADS = 25
HEAD_DIM = 64
SLOTS = 4
SLOT_WIDTH = SLOTS * HEAD_DIM
STRIDE = 3 * HEAD_DIM
AXES = ("rep", "grp")
BLOCK = 256

bf16 = jnp.bfloat16
f32 = jnp.float32


def linear(x, zl, c, y, zh):
    return ((x * 2 + zl) * 2 + c) * 8 + y * 2 + zh


PLACES = [
    (x, zl, c, y, zh)
    for x in range(4)
    for zl in range(2)
    for c in range(2)
    for y in range(4)
    for zh in range(2)
]


def pairs(where):
    return [(linear(*place), linear(*where(*place))) for place in PLACES]


def z_moved(x, zl, c, y, zh, step):
    z = (zh * 2 + zl - step) % 4
    return (x, z % 2, c, y, z // 2)


X_RING = [pairs(lambda x, zl, c, y, zh, k=k: ((x - k) % 4, zl, c, y, zh)) for k in range(4)]
Y_RING = [pairs(lambda x, zl, c, y, zh, k=k: (x, zl, c, (y - k) % 4, zh)) for k in range(4)]
Z_RING = [pairs(lambda x, zl, c, y, zh, k=k: z_moved(x, zl, c, y, zh, k)) for k in range(4)]
CORE = pairs(lambda x, zl, c, y, zh: (x, zl, 1 - c, y, zh))
Z_LOW = pairs(lambda x, zl, c, y, zh: (x, 1 - zl, c, y, zh))
Z_HIGH = pairs(lambda x, zl, c, y, zh: (x, zl, c, y, 1 - zh))
ROLES = pairs(lambda x, zl, c, y, zh: (x, zl, zh, y, c))
OWNERS = [pairs(lambda x, zl, c, y, zh, i=i: (x, zh ^ i, zl, y, c)) for i in range(2)]


def send(value, perm):
    return lax.ppermute(value, AXES, perm)


def pick(stack, index, axis=0):
    return lax.dynamic_index_in_dim(stack, index, axis, keepdims=False)


def placed(parts, me):
    whole = jnp.zeros((4,) + parts[0].shape, parts[0].dtype)
    for k, part in enumerate(parts):
        whole = lax.dynamic_update_index_in_dim(whole, part, (me + k) % 4, 0)
    return whole


def ring_gather(block, ring, me):
    return placed([block] + [send(block, ring[k]) for k in range(1, 4)], me)


def ring_exchange(stack, ring, me):
    return placed(
        [pick(stack, me)] + [send(pick(stack, (me - k) % 4), ring[k]) for k in range(1, 4)], me
    )


def ring_scatter(stack, ring, me):
    total = pick(stack, me).astype(f32)
    for k in range(1, 4):
        total = total + send(pick(stack, (me - k) % 4), ring[k]).astype(f32)
    return total


def paired(own, other, bit, axis=1):
    return jnp.where(
        bit == 0, jnp.stack([own, other], axis), jnp.stack([other, own], axis)
    )


def norm_parts(value, gain, shift):
    center = value - jnp.mean(value, axis=-1, keepdims=True)
    spread = jnp.mean(center * center, axis=-1, keepdims=True)
    factor = lax.rsqrt(spread + 1e-05)
    normed = center * factor
    return (normed * gain + shift, normed, factor)


def norm_back(grad_value, normed, factor, gain):
    grad_normed = grad_value * gain
    mean_first = jnp.mean(grad_normed, axis=-1, keepdims=True)
    mean_second = jnp.mean(grad_normed * normed, axis=-1, keepdims=True)
    return factor * (grad_normed - mean_first - normed * mean_second)


def gelu_tanh(value):
    return (
        0.5
        * value
        * (1.0 + jnp.tanh(0.7978845608028654 * (value + 0.044715 * value * value * value)))
    )


def dot(left, right):
    return jnp.dot(left, right, preferred_element_type=f32)


def dot_rows(left, right):
    return lax.dot_general(left, right, (((0,), (0,)), ((), ())), preferred_element_type=f32)


def dot_cols(left, right):
    return lax.dot_general(left, right, (((1,), (1,)), ((), ())), preferred_element_type=f32)


def attention_kernel(qkv_ref, out_ref, top_ref):
    length = qkv_ref.shape[0]
    for head in range(SLOTS):
        lanes = slice(head * HEAD_DIM, (head + 1) * HEAD_DIM)
        keys = qkv_ref[:, SLOT_WIDTH + head * HEAD_DIM : SLOT_WIDTH + (head + 1) * HEAD_DIM]
        values = qkv_ref[
            :, 2 * SLOT_WIDTH + head * HEAD_DIM : 2 * SLOT_WIDTH + (head + 1) * HEAD_DIM
        ]
        for block in range(length // BLOCK):
            rows = slice(block * BLOCK, (block + 1) * BLOCK)
            width = (block + 1) * BLOCK
            query = qkv_ref[rows, lanes] * bf16(1.0 / math.sqrt(HEAD_DIM))
            scores = dot_cols(query, keys[:width])
            row = lax.broadcasted_iota(jnp.int32, (BLOCK, width), 0) + block * BLOCK
            col = lax.broadcasted_iota(jnp.int32, (BLOCK, width), 1)
            scores = jnp.where(col <= row, scores, -1e30)
            top = jnp.max(scores, axis=-1, keepdims=True)
            probs = jnp.exp(scores - top)
            total = jnp.sum(probs, axis=-1, keepdims=True)
            mixed = dot(probs.astype(bf16), values[:width])
            out_ref[rows, lanes] = (mixed / total).astype(bf16)
            top_ref[rows, head : head + 1] = top + jnp.log(total)


def attention(qkv):
    length = qkv.shape[0]
    return pl.pallas_call(
        attention_kernel,
        out_shape=(
            jax.ShapeDtypeStruct((length, SLOT_WIDTH), bf16),
            jax.ShapeDtypeStruct((length, SLOTS), f32),
        ),
        in_specs=[pl.BlockSpec(memory_space=pltpu.VMEM)],
        out_specs=(
            pl.BlockSpec(memory_space=pltpu.VMEM),
            pl.BlockSpec(memory_space=pltpu.VMEM),
        ),
        compiler_params=pltpu.CompilerParams(vmem_limit_bytes=48 * 2**20),
        name="attention",
    )(qkv)


def attention_back_kernel(qkv_ref, grad_ref, top_ref, delta_ref, out_ref, query_ref):
    length = qkv_ref.shape[0]
    scale = 1.0 / math.sqrt(HEAD_DIM)
    for head in range(SLOTS):
        base = head * HEAD_DIM
        lanes = slice(base, base + HEAD_DIM)
        key_lanes = slice(SLOT_WIDTH + base, SLOT_WIDTH + base + HEAD_DIM)
        value_lanes = slice(2 * SLOT_WIDTH + base, 2 * SLOT_WIDTH + base + HEAD_DIM)
        query = qkv_ref[:, lanes] * bf16(scale)
        grad = grad_ref[:, lanes]
        top = top_ref[head : head + 1, :]
        delta = delta_ref[head : head + 1, :]
        for block in range(length // BLOCK):
            start = block * BLOCK
            rows = slice(start, start + BLOCK)
            width = length - start
            keys = qkv_ref[rows, key_lanes]
            values = qkv_ref[rows, value_lanes]
            scores = dot_cols(keys, query[start:])
            row = lax.broadcasted_iota(jnp.int32, (BLOCK, width), 0)
            col = lax.broadcasted_iota(jnp.int32, (BLOCK, width), 1)
            probs = jnp.where(row <= col, jnp.exp(scores - top[:, start:]), 0.0)
            grad_probs = dot_cols(values, grad[start:])
            grad_scores = (probs * (grad_probs - delta[:, start:])).astype(bf16)
            out_ref[rows, value_lanes] = dot(probs.astype(bf16), grad[start:]).astype(bf16)
            out_ref[rows, key_lanes] = dot(grad_scores, query[start:]).astype(bf16)
            term = dot_rows(grad_scores, keys)
            if block == 0:
                query_ref[...] = term
            else:
                query_ref[start:, :] += term
        out_ref[:, lanes] = (query_ref[...] * scale).astype(bf16)


def attention_back(qkv, grad, top, delta):
    return pl.pallas_call(
        attention_back_kernel,
        out_shape=jax.ShapeDtypeStruct(qkv.shape, bf16),
        in_specs=[pl.BlockSpec(memory_space=pltpu.VMEM)] * 4,
        out_specs=pl.BlockSpec(memory_space=pltpu.VMEM),
        scratch_shapes=[pltpu.VMEM((qkv.shape[0], HEAD_DIM), f32)],
        compiler_params=pltpu.CompilerParams(vmem_limit_bytes=48 * 2**20),
        name="attention_back",
    )(qkv, grad, top, delta)


def per_device(
    tokens,
    ln1_gain,
    ln1_bias,
    w_qkv,
    bias_q,
    bias_v,
    w_out,
    bias_out,
    ln2_gain,
    ln2_bias,
    w_fc,
    bias_fc,
    w_proj,
    bias_proj,
    cotangent,
):
    _, span, width = tokens.shape
    shard = width // 8
    hidden = w_fc.shape[1] // 8
    length = span * 8
    rep = lax.axis_index("rep")
    grp = lax.axis_index("grp")
    x, zl, c = rep // 4, (rep // 2) % 2, rep % 2
    y, zh = grp // 2, grp % 2
    z = zh * 2 + zl
    rank = y * 2 + c

    def group_gather(block):
        own = ring_gather(block, Y_RING, y)
        return paired(own, send(own, CORE), c)

    def group_scatter(parts):
        parts = parts.astype(bf16).reshape((4, 2, span) + parts.shape[1:])
        got = send(pick(parts, 1 - c, 1), CORE)
        both = pick(parts, c, 1).astype(f32) + got.astype(f32)
        low = both.astype(bf16)
        total = pick(both, y)
        for k in range(1, 4):
            total = total + send(pick(low, (y - k) % 4), Y_RING[k]).astype(f32)
        return total

    def to_tokens(parts):
        parts = parts.reshape(4, 2 * span, -1)
        own = ring_exchange(parts, Y_RING, y).reshape(4, 2, span, -1)
        got = send(pick(own, 1 - c, 1), CORE)
        return paired(pick(own, c, 1), got, c)

    def from_tokens(parts):
        got = send(pick(parts, 1 - c, 1), CORE)
        both = paired(pick(parts, c, 1), got, c)
        return ring_exchange(both, Y_RING, y).reshape(length, -1)

    def columns(parts):
        own = ring_exchange(pick(parts, c, 1), Y_RING, y)
        other = send(own, Z_HIGH)
        return paired(own, other, zh).reshape(8 * shard, -1)

    own_tokens = send(tokens.reshape(span, width), ROLES)
    small = jnp.concatenate(
        [ln1_gain, ln1_bias, bias_q, bias_v, bias_out, ln2_gain, ln2_bias, bias_proj]
    ).reshape(2, 4 * shard)
    small = jnp.concatenate([small, bias_fc.reshape(1, hidden)], axis=0)
    small = send(small, ROLES)
    hidden_bias = small[2].astype(f32)
    small_all = group_gather(small).reshape(8, 3, 4 * shard)
    vectors = small_all[:, :2].reshape(8, 8, shard).transpose(1, 0, 2).reshape(8, width)
    vectors = vectors.astype(f32)
    gain_first, shift_first, query_bias, value_bias = [vectors[i] for i in range(4)]
    output_bias, gain_second, shift_second, down_bias = [vectors[i] for i in range(4, 8)]

    all_tokens = group_gather(own_tokens).reshape(length, width)
    slots = [
        [w_qkv[:, p * width + STRIDE * r : p * width + STRIDE * r + SLOT_WIDTH] for p in range(3)]
        for r in range(8)
    ]
    slots = jnp.stack([jnp.concatenate(s, axis=1) for s in slots])
    qkv_cols = columns(slots.reshape(4, 2, shard, 3 * SLOT_WIDTH))
    own_cot = send(cotangent.reshape(span, width), ROLES)
    all_cot = group_gather(own_cot).reshape(length, width)
    out_rows = send(w_out, ROLES)
    out_all = group_gather(out_rows).reshape(width, width)
    fc_cols = columns(w_fc.reshape(shard, 4, 2, hidden).transpose(1, 2, 0, 3))
    proj_rows = send(w_proj, ROLES)

    inputs = own_tokens.astype(f32)
    _, normed_first, factor_first = norm_parts(inputs, gain_first, shift_first)
    first = norm_parts(all_tokens.astype(f32), gain_first, shift_first)[0].astype(bf16)
    zeros = jnp.zeros((SLOT_WIDTH,), f32)
    bias_slots = jnp.concatenate(
        [
            lax.dynamic_slice_in_dim(query_bias, STRIDE * rank, SLOT_WIDTH),
            zeros,
            lax.dynamic_slice_in_dim(value_bias, STRIDE * rank, SLOT_WIDTH),
        ]
    )
    qkv = (dot(first, qkv_cols) + bias_slots).astype(bf16)
    attended_slots, top = attention(qkv)
    attended = to_tokens(attended_slots).reshape(8, span, SLOT_WIDTH)
    attended = jnp.concatenate(
        [attended[r, :, : STRIDE if r < 7 else SLOT_WIDTH] for r in range(8)], axis=1
    )

    middle = inputs + (dot(attended, out_all) + output_bias)
    second, normed_second, factor_second = norm_parts(middle, gain_second, shift_second)
    second_all = group_gather(second.astype(bf16)).reshape(length, width)
    grad_active = dot_cols(all_cot, proj_rows)
    hidden_pre = dot(second_all, fc_cols) + hidden_bias
    active, gelu_pull = jax.vjp(gelu_tanh, hidden_pre)
    active_low = active.astype(bf16)
    grad_hidden = gelu_pull(grad_active)[0].astype(bf16)
    grad_second = group_scatter(dot_cols(grad_hidden, fc_cols))
    output = middle + (group_scatter(dot(active_low, proj_rows)) + down_bias)
    proj_grad = dot_rows(active_low, all_cot).astype(bf16)
    fc_grad = dot_rows(second_all, grad_hidden).astype(bf16)

    grad_middle = own_cot.astype(f32) + norm_back(
        grad_second, normed_second, factor_second, gain_second
    )
    grad_branch = grad_middle.astype(bf16)

    grad_attended = dot_cols(grad_branch, out_all).astype(bf16)
    grad_slots = jnp.stack(
        [grad_attended[:, STRIDE * r : STRIDE * r + SLOT_WIDTH] for r in range(8)]
    ).reshape(4, 2, span, SLOT_WIDTH)
    grad_heads = from_tokens(grad_slots)
    lane = lax.broadcasted_iota(jnp.int32, (1, SLOT_WIDTH), 1)
    grad_heads = jnp.where((lane < STRIDE) | (rank == 7), grad_heads, jnp.zeros_like(grad_heads))
    delta = jnp.sum(
        (grad_heads.astype(f32) * attended_slots.astype(f32)).reshape(length, SLOTS, HEAD_DIM),
        axis=-1,
    )
    grad_mixed = attention_back(qkv, grad_heads, top.T, delta.T)
    grad_first = group_scatter(dot_cols(grad_mixed, qkv_cols))
    qkv_grad = dot_rows(first, grad_mixed).astype(bf16)
    grad_inputs = grad_middle + norm_back(grad_first, normed_first, factor_first, gain_first)

    branch_all = group_gather(grad_branch).reshape(length, width)
    attended_own = from_tokens(
        attended.reshape(span, 4, 2, shard).transpose(1, 2, 0, 3)
    )
    out_grad = dot_rows(attended_own, branch_all).astype(bf16)

    def row_total(parts):
        total = ring_scatter(parts, X_RING, x).astype(bf16)
        total = ring_scatter(total, Z_RING, z).astype(bf16)
        two = paired(send(total, OWNERS[0]), send(total, OWNERS[1]), zl, 0)
        whole = ring_gather(two, X_RING, x)
        return paired(whole, send(whole, CORE), c, 2)

    def column_total(grad):
        count = grad.shape[1]
        total = ring_scatter(grad.reshape(4, 2 * shard, count), X_RING, x).astype(bf16)
        total = ring_scatter(total.reshape(4, shard // 2, count), Z_RING, z).astype(bf16)
        spread = ring_gather(total, X_RING, x)
        spread = ring_exchange(spread, Y_RING, y)
        spread = paired(spread, send(spread, Z_LOW), zl)
        spread = paired(spread, send(spread, CORE), c)
        return spread.reshape(8, shard, count).transpose(1, 0, 2)

    proj_total = row_total(proj_grad.reshape(4, 4, hidden // 16, width))
    proj_total = proj_total.reshape(hidden, width).astype(f32)
    fc_total = column_total(fc_grad).reshape(shard, 8 * hidden).astype(f32)
    out_parts = out_grad.reshape(4, shard // 4, 4, width // 4).transpose(0, 2, 1, 3)
    out_total = row_total(out_parts).reshape(4, 4, shard // 4, width // 4)
    out_total = out_total.transpose(0, 2, 1, 3).reshape(shard, width).astype(f32)
    qkv_parts = column_total(qkv_grad)
    qkv_total = jnp.concatenate(
        [
            qkv_parts[:, r, p * SLOT_WIDTH : p * SLOT_WIDTH + (STRIDE if r < 7 else SLOT_WIDTH)]
            for p in range(3)
            for r in range(8)
        ],
        axis=1,
    ).astype(f32)

    bias_sums = jnp.sum(grad_mixed.astype(f32), axis=0)
    blank = jnp.zeros((width,), f32)
    small_terms = [
        jnp.sum(grad_first * normed_first, axis=0),
        jnp.sum(grad_first, axis=0),
        lax.dynamic_update_slice_in_dim(blank, bias_sums[:SLOT_WIDTH], STRIDE * rank, 0),
        lax.dynamic_update_slice_in_dim(blank, bias_sums[2 * SLOT_WIDTH :], STRIDE * rank, 0),
        jnp.sum(grad_branch.astype(f32), axis=0),
        jnp.sum(grad_second * normed_second, axis=0),
        jnp.sum(grad_second, axis=0),
        jnp.sum(own_cot.astype(f32), axis=0),
        lax.dynamic_update_slice_in_dim(
            jnp.zeros((8 * hidden,), f32),
            jnp.sum(grad_hidden.astype(f32), axis=0),
            hidden * rank,
            0,
        ),
    ]
    small_sum = jnp.concatenate(small_terms).reshape(24, 4 * shard)
    small_sum = small_sum + send(small_sum, CORE)
    for ring, me in ((Y_RING, y), (X_RING, x), (Z_RING, z)):
        small_sum = jnp.sum(ring_gather(small_sum, ring, me), axis=0)
    small_sum = small_sum.reshape(-1)
    owned = [
        lax.dynamic_slice_in_dim(small_sum, width * i + shard * grp, shard) for i in range(8)
    ]
    owned_hidden = lax.dynamic_slice_in_dim(small_sum, width * 8 + hidden * grp, hidden)

    output_home = send(output.astype(bf16), ROLES).reshape(1, span, width)
    inputs_home = send(grad_inputs.astype(bf16), ROLES).astype(f32).reshape(1, span, width)
    return (
        output_home,
        inputs_home,
        owned[0],
        owned[1],
        qkv_total,
        owned[2],
        owned[3],
        out_total,
        owned[4],
        owned[5],
        owned[6],
        fc_total,
        owned_hidden,
        proj_total,
        owned[7],
    )


def solution(mesh):
    in_specs = (
        P("rep", "grp", None),
        P("grp"),
        P("grp"),
        P("grp", None),
        P("grp"),
        P("grp"),
        P("grp", None),
        P("grp"),
        P("grp"),
        P("grp"),
        P("grp", None),
        P("grp"),
        P("grp", None),
        P("grp"),
        P("rep", "grp", None),
    )
    out_specs = (
        P("rep", "grp", None),
        P("rep", "grp", None),
        P("grp"),
        P("grp"),
        P("grp", None),
        P("grp"),
        P("grp"),
        P("grp", None),
        P("grp"),
        P("grp"),
        P("grp"),
        P("grp", None),
        P("grp"),
        P("grp", None),
        P("grp"),
    )
    return jax.shard_map(
        per_device, mesh=mesh, in_specs=in_specs, out_specs=out_specs, check_vma=False
    )
```

```python
import math

import jax
import jax.numpy as jnp
from jax import lax
from jax.experimental import pallas as pl
from jax.experimental.pallas import tpu as pltpu
from jax.sharding import PartitionSpec as P

HEADS = 25
HEAD_DIM = 64
SLOTS = 4
SLOT_WIDTH = SLOTS * HEAD_DIM
STRIDE = 3 * HEAD_DIM
BLOCK = 256

bf16 = jnp.bfloat16
f32 = jnp.float32


LAYOUT = (("x", 4), ("zl", 2), ("c", 2), ("y", 4), ("zh", 2))
REP = ("x", "zl", "c")
GRP = ("y", "zh")
TEAM = ("y", "c")
REPLICAS = ("zl", "x", "zh")
ROLES = [(0, 0), (1, 2), (2, 1), (3, 3)]


def swap_roles(value):
    return lax.ppermute(value, ("c", "zh"), ROLES)


def other_core(value):
    return lax.ppermute(value, "c", [(0, 1), (1, 0)])


def exchange(parts, axes):
    return lax.all_to_all(parts, axes, 0, 0)


def gather(block, axes):
    return lax.all_gather(block, axes, axis=0)


def team_sum(parts):
    return lax.psum_scatter(parts.astype(bf16), TEAM, scatter_dimension=0, tiled=True).astype(f32)


def windows(rows, count):
    tiles = rows // 8
    starts = [tiles * i // count for i in range(count)]
    size = max(b - a for a, b in zip(starts, starts[1:] + [tiles]))
    return size * 8, [8 * s for s in starts]


def joined(parts, starts, rows, axis):
    ends = starts[1:] + [rows]
    return jnp.concatenate(
        [lax.slice_in_dim(p, 0, e - s, axis=axis) for p, s, e in zip(parts, starts, ends)], axis
    )


def norm_parts(value, gain, shift):
    center = value - jnp.mean(value, axis=-1, keepdims=True)
    spread = jnp.mean(center * center, axis=-1, keepdims=True)
    factor = lax.rsqrt(spread + 1e-05)
    normed = center * factor
    return (normed * gain + shift, normed, factor)


def norm_back(grad_value, normed, factor, gain):
    grad_normed = grad_value * gain
    mean_first = jnp.mean(grad_normed, axis=-1, keepdims=True)
    mean_second = jnp.mean(grad_normed * normed, axis=-1, keepdims=True)
    return factor * (grad_normed - mean_first - normed * mean_second)


def dot(left, right):
    return jnp.dot(left, right, preferred_element_type=f32)


def dot_rows(left, right):
    return lax.dot_general(left, right, (((0,), (0,)), ((), ())), preferred_element_type=f32)


def dot_cols(left, right):
    return lax.dot_general(left, right, (((1,), (1,)), ((), ())), preferred_element_type=f32)


def call(kernel, name, out_shape, *operands, scratch=(), flops=0):
    specs = [
        pl.BlockSpec(memory_space=pltpu.SMEM if op.dtype == jnp.int32 else pltpu.VMEM)
        for op in operands
    ]
    out_specs = jax.tree.map(lambda _: pl.BlockSpec(memory_space=pltpu.VMEM), out_shape)
    moved = sum(op.size * op.dtype.itemsize for op in operands)
    moved += sum(o.size * o.dtype.itemsize for o in jax.tree.leaves(out_shape))
    return pl.pallas_call(
        kernel,
        out_shape=out_shape,
        in_specs=specs,
        out_specs=out_specs,
        scratch_shapes=list(scratch),
        compiler_params=pltpu.CompilerParams(vmem_limit_bytes=56 * 2**20),
        cost_estimate=pl.CostEstimate(
            flops=int(flops), bytes_accessed=int(moved), transcendentals=0
        ),
        name=name,
    )(*operands)


def struct(shape, dtype):
    return jax.ShapeDtypeStruct(shape, dtype)


def qkv_columns_kernel(place_ref, weight_ref, out_ref):
    c = place_ref[0]
    width = weight_ref.shape[1] // 3
    for part in range(3):
        for y in range(4):
            start = part * width + 2 * STRIDE * y
            even = weight_ref[:, start : start + SLOT_WIDTH]
            odd = weight_ref[:, start + STRIDE : start + STRIDE + SLOT_WIDTH]
            block = jnp.where(c == 0, even, odd)
            for zh in range(2):
                out_ref[2 * y + zh, :, part * SLOT_WIDTH : (part + 1) * SLOT_WIDTH] = block


def fc_columns_kernel(place_ref, weight_ref, out_ref):
    c = place_ref[0]
    hidden = weight_ref.shape[1] // 8
    for y in range(4):
        start = 2 * hidden * y
        even = weight_ref[:, start : start + hidden]
        odd = weight_ref[:, start + hidden : start + 2 * hidden]
        out_ref[y] = jnp.where(c == 0, even, odd)


def attend_kernel(tokens_ref, cols_ref, norm_ref, bias_ref, first_ref, qkv_ref, out_ref, top_ref):
    length = tokens_ref.shape[0]
    gain = norm_ref[0:1, :]
    shift = norm_ref[1:2, :]
    for block in range(length // BLOCK):
        rows = slice(block * BLOCK, (block + 1) * BLOCK)
        first = norm_parts(tokens_ref[rows, :].astype(f32), gain, shift)[0].astype(bf16)
        first_ref[rows, :] = first
        qkv_ref[rows, :] = (dot(first, cols_ref[...]) + bias_ref[...]).astype(bf16)
    for head in range(SLOTS):
        lanes = slice(head * HEAD_DIM, (head + 1) * HEAD_DIM)
        keys = qkv_ref[:, SLOT_WIDTH + head * HEAD_DIM : SLOT_WIDTH + (head + 1) * HEAD_DIM]
        values = qkv_ref[
            :, 2 * SLOT_WIDTH + head * HEAD_DIM : 2 * SLOT_WIDTH + (head + 1) * HEAD_DIM
        ]
        for block in range(length // BLOCK):
            rows = slice(block * BLOCK, (block + 1) * BLOCK)
            width = (block + 1) * BLOCK
            query = qkv_ref[rows, lanes] * bf16(1.0 / math.sqrt(HEAD_DIM))
            scores = dot_cols(query, keys[:width])
            row = lax.broadcasted_iota(jnp.int32, (BLOCK, width), 0) + block * BLOCK
            col = lax.broadcasted_iota(jnp.int32, (BLOCK, width), 1)
            scores = jnp.where(col <= row, scores, -1e30)
            top = jnp.max(scores, axis=-1, keepdims=True)
            probs = jnp.exp(scores - top)
            total = jnp.sum(probs, axis=-1, keepdims=True)
            mixed = dot(probs.astype(bf16), values[:width])
            out_ref[rows, lanes] = (mixed / total).astype(bf16)
            top_ref[rows, head : head + 1] = top + jnp.log(total)


def branch_kernel(
    place_ref, slots_ref, own_ref, other_ref, tokens_ref, norm_ref, middle_ref, second_ref, parts_ref, flat_ref
):
    c = place_ref[0]
    shard = own_ref.shape[1]
    for rank in range(8):
        wide = STRIDE if rank < 7 else SLOT_WIDTH
        flat_ref[:, STRIDE * rank : STRIDE * rank + wide] = slots_ref[rank, :, :wide]
    for rank in range(8):
        parts_ref[rank] = flat_ref[:, shard * rank : shard * (rank + 1)]
    total = tokens_ref[...].astype(f32) + norm_ref[4:5, :]
    for y in range(4):
        total = total + dot(parts_ref[2 * y + c], own_ref[y])
        total = total + dot(parts_ref[2 * y + 1 - c], other_ref[y])
    middle_ref[...] = total
    second_ref[...] = norm_parts(total, norm_ref[5:6, :], norm_ref[6:7, :])[0].astype(bf16)


def branch_back_kernel(
    place_ref,
    grad_ref,
    middle_ref,
    cot_ref,
    norm_ref,
    own_ref,
    other_ref,
    grad_middle_ref,
    branch_ref,
    slots_ref,
    sums_ref,
    parts_ref,
    flat_ref,
):
    c = place_ref[0]
    shard = own_ref.shape[1]
    gain = norm_ref[5:6, :]
    _, normed, factor = norm_parts(middle_ref[...], gain, gain)
    grad = grad_ref[...].astype(f32)
    cot = cot_ref[...].astype(f32)
    grad_middle = cot + norm_back(grad, normed, factor, gain)
    branch = grad_middle.astype(bf16)
    grad_middle_ref[...] = grad_middle
    branch_ref[...] = branch
    for y in range(4):
        parts_ref[2 * y + c] = dot_cols(branch, own_ref[y]).astype(bf16)
        parts_ref[2 * y + 1 - c] = dot_cols(branch, other_ref[y]).astype(bf16)
    for rank in range(8):
        flat_ref[:, shard * rank : shard * (rank + 1)] = parts_ref[rank]
    for rank in range(8):
        slots_ref[rank] = flat_ref[:, STRIDE * rank : STRIDE * rank + SLOT_WIDTH]
    sums_ref[0:1, :] = jnp.sum(branch.astype(f32), axis=0, keepdims=True)
    sums_ref[1:2, :] = jnp.sum(grad * normed, axis=0, keepdims=True)
    sums_ref[2:3, :] = jnp.sum(grad, axis=0, keepdims=True)
    sums_ref[3:4, :] = jnp.sum(cot, axis=0, keepdims=True)


def hidden_kernel(
    second_ref, cols_ref, bias_ref, grad_ref, active_ref, hidden_ref, sums_ref, out_ref
):
    length = second_ref.shape[0]
    sums = jnp.zeros(sums_ref.shape, f32)
    for block in range(length // BLOCK):
        rows = slice(block * BLOCK, (block + 1) * BLOCK)
        pre = dot(second_ref[rows, :], cols_ref[...]) + bias_ref[...]
        square = pre * pre
        bent = jnp.tanh(0.7978845608028654 * (pre + 0.044715 * square * pre))
        half = 0.5 * (1.0 + bent)
        active_ref[rows, :] = (pre * half).astype(bf16)
        slope = half + 0.5 * pre * (1.0 - bent * bent) * (
            0.7978845608028654 + (3.0 * 0.044715 * 0.7978845608028654) * square
        )
        grad = (grad_ref[rows, :] * slope).astype(bf16)
        hidden_ref[rows, :] = grad
        sums = sums + jnp.sum(grad.astype(f32), axis=0, keepdims=True)
        out_ref[rows, :] = dot_cols(grad, cols_ref[...]).astype(bf16)
    sums_ref[...] = sums


def attend_back_kernel(
    place_ref, qkv_ref, grad_ref, out_ref, top_ref, cols_ref, mixed_ref, first_ref, sums_ref, query_ref
):
    length = qkv_ref.shape[0]
    scale = 1.0 / math.sqrt(HEAD_DIM)
    ones = jnp.ones((8, HEAD_DIM), bf16)
    for head in range(SLOTS):
        base = head * HEAD_DIM
        lanes = slice(base, base + HEAD_DIM)
        key_lanes = slice(SLOT_WIDTH + base, SLOT_WIDTH + base + HEAD_DIM)
        value_lanes = slice(2 * SLOT_WIDTH + base, 2 * SLOT_WIDTH + base + HEAD_DIM)
        query = qkv_ref[:, lanes] * bf16(scale)
        grad = grad_ref[:, lanes]
        if head == SLOTS - 1:
            grad = jnp.where(place_ref[1] == 7, grad, jnp.zeros_like(grad))
        top = top_ref[head : head + 1, :]
        delta = dot_cols(ones, grad * out_ref[:, lanes])[0:1, :]
        for block in range(length // BLOCK):
            start = block * BLOCK
            rows = slice(start, start + BLOCK)
            width = length - start
            keys = qkv_ref[rows, key_lanes]
            values = qkv_ref[rows, value_lanes]
            scores = dot_cols(keys, query[start:])
            row = lax.broadcasted_iota(jnp.int32, (BLOCK, width), 0)
            col = lax.broadcasted_iota(jnp.int32, (BLOCK, width), 1)
            probs = jnp.where(row <= col, jnp.exp(scores - top[:, start:]), 0.0)
            grad_probs = dot_cols(values, grad[start:])
            grad_scores = (probs * (grad_probs - delta[:, start:])).astype(bf16)
            mixed_ref[rows, value_lanes] = dot(probs.astype(bf16), grad[start:]).astype(bf16)
            mixed_ref[rows, key_lanes] = dot(grad_scores, query[start:]).astype(bf16)
            term = dot_rows(grad_scores, keys)
            if block == 0:
                query_ref[...] = term
            else:
                query_ref[start:, :] += term
        mixed_ref[:, lanes] = (query_ref[...] * scale).astype(bf16)
    sums = jnp.zeros(sums_ref.shape, f32)
    for block in range(length // BLOCK):
        rows = slice(block * BLOCK, (block + 1) * BLOCK)
        mixed = mixed_ref[rows, :]
        sums = sums + jnp.sum(mixed.astype(f32), axis=0, keepdims=True)
        first_ref[rows, :] = dot_cols(mixed, cols_ref[...]).astype(bf16)
    sums_ref[...] = sums


def input_back_kernel(grad_ref, tokens_ref, middle_ref, norm_ref, out_ref, sums_ref):
    gain = norm_ref[0:1, :]
    _, normed, factor = norm_parts(tokens_ref[...].astype(f32), gain, gain)
    grad = grad_ref[...].astype(f32)
    out_ref[...] = (middle_ref[...] + norm_back(grad, normed, factor, gain)).astype(bf16)
    sums_ref[0:1, :] = jnp.sum(grad * normed, axis=0, keepdims=True)
    sums_ref[1:2, :] = jnp.sum(grad, axis=0, keepdims=True)


def column_grad_kernel(left_ref, right_ref, out_ref):
    shard = left_ref.shape[1] // 8
    size, starts = windows(shard, 8)
    grad = dot_rows(left_ref[...], right_ref[...])
    for y in range(4):
        for zh in range(2):
            base = (2 * y + zh) * shard
            for i, start in enumerate(starts):
                out_ref[2 * i + zh, y] = grad[base + start : base + start + size].astype(bf16)


def row_grad_kernel(left_ref, right_ref, out_ref):
    size, starts = windows(left_ref.shape[1], 16)
    grad = dot_rows(left_ref[...], right_ref[...])
    for i, start in enumerate(starts):
        out_ref[i] = grad[start : start + size].astype(bf16)


def qkv_total_kernel(place_ref, own_ref, other_ref, out_ref):
    c = place_ref[0]
    width = out_ref.shape[1] // 3
    _, starts = windows(out_ref.shape[0], 8)
    ends = starts[1:] + [out_ref.shape[0]]
    for i, (start, end) in enumerate(zip(starts, ends)):
        for rank in range(8):
            own, other = own_ref[i, rank // 2], other_ref[i, rank // 2]
            block = jnp.where(c == rank % 2, own, other)[: end - start].astype(f32)
            wide = STRIDE if rank < 7 else SLOT_WIDTH
            for part in range(3):
                lanes = slice(part * width + STRIDE * rank, part * width + STRIDE * rank + wide)
                out_ref[start:end, lanes] = block[
                    :, part * SLOT_WIDTH : part * SLOT_WIDTH + wide
                ]


def fc_total_kernel(place_ref, own_ref, other_ref, out_ref):
    c = place_ref[0]
    hidden = out_ref.shape[1] // 8
    _, starts = windows(out_ref.shape[0], 8)
    ends = starts[1:] + [out_ref.shape[0]]
    for i, (start, end) in enumerate(zip(starts, ends)):
        for rank in range(8):
            own, other = own_ref[i, rank // 2], other_ref[i, rank // 2]
            block = jnp.where(c == rank % 2, own, other)[: end - start].astype(f32)
            out_ref[start:end, rank * hidden : (rank + 1) * hidden] = block


def row_total_kernel(place_ref, own_ref, other_ref, out_ref):
    mine = place_ref[2]
    _, starts = windows(out_ref.shape[0], 16)
    ends = starts[1:] + [out_ref.shape[0]]
    for i, (start, end) in enumerate(zip(starts, ends)):
        block = jnp.where(mine == 1, own_ref[i], other_ref[i])
        out_ref[start:end, :] = block[: end - start].astype(f32)


def after(value, *others):
    return lax.optimization_barrier((value,) + others)[0]


def per_device(
    tokens,
    ln1_gain,
    ln1_bias,
    w_qkv,
    bias_q,
    bias_v,
    w_out,
    bias_out,
    ln2_gain,
    ln2_bias,
    w_fc,
    bias_fc,
    w_proj,
    bias_proj,
    cotangent,
):
    _, span, width = tokens.shape
    shard = width // 8
    hidden = w_fc.shape[1] // 8
    length = span * 8
    slots = 3 * SLOT_WIDTH
    c = lax.axis_index("c")
    zh = lax.axis_index("zh")
    rank = lax.axis_index("y") * 2 + c
    place = jnp.stack([c, rank, (c == zh).astype(jnp.int32)]).astype(jnp.int32)

    own_tokens = swap_roles(tokens.reshape(span, width))
    small = jnp.concatenate(
        [ln1_gain, ln1_bias, bias_q, bias_v, bias_out, ln2_gain, ln2_bias, bias_proj, bias_fc]
    ).reshape(3, hidden)
    qkv_parts = call(
        qkv_columns_kernel, "qkv_columns", struct((8, shard, slots), bf16), place, w_qkv
    )
    small_all = exchange(jnp.broadcast_to(small, (8, 3, hidden)), GRP).astype(f32)
    hidden_bias = lax.dynamic_index_in_dim(small_all, rank, 0, keepdims=False)[2:3]
    vectors = small_all[:, :2].reshape(8, 8, shard).transpose(1, 0, 2).reshape(8, width)
    all_tokens = gather(own_tokens, TEAM).reshape(length, width)
    qkv_cols = exchange(qkv_parts, GRP).reshape(width, slots)
    out_rows = swap_roles(w_out)
    own_cot = swap_roles(cotangent.reshape(span, width))
    fc_parts = call(fc_columns_kernel, "fc_columns", struct((4, shard, hidden), bf16), place, w_fc)

    bias_slots = jnp.concatenate(
        [
            lax.dynamic_slice_in_dim(vectors[2], STRIDE * rank, SLOT_WIDTH),
            jnp.zeros((SLOT_WIDTH,), f32),
            lax.dynamic_slice_in_dim(vectors[3], STRIDE * rank, SLOT_WIDTH),
        ]
    ).reshape(1, slots)
    out_rows, own_cot, fc_parts, qkv_cols, all_tokens = lax.optimization_barrier(
        (out_rows, own_cot, fc_parts, qkv_cols, all_tokens)
    )
    out_own = exchange(jnp.broadcast_to(out_rows, (4, shard, width)), "y")
    all_cot = gather(own_cot, TEAM).reshape(length, width)
    fc_own = exchange(fc_parts, "y")

    first, qkv, attended_slots, top = call(
        attend_kernel,
        "attend",
        (
            struct((length, width), bf16),
            struct((length, slots), bf16),
            struct((length, SLOT_WIDTH), bf16),
            struct((length, SLOTS), f32),
        ),
        all_tokens,
        qkv_cols,
        vectors,
        bias_slots,
        flops=2 * length * width * slots,
    )
    out_other = other_core(out_own)
    attended = exchange(attended_slots.reshape(8, span, SLOT_WIDTH), TEAM)
    middle, second, attended_parts = call(
        branch_kernel,
        "branch",
        (
            struct((span, width), f32),
            struct((span, width), bf16),
            struct((8, span, shard), bf16),
        ),
        place,
        attended,
        out_own,
        out_other,
        own_tokens,
        vectors,
        scratch=[pltpu.VMEM((span, width), bf16)],
        flops=2 * span * width * width,
    )

    second_all = gather(second, TEAM).reshape(length, width)
    proj_rows = swap_roles(after(w_proj, fc_own))
    fc_other = lax.ppermute(fc_own, "zh", [(0, 1), (1, 0)])
    fc_cols = jnp.where(
        zh == 0, jnp.stack([fc_own, fc_other], 1), jnp.stack([fc_other, fc_own], 1)
    ).reshape(width, hidden)
    grad_active = dot_cols(all_cot, proj_rows)
    active, grad_hidden, hidden_sums, second_parts = call(
        hidden_kernel,
        "hidden",
        (
            struct((length, hidden), bf16),
            struct((length, hidden), bf16),
            struct((1, hidden), f32),
            struct((length, width), bf16),
        ),
        second_all,
        fc_cols,
        hidden_bias,
        grad_active,
        flops=4 * length * width * hidden,
    )
    grad_second = team_sum(second_parts)
    proj_parts = call(
        row_grad_kernel,
        "proj_grad",
        struct((16, windows(hidden, 16)[0], width), bf16),
        active,
        all_cot,
        flops=2 * length * width * hidden,
    )
    proj_parts = exchange(proj_parts, REPLICAS)
    fc_grad = call(
        column_grad_kernel,
        "fc_grad",
        struct((16, 4, windows(shard, 8)[0], hidden), bf16),
        second_all,
        grad_hidden,
        flops=2 * length * width * hidden,
    )
    down_parts = dot(active, proj_rows).astype(bf16)
    fc_grad = exchange(fc_grad, REPLICAS)

    grad_middle, grad_branch, grad_slots, branch_sums = call(
        branch_back_kernel,
        "branch_back",
        (
            struct((span, width), f32),
            struct((span, width), bf16),
            struct((8, span, SLOT_WIDTH), bf16),
            struct((4, width), f32),
        ),
        place,
        grad_second,
        middle,
        own_cot,
        vectors,
        out_own,
        out_other,
        scratch=[pltpu.VMEM((8, span, shard), bf16), pltpu.VMEM((span, width), bf16)],
        flops=2 * span * width * width,
    )
    grad_heads = exchange(grad_slots, TEAM).reshape(length, SLOT_WIDTH)
    branch_all = gather(after(grad_branch, grad_heads), TEAM).reshape(length, width)
    grad_mixed, first_parts, mixed_sums = call(
        attend_back_kernel,
        "attend_back",
        (
            struct((length, slots), bf16),
            struct((length, width), bf16),
            struct((1, slots), f32),
        ),
        place,
        qkv,
        grad_heads,
        attended_slots,
        top.T,
        qkv_cols,
        scratch=[pltpu.VMEM((length, HEAD_DIM), f32)],
        flops=2 * length * width * slots,
    )
    grad_first = team_sum(first_parts)
    qkv_grad = call(
        column_grad_kernel,
        "qkv_grad",
        struct((16, 4, windows(shard, 8)[0], slots), bf16),
        first,
        grad_mixed,
        flops=2 * length * width * slots,
    )
    qkv_grad = exchange(qkv_grad, REPLICAS)

    def replica_sum(parts):
        return jnp.sum(parts.astype(f32), axis=0).astype(bf16)

    proj_parts = replica_sum(after(proj_parts, grad_mixed))
    fc_grad = exchange(replica_sum(after(fc_grad, grad_mixed)), "y")
    attended_own = exchange(after(attended_parts, grad_mixed), TEAM).reshape(length, shard)
    out_grad = call(
        row_grad_kernel,
        "out_grad",
        struct((16, windows(shard, 16)[0], width), bf16),
        attended_own,
        branch_all,
        flops=2 * length * width * shard,
    )
    out_grad = exchange(out_grad, REPLICAS)
    output = middle + (team_sum(after(down_parts, first_parts)) + vectors[7])

    grad_inputs, first_sums = call(
        input_back_kernel,
        "input_back",
        (struct((span, width), bf16), struct((2, width), f32)),
        grad_first,
        own_tokens,
        grad_middle,
        vectors,
    )
    inputs_home = swap_roles(grad_inputs).astype(f32).reshape(1, span, width)

    blank = jnp.zeros((1, width), f32)
    at = (0, STRIDE * rank)
    small_terms = jnp.concatenate(
        [
            first_sums,
            lax.dynamic_update_slice(blank, mixed_sums[:, :SLOT_WIDTH], at),
            lax.dynamic_update_slice(blank, mixed_sums[:, 2 * SLOT_WIDTH :], at),
            branch_sums,
        ]
    )
    hidden_term = lax.dynamic_update_slice(
        jnp.zeros((8, hidden), f32), hidden_sums, (rank, 0)
    )
    small_terms = small_terms.reshape(8, 8, shard).transpose(1, 0, 2).reshape(8, 2, hidden)
    small_terms = jnp.concatenate([small_terms, hidden_term[:, None]], axis=1)
    small_sum = jnp.sum(exchange(small_terms, GRP), axis=0)
    small_sum = jnp.sum(exchange(jnp.broadcast_to(small_sum, (16, 3, hidden)), REP), axis=0)
    owned = small_sum[:2].reshape(8, shard)

    def row_total(parts, rows, name):
        whole = gather(parts, REPLICAS)
        return call(
            row_total_kernel, name, struct((rows, width), f32), place, whole, other_core(whole)
        )

    proj_total = row_total(proj_parts, hidden, "proj_total")
    fc_whole = gather(fc_grad, ("zl", "x"))
    fc_total = call(
        fc_total_kernel,
        "fc_total",
        struct((shard, 8 * hidden), f32),
        place,
        fc_whole,
        other_core(fc_whole),
    )
    qkv_grad = exchange(replica_sum(qkv_grad), "y")
    qkv_whole = exchange(jnp.broadcast_to(qkv_grad, (8,) + qkv_grad.shape), ("zl", "x"))
    out_total = row_total(replica_sum(out_grad), shard, "out_total")
    qkv_total = call(
        qkv_total_kernel,
        "qkv_total",
        struct((shard, 3 * width), f32),
        place,
        qkv_whole,
        other_core(qkv_whole),
    )

    output_home = swap_roles(output.astype(bf16)).reshape(1, span, width)
    return (
        output_home,
        inputs_home,
        owned[0],
        owned[1],
        qkv_total,
        owned[2],
        owned[3],
        out_total,
        owned[4],
        owned[5],
        owned[6],
        fc_total,
        small_sum[2],
        proj_total,
        owned[7],
    )


def solution(mesh):
    names = tuple(name for name, _ in LAYOUT)
    fine = jax.sharding.Mesh(mesh.devices.reshape([size for _, size in LAYOUT]), names)
    in_specs = (
        P(REP, GRP, None),
        P(GRP),
        P(GRP),
        P(GRP, None),
        P(GRP),
        P(GRP),
        P(GRP, None),
        P(GRP),
        P(GRP),
        P(GRP),
        P(GRP, None),
        P(GRP),
        P(GRP, None),
        P(GRP),
        P(REP, GRP, None),
    )
    out_specs = (
        P(REP, GRP, None),
        P(REP, GRP, None),
        P(GRP),
        P(GRP),
        P(GRP, None),
        P(GRP),
        P(GRP),
        P(GRP, None),
        P(GRP),
        P(GRP),
        P(GRP),
        P(GRP, None),
        P(GRP),
        P(GRP, None),
        P(GRP),
    )
    return jax.shard_map(
        per_device, mesh=fine, in_specs=in_specs, out_specs=out_specs, check_vma=False
    )
```

```python
import functools
import math

import jax
import jax.numpy as jnp
from jax import lax
from jax.experimental import pallas as pl
from jax.experimental.pallas import tpu as pltpu
from jax.sharding import PartitionSpec as P

HEADS = 25
HEAD_DIM = 64
SLOTS = 4
SLOT_WIDTH = SLOTS * HEAD_DIM
STRIDE = 3 * HEAD_DIM
BLOCK = 256

bf16 = jnp.bfloat16
f32 = jnp.float32


LAYOUT = (("x", 4), ("zl", 2), ("c", 2), ("y", 4), ("zh", 2))
REP = ("x", "zl", "c")
GRP = ("y", "zh")
TEAM = ("y", "c")
REPLICAS = ("zl", "x", "zh")
Z_RING = ("zl", "zh")
Z_PLACES = (0, 2, 1, 3)
ROLES = [(0, 0), (1, 2), (2, 1), (3, 3)]


def ring(value, axis, step):
    index = Z_PLACES if axis == Z_RING else range(4)
    return lax.ppermute(value, axis, [(index[(i + step) % 4], index[i]) for i in range(4)])


def ring_all(values, axis):
    return [values[0]] + [ring(values[k], axis, k) for k in range(1, 4)]


def flipped(value, axis):
    return lax.ppermute(value, axis, [(0, 1), (1, 0)])


def swap_roles(value):
    return lax.ppermute(value, ("c", "zh"), ROLES)


def other_core(value):
    return lax.ppermute(value, "c", [(0, 1), (1, 0)])


def exchange(parts, axes):
    return lax.all_to_all(parts, axes, 0, 0)


def gather(block, axes):
    return lax.all_gather(block, axes, axis=0)


def team_sum(parts):
    return lax.psum_scatter(parts.astype(bf16), TEAM, scatter_dimension=0, tiled=True).astype(f32)


def windows(rows, count):
    tiles = rows // 8
    starts = [tiles * i // count for i in range(count)]
    size = max(b - a for a, b in zip(starts, starts[1:] + [tiles]))
    return size * 8, [8 * s for s in starts]


def joined(parts, starts, rows, axis):
    ends = starts[1:] + [rows]
    return jnp.concatenate(
        [lax.slice_in_dim(p, 0, e - s, axis=axis) for p, s, e in zip(parts, starts, ends)], axis
    )


def norm_parts(value, gain, shift):
    center = value - jnp.mean(value, axis=-1, keepdims=True)
    spread = jnp.mean(center * center, axis=-1, keepdims=True)
    factor = lax.rsqrt(spread + 1e-05)
    normed = center * factor
    return (normed * gain + shift, normed, factor)


def norm_back(grad_value, normed, factor, gain):
    grad_normed = grad_value * gain
    mean_first = jnp.mean(grad_normed, axis=-1, keepdims=True)
    mean_second = jnp.mean(grad_normed * normed, axis=-1, keepdims=True)
    return factor * (grad_normed - mean_first - normed * mean_second)


def dot(left, right):
    return jnp.dot(left, right, preferred_element_type=f32)


def dot_rows(left, right):
    return lax.dot_general(left, right, (((0,), (0,)), ((), ())), preferred_element_type=f32)


def dot_cols(left, right):
    return lax.dot_general(left, right, (((1,), (1,)), ((), ())), preferred_element_type=f32)


def call(kernel, name, out_shape, *operands, scratch=(), flops=0):
    specs = [
        pl.BlockSpec(memory_space=pltpu.SMEM if op.dtype == jnp.int32 else pltpu.VMEM)
        for op in operands
    ]
    out_specs = jax.tree.map(lambda _: pl.BlockSpec(memory_space=pltpu.VMEM), out_shape)
    moved = sum(op.size * op.dtype.itemsize for op in operands)
    moved += sum(o.size * o.dtype.itemsize for o in jax.tree.leaves(out_shape))
    return pl.pallas_call(
        kernel,
        out_shape=out_shape,
        in_specs=specs,
        out_specs=out_specs,
        scratch_shapes=list(scratch),
        compiler_params=pltpu.CompilerParams(vmem_limit_bytes=56 * 2**20),
        cost_estimate=pl.CostEstimate(
            flops=int(flops), bytes_accessed=int(moved), transcendentals=0
        ),
        name=name,
    )(*operands)


def struct(shape, dtype):
    return jax.ShapeDtypeStruct(shape, dtype)


Y, C, RANK, ZH, Z, X, ZL, MINE = range(8)


def qkv_columns_kernel(place_ref, weight_ref, *refs):
    out_refs, held_ref = refs[:4], refs[4]
    c = place_ref[C]
    width = weight_ref.shape[1] // 3
    for part in range(3):
        lanes = slice(part * SLOT_WIDTH, (part + 1) * SLOT_WIDTH)
        for y in range(4):
            start = part * width + 2 * STRIDE * y
            even = weight_ref[:, start : start + SLOT_WIDTH]
            odd = weight_ref[:, start + STRIDE : start + STRIDE + SLOT_WIDTH]
            held_ref[y, :, lanes] = jnp.where(c == 0, even, odd)
    for k in range(4):
        out_refs[k][...] = held_ref[lax.rem(place_ref[Y] + 4 - k, 4)]


def fc_columns_kernel(place_ref, weight_ref, *refs):
    out_refs, held_ref = refs[:4], refs[4]
    c = place_ref[C]
    hidden = weight_ref.shape[1] // 8
    for y in range(4):
        start = 2 * hidden * y
        even = weight_ref[:, start : start + hidden]
        odd = weight_ref[:, start + hidden : start + 2 * hidden]
        held_ref[y] = jnp.where(c == 0, even, odd)
    for k in range(4):
        out_refs[k][...] = held_ref[lax.rem(place_ref[Y] + 4 - k, 4)]


def fc_whole_kernel(place_ref, *refs):
    out_ref = refs[8]
    zh = place_ref[ZH]
    for k in range(4):
        y = lax.rem(place_ref[Y] + k, 4)
        out_ref[2 * y + zh] = refs[k][...]
        out_ref[2 * y + 1 - zh] = refs[4 + k][...]


def branch_kernel(place_ref, slots_ref, tokens_ref, norm_ref, *refs):
    rows_refs, (middle_ref, second_ref, parts_ref, flat_ref) = refs[:8], refs[8:]
    c = place_ref[C]
    shard = rows_refs[0].shape[0]
    for rank in range(8):
        wide = STRIDE if rank < 7 else SLOT_WIDTH
        flat_ref[:, STRIDE * rank : STRIDE * rank + wide] = slots_ref[rank, :, :wide]
    for rank in range(8):
        parts_ref[rank] = flat_ref[:, shard * rank : shard * (rank + 1)]
    total = tokens_ref[...].astype(f32) + norm_ref[4:5, :]
    for k in range(4):
        y = lax.rem(place_ref[Y] + k, 4)
        total = total + dot(parts_ref[2 * y + c], rows_refs[k][...])
        total = total + dot(parts_ref[2 * y + 1 - c], rows_refs[4 + k][...])
    middle_ref[...] = total
    second_ref[...] = norm_parts(total, norm_ref[5:6, :], norm_ref[6:7, :])[0].astype(bf16)


def branch_back_kernel(place_ref, grad_ref, middle_ref, cot_ref, norm_ref, *refs):
    rows_refs = refs[:8]
    grad_middle_ref, branch_ref, slots_ref, sums_ref, parts_ref, flat_ref = refs[8:]
    c = place_ref[C]
    shard = rows_refs[0].shape[0]
    gain = norm_ref[5:6, :]
    _, normed, factor = norm_parts(middle_ref[...], gain, gain)
    grad = grad_ref[...].astype(f32)
    cot = cot_ref[...].astype(f32)
    grad_middle = cot + norm_back(grad, normed, factor, gain)
    branch = grad_middle.astype(bf16)
    grad_middle_ref[...] = grad_middle
    branch_ref[...] = branch
    for k in range(4):
        y = lax.rem(place_ref[Y] + k, 4)
        parts_ref[2 * y + c] = dot_cols(branch, rows_refs[k][...]).astype(bf16)
        parts_ref[2 * y + 1 - c] = dot_cols(branch, rows_refs[4 + k][...]).astype(bf16)
    for rank in range(8):
        flat_ref[:, shard * rank : shard * (rank + 1)] = parts_ref[rank]
    for rank in range(8):
        slots_ref[rank] = flat_ref[:, STRIDE * rank : STRIDE * rank + SLOT_WIDTH]
    sums_ref[0:1, :] = jnp.sum(branch.astype(f32), axis=0, keepdims=True)
    sums_ref[1:2, :] = jnp.sum(grad * normed, axis=0, keepdims=True)
    sums_ref[2:3, :] = jnp.sum(grad, axis=0, keepdims=True)
    sums_ref[3:4, :] = jnp.sum(cot, axis=0, keepdims=True)


def column_grad_kernel(left_ref, right_ref, out_ref):
    shard = left_ref.shape[1] // 8
    size, starts = windows(shard, 8)
    grad = dot_rows(left_ref[...], right_ref[...])
    for y in range(4):
        for zh in range(2):
            base = (2 * y + zh) * shard
            for i, start in enumerate(starts):
                out_ref[2 * i + zh, y] = grad[base + start : base + start + size].astype(bf16)


def column_ring_kernel(place_ref, left_ref, right_ref, *refs):
    out_refs, held_ref = refs[:4], refs[4]
    shard = left_ref.shape[1] // 8
    size, starts = windows(shard, 8)
    held_ref[...] = dot_rows(left_ref[...], right_ref[...])
    for k in range(4):
        x = lax.rem(place_ref[X] + 4 - k, 4)
        for z in range(4):
            for y in range(4):
                base = (2 * y + z // 2) * shard + starts[4 * (z % 2)]
                at = pl.multiple_of(base + starts[1] * x, 8)
                out_refs[k][z, y] = held_ref[pl.ds(at, size), :].astype(bf16)


def row_start(rows, index):
    return pl.multiple_of(lax.div(rows // 8 * index, 16) * 8, 8)


def row_ring_kernel(place_ref, left_ref, right_ref, *refs):
    out_refs, held_ref = refs[:4], refs[4]
    rows = left_ref.shape[1]
    size = windows(rows, 16)[0]
    held_ref[...] = dot_rows(left_ref[...], right_ref[...])
    for k in range(4):
        z = lax.rem(place_ref[Z] + 4 - k, 4)
        for x in range(4):
            at = row_start(rows, (lax.rem(z, 2) * 4 + x) * 2 + lax.div(z, 2))
            out_refs[k][x] = held_ref[pl.ds(at, size), :].astype(bf16)


def out_grad_kernel(place_ref, left_ref, *refs):
    blocks, out_ref, held_ref = refs[:8], refs[8], refs[9]
    c = place_ref[C]
    rows = left_ref.shape[2]
    size, starts = windows(rows, 16)
    for k in range(4):
        y = lax.rem(place_ref[Y] + k, 4)
        term = dot_rows(left_ref[2 * y + c], blocks[k][...])
        term = term + dot_rows(left_ref[2 * y + 1 - c], blocks[4 + k][...])
        if k == 0:
            held_ref[...] = term
        else:
            held_ref[...] += term
    for i, start in enumerate(starts):
        out_ref[i] = held_ref[start : start + size, :].astype(bf16)


def fold_kernel(which, place_ref, *refs):
    for k in range(4):
        at = lax.rem(place_ref[which] + 4 - k, 4)
        total = refs[0][at].astype(f32)
        for j in range(1, 4):
            total = total + refs[j][at].astype(f32)
        refs[4 + k][...] = total.astype(bf16)


def stack_kernel(*refs):
    for k, ref in enumerate(refs[:-1]):
        refs[-1][k] = ref[...]


def column_total_kernel(spans, ringed, place_ref, *refs):
    out_ref = refs[8]
    shard = out_ref.shape[0]
    _, starts = windows(shard, 8)
    step = starts[1]
    for j in range(4):
        x = lax.rem(place_ref[X] + j, 4)
        for flip in range(2):
            window = (place_ref[ZL] if flip == 0 else 1 - place_ref[ZL]) * 4 + x
            at = pl.multiple_of(window * step, 8)
            for rank in range(8):
                k = lax.rem(rank // 2 + 4 - place_ref[Y], 4) if ringed else rank // 2
                block = jnp.where(
                    place_ref[C] == rank % 2, refs[j][flip, k], refs[4 + j][flip, k]
                ).astype(f32)
                for source, target, wide in spans[rank]:
                    out_ref[pl.ds(at, step), target : target + wide] = block[
                        :step, source : source + wide
                    ]

                @pl.when(window == 7)
                def _(block=block, rank=rank):
                    for source, target, wide in spans[rank]:
                        out_ref[7 * step + step :, target : target + wide] = block[
                            step:, source : source + wide
                        ]


def row_total_kernel(place_ref, own_ref, other_ref, out_ref):
    mine = place_ref[MINE]
    _, starts = windows(out_ref.shape[0], 16)
    ends = starts[1:] + [out_ref.shape[0]]
    for i, (start, end) in enumerate(zip(starts, ends)):
        block = jnp.where(mine == 1, own_ref[i], other_ref[i])
        out_ref[start:end, :] = block[: end - start].astype(f32)


def attend_kernel(place_ref, tokens_ref, norm_ref, bias_ref, *refs):
    pieces, (first_ref, qkv_ref, out_ref, top_ref, cols_ref) = refs[:8], refs[8:]
    length = tokens_ref.shape[0]
    shard = cols_ref.shape[1]
    zh = place_ref[ZH]
    for k in range(4):
        y = lax.rem(place_ref[Y] + k, 4)
        cols_ref[2 * y + zh] = pieces[k][...]
        cols_ref[2 * y + 1 - zh] = pieces[4 + k][...]
    gain = norm_ref[0:1, :]
    shift = norm_ref[1:2, :]
    for block in range(length // BLOCK):
        rows = slice(block * BLOCK, (block + 1) * BLOCK)
        first = norm_parts(tokens_ref[rows, :].astype(f32), gain, shift)[0].astype(bf16)
        first_ref[rows, :] = first
        mixed = bias_ref[...]
        for g in range(8):
            mixed = mixed + dot(first[:, g * shard : (g + 1) * shard], cols_ref[g])
        qkv_ref[rows, :] = mixed.astype(bf16)
    for head in range(SLOTS):
        lanes = slice(head * HEAD_DIM, (head + 1) * HEAD_DIM)
        keys = qkv_ref[:, SLOT_WIDTH + head * HEAD_DIM : SLOT_WIDTH + (head + 1) * HEAD_DIM]
        values = qkv_ref[
            :, 2 * SLOT_WIDTH + head * HEAD_DIM : 2 * SLOT_WIDTH + (head + 1) * HEAD_DIM
        ]
        for block in range(length // BLOCK):
            rows = slice(block * BLOCK, (block + 1) * BLOCK)
            width = (block + 1) * BLOCK
            query = qkv_ref[rows, lanes] * bf16(1.0 / math.sqrt(HEAD_DIM))
            scores = dot_cols(query, keys[:width])
            row = lax.broadcasted_iota(jnp.int32, (BLOCK, width), 0) + block * BLOCK
            col = lax.broadcasted_iota(jnp.int32, (BLOCK, width), 1)
            scores = jnp.where(col <= row, scores, -1e30)
            top = jnp.max(scores, axis=-1, keepdims=True)
            probs = jnp.exp(scores - top)
            total = jnp.sum(probs, axis=-1, keepdims=True)
            mixed = dot(probs.astype(bf16), values[:width])
            out_ref[rows, lanes] = (mixed / total).astype(bf16)
            top_ref[rows, head : head + 1] = top + jnp.log(total)


def hidden_kernel(
    place_ref, second_ref, cols_ref, bias_ref, grad_ref, active_ref, hidden_ref, sums_ref, out_ref
):
    length = second_ref.shape[0]
    sums = jnp.zeros(sums_ref.shape, f32)
    for block in range(length // BLOCK):
        rows = slice(block * BLOCK, (block + 1) * BLOCK)
        pre = dot(second_ref[rows, :], cols_ref[...]) + bias_ref[...]
        square = pre * pre
        bent = jnp.tanh(0.7978845608028654 * (pre + 0.044715 * square * pre))
        half = 0.5 * (1.0 + bent)
        active_ref[rows, :] = (pre * half).astype(bf16)
        slope = half + 0.5 * pre * (1.0 - bent * bent) * (
            0.7978845608028654 + (3.0 * 0.044715 * 0.7978845608028654) * square
        )
        grad = (grad_ref[rows, :] * slope).astype(bf16)
        hidden_ref[rows, :] = grad
        sums = sums + jnp.sum(grad.astype(f32), axis=0, keepdims=True)
        out_ref[rows, :] = dot_cols(grad, cols_ref[...]).astype(bf16)
    sums_ref[...] = sums


def attend_back_kernel(
    place_ref, qkv_ref, grad_ref, out_ref, top_ref, cols_ref, mixed_ref, first_ref, sums_ref, query_ref
):
    length = qkv_ref.shape[0]
    scale = 1.0 / math.sqrt(HEAD_DIM)
    ones = jnp.ones((8, HEAD_DIM), bf16)
    for head in range(SLOTS):
        base = head * HEAD_DIM
        lanes = slice(base, base + HEAD_DIM)
        key_lanes = slice(SLOT_WIDTH + base, SLOT_WIDTH + base + HEAD_DIM)
        value_lanes = slice(2 * SLOT_WIDTH + base, 2 * SLOT_WIDTH + base + HEAD_DIM)
        query = qkv_ref[:, lanes] * bf16(scale)
        grad = grad_ref[:, lanes]
        if head == SLOTS - 1:
            grad = jnp.where(place_ref[RANK] == 7, grad, jnp.zeros_like(grad))
        top = top_ref[head : head + 1, :]
        delta = dot_cols(ones, grad * out_ref[:, lanes])[0:1, :]
        for block in range(length // BLOCK):
            start = block * BLOCK
            rows = slice(start, start + BLOCK)
            width = length - start
            keys = qkv_ref[rows, key_lanes]
            values = qkv_ref[rows, value_lanes]
            scores = dot_cols(keys, query[start:])
            row = lax.broadcasted_iota(jnp.int32, (BLOCK, width), 0)
            col = lax.broadcasted_iota(jnp.int32, (BLOCK, width), 1)
            probs = jnp.where(row <= col, jnp.exp(scores - top[:, start:]), 0.0)
            grad_probs = dot_cols(values, grad[start:])
            grad_scores = (probs * (grad_probs - delta[:, start:])).astype(bf16)
            mixed_ref[rows, value_lanes] = dot(probs.astype(bf16), grad[start:]).astype(bf16)
            mixed_ref[rows, key_lanes] = dot(grad_scores, query[start:]).astype(bf16)
            term = dot_rows(grad_scores, keys)
            if block == 0:
                query_ref[...] = term
            else:
                query_ref[start:, :] += term
        mixed_ref[:, lanes] = (query_ref[...] * scale).astype(bf16)
    sums = jnp.zeros(sums_ref.shape, f32)
    for block in range(length // BLOCK):
        rows = slice(block * BLOCK, (block + 1) * BLOCK)
        mixed = mixed_ref[rows, :]
        sums = sums + jnp.sum(mixed.astype(f32), axis=0, keepdims=True)
        first_ref[rows, :] = dot_cols(mixed, cols_ref[...]).astype(bf16)
    sums_ref[...] = sums


def input_back_kernel(grad_ref, tokens_ref, middle_ref, norm_ref, out_ref, sums_ref):
    gain = norm_ref[0:1, :]
    _, normed, factor = norm_parts(tokens_ref[...].astype(f32), gain, gain)
    grad = grad_ref[...].astype(f32)
    out_ref[...] = (middle_ref[...] + norm_back(grad, normed, factor, gain)).astype(bf16)
    sums_ref[0:1, :] = jnp.sum(grad * normed, axis=0, keepdims=True)
    sums_ref[1:2, :] = jnp.sum(grad, axis=0, keepdims=True)


def after(value, *others):
    return lax.optimization_barrier((value,) + others)[0]


def per_device(
    tokens,
    ln1_gain,
    ln1_bias,
    w_qkv,
    bias_q,
    bias_v,
    w_out,
    bias_out,
    ln2_gain,
    ln2_bias,
    w_fc,
    bias_fc,
    w_proj,
    bias_proj,
    cotangent,
):
    _, span, width = tokens.shape
    shard = width // 8
    hidden = w_fc.shape[1] // 8
    length = span * 8
    slots = 3 * SLOT_WIDTH
    x, zl, c, y, zh = [lax.axis_index(name) for name, _ in LAYOUT]
    rank = y * 2 + c
    place = jnp.stack(
        [y, c, rank, zh, zh * 2 + zl, x, zl, (c == zh).astype(jnp.int32)]
    ).astype(jnp.int32)

    own_tokens = swap_roles(tokens.reshape(span, width))
    small = jnp.concatenate(
        [ln1_gain, ln1_bias, bias_q, bias_v, bias_out, ln2_gain, ln2_bias, bias_proj, bias_fc]
    ).reshape(3, hidden)
    all_tokens = gather(own_tokens, TEAM).reshape(length, width)
    qkv_parts = call(
        qkv_columns_kernel,
        "qkv_columns",
        [struct((shard, slots), bf16)] * 4,
        place,
        w_qkv,
        scratch=[pltpu.VMEM((4, shard, slots), bf16)],
    )
    qkv_own = ring_all(qkv_parts, "y")
    qkv_other = [flipped(part, "zh") for part in qkv_own]
    small_all = exchange(jnp.broadcast_to(small, (8, 3, hidden)), GRP).astype(f32)
    hidden_bias = lax.dynamic_index_in_dim(small_all, rank, 0, keepdims=False)[2:3]
    vectors = small_all[:, :2].reshape(8, 8, shard).transpose(1, 0, 2).reshape(8, width)
    bias_slots = jnp.concatenate(
        [
            lax.dynamic_slice_in_dim(vectors[2], STRIDE * rank, SLOT_WIDTH),
            jnp.zeros((SLOT_WIDTH,), f32),
            lax.dynamic_slice_in_dim(vectors[3], STRIDE * rank, SLOT_WIDTH),
        ]
    ).reshape(1, slots)
    out_rows = swap_roles(w_out)
    own_cot = swap_roles(cotangent.reshape(span, width))
    fc_parts = call(
        fc_columns_kernel,
        "fc_columns",
        [struct((shard, hidden), bf16)] * 4,
        place,
        w_fc,
        scratch=[pltpu.VMEM((4, shard, hidden), bf16)],
    )

    out_own = ring_all([after(out_rows, *qkv_own)] * 4, "y")
    out_other = [other_core(part) for part in out_own]
    all_cot = gather(after(own_cot, all_tokens), TEAM).reshape(length, width)
    fc_own = ring_all([after(part, *qkv_own) for part in fc_parts], "y")
    fc_other = [flipped(after(part, *qkv_other), "zh") for part in fc_own]
    proj_rows = swap_roles(after(w_proj, *fc_other))

    first, qkv, attended_slots, top, qkv_cols = call(
        attend_kernel,
        "attend",
        (
            struct((length, width), bf16),
            struct((length, slots), bf16),
            struct((length, SLOT_WIDTH), bf16),
            struct((length, SLOTS), f32),
            struct((8, shard, slots), bf16),
        ),
        after(place, bias_slots, out_rows, own_cot, *fc_own),
        all_tokens,
        vectors,
        bias_slots,
        *qkv_own,
        *qkv_other,
        flops=2 * length * width * slots,
    )
    qkv_cols = qkv_cols.reshape(width, slots)
    attended = exchange(attended_slots.reshape(8, span, SLOT_WIDTH), TEAM)
    middle, second, attended_parts = call(
        branch_kernel,
        "branch",
        (
            struct((span, width), f32),
            struct((span, width), bf16),
            struct((8, span, shard), bf16),
        ),
        after(place, *fc_other),
        attended,
        own_tokens,
        vectors,
        *out_own,
        *out_other,
        scratch=[pltpu.VMEM((span, width), bf16)],
        flops=2 * span * width * width,
    )

    second_all = gather(second, TEAM).reshape(length, width)
    attended_own = exchange(attended_parts, TEAM)
    grad_active = dot_cols(after(all_cot, second), proj_rows)
    fc_cols = call(
        fc_whole_kernel,
        "fc_whole",
        struct((8, shard, hidden), bf16),
        place,
        after(fc_own[0], second),
        *fc_own[1:],
        *fc_other,
    ).reshape(width, hidden)
    active, grad_hidden, hidden_sums, second_parts = call(
        hidden_kernel,
        "hidden",
        (
            struct((length, hidden), bf16),
            struct((length, hidden), bf16),
            struct((1, hidden), f32),
            struct((length, width), bf16),
        ),
        after(place, attended_own),
        second_all,
        fc_cols,
        hidden_bias,
        grad_active,
        flops=4 * length * width * hidden,
    )
    grad_second = team_sum(second_parts)
    window = windows(shard, 8)[0]
    fc_grad = call(
        column_ring_kernel,
        "fc_grad",
        [struct((4, 4, window, hidden), bf16)] * 4,
        place,
        second_all,
        grad_hidden,
        scratch=[pltpu.VMEM((width, hidden), f32)],
        flops=2 * length * width * hidden,
    )
    fc_grad = ring_all(fc_grad, "x")
    row_window = windows(hidden, 16)[0]
    proj_grad = call(
        row_ring_kernel,
        "proj_grad",
        [struct((4, row_window, width), bf16)] * 4,
        place,
        active,
        all_cot,
        scratch=[pltpu.VMEM((hidden, width), f32)],
        flops=2 * length * width * hidden,
    )
    proj_grad = ring_all(proj_grad, Z_RING)
    down_parts = dot(active, proj_rows).astype(bf16)

    grad_middle, grad_branch, grad_slots, branch_sums = call(
        branch_back_kernel,
        "branch_back",
        (
            struct((span, width), f32),
            struct((span, width), bf16),
            struct((8, span, SLOT_WIDTH), bf16),
            struct((4, width), f32),
        ),
        after(place, fc_grad[0], proj_grad[0], down_parts),
        grad_second,
        middle,
        own_cot,
        vectors,
        *out_own,
        *out_other,
        scratch=[pltpu.VMEM((8, span, shard), bf16), pltpu.VMEM((span, width), bf16)],
        flops=2 * span * width * width,
    )
    grad_heads = exchange(grad_slots, TEAM).reshape(length, SLOT_WIDTH)
    down = team_sum(after(down_parts, grad_second))
    branch_own = ring_all([after(grad_branch, grad_heads)] * 4, "y")

    def fold(which, parts, name, *behind):
        parts = [after(parts[0], *behind)] + parts[1:]
        return call(
            functools.partial(fold_kernel, which),
            name,
            [struct(parts[0].shape[1:], bf16)] * 4,
            place,
            *parts,
        )

    fc_grad = ring_all(fold(Z, fc_grad, "fc_fold", grad_slots), Z_RING)
    proj_grad = ring_all(fold(X, proj_grad, "proj_fold", grad_slots), "x")
    grad_mixed, first_parts, mixed_sums = call(
        attend_back_kernel,
        "attend_back",
        (
            struct((length, slots), bf16),
            struct((length, width), bf16),
            struct((1, slots), f32),
        ),
        after(place, fc_grad[0], proj_grad[0]),
        qkv,
        grad_heads,
        attended_slots,
        top.T,
        qkv_cols,
        scratch=[pltpu.VMEM((length, HEAD_DIM), f32)],
        flops=2 * length * width * slots,
    )
    grad_first = team_sum(after(first_parts, down))
    qkv_grad = call(
        column_grad_kernel,
        "qkv_grad",
        struct((16, 4, window, slots), bf16),
        first,
        grad_mixed,
        flops=2 * length * width * slots,
    )
    qkv_grad = exchange(qkv_grad, REPLICAS)

    grad_inputs, first_sums = call(
        input_back_kernel,
        "input_back",
        (struct((span, width), bf16), struct((2, width), f32)),
        grad_first,
        own_tokens,
        grad_middle,
        vectors,
    )

    blank = jnp.zeros((1, width), f32)
    at = (0, STRIDE * rank)
    small_terms = jnp.concatenate(
        [
            first_sums,
            lax.dynamic_update_slice(blank, mixed_sums[:, :SLOT_WIDTH], at),
            lax.dynamic_update_slice(blank, mixed_sums[:, 2 * SLOT_WIDTH :], at),
            branch_sums,
        ]
    )
    hidden_term = lax.dynamic_update_slice(
        jnp.zeros((8, hidden), f32), hidden_sums, (rank, 0)
    )
    small_terms = small_terms.reshape(8, 8, shard).transpose(1, 0, 2).reshape(8, 2, hidden)
    small_terms = jnp.concatenate([small_terms, hidden_term[:, None]], axis=1)
    small_sum = jnp.sum(exchange(small_terms, GRP), axis=0)
    small_sum = jnp.sum(exchange(jnp.broadcast_to(small_sum, (16, 3, hidden)), REP), axis=0)
    owned = small_sum[:2].reshape(8, shard)

    def replica_sum(parts):
        return jnp.sum(parts.astype(f32), axis=0).astype(bf16)

    def stacked(parts, name):
        return call(
            stack_kernel, name, struct((len(parts),) + parts[0].shape, bf16), *parts
        )

    def column_spread(parts, name):
        near = stacked(parts, name + "_near")
        both = stacked([near, flipped(near, "zl")], name + "_both")
        own = ring_all([both] * 4, "x")
        return own + [other_core(part) for part in own]

    def row_total(parts, rows, name):
        whole = gather(parts, REPLICAS)
        return call(
            row_total_kernel, name, struct((rows, width), f32), place, whole, other_core(whole)
        )

    fc_grad = ring_all(fold(Y, fc_grad, "fc_fold_last", grad_mixed), "y")
    fc_pieces = column_spread(fc_grad, "fc")
    proj_grad = [after(proj_grad[0], grad_mixed)] + proj_grad[1:]
    proj_sum = sum(part.astype(f32) for part in proj_grad).astype(bf16)
    proj_total = row_total(after(proj_sum, grad_first), hidden, "proj_total")
    branch_own = [after(branch_own[0], grad_mixed)] + branch_own[1:]
    branch_other = [other_core(part) for part in branch_own]
    out_grad = call(
        out_grad_kernel,
        "out_grad",
        struct((16, windows(shard, 16)[0], width), bf16),
        place,
        attended_own,
        *branch_own,
        *branch_other,
        scratch=[pltpu.VMEM((shard, width), f32)],
        flops=2 * length * width * shard,
    )
    out_grad = exchange(after(out_grad, qkv_grad), REPLICAS)
    out_total = row_total(replica_sum(out_grad), shard, "out_total")

    fc_spans = [[(0, rank * hidden, hidden)] for rank in range(8)]
    fc_total = call(
        functools.partial(column_total_kernel, fc_spans, True),
        "fc_total",
        struct((shard, 8 * hidden), f32),
        place,
        *fc_pieces,
    )
    qkv_sum = replica_sum(after(qkv_grad, grad_inputs))
    qkv_sum = exchange(qkv_sum, "y")
    both = stacked([qkv_sum, flipped(qkv_sum, "zl")], "qkv_both")
    own = ring_all([both] * 4, "x")
    qkv_pieces = own + [other_core(part) for part in own]
    qkv_spans = [
        [
            (p * SLOT_WIDTH, p * width + STRIDE * r, STRIDE if r < 7 else SLOT_WIDTH)
            for p in range(3)
        ]
        for r in range(8)
    ]
    qkv_total = call(
        functools.partial(column_total_kernel, qkv_spans, False),
        "qkv_total",
        struct((shard, 3 * width), f32),
        after(place, small_sum, grad_inputs),
        *qkv_pieces,
    )

    inputs_home = swap_roles(grad_inputs).astype(f32).reshape(1, span, width)
    output = middle + (down + vectors[7])
    output_home = swap_roles(output.astype(bf16)).reshape(1, span, width)

    return (
        output_home,
        inputs_home,
        owned[0],
        owned[1],
        qkv_total,
        owned[2],
        owned[3],
        out_total,
        owned[4],
        owned[5],
        owned[6],
        fc_total,
        small_sum[2],
        proj_total,
        owned[7],
    )


def solution(mesh):
    names = tuple(name for name, _ in LAYOUT)
    fine = jax.sharding.Mesh(mesh.devices.reshape([size for _, size in LAYOUT]), names)
    in_specs = (
        P(REP, GRP, None),
        P(GRP),
        P(GRP),
        P(GRP, None),
        P(GRP),
        P(GRP),
        P(GRP, None),
        P(GRP),
        P(GRP),
        P(GRP),
        P(GRP, None),
        P(GRP),
        P(GRP, None),
        P(GRP),
        P(REP, GRP, None),
    )
    out_specs = (
        P(REP, GRP, None),
        P(REP, GRP, None),
        P(GRP),
        P(GRP),
        P(GRP, None),
        P(GRP),
        P(GRP),
        P(GRP, None),
        P(GRP),
        P(GRP),
        P(GRP),
        P(GRP, None),
        P(GRP),
        P(GRP, None),
        P(GRP),
    )
    return jax.shard_map(
        per_device, mesh=fine, in_specs=in_specs, out_specs=out_specs, check_vma=False
    )
```

```python
import functools
import math

import jax
import jax.numpy as jnp
from jax import lax
from jax.experimental import pallas as pl
from jax.experimental.pallas import tpu as pltpu
from jax.sharding import PartitionSpec as P

HEADS = 25
HEAD_DIM = 64
SLOTS = 4
SLOT_WIDTH = SLOTS * HEAD_DIM
STRIDE = 3 * HEAD_DIM
BLOCK = 256

bf16 = jnp.bfloat16
f32 = jnp.float32


LAYOUT = (("x", 4), ("zl", 2), ("c", 2), ("y", 4), ("zh", 2))
REP = ("x", "zl", "c")
GRP = ("y", "zh")
TEAM = ("y", "c")
REPLICAS = ("zl", "x", "zh")
Z_RING = ("zl", "zh")
Z_PLACES = (0, 2, 1, 3)
ROLES = [(0, 0), (1, 2), (2, 1), (3, 3)]


def ring(value, axis, step):
    index = Z_PLACES if axis == Z_RING else range(4)
    return lax.ppermute(value, axis, [(index[(i + step) % 4], index[i]) for i in range(4)])


def ring_all(values, axis):
    return [values[0]] + [ring(values[k], axis, k) for k in range(1, 4)]


def flipped(value, axis):
    return lax.ppermute(value, axis, [(0, 1), (1, 0)])


def swap_roles(value):
    return lax.ppermute(value, ("c", "zh"), ROLES)


def other_core(value):
    return lax.ppermute(value, "c", [(0, 1), (1, 0)])


def exchange(parts, axes):
    return lax.all_to_all(parts, axes, 0, 0)


def gather(block, axes):
    return lax.all_gather(block, axes, axis=0)


def team_sum(parts):
    return lax.psum_scatter(parts.astype(bf16), TEAM, scatter_dimension=0, tiled=True).astype(f32)


def windows(rows, count):
    tiles = rows // 8
    starts = [tiles * i // count for i in range(count)]
    size = max(b - a for a, b in zip(starts, starts[1:] + [tiles]))
    return size * 8, [8 * s for s in starts]


def joined(parts, starts, rows, axis):
    ends = starts[1:] + [rows]
    return jnp.concatenate(
        [lax.slice_in_dim(p, 0, e - s, axis=axis) for p, s, e in zip(parts, starts, ends)], axis
    )


def norm_parts(value, gain, shift):
    center = value - jnp.mean(value, axis=-1, keepdims=True)
    spread = jnp.mean(center * center, axis=-1, keepdims=True)
    factor = lax.rsqrt(spread + 1e-05)
    normed = center * factor
    return (normed * gain + shift, normed, factor)


def norm_back(grad_value, normed, factor, gain):
    grad_normed = grad_value * gain
    mean_first = jnp.mean(grad_normed, axis=-1, keepdims=True)
    mean_second = jnp.mean(grad_normed * normed, axis=-1, keepdims=True)
    return factor * (grad_normed - mean_first - normed * mean_second)


def dot(left, right):
    return jnp.dot(left, right, preferred_element_type=f32)


def dot_rows(left, right):
    return lax.dot_general(left, right, (((0,), (0,)), ((), ())), preferred_element_type=f32)


def dot_cols(left, right):
    return lax.dot_general(left, right, (((1,), (1,)), ((), ())), preferred_element_type=f32)


def call(kernel, name, out_shape, *operands, scratch=(), flops=0):
    specs = [
        pl.BlockSpec(memory_space=pltpu.SMEM if op.dtype == jnp.int32 else pltpu.VMEM)
        for op in operands
    ]
    out_specs = jax.tree.map(lambda _: pl.BlockSpec(memory_space=pltpu.VMEM), out_shape)
    moved = sum(op.size * op.dtype.itemsize for op in operands)
    moved += sum(o.size * o.dtype.itemsize for o in jax.tree.leaves(out_shape))
    return pl.pallas_call(
        kernel,
        out_shape=out_shape,
        in_specs=specs,
        out_specs=out_specs,
        scratch_shapes=list(scratch),
        compiler_params=pltpu.CompilerParams(vmem_limit_bytes=56 * 2**20),
        cost_estimate=pl.CostEstimate(
            flops=int(flops), bytes_accessed=int(moved), transcendentals=0
        ),
        name=name,
    )(*operands)


def struct(shape, dtype):
    return jax.ShapeDtypeStruct(shape, dtype)


Y, C, RANK, ZH, Z, X, ZL, MINE = range(8)


def qkv_columns_kernel(place_ref, weight_ref, *refs):
    out_refs, held_ref = refs[:4], refs[4]
    c = place_ref[C]
    width = weight_ref.shape[1] // 3
    for part in range(3):
        lanes = slice(part * SLOT_WIDTH, (part + 1) * SLOT_WIDTH)
        for y in range(4):
            start = part * width + 2 * STRIDE * y
            even = weight_ref[:, start : start + SLOT_WIDTH]
            odd = weight_ref[:, start + STRIDE : start + STRIDE + SLOT_WIDTH]
            held_ref[y, :, lanes] = jnp.where(c == 0, even, odd)
    for k in range(4):
        out_refs[k][...] = held_ref[lax.rem(place_ref[Y] + 4 - k, 4)]


def fc_columns_kernel(place_ref, weight_ref, *refs):
    out_refs, held_ref = refs[:4], refs[4]
    c = place_ref[C]
    hidden = weight_ref.shape[1] // 8
    for y in range(4):
        start = 2 * hidden * y
        even = weight_ref[:, start : start + hidden]
        odd = weight_ref[:, start + hidden : start + 2 * hidden]
        held_ref[y] = jnp.where(c == 0, even, odd)
    for k in range(4):
        out_refs[k][...] = held_ref[lax.rem(place_ref[Y] + 4 - k, 4)]


def fc_whole_kernel(place_ref, *refs):
    out_ref = refs[8]
    zh = place_ref[ZH]
    for k in range(4):
        y = lax.rem(place_ref[Y] + k, 4)
        out_ref[2 * y + zh] = refs[k][...]
        out_ref[2 * y + 1 - zh] = refs[4 + k][...]


def branch_kernel(place_ref, slots_ref, tokens_ref, norm_ref, *refs):
    rows_refs, (middle_ref, second_ref, parts_ref, flat_ref) = refs[:8], refs[8:]
    c = place_ref[C]
    shard = rows_refs[0].shape[0]
    for rank in range(8):
        wide = STRIDE if rank < 7 else SLOT_WIDTH
        flat_ref[:, STRIDE * rank : STRIDE * rank + wide] = slots_ref[rank, :, :wide]
    for rank in range(8):
        parts_ref[rank] = flat_ref[:, shard * rank : shard * (rank + 1)]
    total = tokens_ref[...].astype(f32) + norm_ref[4:5, :]
    for k in range(4):
        y = lax.rem(place_ref[Y] + k, 4)
        total = total + dot(parts_ref[2 * y + c], rows_refs[k][...])
        total = total + dot(parts_ref[2 * y + 1 - c], rows_refs[4 + k][...])
    middle_ref[...] = total
    second_ref[...] = norm_parts(total, norm_ref[5:6, :], norm_ref[6:7, :])[0].astype(bf16)


def branch_back_kernel(place_ref, grad_ref, middle_ref, cot_ref, norm_ref, *refs):
    rows_refs = refs[:8]
    grad_middle_ref, branch_ref, slots_ref, sums_ref, parts_ref, flat_ref = refs[8:]
    c = place_ref[C]
    shard = rows_refs[0].shape[0]
    gain = norm_ref[5:6, :]
    _, normed, factor = norm_parts(middle_ref[...], gain, gain)
    grad = grad_ref[...].astype(f32)
    cot = cot_ref[...].astype(f32)
    grad_middle = cot + norm_back(grad, normed, factor, gain)
    branch = grad_middle.astype(bf16)
    grad_middle_ref[...] = grad_middle
    branch_ref[...] = branch
    for k in range(4):
        y = lax.rem(place_ref[Y] + k, 4)
        parts_ref[2 * y + c] = dot_cols(branch, rows_refs[k][...]).astype(bf16)
        parts_ref[2 * y + 1 - c] = dot_cols(branch, rows_refs[4 + k][...]).astype(bf16)
    for rank in range(8):
        flat_ref[:, shard * rank : shard * (rank + 1)] = parts_ref[rank]
    for rank in range(8):
        slots_ref[rank] = flat_ref[:, STRIDE * rank : STRIDE * rank + SLOT_WIDTH]
    sums_ref[0:1, :] = jnp.sum(branch.astype(f32), axis=0, keepdims=True)
    sums_ref[1:2, :] = jnp.sum(grad * normed, axis=0, keepdims=True)
    sums_ref[2:3, :] = jnp.sum(grad, axis=0, keepdims=True)
    sums_ref[3:4, :] = jnp.sum(cot, axis=0, keepdims=True)


def column_grad_kernel(left_ref, right_ref, out_ref):
    shard = left_ref.shape[1] // 8
    size, starts = windows(shard, 8)
    grad = dot_rows(left_ref[...], right_ref[...])
    for y in range(4):
        for zh in range(2):
            base = (2 * y + zh) * shard
            for i, start in enumerate(starts):
                out_ref[2 * i + zh, y] = grad[base + start : base + start + size].astype(bf16)


def column_ring_kernel(place_ref, left_ref, right_ref, *refs):
    out_refs, held_ref = refs[:4], refs[4]
    shard = left_ref.shape[1] // 8
    size, starts = windows(shard, 8)
    held_ref[...] = dot_rows(left_ref[...], right_ref[...])
    for k in range(4):
        x = lax.rem(place_ref[X] + 4 - k, 4)
        for z in range(4):
            for y in range(4):
                base = (2 * y + z // 2) * shard + starts[4 * (z % 2)]
                at = pl.multiple_of(base + starts[1] * x, 8)
                out_refs[k][z, y] = held_ref[pl.ds(at, size), :].astype(bf16)


def row_start(rows, index):
    return pl.multiple_of(lax.div(rows // 8 * index, 16) * 8, 8)


def row_ring_kernel(place_ref, left_ref, right_ref, *refs):
    out_refs, held_ref = refs[:4], refs[4]
    rows = left_ref.shape[1]
    size = windows(rows, 16)[0]
    held_ref[...] = dot_rows(left_ref[...], right_ref[...])
    for k in range(4):
        z = lax.rem(place_ref[Z] + 4 - k, 4)
        for x in range(4):
            at = row_start(rows, (lax.rem(z, 2) * 4 + x) * 2 + lax.div(z, 2))
            out_refs[k][x] = held_ref[pl.ds(at, size), :].astype(bf16)


def out_grad_kernel(place_ref, left_ref, *refs):
    blocks, out_ref, held_ref = refs[:8], refs[8], refs[9]
    c = place_ref[C]
    rows = left_ref.shape[2]
    size, starts = windows(rows, 16)
    for k in range(4):
        y = lax.rem(place_ref[Y] + k, 4)
        term = dot_rows(left_ref[2 * y + c], blocks[k][...])
        term = term + dot_rows(left_ref[2 * y + 1 - c], blocks[4 + k][...])
        if k == 0:
            held_ref[...] = term
        else:
            held_ref[...] += term
    for i, start in enumerate(starts):
        out_ref[i] = held_ref[start : start + size, :].astype(bf16)


def fold_kernel(which, place_ref, *refs):
    for k in range(4):
        at = lax.rem(place_ref[which] + 4 - k, 4)
        total = refs[0][at].astype(f32)
        for j in range(1, 4):
            total = total + refs[j][at].astype(f32)
        refs[4 + k][...] = total.astype(bf16)


def stack_kernel(*refs):
    for k, ref in enumerate(refs[:-1]):
        refs[-1][k] = ref[...]


def column_total_kernel(spans, ringed, place_ref, *refs):
    out_ref = refs[8]
    shard = out_ref.shape[0]
    _, starts = windows(shard, 8)
    step = starts[1]
    for j in range(4):
        x = lax.rem(place_ref[X] + j, 4)
        for flip in range(2):
            window = (place_ref[ZL] if flip == 0 else 1 - place_ref[ZL]) * 4 + x
            at = pl.multiple_of(window * step, 8)
            for rank in range(8):
                k = lax.rem(rank // 2 + 4 - place_ref[Y], 4) if ringed else rank // 2
                block = jnp.where(
                    place_ref[C] == rank % 2, refs[j][flip, k], refs[4 + j][flip, k]
                ).astype(f32)
                for source, target, wide in spans[rank]:
                    out_ref[pl.ds(at, step), target : target + wide] = block[
                        :step, source : source + wide
                    ]

                @pl.when(window == 7)
                def _(block=block, rank=rank):
                    for source, target, wide in spans[rank]:
                        out_ref[7 * step + step :, target : target + wide] = block[
                            step:, source : source + wide
                        ]


def row_total_kernel(place_ref, own_ref, other_ref, out_ref):
    mine = place_ref[MINE]
    _, starts = windows(out_ref.shape[0], 16)
    ends = starts[1:] + [out_ref.shape[0]]
    for i, (start, end) in enumerate(zip(starts, ends)):
        block = jnp.where(mine == 1, own_ref[i], other_ref[i])
        out_ref[start:end, :] = block[: end - start].astype(f32)


def attend_kernel(place_ref, tokens_ref, norm_ref, bias_ref, *refs):
    pieces, (first_ref, qkv_ref, out_ref, top_ref, cols_ref) = refs[:8], refs[8:]
    length = tokens_ref.shape[0]
    shard = cols_ref.shape[1]
    zh = place_ref[ZH]
    for k in range(4):
        y = lax.rem(place_ref[Y] + k, 4)
        cols_ref[2 * y + zh] = pieces[k][...]
        cols_ref[2 * y + 1 - zh] = pieces[4 + k][...]
    gain = norm_ref[0:1, :]
    shift = norm_ref[1:2, :]
    for block in range(length // BLOCK):
        rows = slice(block * BLOCK, (block + 1) * BLOCK)
        first = norm_parts(tokens_ref[rows, :].astype(f32), gain, shift)[0].astype(bf16)
        first_ref[rows, :] = first
        mixed = bias_ref[...]
        for g in range(8):
            mixed = mixed + dot(first[:, g * shard : (g + 1) * shard], cols_ref[g])
        qkv_ref[rows, :] = mixed.astype(bf16)
    for head in range(SLOTS):
        lanes = slice(head * HEAD_DIM, (head + 1) * HEAD_DIM)
        keys = qkv_ref[:, SLOT_WIDTH + head * HEAD_DIM : SLOT_WIDTH + (head + 1) * HEAD_DIM]
        values = qkv_ref[
            :, 2 * SLOT_WIDTH + head * HEAD_DIM : 2 * SLOT_WIDTH + (head + 1) * HEAD_DIM
        ]
        for block in range(length // BLOCK):
            rows = slice(block * BLOCK, (block + 1) * BLOCK)
            width = (block + 1) * BLOCK
            query = qkv_ref[rows, lanes] * bf16(1.0 / math.sqrt(HEAD_DIM))
            scores = dot_cols(query, keys[:width])
            row = lax.broadcasted_iota(jnp.int32, (BLOCK, width), 0) + block * BLOCK
            col = lax.broadcasted_iota(jnp.int32, (BLOCK, width), 1)
            scores = jnp.where(col <= row, scores, -1e30)
            top = jnp.max(scores, axis=-1, keepdims=True)
            probs = jnp.exp(scores - top)
            total = jnp.sum(probs, axis=-1, keepdims=True)
            mixed = dot(probs.astype(bf16), values[:width])
            out_ref[rows, lanes] = (mixed / total).astype(bf16)
            top_ref[rows, head : head + 1] = top + jnp.log(total)


def hidden_kernel(
    place_ref, second_ref, cols_ref, bias_ref, grad_ref, active_ref, hidden_ref, sums_ref, out_ref
):
    length = second_ref.shape[0]
    sums = jnp.zeros(sums_ref.shape, f32)
    for block in range(length // BLOCK):
        rows = slice(block * BLOCK, (block + 1) * BLOCK)
        pre = dot(second_ref[rows, :], cols_ref[...]) + bias_ref[...]
        square = pre * pre
        bent = jnp.tanh(0.7978845608028654 * (pre + 0.044715 * square * pre))
        half = 0.5 * (1.0 + bent)
        active_ref[rows, :] = (pre * half).astype(bf16)
        slope = half + 0.5 * pre * (1.0 - bent * bent) * (
            0.7978845608028654 + (3.0 * 0.044715 * 0.7978845608028654) * square
        )
        grad = (grad_ref[rows, :] * slope).astype(bf16)
        hidden_ref[rows, :] = grad
        sums = sums + jnp.sum(grad.astype(f32), axis=0, keepdims=True)
        out_ref[rows, :] = dot_cols(grad, cols_ref[...]).astype(bf16)
    sums_ref[...] = sums


def attend_back_kernel(
    place_ref, qkv_ref, grad_ref, out_ref, top_ref, cols_ref, mixed_ref, first_ref, sums_ref, query_ref
):
    length = qkv_ref.shape[0]
    scale = 1.0 / math.sqrt(HEAD_DIM)
    ones = jnp.ones((8, HEAD_DIM), bf16)
    for head in range(SLOTS):
        base = head * HEAD_DIM
        lanes = slice(base, base + HEAD_DIM)
        key_lanes = slice(SLOT_WIDTH + base, SLOT_WIDTH + base + HEAD_DIM)
        value_lanes = slice(2 * SLOT_WIDTH + base, 2 * SLOT_WIDTH + base + HEAD_DIM)
        query = qkv_ref[:, lanes] * bf16(scale)
        grad = grad_ref[:, lanes]
        if head == SLOTS - 1:
            grad = jnp.where(place_ref[RANK] == 7, grad, jnp.zeros_like(grad))
        top = top_ref[head : head + 1, :]
        delta = dot_cols(ones, grad * out_ref[:, lanes])[0:1, :]
        for block in range(length // BLOCK):
            start = block * BLOCK
            rows = slice(start, start + BLOCK)
            width = length - start
            keys = qkv_ref[rows, key_lanes]
            values = qkv_ref[rows, value_lanes]
            scores = dot_cols(keys, query[start:])
            row = lax.broadcasted_iota(jnp.int32, (BLOCK, width), 0)
            col = lax.broadcasted_iota(jnp.int32, (BLOCK, width), 1)
            probs = jnp.where(row <= col, jnp.exp(scores - top[:, start:]), 0.0)
            grad_probs = dot_cols(values, grad[start:])
            grad_scores = (probs * (grad_probs - delta[:, start:])).astype(bf16)
            mixed_ref[rows, value_lanes] = dot(probs.astype(bf16), grad[start:]).astype(bf16)
            mixed_ref[rows, key_lanes] = dot(grad_scores, query[start:]).astype(bf16)
            term = dot_rows(grad_scores, keys)
            if block == 0:
                query_ref[...] = term
            else:
                query_ref[start:, :] += term
        mixed_ref[:, lanes] = (query_ref[...] * scale).astype(bf16)
    sums = jnp.zeros(sums_ref.shape, f32)
    for block in range(length // BLOCK):
        rows = slice(block * BLOCK, (block + 1) * BLOCK)
        mixed = mixed_ref[rows, :]
        sums = sums + jnp.sum(mixed.astype(f32), axis=0, keepdims=True)
        first_ref[rows, :] = dot_cols(mixed, cols_ref[...]).astype(bf16)
    sums_ref[...] = sums


def input_back_kernel(grad_ref, tokens_ref, middle_ref, norm_ref, out_ref, sums_ref):
    gain = norm_ref[0:1, :]
    _, normed, factor = norm_parts(tokens_ref[...].astype(f32), gain, gain)
    grad = grad_ref[...].astype(f32)
    out_ref[...] = (middle_ref[...] + norm_back(grad, normed, factor, gain)).astype(bf16)
    sums_ref[0:1, :] = jnp.sum(grad * normed, axis=0, keepdims=True)
    sums_ref[1:2, :] = jnp.sum(grad, axis=0, keepdims=True)


def after(value, *others):
    return lax.optimization_barrier((value,) + others)[0]


def per_device(
    tokens,
    ln1_gain,
    ln1_bias,
    w_qkv,
    bias_q,
    bias_v,
    w_out,
    bias_out,
    ln2_gain,
    ln2_bias,
    w_fc,
    bias_fc,
    w_proj,
    bias_proj,
    cotangent,
):
    _, span, width = tokens.shape
    shard = width // 8
    hidden = w_fc.shape[1] // 8
    length = span * 8
    slots = 3 * SLOT_WIDTH
    x, zl, c, y, zh = [lax.axis_index(name) for name, _ in LAYOUT]
    rank = y * 2 + c
    place = jnp.stack(
        [y, c, rank, zh, zh * 2 + zl, x, zl, (c == zh).astype(jnp.int32)]
    ).astype(jnp.int32)

    own_tokens = swap_roles(tokens.reshape(span, width))
    small = jnp.concatenate(
        [ln1_gain, ln1_bias, bias_q, bias_v, bias_out, ln2_gain, ln2_bias, bias_proj, bias_fc]
    ).reshape(3, hidden)
    small_all = exchange(jnp.broadcast_to(small, (8, 3, hidden)), GRP)
    all_tokens = gather(own_tokens, TEAM).reshape(length, width)
    place = after(place, small_all)
    qkv_parts = call(
        qkv_columns_kernel,
        "qkv_columns",
        [struct((shard, slots), bf16)] * 4,
        place,
        w_qkv,
        scratch=[pltpu.VMEM((4, shard, slots), bf16)],
    )
    qkv_own = ring_all(qkv_parts, "y")
    qkv_other = [flipped(part, "zh") for part in qkv_own]
    out_rows = swap_roles(after(w_out, small_all))
    own_cot = swap_roles(after(cotangent, qkv_parts[0]).reshape(span, width))
    place = after(place, qkv_parts[0])
    fc_parts = call(
        fc_columns_kernel,
        "fc_columns",
        [struct((shard, hidden), bf16)] * 4,
        place,
        w_fc,
        scratch=[pltpu.VMEM((4, shard, hidden), bf16)],
    )
    place = after(place, fc_parts[0])

    small_all = small_all.astype(f32)
    hidden_bias = lax.dynamic_index_in_dim(small_all, rank, 0, keepdims=False)[2:3]
    vectors = small_all[:, :2].reshape(8, 8, shard).transpose(1, 0, 2).reshape(8, width)
    bias_slots = jnp.concatenate(
        [
            lax.dynamic_slice_in_dim(vectors[2], STRIDE * rank, SLOT_WIDTH),
            jnp.zeros((SLOT_WIDTH,), f32),
            lax.dynamic_slice_in_dim(vectors[3], STRIDE * rank, SLOT_WIDTH),
        ]
    ).reshape(1, slots)

    out_own = ring_all([after(out_rows, *qkv_own)] * 4, "y")
    out_other = [other_core(part) for part in out_own]
    all_cot = gather(after(own_cot, *qkv_own), TEAM).reshape(length, width)
    proj_rows = swap_roles(after(w_proj, *qkv_other))
    fc_own = ring_all([after(part, *out_own) for part in fc_parts], "y")
    fc_other = [flipped(after(part, proj_rows), "zh") for part in fc_own]

    first, qkv, attended_slots, top, qkv_cols = call(
        attend_kernel,
        "attend",
        (
            struct((length, width), bf16),
            struct((length, slots), bf16),
            struct((length, SLOT_WIDTH), bf16),
            struct((length, SLOTS), f32),
            struct((8, shard, slots), bf16),
        ),
        after(place, bias_slots),
        all_tokens,
        vectors,
        bias_slots,
        *qkv_own,
        *qkv_other,
        flops=2 * length * width * slots,
    )
    qkv_cols = qkv_cols.reshape(width, slots)
    attended = exchange(attended_slots.reshape(8, span, SLOT_WIDTH), TEAM)
    middle, second, attended_parts = call(
        branch_kernel,
        "branch",
        (
            struct((span, width), f32),
            struct((span, width), bf16),
            struct((8, span, shard), bf16),
        ),
        after(place, proj_rows, *fc_own),
        attended,
        own_tokens,
        vectors,
        *out_own,
        *out_other,
        scratch=[pltpu.VMEM((span, width), bf16)],
        flops=2 * span * width * width,
    )

    second_all = gather(second, TEAM).reshape(length, width)
    attended_own = exchange(attended_parts, TEAM)
    grad_active = dot_cols(after(all_cot, second), proj_rows)
    fc_cols = call(
        fc_whole_kernel,
        "fc_whole",
        struct((8, shard, hidden), bf16),
        place,
        after(fc_own[0], second),
        *fc_own[1:],
        *fc_other,
    ).reshape(width, hidden)
    active, grad_hidden, hidden_sums, second_parts = call(
        hidden_kernel,
        "hidden",
        (
            struct((length, hidden), bf16),
            struct((length, hidden), bf16),
            struct((1, hidden), f32),
            struct((length, width), bf16),
        ),
        after(place, attended_own),
        second_all,
        fc_cols,
        hidden_bias,
        grad_active,
        flops=4 * length * width * hidden,
    )
    grad_second = team_sum(second_parts)
    window = windows(shard, 8)[0]
    fc_grad = call(
        column_ring_kernel,
        "fc_grad",
        [struct((4, 4, window, hidden), bf16)] * 4,
        place,
        second_all,
        grad_hidden,
        scratch=[pltpu.VMEM((width, hidden), f32)],
        flops=2 * length * width * hidden,
    )
    fc_grad = ring_all(fc_grad, "x")
    row_window = windows(hidden, 16)[0]
    proj_grad = call(
        row_ring_kernel,
        "proj_grad",
        [struct((4, row_window, width), bf16)] * 4,
        place,
        active,
        all_cot,
        scratch=[pltpu.VMEM((hidden, width), f32)],
        flops=2 * length * width * hidden,
    )
    proj_grad = ring_all(proj_grad, Z_RING)
    down_parts = dot(active, proj_rows).astype(bf16)

    grad_middle, grad_branch, grad_slots, branch_sums = call(
        branch_back_kernel,
        "branch_back",
        (
            struct((span, width), f32),
            struct((span, width), bf16),
            struct((8, span, SLOT_WIDTH), bf16),
            struct((4, width), f32),
        ),
        after(place, fc_grad[0], proj_grad[0], down_parts),
        grad_second,
        middle,
        own_cot,
        vectors,
        *out_own,
        *out_other,
        scratch=[pltpu.VMEM((8, span, shard), bf16), pltpu.VMEM((span, width), bf16)],
        flops=2 * span * width * width,
    )
    grad_heads = exchange(grad_slots, TEAM).reshape(length, SLOT_WIDTH)
    down = team_sum(after(down_parts, grad_second))
    branch_own = ring_all([after(grad_branch, grad_heads)] * 4, "y")

    def fold(which, parts, name, *behind):
        parts = [after(parts[0], *behind)] + parts[1:]
        return call(
            functools.partial(fold_kernel, which),
            name,
            [struct(parts[0].shape[1:], bf16)] * 4,
            place,
            *parts,
        )

    fc_grad = ring_all(fold(Z, fc_grad, "fc_fold", grad_slots), Z_RING)
    proj_grad = ring_all(fold(X, proj_grad, "proj_fold", grad_slots), "x")
    grad_mixed, first_parts, mixed_sums = call(
        attend_back_kernel,
        "attend_back",
        (
            struct((length, slots), bf16),
            struct((length, width), bf16),
            struct((1, slots), f32),
        ),
        after(place, fc_grad[0], proj_grad[0]),
        qkv,
        grad_heads,
        attended_slots,
        top.T,
        qkv_cols,
        scratch=[pltpu.VMEM((length, HEAD_DIM), f32)],
        flops=2 * length * width * slots,
    )
    grad_first = team_sum(after(first_parts, down))
    qkv_grad = call(
        column_grad_kernel,
        "qkv_grad",
        struct((16, 4, window, slots), bf16),
        first,
        grad_mixed,
        flops=2 * length * width * slots,
    )
    place = after(place, qkv_grad)
    qkv_grad = exchange(qkv_grad, REPLICAS)

    def replica_sum(parts):
        return jnp.sum(parts.astype(f32), axis=0).astype(bf16)

    def stacked(parts, name):
        return call(
            stack_kernel, name, struct((len(parts),) + parts[0].shape, bf16), *parts
        )

    def column_spread(near, name):
        both = stacked([near, flipped(near, "zl")], name + "_both")
        own = ring_all([both] * 4, "x")
        return own + [other_core(part) for part in own]

    def row_total(whole, rows, name):
        return call(
            row_total_kernel, name, struct((rows, width), f32), place, whole, other_core(whole)
        )

    fc_grad = ring_all(fold(Y, fc_grad, "fc_fold_last", place), "y")
    proj_grad = [after(proj_grad[0], place)] + proj_grad[1:]
    proj_sum = sum(part.astype(f32) for part in proj_grad).astype(bf16)
    grad_inputs, first_sums = call(
        input_back_kernel,
        "input_back",
        (struct((span, width), bf16), struct((2, width), f32)),
        grad_first,
        own_tokens,
        grad_middle,
        after(vectors, fc_grad[0], proj_sum),
    )
    inputs_home = swap_roles(grad_inputs).astype(f32).reshape(1, span, width)
    output = middle + (after(down, grad_inputs) + vectors[7])
    output_home = swap_roles(output.astype(bf16)).reshape(1, span, width)
    proj_whole = gather(after(proj_sum, grad_first), REPLICAS)
    place = after(place, grad_inputs)
    fc_pieces = column_spread(stacked([after(fc_grad[0], place)] + fc_grad[1:], "fc_near"), "fc")

    branch_other = [other_core(part) for part in branch_own]
    out_grad = call(
        out_grad_kernel,
        "out_grad",
        struct((16, windows(shard, 16)[0], width), bf16),
        place,
        attended_own,
        *branch_own,
        *branch_other,
        scratch=[pltpu.VMEM((shard, width), f32)],
        flops=2 * length * width * shard,
    )
    place = after(place, out_grad)
    qkv_sum = exchange(replica_sum(after(qkv_grad, place)), "y")
    out_grad = exchange(after(out_grad, qkv_sum), REPLICAS)
    qkv_pieces = column_spread(qkv_sum, "qkv")

    blank = jnp.zeros((1, width), f32)
    at = (0, STRIDE * rank)
    small_terms = jnp.concatenate(
        [
            first_sums,
            lax.dynamic_update_slice(blank, mixed_sums[:, :SLOT_WIDTH], at),
            lax.dynamic_update_slice(blank, mixed_sums[:, 2 * SLOT_WIDTH :], at),
            branch_sums,
        ]
    )
    hidden_term = lax.dynamic_update_slice(
        jnp.zeros((8, hidden), f32), hidden_sums, (rank, 0)
    )
    small_terms = small_terms.reshape(8, 8, shard).transpose(1, 0, 2).reshape(8, 2, hidden)
    small_terms = jnp.concatenate([small_terms, hidden_term[:, None]], axis=1)
    small_sum = jnp.sum(exchange(after(small_terms, out_grad), GRP), axis=0)
    out_sum = replica_sum(out_grad)
    out_whole = exchange(
        after(jnp.broadcast_to(out_sum, (16,) + out_sum.shape), small_sum), REPLICAS
    )
    small_sum = jnp.broadcast_to(after(small_sum, out_whole), (16, 3, hidden))
    small_sum = jnp.sum(exchange(small_sum, REP), axis=0)
    owned = small_sum[:2].reshape(8, shard)

    fc_spans = [[(0, rank * hidden, hidden)] for rank in range(8)]
    fc_total = call(
        functools.partial(column_total_kernel, fc_spans, True),
        "fc_total",
        struct((shard, 8 * hidden), f32),
        after(place, qkv_sum),
        *fc_pieces,
    )
    proj_total = row_total(proj_whole, hidden, "proj_total")
    out_total = row_total(out_whole, shard, "out_total")
    qkv_spans = [
        [
            (p * SLOT_WIDTH, p * width + STRIDE * r, STRIDE if r < 7 else SLOT_WIDTH)
            for p in range(3)
        ]
        for r in range(8)
    ]
    qkv_total = call(
        functools.partial(column_total_kernel, qkv_spans, False),
        "qkv_total",
        struct((shard, 3 * width), f32),
        after(place, fc_total),
        *qkv_pieces,
    )
    return (
        output_home,
        inputs_home,
        owned[0],
        owned[1],
        qkv_total,
        owned[2],
        owned[3],
        out_total,
        owned[4],
        owned[5],
        owned[6],
        fc_total,
        small_sum[2],
        proj_total,
        owned[7],
    )


def solution(mesh):
    names = tuple(name for name, _ in LAYOUT)
    fine = jax.sharding.Mesh(mesh.devices.reshape([size for _, size in LAYOUT]), names)
    in_specs = (
        P(REP, GRP, None),
        P(GRP),
        P(GRP),
        P(GRP, None),
        P(GRP),
        P(GRP),
        P(GRP, None),
        P(GRP),
        P(GRP),
        P(GRP),
        P(GRP, None),
        P(GRP),
        P(GRP, None),
        P(GRP),
        P(REP, GRP, None),
    )
    out_specs = (
        P(REP, GRP, None),
        P(REP, GRP, None),
        P(GRP),
        P(GRP),
        P(GRP, None),
        P(GRP),
        P(GRP),
        P(GRP, None),
        P(GRP),
        P(GRP),
        P(GRP),
        P(GRP, None),
        P(GRP),
        P(GRP, None),
        P(GRP),
    )
    return jax.shard_map(
        per_device, mesh=fine, in_specs=in_specs, out_specs=out_specs, check_vma=False
    )
```

```python
import functools
import math

import jax
import jax.numpy as jnp
from jax import lax
from jax.experimental import pallas as pl
from jax.experimental.pallas import tpu as pltpu
from jax.sharding import PartitionSpec as P

HEADS = 25
HEAD_DIM = 64
SLOTS = 4
SLOT_WIDTH = SLOTS * HEAD_DIM
STRIDE = 3 * HEAD_DIM
BLOCK = 256

bf16 = jnp.bfloat16
f32 = jnp.float32


LAYOUT = (("x", 4), ("zl", 2), ("c", 2), ("y", 4), ("zh", 2))
REP = ("x", "zl", "c")
GRP = ("y", "zh")
TEAM = ("y", "c")
REPLICAS = ("zl", "x", "zh")
Z_RING = ("zl", "zh")
Z_PLACES = (0, 2, 1, 3)
ROLES = [(0, 0), (1, 2), (2, 1), (3, 3)]


def ring(value, axis, step):
    index = Z_PLACES if axis == Z_RING else range(4)
    return lax.ppermute(value, axis, [(index[(i + step) % 4], index[i]) for i in range(4)])


def ring_all(values, axis):
    return [values[0]] + [ring(values[k], axis, k) for k in range(1, 4)]


def flipped(value, axis):
    return lax.ppermute(value, axis, [(0, 1), (1, 0)])


def swap_roles(value):
    return lax.ppermute(value, ("c", "zh"), ROLES)


def swap_selected(value, stays):
    return jnp.where(stays, value, lax.ppermute(value, ("c", "zh"), ROLES[1:3]))


def other_core(value):
    return lax.ppermute(value, "c", [(0, 1), (1, 0)])


def exchange(parts, axes):
    return lax.all_to_all(parts, axes, 0, 0)


def gather(block, axes):
    return lax.all_gather(block, axes, axis=0)


def team_sum(parts):
    return lax.psum_scatter(parts.astype(bf16), TEAM, scatter_dimension=0, tiled=True)


def windows(rows, count):
    tiles = rows // 8
    starts = [tiles * i // count for i in range(count)]
    size = max(b - a for a, b in zip(starts, starts[1:] + [tiles]))
    return size * 8, [8 * s for s in starts]


def joined(parts, starts, rows, axis):
    ends = starts[1:] + [rows]
    return jnp.concatenate(
        [lax.slice_in_dim(p, 0, e - s, axis=axis) for p, s, e in zip(parts, starts, ends)], axis
    )


def norm_parts(value, gain, shift):
    center = value - jnp.mean(value, axis=-1, keepdims=True)
    spread = jnp.mean(center * center, axis=-1, keepdims=True)
    factor = lax.rsqrt(spread + 1e-05)
    normed = center * factor
    return (normed * gain + shift, normed, factor)


def norm_back(grad_value, normed, factor, gain):
    grad_normed = grad_value * gain
    mean_first = jnp.mean(grad_normed, axis=-1, keepdims=True)
    mean_second = jnp.mean(grad_normed * normed, axis=-1, keepdims=True)
    return factor * (grad_normed - mean_first - normed * mean_second)


def dot(left, right):
    return jnp.dot(left, right, preferred_element_type=f32)


def dot_rows(left, right):
    return lax.dot_general(left, right, (((0,), (0,)), ((), ())), preferred_element_type=f32)


def dot_cols(left, right):
    return lax.dot_general(left, right, (((1,), (1,)), ((), ())), preferred_element_type=f32)


def call(kernel, name, out_shape, *operands, scratch=(), flops=0):
    specs = [
        pl.BlockSpec(memory_space=pltpu.SMEM if op.dtype == jnp.int32 else pltpu.VMEM)
        for op in operands
    ]
    out_specs = jax.tree.map(lambda _: pl.BlockSpec(memory_space=pltpu.VMEM), out_shape)
    moved = sum(op.size * op.dtype.itemsize for op in operands)
    moved += sum(o.size * o.dtype.itemsize for o in jax.tree.leaves(out_shape))
    return pl.pallas_call(
        kernel,
        out_shape=out_shape,
        in_specs=specs,
        out_specs=out_specs,
        scratch_shapes=list(scratch),
        compiler_params=pltpu.CompilerParams(vmem_limit_bytes=56 * 2**20),
        cost_estimate=pl.CostEstimate(
            flops=int(3 * flops), bytes_accessed=int(moved), transcendentals=0
        ),
        name=name,
    )(*operands)


def struct(shape, dtype):
    return jax.ShapeDtypeStruct(shape, dtype)


Y, C, RANK, ZH, Z, X, ZL, MINE = range(8)


def qkv_columns_kernel(place_ref, weight_ref, *refs):
    out_refs, held_ref = refs[:4], refs[4]
    c = place_ref[C]
    width = weight_ref.shape[1] // 3
    for part in range(3):
        lanes = slice(part * SLOT_WIDTH, (part + 1) * SLOT_WIDTH)
        for y in range(4):
            start = part * width + 2 * STRIDE * y
            even = weight_ref[:, start : start + SLOT_WIDTH]
            odd = weight_ref[:, start + STRIDE : start + STRIDE + SLOT_WIDTH]
            held_ref[y, :, lanes] = jnp.where(c == 0, even, odd)
    for k in range(4):
        out_refs[k][...] = held_ref[lax.rem(place_ref[Y] + 4 - k, 4)]


def fc_columns_kernel(place_ref, weight_ref, *refs):
    out_refs, held_ref = refs[:4], refs[4]
    c = place_ref[C]
    hidden = weight_ref.shape[1] // 8
    for y in range(4):
        start = 2 * hidden * y
        even = weight_ref[:, start : start + hidden]
        odd = weight_ref[:, start + hidden : start + 2 * hidden]
        held_ref[y] = jnp.where(c == 0, even, odd)
    for k in range(4):
        out_refs[k][...] = held_ref[lax.rem(place_ref[Y] + 4 - k, 4)]


def fc_whole_kernel(place_ref, *refs):
    out_ref = refs[8]
    zh = place_ref[ZH]
    for k in range(4):
        y = lax.rem(place_ref[Y] + k, 4)
        out_ref[2 * y + zh] = refs[k][...]
        out_ref[2 * y + 1 - zh] = refs[4 + k][...]


def branch_kernel(
    slots_ref, tokens_ref, norm_ref, rows_ref, middle_ref, second_ref, parts_ref, flat_ref
):
    shard = parts_ref.shape[2]
    for rank in range(8):
        wide = STRIDE if rank < 7 else SLOT_WIDTH
        flat_ref[:, STRIDE * rank : STRIDE * rank + wide] = slots_ref[rank, :, :wide]
    for rank in range(8):
        parts_ref[rank] = flat_ref[:, shard * rank : shard * (rank + 1)]
    total = tokens_ref[...].astype(f32) + norm_ref[4:5, :] + dot(flat_ref[...], rows_ref[...])
    middle_ref[...] = total
    second_ref[...] = norm_parts(total, norm_ref[5:6, :], norm_ref[6:7, :])[0].astype(bf16)


def branch_back_kernel(
    place_ref,
    grad_ref,
    middle_ref,
    cot_ref,
    norm_ref,
    rows_ref,
    grad_middle_ref,
    branch_ref,
    slots_ref,
    sums_ref,
    flat_ref,
):
    gain = norm_ref[5:6, :]
    _, normed, factor = norm_parts(middle_ref[...], gain, gain)
    grad = grad_ref[...].astype(f32)
    cot = cot_ref[...].astype(f32)
    grad_middle = cot + norm_back(grad, normed, factor, gain)
    branch = grad_middle.astype(bf16)
    grad_middle_ref[...] = grad_middle
    branch_ref[...] = branch
    flat_ref[...] = dot_cols(branch, rows_ref[...]).astype(bf16)
    for rank in range(8):
        slots_ref[rank] = flat_ref[:, STRIDE * rank : STRIDE * rank + SLOT_WIDTH]
    sums_ref[0:1, :] = jnp.sum(branch.astype(f32), axis=0, keepdims=True)
    sums_ref[1:2, :] = jnp.sum(grad * normed, axis=0, keepdims=True)
    sums_ref[2:3, :] = jnp.sum(grad, axis=0, keepdims=True)
    sums_ref[3:4, :] = jnp.sum(cot, axis=0, keepdims=True)


def column_grad_kernel(left_ref, right_ref, out_ref):
    shard = left_ref.shape[1] // 8
    size, starts = windows(shard, 8)
    grad = dot_rows(left_ref[...], right_ref[...])
    for y in range(4):
        for zh in range(2):
            base = (2 * y + zh) * shard
            for i, start in enumerate(starts):
                out_ref[2 * i + zh, y] = grad[base + start : base + start + size].astype(bf16)


def column_ring_kernel(place_ref, left_ref, right_ref, *refs):
    out_refs, held_ref = refs[:4], refs[4]
    shard = left_ref.shape[1] // 8
    size, starts = windows(shard, 8)
    held_ref[...] = dot_rows(left_ref[...], right_ref[...])
    for k in range(4):
        x = lax.rem(place_ref[X] + 4 - k, 4)
        for z in range(4):
            for y in range(4):
                base = (2 * y + z // 2) * shard + starts[4 * (z % 2)]
                at = pl.multiple_of(base + starts[1] * x, 8)
                out_refs[k][z, y] = held_ref[pl.ds(at, size), :].astype(bf16)


def row_grad_kernel(left_ref, right_ref, out_ref):
    rows = left_ref.shape[1]
    size, starts = windows(rows, 16)
    grad = dot_rows(left_ref[...], right_ref[...])
    for i, start in enumerate(starts):
        zl, x, zh = i // 8, i // 2 % 4, i % 2
        out_ref[2 * zl + zh, x] = grad[start : start + size].astype(bf16)


def out_grad_kernel(place_ref, left_ref, *refs):
    blocks, out_ref, held_ref = refs[:8], refs[8], refs[9]
    c = place_ref[C]
    rows = left_ref.shape[2]
    size, starts = windows(rows, 16)
    for k in range(4):
        y = lax.rem(place_ref[Y] + k, 4)
        term = dot_rows(left_ref[2 * y + c], blocks[k][...])
        term = term + dot_rows(left_ref[2 * y + 1 - c], blocks[4 + k][...])
        if k == 0:
            held_ref[...] = term
        else:
            held_ref[...] += term
    for i, start in enumerate(starts):
        out_ref[i] = held_ref[start : start + size, :].astype(bf16)


def fold_kernel(which, place_ref, *refs):
    for k in range(4):
        at = lax.rem(place_ref[which] + 4 - k, 4)
        total = refs[0][at].astype(f32)
        for j in range(1, 4):
            total = total + refs[j][at].astype(f32)
        refs[4 + k][...] = total.astype(bf16)


def fold_stack_kernel(which, place_ref, parts_ref, *refs):
    for k in range(4):
        at = lax.rem(place_ref[which] + 4 - k, 4)
        total = parts_ref[0, at].astype(f32)
        for j in range(1, 4):
            total = total + parts_ref[j, at].astype(f32)
        refs[k][...] = total.astype(bf16)


def stack_kernel(*refs):
    for k, ref in enumerate(refs[:-1]):
        refs[-1][k] = ref[...]


def column_total_kernel(spans, ringed, place_ref, *refs):
    out_ref = refs[8]
    shard = out_ref.shape[0]
    _, starts = windows(shard, 8)
    step = starts[1]
    for j in range(4):
        x = lax.rem(place_ref[X] + j, 4)
        for flip in range(2):
            window = (place_ref[ZL] if flip == 0 else 1 - place_ref[ZL]) * 4 + x
            at = pl.multiple_of(window * step, 8)
            for rank in range(8):
                k = lax.rem(rank // 2 + 4 - place_ref[Y], 4) if ringed else rank // 2
                block = jnp.where(
                    place_ref[C] == rank % 2, refs[j][flip, k], refs[4 + j][flip, k]
                ).astype(f32)
                for source, target, wide in spans[rank]:
                    out_ref[pl.ds(at, step), target : target + wide] = block[
                        :step, source : source + wide
                    ]

                @pl.when(window == 7)
                def _(block=block, rank=rank):
                    for source, target, wide in spans[rank]:
                        out_ref[7 * step + step :, target : target + wide] = block[
                            step:, source : source + wide
                        ]


def row_total_kernel(place_ref, own_ref, other_ref, out_ref):
    mine = place_ref[MINE]
    _, starts = windows(out_ref.shape[0], 16)
    ends = starts[1:] + [out_ref.shape[0]]
    for i, (start, end) in enumerate(zip(starts, ends)):
        block = jnp.where(mine == 1, own_ref[i], other_ref[i])
        out_ref[start:end, :] = block[: end - start].astype(f32)


def attend_kernel(place_ref, tokens_ref, norm_ref, bias_ref, *refs):
    pieces, (first_ref, qkv_ref, out_ref, top_ref, cols_ref) = refs[:8], refs[8:]
    length = tokens_ref.shape[0]
    shard = cols_ref.shape[1]
    zh = place_ref[ZH]
    for k in range(4):
        y = lax.rem(place_ref[Y] + k, 4)
        cols_ref[2 * y + zh] = pieces[k][...]
        cols_ref[2 * y + 1 - zh] = pieces[4 + k][...]
    gain = norm_ref[0:1, :]
    shift = norm_ref[1:2, :]
    for block in range(length // BLOCK):
        rows = slice(block * BLOCK, (block + 1) * BLOCK)
        first = norm_parts(tokens_ref[rows, :].astype(f32), gain, shift)[0].astype(bf16)
        first_ref[rows, :] = first
        mixed = bias_ref[...]
        for g in range(8):
            mixed = mixed + dot(first[:, g * shard : (g + 1) * shard], cols_ref[g])
        qkv_ref[rows, :] = mixed.astype(bf16)
    for head in range(SLOTS):
        lanes = slice(head * HEAD_DIM, (head + 1) * HEAD_DIM)
        keys = qkv_ref[:, SLOT_WIDTH + head * HEAD_DIM : SLOT_WIDTH + (head + 1) * HEAD_DIM]
        values = qkv_ref[
            :, 2 * SLOT_WIDTH + head * HEAD_DIM : 2 * SLOT_WIDTH + (head + 1) * HEAD_DIM
        ]
        for block in range(length // BLOCK):
            rows = slice(block * BLOCK, (block + 1) * BLOCK)
            width = (block + 1) * BLOCK
            query = qkv_ref[rows, lanes] * bf16(1.0 / math.sqrt(HEAD_DIM))
            scores = dot_cols(query, keys[:width])
            row = lax.broadcasted_iota(jnp.int32, (BLOCK, width), 0) + block * BLOCK
            col = lax.broadcasted_iota(jnp.int32, (BLOCK, width), 1)
            scores = jnp.where(col <= row, scores, -1e30)
            top = jnp.max(scores, axis=-1, keepdims=True)
            probs = jnp.exp(scores - top)
            total = jnp.sum(probs, axis=-1, keepdims=True)
            mixed = dot(probs.astype(bf16), values[:width])
            out_ref[rows, lanes] = (mixed / total).astype(bf16)
            top_ref[rows, head : head + 1] = top + jnp.log(total)


def hidden_kernel(
    place_ref, second_ref, cols_ref, bias_ref, grad_ref, active_ref, hidden_ref, sums_ref, out_ref
):
    length = second_ref.shape[0]
    sums = jnp.zeros(sums_ref.shape, f32)
    for block in range(length // BLOCK):
        rows = slice(block * BLOCK, (block + 1) * BLOCK)
        pre = dot(second_ref[rows, :], cols_ref[...]) + bias_ref[...]
        square = pre * pre
        bent = jnp.tanh(0.7978845608028654 * (pre + 0.044715 * square * pre))
        half = 0.5 * (1.0 + bent)
        active_ref[rows, :] = (pre * half).astype(bf16)
        slope = half + 0.5 * pre * (1.0 - bent * bent) * (
            0.7978845608028654 + (3.0 * 0.044715 * 0.7978845608028654) * square
        )
        grad = (grad_ref[rows, :] * slope).astype(bf16)
        hidden_ref[rows, :] = grad
        sums = sums + jnp.sum(grad.astype(f32), axis=0, keepdims=True)
        out_ref[rows, :] = dot_cols(grad, cols_ref[...]).astype(bf16)
    sums_ref[...] = sums


def attend_back_kernel(
    place_ref, qkv_ref, grad_ref, out_ref, top_ref, cols_ref, mixed_ref, first_ref, sums_ref, query_ref
):
    length = qkv_ref.shape[0]
    scale = 1.0 / math.sqrt(HEAD_DIM)
    ones = jnp.ones((8, HEAD_DIM), bf16)
    for head in range(SLOTS):
        base = head * HEAD_DIM
        lanes = slice(base, base + HEAD_DIM)
        key_lanes = slice(SLOT_WIDTH + base, SLOT_WIDTH + base + HEAD_DIM)
        value_lanes = slice(2 * SLOT_WIDTH + base, 2 * SLOT_WIDTH + base + HEAD_DIM)
        query = qkv_ref[:, lanes] * bf16(scale)
        grad = grad_ref[:, lanes]
        if head == SLOTS - 1:
            grad = jnp.where(place_ref[RANK] == 7, grad, jnp.zeros_like(grad))
        top = top_ref[head : head + 1, :]
        delta = dot_cols(ones, grad * out_ref[:, lanes])[0:1, :]
        for block in range(length // BLOCK):
            start = block * BLOCK
            rows = slice(start, start + BLOCK)
            width = length - start
            keys = qkv_ref[rows, key_lanes]
            values = qkv_ref[rows, value_lanes]
            scores = dot_cols(keys, query[start:])
            row = lax.broadcasted_iota(jnp.int32, (BLOCK, width), 0)
            col = lax.broadcasted_iota(jnp.int32, (BLOCK, width), 1)
            probs = jnp.where(row <= col, jnp.exp(scores - top[:, start:]), 0.0)
            grad_probs = dot_cols(values, grad[start:])
            grad_scores = (probs * (grad_probs - delta[:, start:])).astype(bf16)
            mixed_ref[rows, value_lanes] = dot(probs.astype(bf16), grad[start:]).astype(bf16)
            mixed_ref[rows, key_lanes] = dot(grad_scores, query[start:]).astype(bf16)
            term = dot_rows(grad_scores, keys)
            if block == 0:
                query_ref[...] = term
            else:
                query_ref[start:, :] += term
        mixed_ref[:, lanes] = (query_ref[...] * scale).astype(bf16)
    sums = jnp.zeros(sums_ref.shape, f32)
    for block in range(length // BLOCK):
        rows = slice(block * BLOCK, (block + 1) * BLOCK)
        mixed = mixed_ref[rows, :]
        sums = sums + jnp.sum(mixed.astype(f32), axis=0, keepdims=True)
        first_ref[rows, :] = dot_cols(mixed, cols_ref[...]).astype(bf16)
    sums_ref[...] = sums


def input_back_kernel(grad_ref, tokens_ref, middle_ref, norm_ref, out_ref, sums_ref):
    gain = norm_ref[0:1, :]
    _, normed, factor = norm_parts(tokens_ref[...].astype(f32), gain, gain)
    grad = grad_ref[...].astype(f32)
    out_ref[...] = (middle_ref[...] + norm_back(grad, normed, factor, gain)).astype(bf16)
    sums_ref[0:1, :] = jnp.sum(grad * normed, axis=0, keepdims=True)
    sums_ref[1:2, :] = jnp.sum(grad, axis=0, keepdims=True)


def after(value, *others):
    return lax.optimization_barrier((value,) + others)[0]


def per_device(
    tokens,
    ln1_gain,
    ln1_bias,
    w_qkv,
    bias_q,
    bias_v,
    w_out,
    bias_out,
    ln2_gain,
    ln2_bias,
    w_fc,
    bias_fc,
    w_proj,
    bias_proj,
    cotangent,
):
    _, span, width = tokens.shape
    shard = width // 8
    hidden = w_fc.shape[1] // 8
    length = span * 8
    slots = 3 * SLOT_WIDTH
    x, zl, c, y, zh = [lax.axis_index(name) for name, _ in LAYOUT]
    rank = y * 2 + c
    place = jnp.stack(
        [y, c, rank, zh, zh * 2 + zl, x, zl, (c == zh).astype(jnp.int32)]
    ).astype(jnp.int32)

    stays = c == zh
    own_tokens = swap_roles(tokens.reshape(span, width))
    all_tokens = gather(own_tokens, TEAM).reshape(length, width)
    qkv_parts = call(
        qkv_columns_kernel,
        "qkv_columns",
        [struct((shard, slots), bf16)] * 4,
        place,
        w_qkv,
        scratch=[pltpu.VMEM((4, shard, slots), bf16)],
    )
    qkv_own = ring_all(qkv_parts, "y")
    qkv_other = [flipped(part, "zh") for part in qkv_own]
    small = jnp.concatenate(
        [ln1_gain, ln1_bias, bias_q, bias_v, bias_out, ln2_gain, ln2_bias, bias_proj, bias_fc]
    ).reshape(3, hidden)
    small_all = exchange(
        after(jnp.broadcast_to(small, (8, 3, hidden)), qkv_parts[0]), GRP
    )
    out_rows = swap_roles(after(w_out, small_all))
    own_cot = swap_roles(after(cotangent, out_rows).reshape(span, width))
    place = after(place, small_all)
    fc_parts = call(
        fc_columns_kernel,
        "fc_columns",
        [struct((shard, hidden), bf16)] * 4,
        place,
        w_fc,
        scratch=[pltpu.VMEM((4, shard, hidden), bf16)],
    )
    place = after(place, fc_parts[0])

    small_all = small_all.astype(f32)
    hidden_bias = lax.dynamic_index_in_dim(small_all, rank, 0, keepdims=False)[2:3]
    vectors = small_all[:, :2].reshape(8, 8, shard).transpose(1, 0, 2).reshape(8, width)
    bias_slots = jnp.concatenate(
        [
            lax.dynamic_slice_in_dim(vectors[2], STRIDE * rank, SLOT_WIDTH),
            jnp.zeros((SLOT_WIDTH,), f32),
            lax.dynamic_slice_in_dim(vectors[3], STRIDE * rank, SLOT_WIDTH),
        ]
    ).reshape(1, slots)

    out_all = gather(after(out_rows, *qkv_own), TEAM).reshape(width, width)
    all_cot = gather(after(own_cot, *qkv_other), TEAM).reshape(length, width)
    proj_rows = swap_selected(after(w_proj, *qkv_other), stays)
    fc_own = ring_all([after(part, *qkv_other) for part in fc_parts], "y")

    first, qkv, attended_slots, top, qkv_cols = call(
        attend_kernel,
        "attend",
        (
            struct((length, width), bf16),
            struct((length, slots), bf16),
            struct((length, SLOT_WIDTH), bf16),
            struct((length, SLOTS), f32),
            struct((8, shard, slots), bf16),
        ),
        after(place, bias_slots),
        all_tokens,
        vectors,
        bias_slots,
        *qkv_own,
        *qkv_other,
        flops=2 * length * width * slots,
    )
    qkv_cols = qkv_cols.reshape(width, slots)
    fc_other = [flipped(after(part, qkv), "zh") for part in fc_own]
    attended = exchange(attended_slots.reshape(8, span, SLOT_WIDTH), TEAM)
    middle, second, attended_parts = call(
        branch_kernel,
        "branch",
        (
            struct((span, width), f32),
            struct((span, width), bf16),
            struct((8, span, shard), bf16),
        ),
        attended,
        own_tokens,
        vectors,
        out_all,
        scratch=[pltpu.VMEM((span, width), bf16)],
        flops=2 * span * width * width,
    )

    second_all = gather(second, TEAM).reshape(length, width)
    attended_own = exchange(attended_parts, TEAM)
    grad_active = dot_cols(after(all_cot, second), proj_rows)
    fc_cols = call(
        fc_whole_kernel,
        "fc_whole",
        struct((8, shard, hidden), bf16),
        place,
        after(fc_own[0], second),
        *fc_own[1:],
        *fc_other,
    ).reshape(width, hidden)
    active, grad_hidden, hidden_sums, second_parts = call(
        hidden_kernel,
        "hidden",
        (
            struct((length, hidden), bf16),
            struct((length, hidden), bf16),
            struct((1, hidden), f32),
            struct((length, width), bf16),
        ),
        after(place, attended_own),
        second_all,
        fc_cols,
        hidden_bias,
        grad_active,
        flops=4 * length * width * hidden,
    )
    grad_second = team_sum(second_parts)
    window = windows(shard, 8)[0]
    fc_grad = call(
        column_ring_kernel,
        "fc_grad",
        [struct((4, 4, window, hidden), bf16)] * 4,
        place,
        second_all,
        grad_hidden,
        scratch=[pltpu.VMEM((width, hidden), f32)],
        flops=2 * length * width * hidden,
    )
    fc_grad = ring_all(fc_grad, "x")
    row_window = windows(hidden, 16)[0]
    proj_grad = call(
        row_grad_kernel,
        "proj_grad",
        struct((4, 4, row_window, width), bf16),
        active,
        all_cot,
        flops=2 * length * width * hidden,
    )
    down_parts = dot(active, proj_rows).astype(bf16)
    grad_second = after(grad_second, fc_grad[0], proj_grad, down_parts)

    grad_middle, grad_branch, grad_slots, branch_sums = call(
        branch_back_kernel,
        "branch_back",
        (
            struct((span, width), f32),
            struct((span, width), bf16),
            struct((8, span, SLOT_WIDTH), bf16),
            struct((4, width), f32),
        ),
        place,
        grad_second,
        middle,
        own_cot,
        vectors,
        out_all,
        scratch=[pltpu.VMEM((span, width), bf16)],
        flops=2 * span * width * width,
    )
    grad_heads = exchange(grad_slots, TEAM).reshape(length, SLOT_WIDTH)
    down = team_sum(after(down_parts, grad_second))
    proj_grad = exchange(after(proj_grad, grad_heads), Z_RING)

    def fold(which, parts, name, *behind):
        parts = [after(parts[0], *behind)] + parts[1:]
        return call(
            functools.partial(fold_kernel, which),
            name,
            [struct(parts[0].shape[1:], bf16)] * 4,
            place,
            *parts,
        )

    grad_mixed, first_parts, mixed_sums = call(
        attend_back_kernel,
        "attend_back",
        (
            struct((length, slots), bf16),
            struct((length, width), bf16),
            struct((1, slots), f32),
        ),
        place,
        qkv,
        grad_heads,
        attended_slots,
        top.T,
        qkv_cols,
        scratch=[pltpu.VMEM((length, HEAD_DIM), f32)],
        flops=2 * length * width * slots,
    )
    grad_first = team_sum(after(first_parts, down))
    place = after(place, grad_mixed)
    proj_grad = ring_all(
        call(
            functools.partial(fold_stack_kernel, X),
            "proj_fold",
            [struct((row_window, width), bf16)] * 4,
            place,
            proj_grad,
        ),
        "x",
    )
    fc_grad = fold(Z, fc_grad, "fc_fold", place)
    qkv_grad = call(
        column_grad_kernel,
        "qkv_grad",
        struct((16, 4, window, slots), bf16),
        after(first, fc_grad[0], proj_grad[0]),
        grad_mixed,
        flops=2 * length * width * slots,
    )
    place = after(place, qkv_grad)
    fc_grad = ring_all(fc_grad, Z_RING)
    branch_own = ring_all([after(grad_branch, grad_mixed)] * 4, "y")
    qkv_grad = exchange(after(qkv_grad, *fc_grad, *proj_grad), REPLICAS)
    grad_first = after(grad_first, qkv_grad)

    def replica_sum(parts):
        return jnp.sum(parts.astype(f32), axis=0).astype(bf16)

    def stacked(parts, name):
        return call(
            stack_kernel, name, struct((len(parts),) + parts[0].shape, bf16), *parts
        )

    def column_spread(near, name):
        both = stacked([near, flipped(near, "zl")], name + "_both")
        return ring_all([both] * 4, "x")

    def row_total(whole, rows, name, *behind):
        whole = after(whole, *behind)
        return call(
            row_total_kernel, name, struct((rows, width), f32), place, whole, other_core(whole)
        )

    fc_grad = ring_all(fold(Y, fc_grad, "fc_fold_last", place), "y")
    proj_sum = sum(part.astype(f32) for part in proj_grad).astype(bf16)
    proj_whole = gather(after(proj_sum, grad_first), REPLICAS)
    fc_own_pieces = column_spread(stacked(fc_grad, "fc_near"), "fc")
    branch_other = [other_core(part) for part in branch_own]
    out_grad = call(
        out_grad_kernel,
        "out_grad",
        struct((16, windows(shard, 16)[0], width), bf16),
        after(place, fc_grad[1]),
        attended_own,
        *branch_own,
        *branch_other,
        scratch=[pltpu.VMEM((shard, width), f32)],
        flops=2 * length * width * shard,
    )
    grad_inputs, first_sums = call(
        input_back_kernel,
        "input_back",
        (struct((span, width), bf16), struct((2, width), f32)),
        grad_first,
        own_tokens,
        grad_middle,
        after(vectors, qkv_grad, out_grad, *fc_own_pieces),
    )
    inputs_home = swap_roles(grad_inputs).astype(f32).reshape(1, span, width)
    output = middle + (after(down, grad_inputs).astype(f32) + vectors[7])
    output_home = swap_roles(output.astype(bf16)).reshape(1, span, width)
    place = after(place, grad_inputs)
    fc_own_pieces = [after(part, grad_inputs) for part in fc_own_pieces]
    fc_pieces = fc_own_pieces + [other_core(part) for part in fc_own_pieces]
    place = after(place, out_grad)
    qkv_sum = exchange(replica_sum(after(qkv_grad, place)), "y")
    out_grad = exchange(after(out_grad, qkv_sum), REPLICAS)
    qkv_pieces = column_spread(qkv_sum, "qkv")
    qkv_pieces = qkv_pieces + [other_core(part) for part in qkv_pieces]

    blank = jnp.zeros((1, width), f32)
    at = (0, STRIDE * rank)
    small_terms = jnp.concatenate(
        [
            first_sums,
            lax.dynamic_update_slice(blank, mixed_sums[:, :SLOT_WIDTH], at),
            lax.dynamic_update_slice(blank, mixed_sums[:, 2 * SLOT_WIDTH :], at),
            branch_sums,
        ]
    )
    hidden_term = lax.dynamic_update_slice(
        jnp.zeros((8, hidden), f32), hidden_sums, (rank, 0)
    )
    small_terms = small_terms.reshape(8, 8, shard).transpose(1, 0, 2).reshape(8, 2, hidden)
    small_terms = jnp.concatenate([small_terms, hidden_term[:, None]], axis=1)
    small_sum = jnp.sum(exchange(after(small_terms, out_grad), GRP), axis=0)
    out_sum = replica_sum(out_grad)
    out_whole = exchange(
        after(jnp.broadcast_to(out_sum, (16,) + out_sum.shape), small_sum), REPLICAS
    )
    small_sum = jnp.broadcast_to(after(small_sum, out_whole), (16, 3, hidden))
    small_sum = jnp.sum(exchange(small_sum, REP), axis=0)
    owned = small_sum[:2].reshape(8, shard)

    fc_spans = [[(0, rank * hidden, hidden)] for rank in range(8)]
    fc_total = call(
        functools.partial(column_total_kernel, fc_spans, True),
        "fc_total",
        struct((shard, 8 * hidden), f32),
        after(place, qkv_sum),
        *fc_pieces,
    )
    proj_total = row_total(proj_whole, hidden, "proj_total", out_whole)
    out_total = row_total(out_whole, shard, "out_total")
    qkv_spans = [
        [
            (p * SLOT_WIDTH, p * width + STRIDE * r, STRIDE if r < 7 else SLOT_WIDTH)
            for p in range(3)
        ]
        for r in range(8)
    ]
    qkv_total = call(
        functools.partial(column_total_kernel, qkv_spans, False),
        "qkv_total",
        struct((shard, 3 * width), f32),
        after(place, fc_total),
        *qkv_pieces,
    )
    return (
        output_home,
        inputs_home,
        owned[0],
        owned[1],
        qkv_total,
        owned[2],
        owned[3],
        out_total,
        owned[4],
        owned[5],
        owned[6],
        fc_total,
        small_sum[2],
        proj_total,
        owned[7],
    )


def solution(mesh):
    names = tuple(name for name, _ in LAYOUT)
    fine = jax.sharding.Mesh(mesh.devices.reshape([size for _, size in LAYOUT]), names)
    in_specs = (
        P(REP, GRP, None),
        P(GRP),
        P(GRP),
        P(GRP, None),
        P(GRP),
        P(GRP),
        P(GRP, None),
        P(GRP),
        P(GRP),
        P(GRP),
        P(GRP, None),
        P(GRP),
        P(GRP, None),
        P(GRP),
        P(REP, GRP, None),
    )
    out_specs = (
        P(REP, GRP, None),
        P(REP, GRP, None),
        P(GRP),
        P(GRP),
        P(GRP, None),
        P(GRP),
        P(GRP),
        P(GRP, None),
        P(GRP),
        P(GRP),
        P(GRP),
        P(GRP, None),
        P(GRP),
        P(GRP, None),
        P(GRP),
    )
    return jax.shard_map(
        per_device, mesh=fine, in_specs=in_specs, out_specs=out_specs, check_vma=False
    )
```

```python
import functools
import math

import jax
import jax.numpy as jnp
from jax import lax
from jax.experimental import pallas as pl
from jax.experimental.pallas import tpu as pltpu
from jax.sharding import PartitionSpec as P

HEADS = 25
HEAD_DIM = 64
SLOTS = 4
SLOT_WIDTH = SLOTS * HEAD_DIM
STRIDE = 3 * HEAD_DIM
BLOCK = 256

bf16 = jnp.bfloat16
f32 = jnp.float32


LAYOUT = (("x", 4), ("zl", 2), ("c", 2), ("y", 4), ("zh", 2))
REP = ("x", "zl", "c")
GRP = ("y", "zh")
TEAM = ("y", "c")
ROLES = [(0, 0), (1, 2), (2, 1), (3, 3)]


def ring(value, axis, step):
    return lax.ppermute(value, axis, [((i + step) % 4, i) for i in range(4)])


def ring_all(values, axis):
    return [values[0]] + [ring(values[k], axis, k) for k in range(1, 4)]


def flipped(value, axis):
    return lax.ppermute(value, axis, [(0, 1), (1, 0)])


def swap_roles(value):
    return lax.ppermute(value, ("c", "zh"), ROLES)


def swap_selected(value, stays):
    return jnp.where(stays, value, lax.ppermute(value, ("c", "zh"), ROLES[1:3]))


def other_core(value):
    return lax.ppermute(value, "c", [(0, 1), (1, 0)])


def exchange(parts, axes):
    return lax.all_to_all(parts, axes, 0, 0)


def gather(block, axes):
    return lax.all_gather(block, axes, axis=0)


def team_sum(parts):
    return lax.psum_scatter(parts.astype(bf16), TEAM, scatter_dimension=0, tiled=True)


def norm_parts(value, gain, shift):
    center = value - jnp.mean(value, axis=-1, keepdims=True)
    spread = jnp.mean(center * center, axis=-1, keepdims=True)
    factor = lax.rsqrt(spread + 1e-05)
    normed = center * factor
    return (normed * gain + shift, normed, factor)


def norm_back(grad_value, normed, factor, gain):
    grad_normed = grad_value * gain
    mean_first = jnp.mean(grad_normed, axis=-1, keepdims=True)
    mean_second = jnp.mean(grad_normed * normed, axis=-1, keepdims=True)
    return factor * (grad_normed - mean_first - normed * mean_second)


def dot(left, right):
    return jnp.dot(left, right, preferred_element_type=f32)


def dot_rows(left, right):
    return lax.dot_general(left, right, (((0,), (0,)), ((), ())), preferred_element_type=f32)


def dot_cols(left, right):
    return lax.dot_general(left, right, (((1,), (1,)), ((), ())), preferred_element_type=f32)


def call(kernel, name, out_shape, *operands, scratch=(), flops=0):
    specs = [
        pl.BlockSpec(memory_space=pltpu.SMEM if op.dtype == jnp.int32 else pltpu.VMEM)
        for op in operands
    ]
    out_specs = jax.tree.map(lambda _: pl.BlockSpec(memory_space=pltpu.VMEM), out_shape)
    moved = sum(op.size * op.dtype.itemsize for op in operands)
    moved += sum(o.size * o.dtype.itemsize for o in jax.tree.leaves(out_shape))
    return pl.pallas_call(
        kernel,
        out_shape=out_shape,
        in_specs=specs,
        out_specs=out_specs,
        scratch_shapes=list(scratch),
        compiler_params=pltpu.CompilerParams(vmem_limit_bytes=56 * 2**20),
        cost_estimate=pl.CostEstimate(
            flops=int(3 * flops), bytes_accessed=int(moved), transcendentals=0
        ),
        name=name,
    )(*operands)


def struct(shape, dtype):
    return jax.ShapeDtypeStruct(shape, dtype)


Y, C, RANK, ZH, Z, X, ZL, MINE = range(8)


def qkv_columns_kernel(place_ref, weight_ref, out_ref):
    c = place_ref[C]
    width = weight_ref.shape[1] // 3
    for part in range(3):
        for y in range(4):
            start = part * width + 2 * STRIDE * y
            even = weight_ref[:, start : start + SLOT_WIDTH]
            odd = weight_ref[:, start + STRIDE : start + STRIDE + SLOT_WIDTH]
            block = jnp.where(c == 0, even, odd)
            for zh in range(2):
                out_ref[2 * y + zh, :, part * SLOT_WIDTH : (part + 1) * SLOT_WIDTH] = block


def fc_columns_kernel(place_ref, weight_ref, out_ref):
    c = place_ref[C]
    hidden = weight_ref.shape[1] // 8
    for y in range(4):
        start = 2 * hidden * y
        even = weight_ref[:, start : start + hidden]
        odd = weight_ref[:, start + hidden : start + 2 * hidden]
        block = jnp.where(c == 0, even, odd)
        for zh in range(2):
            out_ref[2 * y + zh] = block


def branch_kernel(
    slots_ref, tokens_ref, norm_ref, rows_ref, middle_ref, second_ref, parts_ref, flat_ref
):
    shard = parts_ref.shape[2]
    for rank in range(8):
        wide = STRIDE if rank < 7 else SLOT_WIDTH
        flat_ref[:, STRIDE * rank : STRIDE * rank + wide] = slots_ref[rank, :, :wide]
    for rank in range(8):
        parts_ref[rank] = flat_ref[:, shard * rank : shard * (rank + 1)]
    total = tokens_ref[...].astype(f32) + norm_ref[4:5, :] + dot(flat_ref[...], rows_ref[...])
    middle_ref[...] = total
    second_ref[...] = norm_parts(total, norm_ref[5:6, :], norm_ref[6:7, :])[0].astype(bf16)


def branch_back_kernel(
    place_ref,
    grad_ref,
    middle_ref,
    cot_ref,
    norm_ref,
    rows_ref,
    grad_middle_ref,
    branch_ref,
    slots_ref,
    sums_ref,
    flat_ref,
):
    gain = norm_ref[5:6, :]
    _, normed, factor = norm_parts(middle_ref[...], gain, gain)
    grad = grad_ref[...].astype(f32)
    cot = cot_ref[...].astype(f32)
    grad_middle = cot + norm_back(grad, normed, factor, gain)
    branch = grad_middle.astype(bf16)
    grad_middle_ref[...] = grad_middle
    branch_ref[...] = branch
    flat_ref[...] = dot_cols(branch, rows_ref[...]).astype(bf16)
    for rank in range(8):
        slots_ref[rank] = flat_ref[:, STRIDE * rank : STRIDE * rank + SLOT_WIDTH]
    sums_ref[0:1, :] = jnp.sum(branch.astype(f32), axis=0, keepdims=True)
    sums_ref[1:2, :] = jnp.sum(grad * normed, axis=0, keepdims=True)
    sums_ref[2:3, :] = jnp.sum(grad, axis=0, keepdims=True)
    sums_ref[3:4, :] = jnp.sum(cot, axis=0, keepdims=True)


def weight_grad_kernel(left_ref, right_ref, out_ref):
    out_ref[...] = dot_rows(left_ref[...], right_ref[...]).astype(bf16)


def out_grad_kernel(place_ref, left_ref, *refs):
    blocks, out_ref, held_ref = refs[:8], refs[8], refs[9]
    c = place_ref[C]
    rows = held_ref.shape[0]
    for k in range(4):
        y = lax.rem(place_ref[Y] + k, 4)
        term = dot_rows(left_ref[2 * y + c], blocks[k][...])
        term = term + dot_rows(left_ref[2 * y + 1 - c], blocks[4 + k][...])
        if k == 0:
            held_ref[...] = term
        else:
            held_ref[...] += term
    out_ref[:rows, :] = held_ref[...].astype(bf16)
    out_ref[rows:, :] = jnp.zeros((out_ref.shape[0] - rows, out_ref.shape[1]), bf16)


def column_total_kernel(spans, place_ref, own_ref, other_ref, out_ref):
    c = place_ref[C]
    for rank in range(8):
        own, other = own_ref[rank % 4], other_ref[rank % 4]
        block = jnp.where(c == rank // 4, own, other).astype(f32)
        for source, target, wide in spans[rank]:
            out_ref[:, target : target + wide] = block[:, source : source + wide]


def row_total_kernel(place_ref, own_ref, other_ref, out_ref):
    c = place_ref[C]
    rows, half = out_ref.shape[0], own_ref.shape[0]
    for part in range(2):
        block = jnp.where(c == part, own_ref[...], other_ref[...]).astype(f32)
        out_ref[part * half : min(rows, (part + 1) * half), :] = block[: rows - part * half]


def attend_kernel(tokens_ref, cols_ref, norm_ref, bias_ref, first_ref, qkv_ref, out_ref, top_ref):
    length = tokens_ref.shape[0]
    gain = norm_ref[0:1, :]
    shift = norm_ref[1:2, :]
    for block in range(length // BLOCK):
        rows = slice(block * BLOCK, (block + 1) * BLOCK)
        first = norm_parts(tokens_ref[rows, :].astype(f32), gain, shift)[0].astype(bf16)
        first_ref[rows, :] = first
        qkv_ref[rows, :] = (dot(first, cols_ref[...]) + bias_ref[...]).astype(bf16)
    for head in range(SLOTS):
        lanes = slice(head * HEAD_DIM, (head + 1) * HEAD_DIM)
        keys = qkv_ref[:, SLOT_WIDTH + head * HEAD_DIM : SLOT_WIDTH + (head + 1) * HEAD_DIM]
        values = qkv_ref[
            :, 2 * SLOT_WIDTH + head * HEAD_DIM : 2 * SLOT_WIDTH + (head + 1) * HEAD_DIM
        ]
        for block in range(length // BLOCK):
            rows = slice(block * BLOCK, (block + 1) * BLOCK)
            width = (block + 1) * BLOCK
            query = qkv_ref[rows, lanes] * bf16(1.0 / math.sqrt(HEAD_DIM))
            scores = dot_cols(query, keys[:width])
            row = lax.broadcasted_iota(jnp.int32, (BLOCK, width), 0) + block * BLOCK
            col = lax.broadcasted_iota(jnp.int32, (BLOCK, width), 1)
            scores = jnp.where(col <= row, scores, -1e30)
            top = jnp.max(scores, axis=-1, keepdims=True)
            probs = jnp.exp(scores - top)
            total = jnp.sum(probs, axis=-1, keepdims=True)
            mixed = dot(probs.astype(bf16), values[:width])
            out_ref[rows, lanes] = (mixed / total).astype(bf16)
            top_ref[rows, head : head + 1] = top + jnp.log(total)


def hidden_kernel(
    place_ref, second_ref, cols_ref, bias_ref, grad_ref, active_ref, hidden_ref, sums_ref, out_ref
):
    length = second_ref.shape[0]
    sums = jnp.zeros(sums_ref.shape, f32)
    for block in range(length // BLOCK):
        rows = slice(block * BLOCK, (block + 1) * BLOCK)
        pre = dot(second_ref[rows, :], cols_ref[...]) + bias_ref[...]
        square = pre * pre
        bent = jnp.tanh(0.7978845608028654 * (pre + 0.044715 * square * pre))
        half = 0.5 * (1.0 + bent)
        active_ref[rows, :] = (pre * half).astype(bf16)
        slope = half + 0.5 * pre * (1.0 - bent * bent) * (
            0.7978845608028654 + (3.0 * 0.044715 * 0.7978845608028654) * square
        )
        grad = (grad_ref[rows, :] * slope).astype(bf16)
        hidden_ref[rows, :] = grad
        sums = sums + jnp.sum(grad.astype(f32), axis=0, keepdims=True)
        out_ref[rows, :] = dot_cols(grad, cols_ref[...]).astype(bf16)
    sums_ref[...] = sums


def attend_back_kernel(
    place_ref, qkv_ref, grad_ref, out_ref, top_ref, cols_ref, mixed_ref, first_ref, sums_ref, query_ref
):
    length = qkv_ref.shape[0]
    scale = 1.0 / math.sqrt(HEAD_DIM)
    ones = jnp.ones((8, HEAD_DIM), bf16)
    for head in range(SLOTS):
        base = head * HEAD_DIM
        lanes = slice(base, base + HEAD_DIM)
        key_lanes = slice(SLOT_WIDTH + base, SLOT_WIDTH + base + HEAD_DIM)
        value_lanes = slice(2 * SLOT_WIDTH + base, 2 * SLOT_WIDTH + base + HEAD_DIM)
        query = qkv_ref[:, lanes] * bf16(scale)
        grad = grad_ref[:, lanes]
        if head == SLOTS - 1:
            grad = jnp.where(place_ref[RANK] == 7, grad, jnp.zeros_like(grad))
        top = top_ref[head : head + 1, :]
        delta = dot_cols(ones, grad * out_ref[:, lanes])[0:1, :]
        for block in range(length // BLOCK):
            start = block * BLOCK
            rows = slice(start, start + BLOCK)
            width = length - start
            keys = qkv_ref[rows, key_lanes]
            values = qkv_ref[rows, value_lanes]
            scores = dot_cols(keys, query[start:])
            row = lax.broadcasted_iota(jnp.int32, (BLOCK, width), 0)
            col = lax.broadcasted_iota(jnp.int32, (BLOCK, width), 1)
            probs = jnp.where(row <= col, jnp.exp(scores - top[:, start:]), 0.0)
            grad_probs = dot_cols(values, grad[start:])
            grad_scores = (probs * (grad_probs - delta[:, start:])).astype(bf16)
            mixed_ref[rows, value_lanes] = dot(probs.astype(bf16), grad[start:]).astype(bf16)
            mixed_ref[rows, key_lanes] = dot(grad_scores, query[start:]).astype(bf16)
            term = dot_rows(grad_scores, keys)
            if block == 0:
                query_ref[...] = term
            else:
                query_ref[start:, :] += term
        mixed_ref[:, lanes] = (query_ref[...] * scale).astype(bf16)
    sums = jnp.zeros(sums_ref.shape, f32)
    for block in range(length // BLOCK):
        rows = slice(block * BLOCK, (block + 1) * BLOCK)
        mixed = mixed_ref[rows, :]
        sums = sums + jnp.sum(mixed.astype(f32), axis=0, keepdims=True)
        first_ref[rows, :] = dot_cols(mixed, cols_ref[...]).astype(bf16)
    sums_ref[...] = sums


def input_back_kernel(grad_ref, tokens_ref, middle_ref, norm_ref, out_ref, sums_ref):
    gain = norm_ref[0:1, :]
    _, normed, factor = norm_parts(tokens_ref[...].astype(f32), gain, gain)
    grad = grad_ref[...].astype(f32)
    out_ref[...] = (middle_ref[...] + norm_back(grad, normed, factor, gain)).astype(bf16)
    sums_ref[0:1, :] = jnp.sum(grad * normed, axis=0, keepdims=True)
    sums_ref[1:2, :] = jnp.sum(grad, axis=0, keepdims=True)


def after(value, *others):
    return lax.optimization_barrier((value,) + others)[0]


def per_device(
    tokens,
    ln1_gain,
    ln1_bias,
    w_qkv,
    bias_q,
    bias_v,
    w_out,
    bias_out,
    ln2_gain,
    ln2_bias,
    w_fc,
    bias_fc,
    w_proj,
    bias_proj,
    cotangent,
):
    _, span, width = tokens.shape
    shard = width // 8
    hidden = w_fc.shape[1] // 8
    length = span * 8
    slots = 3 * SLOT_WIDTH
    x, zl, c, y, zh = [lax.axis_index(name) for name, _ in LAYOUT]
    rank = y * 2 + c
    place = jnp.stack(
        [y, c, rank, zh, zh * 2 + zl, x, zl, (c == zh).astype(jnp.int32)]
    ).astype(jnp.int32)

    stays = c == zh
    own_tokens = swap_roles(tokens.reshape(span, width))
    all_tokens = gather(own_tokens, TEAM).reshape(length, width)
    qkv_parts = call(
        qkv_columns_kernel, "qkv_columns", struct((8, shard, slots), bf16), place, w_qkv
    )
    qkv_cols = exchange(qkv_parts, GRP).reshape(width, slots)
    place = after(place, qkv_parts)
    fc_parts = call(fc_columns_kernel, "fc_columns", struct((8, shard, hidden), bf16), place, w_fc)
    out_rows = swap_roles(after(w_out, qkv_parts))
    small = jnp.concatenate(
        [ln1_gain, ln1_bias, bias_q, bias_v, bias_out, ln2_gain, ln2_bias, bias_proj, bias_fc]
    ).reshape(3, hidden)
    small_all = exchange(after(jnp.broadcast_to(small, (8, 3, hidden)), qkv_cols), GRP)
    own_cot = swap_roles(after(cotangent, qkv_cols).reshape(span, width))

    small_all = small_all.astype(f32)
    hidden_bias = lax.dynamic_index_in_dim(small_all, rank, 0, keepdims=False)[2:3]
    vectors = small_all[:, :2].reshape(8, 8, shard).transpose(1, 0, 2).reshape(8, width)
    bias_slots = jnp.concatenate(
        [
            lax.dynamic_slice_in_dim(vectors[2], STRIDE * rank, SLOT_WIDTH),
            jnp.zeros((SLOT_WIDTH,), f32),
            lax.dynamic_slice_in_dim(vectors[3], STRIDE * rank, SLOT_WIDTH),
        ]
    ).reshape(1, slots)

    out_all = gather(out_rows, TEAM).reshape(width, width)
    all_cot = gather(after(own_cot, out_rows), TEAM).reshape(length, width)
    proj_rows = swap_selected(after(w_proj, small_all), stays)

    first, qkv, attended_slots, top = call(
        attend_kernel,
        "attend",
        (
            struct((length, width), bf16),
            struct((length, slots), bf16),
            struct((length, SLOT_WIDTH), bf16),
            struct((length, SLOTS), f32),
        ),
        all_tokens,
        qkv_cols,
        vectors,
        after(bias_slots, fc_parts),
        flops=2 * length * width * slots,
    )
    attended = exchange(
        after(attended_slots, proj_rows).reshape(8, span, SLOT_WIDTH), TEAM
    )
    middle, second, attended_parts = call(
        branch_kernel,
        "branch",
        (
            struct((span, width), f32),
            struct((span, width), bf16),
            struct((8, span, shard), bf16),
        ),
        attended,
        own_tokens,
        vectors,
        out_all,
        scratch=[pltpu.VMEM((span, width), bf16)],
        flops=2 * span * width * width,
    )

    second_all = gather(second, TEAM).reshape(length, width)
    fc_cols = exchange(after(fc_parts, second), GRP).reshape(width, hidden)
    grad_active = dot_cols(after(all_cot, second), proj_rows)
    active, grad_hidden, hidden_sums, second_parts = call(
        hidden_kernel,
        "hidden",
        (
            struct((length, hidden), bf16),
            struct((length, hidden), bf16),
            struct((1, hidden), f32),
            struct((length, width), bf16),
        ),
        place,
        second_all,
        fc_cols,
        hidden_bias,
        grad_active,
        flops=4 * length * width * hidden,
    )
    grad_second = team_sum(second_parts)
    fc_grad = call(
        weight_grad_kernel,
        "fc_grad",
        struct((width, hidden), bf16),
        second_all,
        grad_hidden,
        flops=2 * length * width * hidden,
    )
    fc_grad = swap_roles(fc_grad)
    proj_grad = call(
        weight_grad_kernel,
        "proj_grad",
        struct((hidden, width), bf16),
        active,
        all_cot,
        flops=2 * length * width * hidden,
    )
    down_parts = dot(active, proj_rows).astype(bf16)
    grad_second = after(grad_second, fc_grad, proj_grad, down_parts)

    grad_middle, grad_branch, grad_slots, branch_sums = call(
        branch_back_kernel,
        "branch_back",
        (
            struct((span, width), f32),
            struct((span, width), bf16),
            struct((8, span, SLOT_WIDTH), bf16),
            struct((4, width), f32),
        ),
        place,
        grad_second,
        middle,
        own_cot,
        vectors,
        out_all,
        scratch=[pltpu.VMEM((span, width), bf16)],
        flops=2 * span * width * width,
    )
    grad_heads = exchange(grad_slots, TEAM).reshape(length, SLOT_WIDTH)
    down = team_sum(after(down_parts, grad_second))
    attended_own = exchange(after(attended_parts, fc_grad), TEAM)
    proj_grad = swap_roles(after(proj_grad, grad_heads))
    fc_grad = exchange(after(fc_grad, grad_heads).reshape(8, shard, hidden), GRP)

    grad_mixed, first_parts, mixed_sums = call(
        attend_back_kernel,
        "attend_back",
        (
            struct((length, slots), bf16),
            struct((length, width), bf16),
            struct((1, slots), f32),
        ),
        place,
        qkv,
        grad_heads,
        attended_slots,
        top.T,
        qkv_cols,
        scratch=[pltpu.VMEM((length, HEAD_DIM), f32)],
        flops=2 * length * width * slots,
    )
    grad_first = team_sum(after(first_parts, down))
    qkv_grad = call(
        weight_grad_kernel,
        "qkv_grad",
        struct((width, slots), bf16),
        after(first, down),
        grad_mixed,
        flops=2 * length * width * slots,
    )
    place = after(place, qkv_grad)
    qkv_grad = swap_roles(qkv_grad)

    def halved(parts):
        give = lax.dynamic_index_in_dim(parts, 1 - c, 0, keepdims=False)
        keep = lax.dynamic_index_in_dim(parts, c, 0, keepdims=False)
        return (keep.astype(f32) + other_core(give).astype(f32)).astype(bf16)

    fc_half = halved(fc_grad.reshape(2, 4, shard, hidden))
    proj_half = halved(proj_grad.reshape(2, hidden // 2, width))
    fc_half, proj_half = lax.psum(after((fc_half, proj_half), grad_first), ("x", "zl"))

    branch_own = ring_all([after(grad_branch, qkv_grad)] * 4, "y")
    branch_other = [other_core(part) for part in branch_own]
    pad = shard // 2 // 8 * 8 + 8
    out_grad = call(
        out_grad_kernel,
        "out_grad",
        struct((2 * pad, width), bf16),
        place,
        attended_own,
        *branch_own,
        *branch_other,
        scratch=[pltpu.VMEM((shard, width), f32)],
        flops=2 * length * width * shard,
    )
    qkv_grad = exchange(qkv_grad.reshape(8, shard, slots), GRP)
    out_grad = swap_roles(out_grad)
    qkv_half = halved(qkv_grad.reshape(2, 4, shard, slots))
    out_half = halved(out_grad.reshape(2, pad, width))
    qkv_half, out_half = lax.psum(after((qkv_half, out_half), fc_half), ("x", "zl"))

    grad_inputs, first_sums = call(
        input_back_kernel,
        "input_back",
        (struct((span, width), bf16), struct((2, width), f32)),
        grad_first,
        own_tokens,
        grad_middle,
        after(vectors, qkv_grad),
    )
    inputs_home = swap_roles(grad_inputs).astype(f32).reshape(1, span, width)
    output = middle + (down.astype(f32) + vectors[7])
    output_home = swap_roles(output.astype(bf16)).reshape(1, span, width)

    blank = jnp.zeros((1, width), f32)
    at = (0, STRIDE * rank)
    small_terms = jnp.concatenate(
        [
            first_sums,
            lax.dynamic_update_slice(blank, mixed_sums[:, :SLOT_WIDTH], at),
            lax.dynamic_update_slice(blank, mixed_sums[:, 2 * SLOT_WIDTH :], at),
            branch_sums,
        ]
    )
    hidden_term = lax.dynamic_update_slice(
        jnp.zeros((8, hidden), f32), hidden_sums, (rank, 0)
    )
    small_terms = small_terms.reshape(8, 8, shard).transpose(1, 0, 2).reshape(8, 2, hidden)
    small_terms = jnp.concatenate([small_terms, hidden_term[:, None]], axis=1)
    small_sum = jnp.sum(exchange(small_terms, GRP), axis=0)
    small_sum = jnp.sum(exchange(jnp.broadcast_to(small_sum, (16, 3, hidden)), REP), axis=0)
    owned = small_sum[:2].reshape(8, shard)

    def column_total(half, spans, name):
        count = max(target + wide for span in spans for _, target, wide in span)
        return call(
            functools.partial(column_total_kernel, spans),
            name,
            struct((shard, count), f32),
            place,
            half,
            other_core(half),
        )

    def row_total(half, rows, name):
        return call(
            row_total_kernel, name, struct((rows, width), f32), place, half, other_core(half)
        )

    fc_total = column_total(fc_half, [[(0, r * hidden, hidden)] for r in range(8)], "fc_total")
    proj_total = row_total(proj_half, hidden, "proj_total")
    qkv_spans = [
        [
            (p * SLOT_WIDTH, p * width + STRIDE * r, STRIDE if r < 7 else SLOT_WIDTH)
            for p in range(3)
        ]
        for r in range(8)
    ]
    qkv_total = column_total(qkv_half, qkv_spans, "qkv_total")
    out_total = row_total(out_half, shard, "out_total")
    return (
        output_home,
        inputs_home,
        owned[0],
        owned[1],
        qkv_total,
        owned[2],
        owned[3],
        out_total,
        owned[4],
        owned[5],
        owned[6],
        fc_total,
        small_sum[2],
        proj_total,
        owned[7],
    )


def solution(mesh):
    names = tuple(name for name, _ in LAYOUT)
    fine = jax.sharding.Mesh(mesh.devices.reshape([size for _, size in LAYOUT]), names)
    in_specs = (
        P(REP, GRP, None),
        P(GRP),
        P(GRP),
        P(GRP, None),
        P(GRP),
        P(GRP),
        P(GRP, None),
        P(GRP),
        P(GRP),
        P(GRP),
        P(GRP, None),
        P(GRP),
        P(GRP, None),
        P(GRP),
        P(REP, GRP, None),
    )
    out_specs = (
        P(REP, GRP, None),
        P(REP, GRP, None),
        P(GRP),
        P(GRP),
        P(GRP, None),
        P(GRP),
        P(GRP),
        P(GRP, None),
        P(GRP),
        P(GRP),
        P(GRP),
        P(GRP, None),
        P(GRP),
        P(GRP, None),
        P(GRP),
    )
    return jax.shard_map(
        per_device, mesh=fine, in_specs=in_specs, out_specs=out_specs, check_vma=False
    )
```

```python
import functools
import math

import jax
import jax.numpy as jnp
from jax import lax
from jax.experimental import pallas as pl
from jax.experimental.pallas import tpu as pltpu
from jax.sharding import PartitionSpec as P

HEADS = 25
HEAD_DIM = 64
SLOTS = 4
SLOT_WIDTH = SLOTS * HEAD_DIM
STRIDE = 3 * HEAD_DIM
BLOCK = 256

bf16 = jnp.bfloat16
f32 = jnp.float32


LAYOUT = (("x", 4), ("zl", 2), ("c", 2), ("y", 4), ("zh", 2))
REP = ("x", "zl", "c")
GRP = ("y", "zh")
TEAM = ("y", "c")
REPLICAS = ("zl", "x", "zh")
Z_RING = ("zl", "zh")
Z_PLACES = (0, 2, 1, 3)
ROLES = [(0, 0), (1, 2), (2, 1), (3, 3)]


def ring(value, axis, step):
    index = Z_PLACES if axis == Z_RING else range(4)
    return lax.ppermute(value, axis, [(index[(i + step) % 4], index[i]) for i in range(4)])


def ring_all(values, axis):
    return [values[0]] + [ring(values[k], axis, k) for k in range(1, 4)]


def flipped(value, axis):
    return lax.ppermute(value, axis, [(0, 1), (1, 0)])


def swap_roles(value):
    return lax.ppermute(value, ("c", "zh"), ROLES)


def swap_selected(value, stays):
    return jnp.where(stays, value, lax.ppermute(value, ("c", "zh"), ROLES[1:3]))


def other_core(value):
    return lax.ppermute(value, "c", [(0, 1), (1, 0)])


def exchange(parts, axes):
    return lax.all_to_all(parts, axes, 0, 0)


def gather(block, axes):
    return lax.all_gather(block, axes, axis=0)


def team_sum(parts):
    return lax.psum_scatter(parts.astype(bf16), TEAM, scatter_dimension=0, tiled=True)


def windows(rows, count):
    tiles = rows // 8
    starts = [tiles * i // count for i in range(count)]
    size = max(b - a for a, b in zip(starts, starts[1:] + [tiles]))
    return size * 8, [8 * s for s in starts]


def joined(parts, starts, rows, axis):
    ends = starts[1:] + [rows]
    return jnp.concatenate(
        [lax.slice_in_dim(p, 0, e - s, axis=axis) for p, s, e in zip(parts, starts, ends)], axis
    )


def norm_parts(value, gain, shift):
    center = value - jnp.mean(value, axis=-1, keepdims=True)
    spread = jnp.mean(center * center, axis=-1, keepdims=True)
    factor = lax.rsqrt(spread + 1e-05)
    normed = center * factor
    return (normed * gain + shift, normed, factor)


def norm_back(grad_value, normed, factor, gain):
    grad_normed = grad_value * gain
    mean_first = jnp.mean(grad_normed, axis=-1, keepdims=True)
    mean_second = jnp.mean(grad_normed * normed, axis=-1, keepdims=True)
    return factor * (grad_normed - mean_first - normed * mean_second)


def dot(left, right):
    return jnp.dot(left, right, preferred_element_type=f32)


def dot_rows(left, right):
    return lax.dot_general(left, right, (((0,), (0,)), ((), ())), preferred_element_type=f32)


def dot_cols(left, right):
    return lax.dot_general(left, right, (((1,), (1,)), ((), ())), preferred_element_type=f32)


def call(kernel, name, out_shape, *operands, scratch=(), flops=0):
    specs = [
        pl.BlockSpec(memory_space=pltpu.SMEM if op.dtype == jnp.int32 else pltpu.VMEM)
        for op in operands
    ]
    out_specs = jax.tree.map(lambda _: pl.BlockSpec(memory_space=pltpu.VMEM), out_shape)
    moved = sum(op.size * op.dtype.itemsize for op in operands)
    moved += sum(o.size * o.dtype.itemsize for o in jax.tree.leaves(out_shape))
    return pl.pallas_call(
        kernel,
        out_shape=out_shape,
        in_specs=specs,
        out_specs=out_specs,
        scratch_shapes=list(scratch),
        compiler_params=pltpu.CompilerParams(vmem_limit_bytes=56 * 2**20),
        cost_estimate=pl.CostEstimate(
            flops=int(flops), bytes_accessed=int(moved), transcendentals=0
        ),
        name=name,
    )(*operands)


def struct(shape, dtype):
    return jax.ShapeDtypeStruct(shape, dtype)


Y, C, RANK, ZH, Z, X, ZL, MINE = range(8)


def qkv_columns_kernel(place_ref, weight_ref, *refs):
    out_refs, held_ref = refs[:4], refs[4]
    c = place_ref[C]
    width = weight_ref.shape[1] // 3
    for part in range(3):
        lanes = slice(part * SLOT_WIDTH, (part + 1) * SLOT_WIDTH)
        for y in range(4):
            start = part * width + 2 * STRIDE * y
            even = weight_ref[:, start : start + SLOT_WIDTH]
            odd = weight_ref[:, start + STRIDE : start + STRIDE + SLOT_WIDTH]
            held_ref[y, :, lanes] = jnp.where(c == 0, even, odd)
    for k in range(4):
        out_refs[k][...] = held_ref[lax.rem(place_ref[Y] + 4 - k, 4)]


def fc_columns_kernel(place_ref, weight_ref, *refs):
    out_refs, held_ref = refs[:4], refs[4]
    c = place_ref[C]
    hidden = weight_ref.shape[1] // 8
    for y in range(4):
        start = 2 * hidden * y
        even = weight_ref[:, start : start + hidden]
        odd = weight_ref[:, start + hidden : start + 2 * hidden]
        held_ref[y] = jnp.where(c == 0, even, odd)
    for k in range(4):
        out_refs[k][...] = held_ref[lax.rem(place_ref[Y] + 4 - k, 4)]


def fc_whole_kernel(place_ref, *refs):
    out_ref = refs[8]
    zh = place_ref[ZH]
    for k in range(4):
        y = lax.rem(place_ref[Y] + k, 4)
        out_ref[2 * y + zh] = refs[k][...]
        out_ref[2 * y + 1 - zh] = refs[4 + k][...]


def branch_kernel(
    slots_ref, tokens_ref, norm_ref, rows_ref, middle_ref, second_ref, parts_ref, flat_ref
):
    shard = parts_ref.shape[2]
    for rank in range(8):
        wide = STRIDE if rank < 7 else SLOT_WIDTH
        flat_ref[:, STRIDE * rank : STRIDE * rank + wide] = slots_ref[rank, :, :wide]
    for rank in range(8):
        parts_ref[rank] = flat_ref[:, shard * rank : shard * (rank + 1)]
    total = tokens_ref[...].astype(f32) + norm_ref[4:5, :] + dot(flat_ref[...], rows_ref[...])
    middle_ref[...] = total
    second_ref[...] = norm_parts(total, norm_ref[5:6, :], norm_ref[6:7, :])[0].astype(bf16)


def branch_back_kernel(
    place_ref,
    grad_ref,
    middle_ref,
    cot_ref,
    norm_ref,
    rows_ref,
    grad_middle_ref,
    branch_ref,
    slots_ref,
    sums_ref,
    flat_ref,
):
    gain = norm_ref[5:6, :]
    _, normed, factor = norm_parts(middle_ref[...], gain, gain)
    grad = grad_ref[...].astype(f32)
    cot = cot_ref[...].astype(f32)
    grad_middle = cot + norm_back(grad, normed, factor, gain)
    branch = grad_middle.astype(bf16)
    grad_middle_ref[...] = grad_middle
    branch_ref[...] = branch
    flat_ref[...] = dot_cols(branch, rows_ref[...]).astype(bf16)
    for rank in range(8):
        slots_ref[rank] = flat_ref[:, STRIDE * rank : STRIDE * rank + SLOT_WIDTH]
    sums_ref[0:1, :] = jnp.sum(branch.astype(f32), axis=0, keepdims=True)
    sums_ref[1:2, :] = jnp.sum(grad * normed, axis=0, keepdims=True)
    sums_ref[2:3, :] = jnp.sum(grad, axis=0, keepdims=True)
    sums_ref[3:4, :] = jnp.sum(cot, axis=0, keepdims=True)


def column_grad_kernel(left_ref, right_ref, out_ref):
    shard = left_ref.shape[1] // 8
    size, starts = windows(shard, 8)
    grad = dot_rows(left_ref[...], right_ref[...])
    for y in range(4):
        for zh in range(2):
            base = (2 * y + zh) * shard
            for i, start in enumerate(starts):
                out_ref[2 * i + zh, y] = grad[base + start : base + start + size].astype(bf16)


def column_ring_kernel(place_ref, left_ref, right_ref, *refs):
    out_refs, held_ref = refs[:4], refs[4]
    shard = left_ref.shape[1] // 8
    size, starts = windows(shard, 8)
    held_ref[...] = dot_rows(left_ref[...], right_ref[...])
    for k in range(4):
        x = lax.rem(place_ref[X] + 4 - k, 4)
        for z in range(4):
            for y in range(4):
                base = (2 * y + z // 2) * shard + starts[4 * (z % 2)]
                at = pl.multiple_of(base + starts[1] * x, 8)
                out_refs[k][z, y] = held_ref[pl.ds(at, size), :].astype(bf16)


def row_grad_kernel(place_ref, left_ref, right_ref, *refs):
    out_refs, held_ref = refs[:4], refs[4]
    rows = left_ref.shape[1]
    size = windows(rows, 16)[0]
    held_ref[...] = dot_rows(left_ref[...], right_ref[...])
    for k in range(4):
        z = lax.rem(place_ref[Z] + 4 - k, 4)
        for x in range(4):
            window = (lax.rem(z, 2) * 4 + x) * 2 + lax.div(z, 2)
            at = pl.multiple_of(lax.div(rows // 8 * window, 16) * 8, 8)
            out_refs[k][x] = held_ref[pl.ds(at, size), :].astype(bf16)


def out_grad_kernel(place_ref, left_ref, *refs):
    blocks, out_ref, held_ref = refs[:8], refs[8], refs[9]
    c = place_ref[C]
    rows = left_ref.shape[2]
    size, starts = windows(rows, 16)
    for k in range(4):
        y = lax.rem(place_ref[Y] + k, 4)
        term = dot_rows(left_ref[2 * y + c], blocks[k][...])
        term = term + dot_rows(left_ref[2 * y + 1 - c], blocks[4 + k][...])
        if k == 0:
            held_ref[...] = term
        else:
            held_ref[...] += term
    for i, start in enumerate(starts):
        out_ref[i] = held_ref[start : start + size, :].astype(bf16)


def fold_kernel(which, place_ref, *refs):
    for k in range(4):
        at = lax.rem(place_ref[which] + 4 - k, 4)
        total = refs[0][at].astype(f32)
        for j in range(1, 4):
            total = total + refs[j][at].astype(f32)
        refs[4 + k][...] = total.astype(bf16)


def stack_kernel(*refs):
    for k, ref in enumerate(refs[:-1]):
        refs[-1][k] = ref[...]


def column_total_kernel(spans, ringed, place_ref, *refs):
    out_ref = refs[8]
    shard = out_ref.shape[0]
    _, starts = windows(shard, 8)
    step = starts[1]
    for j in range(4):
        x = lax.rem(place_ref[X] + j, 4)
        for flip in range(2):
            window = (place_ref[ZL] if flip == 0 else 1 - place_ref[ZL]) * 4 + x
            at = pl.multiple_of(window * step, 8)
            for rank in range(8):
                k = lax.rem(rank // 2 + 4 - place_ref[Y], 4) if ringed else rank // 2
                block = jnp.where(
                    place_ref[C] == rank % 2, refs[j][flip, k], refs[4 + j][flip, k]
                ).astype(f32)
                for source, target, wide in spans[rank]:
                    out_ref[pl.ds(at, step), target : target + wide] = block[
                        :step, source : source + wide
                    ]

                @pl.when(window == 7)
                def _(block=block, rank=rank):
                    for source, target, wide in spans[rank]:
                        out_ref[7 * step + step :, target : target + wide] = block[
                            step:, source : source + wide
                        ]


def row_total_kernel(place_ref, own_ref, other_ref, out_ref):
    mine = place_ref[MINE]
    _, starts = windows(out_ref.shape[0], 16)
    ends = starts[1:] + [out_ref.shape[0]]
    for i, (start, end) in enumerate(zip(starts, ends)):
        block = jnp.where(mine == 1, own_ref[i], other_ref[i])
        out_ref[start:end, :] = block[: end - start].astype(f32)


def attend_kernel(place_ref, tokens_ref, norm_ref, bias_ref, *refs):
    pieces, (first_ref, qkv_ref, out_ref, top_ref, cols_ref) = refs[:8], refs[8:]
    length = tokens_ref.shape[0]
    shard = cols_ref.shape[1]
    zh = place_ref[ZH]
    for k in range(4):
        y = lax.rem(place_ref[Y] + k, 4)
        cols_ref[2 * y + zh] = pieces[k][...]
        cols_ref[2 * y + 1 - zh] = pieces[4 + k][...]
    gain = norm_ref[0:1, :]
    shift = norm_ref[1:2, :]
    for block in range(length // BLOCK):
        rows = slice(block * BLOCK, (block + 1) * BLOCK)
        first = norm_parts(tokens_ref[rows, :].astype(f32), gain, shift)[0].astype(bf16)
        first_ref[rows, :] = first
        mixed = bias_ref[...]
        for g in range(8):
            mixed = mixed + dot(first[:, g * shard : (g + 1) * shard], cols_ref[g])
        qkv_ref[rows, :] = mixed.astype(bf16)
    for head in range(SLOTS):
        lanes = slice(head * HEAD_DIM, (head + 1) * HEAD_DIM)
        keys = qkv_ref[:, SLOT_WIDTH + head * HEAD_DIM : SLOT_WIDTH + (head + 1) * HEAD_DIM]
        values = qkv_ref[
            :, 2 * SLOT_WIDTH + head * HEAD_DIM : 2 * SLOT_WIDTH + (head + 1) * HEAD_DIM
        ]
        for block in range(length // BLOCK):
            rows = slice(block * BLOCK, (block + 1) * BLOCK)
            width = (block + 1) * BLOCK
            query = qkv_ref[rows, lanes] * bf16(1.0 / math.sqrt(HEAD_DIM))
            scores = dot_cols(query, keys[:width])
            row = lax.broadcasted_iota(jnp.int32, (BLOCK, width), 0) + block * BLOCK
            col = lax.broadcasted_iota(jnp.int32, (BLOCK, width), 1)
            scores = jnp.where(col <= row, scores, -1e30)
            top = jnp.max(scores, axis=-1, keepdims=True)
            probs = jnp.exp(scores - top)
            total = jnp.sum(probs, axis=-1, keepdims=True)
            mixed = dot(probs.astype(bf16), values[:width])
            out_ref[rows, lanes] = (mixed / total).astype(bf16)
            top_ref[rows, head : head + 1] = top + jnp.log(total)


def hidden_kernel(
    place_ref, second_ref, cols_ref, bias_ref, grad_ref, active_ref, hidden_ref, sums_ref, out_ref
):
    length = second_ref.shape[0]
    sums = jnp.zeros(sums_ref.shape, f32)
    for block in range(length // BLOCK):
        rows = slice(block * BLOCK, (block + 1) * BLOCK)
        pre = dot(second_ref[rows, :], cols_ref[...]) + bias_ref[...]
        square = pre * pre
        bent = jnp.tanh(0.7978845608028654 * (pre + 0.044715 * square * pre))
        half = 0.5 * (1.0 + bent)
        active_ref[rows, :] = (pre * half).astype(bf16)
        slope = half + 0.5 * pre * (1.0 - bent * bent) * (
            0.7978845608028654 + (3.0 * 0.044715 * 0.7978845608028654) * square
        )
        grad = (grad_ref[rows, :] * slope).astype(bf16)
        hidden_ref[rows, :] = grad
        sums = sums + jnp.sum(grad.astype(f32), axis=0, keepdims=True)
        out_ref[rows, :] = dot_cols(grad, cols_ref[...]).astype(bf16)
    sums_ref[...] = sums


def attend_back_kernel(
    place_ref,
    qkv_ref,
    grad_ref,
    out_ref,
    top_ref,
    cols_ref,
    down_ref,
    mixed_ref,
    parts_ref,
    sums_ref,
    query_ref,
):
    length = qkv_ref.shape[0]
    scale = 1.0 / math.sqrt(HEAD_DIM)
    ones = jnp.ones((8, HEAD_DIM), bf16)
    for head in range(SLOTS):
        base = head * HEAD_DIM
        lanes = slice(base, base + HEAD_DIM)
        key_lanes = slice(SLOT_WIDTH + base, SLOT_WIDTH + base + HEAD_DIM)
        value_lanes = slice(2 * SLOT_WIDTH + base, 2 * SLOT_WIDTH + base + HEAD_DIM)
        query = qkv_ref[:, lanes] * bf16(scale)
        grad = grad_ref[:, lanes]
        if head == SLOTS - 1:
            grad = jnp.where(place_ref[RANK] == 7, grad, jnp.zeros_like(grad))
        top = top_ref[head : head + 1, :]
        delta = dot_cols(ones, grad * out_ref[:, lanes])[0:1, :]
        for block in range(length // BLOCK):
            start = block * BLOCK
            rows = slice(start, start + BLOCK)
            width = length - start
            keys = qkv_ref[rows, key_lanes]
            values = qkv_ref[rows, value_lanes]
            scores = dot_cols(keys, query[start:])
            row = lax.broadcasted_iota(jnp.int32, (BLOCK, width), 0)
            col = lax.broadcasted_iota(jnp.int32, (BLOCK, width), 1)
            probs = jnp.where(row <= col, jnp.exp(scores - top[:, start:]), 0.0)
            grad_probs = dot_cols(values, grad[start:])
            grad_scores = (probs * (grad_probs - delta[:, start:])).astype(bf16)
            mixed_ref[rows, value_lanes] = dot(probs.astype(bf16), grad[start:]).astype(bf16)
            mixed_ref[rows, key_lanes] = dot(grad_scores, query[start:]).astype(bf16)
            term = dot_rows(grad_scores, keys)
            if block == 0:
                query_ref[...] = term
            else:
                query_ref[start:, :] += term
        mixed_ref[:, lanes] = (query_ref[...] * scale).astype(bf16)
    sums = jnp.zeros(sums_ref.shape, f32)
    for block in range(length // BLOCK):
        rows = slice(block * BLOCK, (block + 1) * BLOCK)
        mixed = mixed_ref[rows, :]
        sums = sums + jnp.sum(mixed.astype(f32), axis=0, keepdims=True)
        first = dot_cols(mixed, cols_ref[...]).astype(bf16)
        for half in range(2):
            rank = 2 * block + half
            parts_ref[rank, 0] = first[half * BLOCK // 2 : (half + 1) * BLOCK // 2]
            parts_ref[rank, 1] = down_ref[rank]
    sums_ref[...] = sums


def input_back_kernel(
    parts_ref, tokens_ref, middle_ref, grad_ref, norm_ref, out_ref, sums_ref
):
    gain = norm_ref[0:1, :]
    _, normed, factor = norm_parts(tokens_ref[...].astype(f32), gain, gain)
    grad = parts_ref[0].astype(f32)
    out_ref[0] = (grad_ref[...] + norm_back(grad, normed, factor, gain)).astype(bf16)
    down = parts_ref[1].astype(f32) + norm_ref[7:8, :]
    out_ref[1] = (middle_ref[...] + down).astype(bf16)
    sums_ref[0:1, :] = jnp.sum(grad * normed, axis=0, keepdims=True)
    sums_ref[1:2, :] = jnp.sum(grad, axis=0, keepdims=True)


def after(value, *others):
    return lax.optimization_barrier((value,) + others)[0]


def per_device(
    tokens,
    ln1_gain,
    ln1_bias,
    w_qkv,
    bias_q,
    bias_v,
    w_out,
    bias_out,
    ln2_gain,
    ln2_bias,
    w_fc,
    bias_fc,
    w_proj,
    bias_proj,
    cotangent,
):
    _, span, width = tokens.shape
    shard = width // 8
    hidden = w_fc.shape[1] // 8
    length = span * 8
    slots = 3 * SLOT_WIDTH
    x, zl, c, y, zh = [lax.axis_index(name) for name, _ in LAYOUT]
    rank = y * 2 + c
    place = jnp.stack(
        [y, c, rank, zh, zh * 2 + zl, x, zl, (c == zh).astype(jnp.int32)]
    ).astype(jnp.int32)

    stays = c == zh
    own_tokens = swap_roles(tokens.reshape(span, width))
    all_tokens = gather(own_tokens, TEAM).reshape(length, width)
    out_rows = swap_roles(w_out)
    proj_came = lax.ppermute(after(w_proj, own_tokens), ("c", "zh"), ROLES[1:3])
    qkv_parts = call(
        qkv_columns_kernel,
        "qkv_columns",
        [struct((shard, slots), bf16)] * 4,
        place,
        w_qkv,
        scratch=[pltpu.VMEM((4, shard, slots), bf16)],
    )
    qkv_own = ring_all(qkv_parts, "y")
    small = jnp.concatenate(
        [ln1_gain, ln1_bias, bias_q, bias_v, bias_out, ln2_gain, ln2_bias, bias_proj, bias_fc]
    ).reshape(3, hidden)
    small_all = exchange(
        after(jnp.broadcast_to(small, (8, 3, hidden)), qkv_parts[0]), GRP
    )
    qkv_other = [flipped(after(part, proj_came, out_rows), "zh") for part in qkv_own]
    place = after(place, small_all)
    fc_parts = call(
        fc_columns_kernel,
        "fc_columns",
        [struct((shard, hidden), bf16)] * 4,
        place,
        w_fc,
        scratch=[pltpu.VMEM((4, shard, hidden), bf16)],
    )
    own_cot = swap_roles(after(cotangent, *qkv_other).reshape(span, width))

    small_all = small_all.astype(f32)
    hidden_bias = lax.dynamic_index_in_dim(small_all, rank, 0, keepdims=False)[2:3]
    vectors = small_all[:, :2].reshape(8, 8, shard).transpose(1, 0, 2).reshape(8, width)
    bias_slots = jnp.concatenate(
        [
            lax.dynamic_slice_in_dim(vectors[2], STRIDE * rank, SLOT_WIDTH),
            jnp.zeros((SLOT_WIDTH,), f32),
            lax.dynamic_slice_in_dim(vectors[3], STRIDE * rank, SLOT_WIDTH),
        ]
    ).reshape(1, slots)

    out_all = gather(out_rows, TEAM).reshape(width, width)
    all_cot = gather(after(own_cot, out_rows), TEAM).reshape(length, width)
    proj_rows = jnp.where(stays, w_proj, after(proj_came, *qkv_other))
    fc_own = ring_all([after(part, *qkv_other) for part in fc_parts], "y")

    first, qkv, attended_slots, top, qkv_cols = call(
        attend_kernel,
        "attend",
        (
            struct((length, width), bf16),
            struct((length, slots), bf16),
            struct((length, SLOT_WIDTH), bf16),
            struct((length, SLOTS), f32),
            struct((8, shard, slots), bf16),
        ),
        after(place, bias_slots),
        all_tokens,
        vectors,
        bias_slots,
        *qkv_own,
        *qkv_other,
        flops=2 * length * width * slots,
    )
    qkv_cols = qkv_cols.reshape(width, slots)
    fc_other = [flipped(part, "zh") for part in fc_own]
    attended = exchange(after(attended_slots, *fc_own).reshape(8, span, SLOT_WIDTH), TEAM)
    middle, second, attended_parts = call(
        branch_kernel,
        "branch",
        (
            struct((span, width), f32),
            struct((span, width), bf16),
            struct((8, span, shard), bf16),
        ),
        attended,
        own_tokens,
        vectors,
        out_all,
        scratch=[pltpu.VMEM((span, width), bf16)],
        flops=2 * span * width * width,
    )

    second_all = gather(second, TEAM).reshape(length, width)
    attended_own = exchange(after(attended_parts, *fc_other), TEAM)
    grad_active = dot_cols(after(all_cot, second), proj_rows)
    fc_cols = call(
        fc_whole_kernel,
        "fc_whole",
        struct((8, shard, hidden), bf16),
        place,
        after(fc_own[0], second),
        *fc_own[1:],
        *fc_other,
    ).reshape(width, hidden)
    active, grad_hidden, hidden_sums, second_parts = call(
        hidden_kernel,
        "hidden",
        (
            struct((length, hidden), bf16),
            struct((length, hidden), bf16),
            struct((1, hidden), f32),
            struct((length, width), bf16),
        ),
        after(place, attended_own),
        second_all,
        fc_cols,
        hidden_bias,
        grad_active,
        flops=4 * length * width * hidden,
    )
    grad_second = team_sum(second_parts)
    window = windows(shard, 8)[0]
    fc_grad = call(
        column_ring_kernel,
        "fc_grad",
        [struct((4, 4, window, hidden), bf16)] * 4,
        place,
        second_all,
        grad_hidden,
        scratch=[pltpu.VMEM((width, hidden), f32)],
        flops=2 * length * width * hidden,
    )
    fc_grad = ring_all(fc_grad, "x")
    row_window = windows(hidden, 16)[0]
    proj_grad = call(
        row_grad_kernel,
        "proj_grad",
        [struct((4, row_window, width), bf16)] * 4,
        place,
        active,
        all_cot,
        scratch=[pltpu.VMEM((hidden, width), f32)],
        flops=2 * length * width * hidden,
    )
    down_parts = dot(active, proj_rows).astype(bf16)

    grad_middle, grad_branch, grad_slots, branch_sums = call(
        branch_back_kernel,
        "branch_back",
        (
            struct((span, width), f32),
            struct((span, width), bf16),
            struct((8, span, SLOT_WIDTH), bf16),
            struct((4, width), f32),
        ),
        after(place, fc_grad[0], proj_grad[0], down_parts),
        grad_second,
        middle,
        own_cot,
        vectors,
        out_all,
        scratch=[pltpu.VMEM((span, width), bf16)],
        flops=2 * span * width * width,
    )
    grad_heads = exchange(grad_slots, TEAM).reshape(length, SLOT_WIDTH)

    def fold(which, parts, name, *behind):
        parts = [after(parts[0], *behind)] + parts[1:]
        return call(
            functools.partial(fold_kernel, which),
            name,
            [struct(parts[0].shape[1:], bf16)] * 4,
            place,
            *parts,
        )

    fc_grad = fold(Z, fc_grad, "fc_fold", grad_slots)
    proj_grad = ring_all([after(part, fc_grad[0]) for part in proj_grad], Z_RING)
    grad_mixed, last_parts, mixed_sums = call(
        attend_back_kernel,
        "attend_back",
        (
            struct((length, slots), bf16),
            struct((8, 2, span, width), bf16),
            struct((1, slots), f32),
        ),
        after(place, fc_grad[0]),
        qkv,
        grad_heads,
        attended_slots,
        top.T,
        qkv_cols,
        down_parts.reshape(8, span, width),
        scratch=[pltpu.VMEM((length, HEAD_DIM), f32)],
        flops=2 * length * width * slots,
    )
    last = team_sum(last_parts.reshape(2 * length, width)).reshape(2, span, width)
    qkv_grad = call(
        column_grad_kernel,
        "qkv_grad",
        struct((16, 4, window, slots), bf16),
        first,
        grad_mixed,
        flops=2 * length * width * slots,
    )
    place = after(place, qkv_grad)
    qkv_grad = exchange(qkv_grad, REPLICAS)
    fc_grad = ring_all([after(part, place) for part in fc_grad], Z_RING)
    branch_own = ring_all([after(grad_branch, qkv_grad)] * 4, "y")

    def replica_sum(parts):
        return jnp.sum(parts.astype(f32), axis=0).astype(bf16)

    def stacked(parts, name):
        return call(
            stack_kernel, name, struct((len(parts),) + parts[0].shape, bf16), *parts
        )

    def row_total(whole, rows, name, *behind):
        whole = after(whole, *behind)
        return call(
            row_total_kernel, name, struct((rows, width), f32), place, whole, other_core(whole)
        )

    fc_grad = ring_all(fold(Y, fc_grad, "fc_fold_last", place), "y")
    fc_near = stacked(fc_grad, "fc_near")
    fc_both = stacked([fc_near, flipped(fc_near, "zl")], "fc_both")
    branch_other = [other_core(part) for part in branch_own]
    out_grad = call(
        out_grad_kernel,
        "out_grad",
        struct((16, windows(shard, 16)[0], width), bf16),
        place,
        attended_own,
        *branch_own,
        *branch_other,
        scratch=[pltpu.VMEM((shard, width), f32)],
        flops=2 * length * width * shard,
    )

    place = after(place, qkv_grad)
    qkv_sum = exchange(replica_sum(after(qkv_grad, fc_both)), "y")
    proj_grad = ring_all(fold(X, proj_grad, "proj_fold", place), "x")
    proj_sum = sum(part.astype(f32) for part in proj_grad).astype(bf16)
    proj_whole = gather(proj_sum, REPLICAS)
    qkv_both = stacked([qkv_sum, flipped(qkv_sum, "zl")], "qkv_both")
    qkv_pieces = ring_all([qkv_both] * 4, "x")
    out_grad = exchange(after(out_grad, qkv_both), REPLICAS)
    fc_pieces = ring_all([after(fc_both, *qkv_pieces)] * 4, "x")
    results, first_sums = call(
        input_back_kernel,
        "input_back",
        (struct((2, span, width), bf16), struct((2, width), f32)),
        last,
        own_tokens,
        middle,
        grad_middle,
        after(vectors, *qkv_pieces),
    )
    results_home = swap_roles(results)

    blank = jnp.zeros((1, width), f32)
    at = (0, STRIDE * rank)
    small_terms = jnp.concatenate(
        [
            first_sums,
            lax.dynamic_update_slice(blank, mixed_sums[:, :SLOT_WIDTH], at),
            lax.dynamic_update_slice(blank, mixed_sums[:, 2 * SLOT_WIDTH :], at),
            branch_sums,
        ]
    )
    hidden_term = lax.dynamic_update_slice(
        jnp.zeros((8, hidden), f32), hidden_sums, (rank, 0)
    )
    small_terms = small_terms.reshape(8, 8, shard).transpose(1, 0, 2).reshape(8, 2, hidden)
    small_terms = jnp.concatenate([small_terms, hidden_term[:, None]], axis=1)
    small_sum = jnp.sum(exchange(after(small_terms, out_grad), GRP), axis=0)
    out_sum = replica_sum(out_grad)
    out_whole = exchange(
        after(jnp.broadcast_to(out_sum, (16,) + out_sum.shape), small_sum), REPLICAS
    )
    small_sum = jnp.broadcast_to(after(small_sum, out_whole), (16, 3, hidden))
    small_sum = jnp.sum(exchange(small_sum, REP), axis=0)
    owned = small_sum[:2].reshape(8, shard)

    qkv_pieces = qkv_pieces + [other_core(part) for part in qkv_pieces]
    qkv_spans = [
        [
            (p * SLOT_WIDTH, p * width + STRIDE * r, STRIDE if r < 7 else SLOT_WIDTH)
            for p in range(3)
        ]
        for r in range(8)
    ]
    qkv_total = call(
        functools.partial(column_total_kernel, qkv_spans, False),
        "qkv_total",
        struct((shard, 3 * width), f32),
        after(place, results, out_grad),
        *qkv_pieces,
    )
    fc_pieces = fc_pieces + [other_core(after(part, qkv_total)) for part in fc_pieces]
    fc_spans = [[(0, rank * hidden, hidden)] for rank in range(8)]
    fc_total = call(
        functools.partial(column_total_kernel, fc_spans, True),
        "fc_total",
        struct((shard, 8 * hidden), f32),
        after(place, out_whole, small_sum),
        *fc_pieces,
    )
    out_total = row_total(out_whole, shard, "out_total", fc_total)
    proj_total = row_total(proj_whole, hidden, "proj_total", fc_total)
    return (
        results_home[1].reshape(1, span, width),
        results_home[0].astype(f32).reshape(1, span, width),
        owned[0],
        owned[1],
        qkv_total,
        owned[2],
        owned[3],
        out_total,
        owned[4],
        owned[5],
        owned[6],
        fc_total,
        small_sum[2],
        proj_total,
        owned[7],
    )


def solution(mesh):
    names = tuple(name for name, _ in LAYOUT)
    fine = jax.sharding.Mesh(mesh.devices.reshape([size for _, size in LAYOUT]), names)
    in_specs = (
        P(REP, GRP, None),
        P(GRP),
        P(GRP),
        P(GRP, None),
        P(GRP),
        P(GRP),
        P(GRP, None),
        P(GRP),
        P(GRP),
        P(GRP),
        P(GRP, None),
        P(GRP),
        P(GRP, None),
        P(GRP),
        P(REP, GRP, None),
    )
    out_specs = (
        P(REP, GRP, None),
        P(REP, GRP, None),
        P(GRP),
        P(GRP),
        P(GRP, None),
        P(GRP),
        P(GRP),
        P(GRP, None),
        P(GRP),
        P(GRP),
        P(GRP),
        P(GRP, None),
        P(GRP),
        P(GRP, None),
        P(GRP),
    )
    return jax.shard_map(
        per_device, mesh=fine, in_specs=in_specs, out_specs=out_specs, check_vma=False
    )
```

```python
import functools
import math

import jax
import jax.numpy as jnp
from jax import lax
from jax.experimental import pallas as pl
from jax.experimental.pallas import tpu as pltpu
from jax.sharding import PartitionSpec as P

HEADS = 25
HEAD_DIM = 64
SLOTS = 4
SLOT_WIDTH = SLOTS * HEAD_DIM
STRIDE = 3 * HEAD_DIM
BLOCK = 256

bf16 = jnp.bfloat16
f32 = jnp.float32


LAYOUT = (("x", 4), ("zl", 2), ("c", 2), ("y", 4), ("zh", 2))
REP = ("x", "zl", "c")
GRP = ("y", "zh")
TEAM = ("y", "c")
REPLICAS = ("zl", "x", "zh")
Z_RING = ("zl", "zh")
Z_PLACES = (0, 2, 1, 3)
ROLES = [(0, 0), (1, 2), (2, 1), (3, 3)]


def ring(value, axis, step):
    index = Z_PLACES if axis == Z_RING else range(4)
    return lax.ppermute(value, axis, [(index[(i + step) % 4], index[i]) for i in range(4)])


def ring_all(values, axis):
    return [values[0]] + [ring(values[k], axis, k) for k in range(1, 4)]


def flipped(value, axis):
    return lax.ppermute(value, axis, [(0, 1), (1, 0)])


def swap_roles(value):
    return lax.ppermute(value, ("c", "zh"), ROLES)


def swap_selected(value, stays):
    return jnp.where(stays, value, lax.ppermute(value, ("c", "zh"), ROLES[1:3]))


def other_core(value):
    return lax.ppermute(value, "c", [(0, 1), (1, 0)])


def exchange(parts, axes):
    return lax.all_to_all(parts, axes, 0, 0)


def gather(block, axes):
    return lax.all_gather(block, axes, axis=0)


def team_sum(parts):
    return lax.psum_scatter(parts.astype(bf16), TEAM, scatter_dimension=0, tiled=True)


def windows(rows, count):
    tiles = rows // 8
    starts = [tiles * i // count for i in range(count)]
    size = max(b - a for a, b in zip(starts, starts[1:] + [tiles]))
    return size * 8, [8 * s for s in starts]


def joined(parts, starts, rows, axis):
    ends = starts[1:] + [rows]
    return jnp.concatenate(
        [lax.slice_in_dim(p, 0, e - s, axis=axis) for p, s, e in zip(parts, starts, ends)], axis
    )


def norm_parts(value, gain, shift):
    center = value - jnp.mean(value, axis=-1, keepdims=True)
    spread = jnp.mean(center * center, axis=-1, keepdims=True)
    factor = lax.rsqrt(spread + 1e-05)
    normed = center * factor
    return (normed * gain + shift, normed, factor)


def norm_back(grad_value, normed, factor, gain):
    grad_normed = grad_value * gain
    mean_first = jnp.mean(grad_normed, axis=-1, keepdims=True)
    mean_second = jnp.mean(grad_normed * normed, axis=-1, keepdims=True)
    return factor * (grad_normed - mean_first - normed * mean_second)


def dot(left, right):
    return jnp.dot(left, right, preferred_element_type=f32)


def dot_rows(left, right):
    return lax.dot_general(left, right, (((0,), (0,)), ((), ())), preferred_element_type=f32)


def dot_cols(left, right):
    return lax.dot_general(left, right, (((1,), (1,)), ((), ())), preferred_element_type=f32)


def call(kernel, name, out_shape, *operands, scratch=(), flops=0, light=False):
    specs = [
        pl.BlockSpec(memory_space=pltpu.SMEM if op.dtype == jnp.int32 else pltpu.VMEM)
        for op in operands
    ]
    out_specs = jax.tree.map(lambda _: pl.BlockSpec(memory_space=pltpu.VMEM), out_shape)
    moved = sum(op.size * op.dtype.itemsize for op in operands)
    moved += sum(o.size * o.dtype.itemsize for o in jax.tree.leaves(out_shape))
    return pl.pallas_call(
        kernel,
        out_shape=out_shape,
        in_specs=specs,
        out_specs=out_specs,
        scratch_shapes=list(scratch),
        compiler_params=pltpu.CompilerParams(vmem_limit_bytes=56 * 2**20),
        cost_estimate=pl.CostEstimate(
            flops=1 if light else int(flops),
            bytes_accessed=1 if light else int(moved),
            transcendentals=0,
        ),
        name=name,
    )(*operands)


def struct(shape, dtype):
    return jax.ShapeDtypeStruct(shape, dtype)


Y, C, RANK, ZH, Z, X, ZL, MINE = range(8)


def qkv_columns_kernel(place_ref, weight_ref, *refs):
    out_refs, held_ref = refs[:4], refs[4]
    c = place_ref[C]
    width = weight_ref.shape[1] // 3
    for part in range(3):
        lanes = slice(part * SLOT_WIDTH, (part + 1) * SLOT_WIDTH)
        for y in range(4):
            start = part * width + 2 * STRIDE * y
            even = weight_ref[:, start : start + SLOT_WIDTH]
            odd = weight_ref[:, start + STRIDE : start + STRIDE + SLOT_WIDTH]
            held_ref[y, :, lanes] = jnp.where(c == 0, even, odd)
    for k in range(4):
        out_refs[k][...] = held_ref[lax.rem(place_ref[Y] + 4 - k, 4)]


def fc_columns_kernel(place_ref, weight_ref, *refs):
    out_refs, held_ref = refs[:4], refs[4]
    c = place_ref[C]
    hidden = weight_ref.shape[1] // 8
    for y in range(4):
        start = 2 * hidden * y
        even = weight_ref[:, start : start + hidden]
        odd = weight_ref[:, start + hidden : start + 2 * hidden]
        held_ref[y] = jnp.where(c == 0, even, odd)
    for k in range(4):
        out_refs[k][...] = held_ref[lax.rem(place_ref[Y] + 4 - k, 4)]


def fc_whole_kernel(place_ref, *refs):
    out_ref = refs[8]
    zh = place_ref[ZH]
    for k in range(4):
        y = lax.rem(place_ref[Y] + k, 4)
        out_ref[2 * y + zh] = refs[k][...]
        out_ref[2 * y + 1 - zh] = refs[4 + k][...]


def branch_kernel(
    slots_ref, tokens_ref, norm_ref, rows_ref, middle_ref, second_ref, parts_ref, flat_ref
):
    shard = parts_ref.shape[2]
    for rank in range(8):
        wide = STRIDE if rank < 7 else SLOT_WIDTH
        flat_ref[:, STRIDE * rank : STRIDE * rank + wide] = slots_ref[rank, :, :wide]
    for rank in range(8):
        parts_ref[rank] = flat_ref[:, shard * rank : shard * (rank + 1)]
    total = tokens_ref[...].astype(f32) + norm_ref[4:5, :] + dot(flat_ref[...], rows_ref[...])
    middle_ref[...] = total
    second_ref[...] = norm_parts(total, norm_ref[5:6, :], norm_ref[6:7, :])[0].astype(bf16)


def branch_back_kernel(
    place_ref,
    grad_ref,
    middle_ref,
    cot_ref,
    norm_ref,
    rows_ref,
    grad_middle_ref,
    branch_ref,
    slots_ref,
    sums_ref,
    flat_ref,
):
    gain = norm_ref[5:6, :]
    _, normed, factor = norm_parts(middle_ref[...], gain, gain)
    grad = grad_ref[...].astype(f32)
    cot = cot_ref[...].astype(f32)
    grad_middle = cot + norm_back(grad, normed, factor, gain)
    branch = grad_middle.astype(bf16)
    grad_middle_ref[...] = grad_middle
    branch_ref[...] = branch
    flat_ref[...] = dot_cols(branch, rows_ref[...]).astype(bf16)
    for rank in range(8):
        slots_ref[rank] = flat_ref[:, STRIDE * rank : STRIDE * rank + SLOT_WIDTH]
    sums_ref[0:1, :] = jnp.sum(branch.astype(f32), axis=0, keepdims=True)
    sums_ref[1:2, :] = jnp.sum(grad * normed, axis=0, keepdims=True)
    sums_ref[2:3, :] = jnp.sum(grad, axis=0, keepdims=True)
    sums_ref[3:4, :] = jnp.sum(cot, axis=0, keepdims=True)


def column_ring_kernel(place_ref, left_ref, right_ref, *refs):
    out_refs, held_ref = refs[:4], refs[4]
    shard = left_ref.shape[1] // 8
    size, starts = windows(shard, 8)
    held_ref[...] = dot_rows(left_ref[...], right_ref[...])
    for k in range(4):
        x = lax.rem(place_ref[X] + 4 - k, 4)
        for z in range(4):
            for y in range(4):
                base = (2 * y + z // 2) * shard + starts[4 * (z % 2)]
                at = pl.multiple_of(base + starts[1] * x, 8)
                out_refs[k][z, y] = held_ref[pl.ds(at, size), :].astype(bf16)


def row_grad_kernel(place_ref, left_ref, right_ref, *refs):
    out_refs, held_ref = refs[:4], refs[4]
    rows = left_ref.shape[1]
    size = windows(rows, 16)[0]
    held_ref[...] = dot_rows(left_ref[...], right_ref[...])
    for k in range(4):
        z = lax.rem(place_ref[Z] + 4 - k, 4)
        for x in range(4):
            window = (lax.rem(z, 2) * 4 + x) * 2 + lax.div(z, 2)
            at = pl.multiple_of(lax.div(rows // 8 * window, 16) * 8, 8)
            out_refs[k][x] = held_ref[pl.ds(at, size), :].astype(bf16)


def last_grads_kernel(place_ref, first_ref, mixed_ref, attended_ref, branch_ref, out_ref, held_ref):
    shard = first_ref.shape[1] // 8
    slots = mixed_ref.shape[1]
    size, starts = windows(shard, 8)
    held_ref[...] = dot_rows(first_ref[...], mixed_ref[...])
    for y in range(4):
        for zh in range(2):
            base = (2 * y + zh) * shard
            for i, start in enumerate(starts):
                rows = slice(y % 2 * size, (y % 2 + 1) * size)
                lanes = slice(y // 2 * slots, (y // 2 + 1) * slots)
                block = held_ref[base + start : base + start + size, :]
                out_ref[2 * i + zh, rows, lanes] = block.astype(bf16)
    size_out, starts_out = windows(shard, 16)
    grad = dot_rows(attended_ref[...], branch_ref[...])
    rest = jnp.zeros((2 * size, out_ref.shape[2] - 2 * slots), bf16)
    for i, start in enumerate(starts_out):
        out_ref[i, : 2 * size, 2 * slots :] = rest
        out_ref[i, 2 * size :, :] = grad[start : start + size_out].astype(bf16)


def last_sum_kernel(parts_ref, qkv_ref, out_ref):
    size, slots = qkv_ref.shape[1:]
    total = parts_ref[0].astype(f32)
    for i in range(1, 16):
        total = total + parts_ref[i].astype(f32)
    total = total.astype(bf16)
    for y in range(4):
        rows = slice(y % 2 * size, (y % 2 + 1) * size)
        qkv_ref[y] = total[rows, y // 2 * slots : (y // 2 + 1) * slots]
    out_ref[...] = total[2 * size :, :]


def fold_kernel(which, place_ref, *refs):
    for k in range(4):
        at = lax.rem(place_ref[which] + 4 - k, 4)
        total = refs[0][at].astype(f32)
        for j in range(1, 4):
            total = total + refs[j][at].astype(f32)
        refs[4 + k][...] = total.astype(bf16)


def stack_kernel(*refs):
    for k, ref in enumerate(refs[:-1]):
        refs[-1][k] = ref[...]


def column_total_kernel(spans, ringed, place_ref, *refs):
    out_ref = refs[8]
    shard = out_ref.shape[0]
    _, starts = windows(shard, 8)
    step = starts[1]
    for j in range(4):
        x = lax.rem(place_ref[X] + j, 4)
        for flip in range(2):
            window = (place_ref[ZL] if flip == 0 else 1 - place_ref[ZL]) * 4 + x
            at = pl.multiple_of(window * step, 8)
            for rank in range(8):
                k = lax.rem(rank // 2 + 4 - place_ref[Y], 4) if ringed else rank // 2
                block = jnp.where(
                    place_ref[C] == rank % 2, refs[j][flip, k], refs[4 + j][flip, k]
                ).astype(f32)
                for source, target, wide in spans[rank]:
                    out_ref[pl.ds(at, step), target : target + wide] = block[
                        :step, source : source + wide
                    ]

                @pl.when(window == 7)
                def _(block=block, rank=rank):
                    for source, target, wide in spans[rank]:
                        out_ref[7 * step + step :, target : target + wide] = block[
                            step:, source : source + wide
                        ]


def row_total_kernel(place_ref, own_ref, other_ref, out_ref):
    mine = place_ref[MINE]
    _, starts = windows(out_ref.shape[0], 16)
    ends = starts[1:] + [out_ref.shape[0]]
    for i, (start, end) in enumerate(zip(starts, ends)):
        block = jnp.where(mine == 1, own_ref[i], other_ref[i])
        out_ref[start:end, :] = block[: end - start].astype(f32)


def attend_kernel(place_ref, tokens_ref, norm_ref, bias_ref, *refs):
    pieces, (first_ref, qkv_ref, out_ref, top_ref, cols_ref) = refs[:8], refs[8:]
    length = tokens_ref.shape[0]
    shard = cols_ref.shape[1]
    zh = place_ref[ZH]
    for k in range(4):
        y = lax.rem(place_ref[Y] + k, 4)
        cols_ref[2 * y + zh] = pieces[k][...]
        cols_ref[2 * y + 1 - zh] = pieces[4 + k][...]
    gain = norm_ref[0:1, :]
    shift = norm_ref[1:2, :]
    for block in range(length // BLOCK):
        rows = slice(block * BLOCK, (block + 1) * BLOCK)
        first = norm_parts(tokens_ref[rows, :].astype(f32), gain, shift)[0].astype(bf16)
        first_ref[rows, :] = first
        mixed = bias_ref[...]
        for g in range(8):
            mixed = mixed + dot(first[:, g * shard : (g + 1) * shard], cols_ref[g])
        qkv_ref[rows, :] = mixed.astype(bf16)
    for head in range(SLOTS):
        lanes = slice(head * HEAD_DIM, (head + 1) * HEAD_DIM)
        keys = qkv_ref[:, SLOT_WIDTH + head * HEAD_DIM : SLOT_WIDTH + (head + 1) * HEAD_DIM]
        values = qkv_ref[
            :, 2 * SLOT_WIDTH + head * HEAD_DIM : 2 * SLOT_WIDTH + (head + 1) * HEAD_DIM
        ]
        for block in range(length // BLOCK):
            rows = slice(block * BLOCK, (block + 1) * BLOCK)
            width = (block + 1) * BLOCK
            query = qkv_ref[rows, lanes] * bf16(1.0 / math.sqrt(HEAD_DIM))
            scores = dot_cols(query, keys[:width])
            row = lax.broadcasted_iota(jnp.int32, (BLOCK, width), 0) + block * BLOCK
            col = lax.broadcasted_iota(jnp.int32, (BLOCK, width), 1)
            scores = jnp.where(col <= row, scores, -1e30)
            top = jnp.max(scores, axis=-1, keepdims=True)
            probs = jnp.exp(scores - top)
            total = jnp.sum(probs, axis=-1, keepdims=True)
            mixed = dot(probs.astype(bf16), values[:width])
            out_ref[rows, lanes] = (mixed / total).astype(bf16)
            top_ref[rows, head : head + 1] = top + jnp.log(total)


def hidden_kernel(
    place_ref, second_ref, cols_ref, bias_ref, grad_ref, active_ref, hidden_ref, sums_ref, out_ref
):
    length = second_ref.shape[0]
    sums = jnp.zeros(sums_ref.shape, f32)
    for block in range(length // BLOCK):
        rows = slice(block * BLOCK, (block + 1) * BLOCK)
        pre = dot(second_ref[rows, :], cols_ref[...]) + bias_ref[...]
        square = pre * pre
        bent = jnp.tanh(0.7978845608028654 * (pre + 0.044715 * square * pre))
        half = 0.5 * (1.0 + bent)
        active_ref[rows, :] = (pre * half).astype(bf16)
        slope = half + 0.5 * pre * (1.0 - bent * bent) * (
            0.7978845608028654 + (3.0 * 0.044715 * 0.7978845608028654) * square
        )
        grad = (grad_ref[rows, :] * slope).astype(bf16)
        hidden_ref[rows, :] = grad
        sums = sums + jnp.sum(grad.astype(f32), axis=0, keepdims=True)
        out_ref[rows, :] = dot_cols(grad, cols_ref[...]).astype(bf16)
    sums_ref[...] = sums


def down_kernel(active_ref, rows_ref, out_ref):
    for block in range(active_ref.shape[0] // BLOCK):
        rows = slice(block * BLOCK, (block + 1) * BLOCK)
        out_ref[rows, :] = dot(active_ref[rows, :], rows_ref[...]).astype(bf16)


def attend_back_kernel(
    place_ref,
    qkv_ref,
    grad_ref,
    out_ref,
    top_ref,
    cols_ref,
    down_ref,
    mixed_ref,
    parts_ref,
    sums_ref,
    query_ref,
):
    length = qkv_ref.shape[0]
    scale = 1.0 / math.sqrt(HEAD_DIM)
    ones = jnp.ones((8, HEAD_DIM), bf16)
    for head in range(SLOTS):
        base = head * HEAD_DIM
        lanes = slice(base, base + HEAD_DIM)
        key_lanes = slice(SLOT_WIDTH + base, SLOT_WIDTH + base + HEAD_DIM)
        value_lanes = slice(2 * SLOT_WIDTH + base, 2 * SLOT_WIDTH + base + HEAD_DIM)
        query = qkv_ref[:, lanes] * bf16(scale)
        grad = grad_ref[:, lanes]
        if head == SLOTS - 1:
            grad = jnp.where(place_ref[RANK] == 7, grad, jnp.zeros_like(grad))
        top = top_ref[head : head + 1, :]
        delta = dot_cols(ones, grad * out_ref[:, lanes])[0:1, :]
        for block in range(length // BLOCK):
            start = block * BLOCK
            rows = slice(start, start + BLOCK)
            width = length - start
            keys = qkv_ref[rows, key_lanes]
            values = qkv_ref[rows, value_lanes]
            scores = dot_cols(keys, query[start:])
            row = lax.broadcasted_iota(jnp.int32, (BLOCK, width), 0)
            col = lax.broadcasted_iota(jnp.int32, (BLOCK, width), 1)
            probs = jnp.where(row <= col, jnp.exp(scores - top[:, start:]), 0.0)
            grad_probs = dot_cols(values, grad[start:])
            grad_scores = (probs * (grad_probs - delta[:, start:])).astype(bf16)
            mixed_ref[rows, value_lanes] = dot(probs.astype(bf16), grad[start:]).astype(bf16)
            mixed_ref[rows, key_lanes] = dot(grad_scores, query[start:]).astype(bf16)
            term = dot_rows(grad_scores, keys)
            if block == 0:
                query_ref[...] = term
            else:
                query_ref[start:, :] += term
        mixed_ref[:, lanes] = (query_ref[...] * scale).astype(bf16)
    sums = jnp.zeros(sums_ref.shape, f32)
    for block in range(length // BLOCK):
        rows = slice(block * BLOCK, (block + 1) * BLOCK)
        mixed = mixed_ref[rows, :]
        sums = sums + jnp.sum(mixed.astype(f32), axis=0, keepdims=True)
        first = dot_cols(mixed, cols_ref[...]).astype(bf16)
        for half in range(2):
            rank = 2 * block + half
            parts_ref[rank, 0] = first[half * BLOCK // 2 : (half + 1) * BLOCK // 2]
            parts_ref[rank, 1] = down_ref[rank]
    sums_ref[...] = sums


def input_back_kernel(
    parts_ref, tokens_ref, middle_ref, grad_ref, norm_ref, out_ref, sums_ref
):
    gain = norm_ref[0:1, :]
    _, normed, factor = norm_parts(tokens_ref[...].astype(f32), gain, gain)
    grad = parts_ref[0].astype(f32)
    out_ref[0] = (grad_ref[...] + norm_back(grad, normed, factor, gain)).astype(bf16)
    down = parts_ref[1].astype(f32) + norm_ref[7:8, :]
    out_ref[1] = (middle_ref[...] + down).astype(bf16)
    sums_ref[0:1, :] = jnp.sum(grad * normed, axis=0, keepdims=True)
    sums_ref[1:2, :] = jnp.sum(grad, axis=0, keepdims=True)


def after(value, *others):
    return lax.optimization_barrier((value,) + others)[0]


def per_device(
    tokens,
    ln1_gain,
    ln1_bias,
    w_qkv,
    bias_q,
    bias_v,
    w_out,
    bias_out,
    ln2_gain,
    ln2_bias,
    w_fc,
    bias_fc,
    w_proj,
    bias_proj,
    cotangent,
):
    _, span, width = tokens.shape
    shard = width // 8
    hidden = w_fc.shape[1] // 8
    length = span * 8
    slots = 3 * SLOT_WIDTH
    x, zl, c, y, zh = [lax.axis_index(name) for name, _ in LAYOUT]
    rank = y * 2 + c
    place = jnp.stack(
        [y, c, rank, zh, zh * 2 + zl, x, zl, (c == zh).astype(jnp.int32)]
    ).astype(jnp.int32)

    stays = c == zh
    own_tokens = swap_roles(tokens.reshape(span, width))
    all_tokens = gather(own_tokens, TEAM).reshape(length, width)
    out_rows = swap_roles(w_out)
    qkv_parts = call(
        qkv_columns_kernel,
        "qkv_columns",
        [struct((shard, slots), bf16)] * 4,
        place,
        w_qkv,
        scratch=[pltpu.VMEM((4, shard, slots), bf16)],
    )
    qkv_own = ring_all(qkv_parts, "y")
    small = jnp.concatenate(
        [ln1_gain, ln1_bias, bias_q, bias_v, bias_out, ln2_gain, ln2_bias, bias_proj, bias_fc]
    ).reshape(3, hidden)
    small_all = exchange(
        after(jnp.broadcast_to(small, (8, 3, hidden)), qkv_parts[0]), GRP
    )
    qkv_other = [flipped(after(part, small_all), "zh") for part in qkv_own]
    place = after(place, small_all)
    fc_parts = call(
        fc_columns_kernel,
        "fc_columns",
        [struct((shard, hidden), bf16)] * 4,
        place,
        w_fc,
        scratch=[pltpu.VMEM((4, shard, hidden), bf16)],
    )
    own_cot = swap_roles(after(cotangent, *qkv_other).reshape(span, width))

    small_all = small_all.astype(f32)
    hidden_bias = lax.dynamic_index_in_dim(small_all, rank, 0, keepdims=False)[2:3]
    vectors = small_all[:, :2].reshape(8, 8, shard).transpose(1, 0, 2).reshape(8, width)
    bias_slots = jnp.concatenate(
        [
            lax.dynamic_slice_in_dim(vectors[2], STRIDE * rank, SLOT_WIDTH),
            jnp.zeros((SLOT_WIDTH,), f32),
            lax.dynamic_slice_in_dim(vectors[3], STRIDE * rank, SLOT_WIDTH),
        ]
    ).reshape(1, slots)

    out_all = gather(out_rows, TEAM).reshape(width, width)
    all_cot = gather(after(own_cot, out_rows), TEAM).reshape(length, width)
    proj_came = lax.ppermute(after(w_proj, *qkv_other), ("c", "zh"), ROLES[1:3])
    proj_rows = jnp.where(stays, w_proj, proj_came)
    fc_own = ring_all([after(part, *qkv_other) for part in fc_parts], "y")

    first, qkv, attended_slots, top, qkv_cols = call(
        attend_kernel,
        "attend",
        (
            struct((length, width), bf16),
            struct((length, slots), bf16),
            struct((length, SLOT_WIDTH), bf16),
            struct((length, SLOTS), f32),
            struct((8, shard, slots), bf16),
        ),
        after(place, bias_slots),
        all_tokens,
        vectors,
        bias_slots,
        *qkv_own,
        *qkv_other,
        flops=2 * length * width * slots,
    )
    qkv_cols = qkv_cols.reshape(width, slots)
    fc_other = [flipped(part, "zh") for part in fc_own]
    attended = exchange(
        after(attended_slots, proj_came, *fc_own).reshape(8, span, SLOT_WIDTH), TEAM
    )
    middle, second, attended_parts = call(
        branch_kernel,
        "branch",
        (
            struct((span, width), f32),
            struct((span, width), bf16),
            struct((8, span, shard), bf16),
        ),
        attended,
        own_tokens,
        vectors,
        out_all,
        scratch=[pltpu.VMEM((span, width), bf16)],
        flops=2 * span * width * width,
    )

    second_all = gather(second, TEAM).reshape(length, width)
    attended_own = exchange(after(attended_parts, second), TEAM)
    grad_active = dot_cols(after(all_cot, second), proj_rows)
    fc_cols = call(
        fc_whole_kernel,
        "fc_whole",
        struct((8, shard, hidden), bf16),
        place,
        after(fc_own[0], grad_active),
        *fc_own[1:],
        *fc_other,
    ).reshape(width, hidden)
    active, grad_hidden, hidden_sums, second_parts = call(
        hidden_kernel,
        "hidden",
        (
            struct((length, hidden), bf16),
            struct((length, hidden), bf16),
            struct((1, hidden), f32),
            struct((length, width), bf16),
        ),
        after(place, attended_own),
        second_all,
        fc_cols,
        hidden_bias,
        grad_active,
        flops=4 * length * width * hidden,
    )
    grad_second = team_sum(second_parts)
    window = windows(shard, 8)[0]
    fc_grad = call(
        column_ring_kernel,
        "fc_grad",
        [struct((4, 4, window, hidden), bf16)] * 4,
        place,
        second_all,
        grad_hidden,
        scratch=[pltpu.VMEM((width, hidden), f32)],
        flops=2 * length * width * hidden,
    )
    fc_grad = ring_all(fc_grad, "x")
    row_window = windows(hidden, 16)[0]
    proj_grad = call(
        row_grad_kernel,
        "proj_grad",
        [struct((4, row_window, width), bf16)] * 4,
        after(place, fc_grad[0]),
        active,
        all_cot,
        scratch=[pltpu.VMEM((hidden, width), f32)],
        flops=2 * length * width * hidden,
    )
    down_parts = call(
        down_kernel,
        "down",
        struct((length, width), bf16),
        after(active, proj_grad[0]),
        proj_rows,
        light=True,
    )
    proj_near = [ring(proj_grad[k], Z_RING, k) for k in (1, 3)]
    proj_far = ring(after(proj_grad[2], *proj_near), Z_RING, 2)
    proj_grad = [proj_grad[0], proj_near[0], proj_far, proj_near[1]]

    grad_middle, grad_branch, grad_slots, branch_sums = call(
        branch_back_kernel,
        "branch_back",
        (
            struct((span, width), f32),
            struct((span, width), bf16),
            struct((8, span, SLOT_WIDTH), bf16),
            struct((4, width), f32),
        ),
        after(place, *fc_grad, proj_grad[1], proj_grad[3], down_parts),
        grad_second,
        middle,
        own_cot,
        vectors,
        out_all,
        scratch=[pltpu.VMEM((span, width), bf16)],
        flops=2 * span * width * width,
    )
    grad_heads = exchange(grad_slots, TEAM).reshape(length, SLOT_WIDTH)

    def fold(which, parts, name, *behind):
        parts = [after(parts[0], *behind)] + parts[1:]
        return call(
            functools.partial(fold_kernel, which),
            name,
            [struct(parts[0].shape[1:], bf16)] * 4,
            place,
            *parts,
        )

    fc_grad = ring_all(fold(Z, fc_grad, "fc_fold", grad_slots), Z_RING)
    branch_all = gather(grad_branch, TEAM).reshape(length, width)
    grad_mixed, last_parts, mixed_sums = call(
        attend_back_kernel,
        "attend_back",
        (
            struct((length, slots), bf16),
            struct((8, 2, span, width), bf16),
            struct((1, slots), f32),
        ),
        after(place, proj_far, *fc_grad),
        qkv,
        grad_heads,
        attended_slots,
        top.T,
        qkv_cols,
        down_parts.reshape(8, span, width),
        scratch=[pltpu.VMEM((length, HEAD_DIM), f32)],
        flops=2 * length * width * slots,
    )
    last = team_sum(last_parts.reshape(2 * length, width)).reshape(2, span, width)
    fc_grad = ring_all(fold(Y, fc_grad, "fc_fold_last", grad_mixed), "y")
    proj_grad = ring_all(fold(X, proj_grad, "proj_fold", grad_mixed), "x")
    last_grads = call(
        last_grads_kernel,
        "last_grads",
        struct((16, 2 * window + windows(shard, 16)[0], width), bf16),
        place,
        after(first, fc_grad[0], proj_grad[0]),
        grad_mixed,
        attended_own.reshape(length, shard),
        branch_all,
        scratch=[pltpu.VMEM((width, slots), f32)],
        flops=2 * length * width * (slots + shard),
    )
    place = after(place, last_grads)
    last_grads = exchange(after(last_grads, *fc_grad, *proj_grad), REPLICAS)

    def stacked(parts, name):
        return call(
            stack_kernel, name, struct((len(parts),) + parts[0].shape, bf16), *parts
        )

    def row_total(whole, rows, name, *behind):
        whole = after(whole, *behind)
        return call(
            row_total_kernel, name, struct((rows, width), f32), place, whole, other_core(whole)
        )

    proj_sum = sum(part.astype(f32) for part in [after(proj_grad[0], place)] + proj_grad[1:])
    proj_whole = gather(proj_sum.astype(bf16), REPLICAS)
    fc_near = stacked([after(fc_grad[0], place)] + fc_grad[1:], "fc_near")
    fc_both = stacked([fc_near, flipped(fc_near, "zl")], "fc_both")
    qkv_sum, out_sum = call(
        last_sum_kernel,
        "last_sum",
        (struct((4, window, slots), bf16), struct((windows(shard, 16)[0], width), bf16)),
        after(last_grads, fc_both),
    )
    qkv_sum = exchange(qkv_sum, "y")
    qkv_both = stacked([qkv_sum, flipped(qkv_sum, "zl")], "qkv_both")
    qkv_pieces = ring_all([qkv_both] * 4, "x")
    fc_pieces = ring_all([after(fc_both, *qkv_pieces)] * 4, "x")
    results, first_sums = call(
        input_back_kernel,
        "input_back",
        (struct((2, span, width), bf16), struct((2, width), f32)),
        last,
        own_tokens,
        middle,
        grad_middle,
        after(vectors, qkv_sum),
    )
    results_home = swap_roles(results)

    blank = jnp.zeros((1, width), f32)
    at = (0, STRIDE * rank)
    small_terms = jnp.concatenate(
        [
            first_sums,
            lax.dynamic_update_slice(blank, mixed_sums[:, :SLOT_WIDTH], at),
            lax.dynamic_update_slice(blank, mixed_sums[:, 2 * SLOT_WIDTH :], at),
            branch_sums,
        ]
    )
    hidden_term = lax.dynamic_update_slice(
        jnp.zeros((8, hidden), f32), hidden_sums, (rank, 0)
    )
    small_terms = small_terms.reshape(8, 8, shard).transpose(1, 0, 2).reshape(8, 2, hidden)
    small_terms = jnp.concatenate([small_terms, hidden_term[:, None]], axis=1)
    small_sum = jnp.sum(exchange(after(small_terms, qkv_both), GRP), axis=0)
    out_whole = exchange(
        after(jnp.broadcast_to(out_sum, (16,) + out_sum.shape), small_sum), REPLICAS
    )
    small_last = jnp.broadcast_to(after(small_sum, out_whole), (16, 3, hidden))
    small_last = jnp.sum(exchange(small_last, REP), axis=0)
    owned = small_last[:2].reshape(8, shard)

    qkv_pieces = qkv_pieces + [other_core(part) for part in qkv_pieces]
    qkv_spans = [
        [
            (p * SLOT_WIDTH, p * width + STRIDE * r, STRIDE if r < 7 else SLOT_WIDTH)
            for p in range(3)
        ]
        for r in range(8)
    ]
    qkv_total = call(
        functools.partial(column_total_kernel, qkv_spans, False),
        "qkv_total",
        struct((shard, 3 * width), f32),
        after(place, results, small_sum),
        *qkv_pieces,
    )
    fc_pieces = fc_pieces + [other_core(after(part, qkv_total)) for part in fc_pieces]
    fc_spans = [[(0, rank * hidden, hidden)] for rank in range(8)]
    fc_total = call(
        functools.partial(column_total_kernel, fc_spans, True),
        "fc_total",
        struct((shard, 8 * hidden), f32),
        after(place, out_whole, small_last),
        *fc_pieces,
    )
    out_total = row_total(out_whole, shard, "out_total", fc_total)
    proj_total = row_total(proj_whole, hidden, "proj_total", fc_total)
    return (
        results_home[1].reshape(1, span, width),
        results_home[0].astype(f32).reshape(1, span, width),
        owned[0],
        owned[1],
        qkv_total,
        owned[2],
        owned[3],
        out_total,
        owned[4],
        owned[5],
        owned[6],
        fc_total,
        small_last[2],
        proj_total,
        owned[7],
    )


def solution(mesh):
    names = tuple(name for name, _ in LAYOUT)
    fine = jax.sharding.Mesh(mesh.devices.reshape([size for _, size in LAYOUT]), names)
    in_specs = (
        P(REP, GRP, None),
        P(GRP),
        P(GRP),
        P(GRP, None),
        P(GRP),
        P(GRP),
        P(GRP, None),
        P(GRP),
        P(GRP),
        P(GRP),
        P(GRP, None),
        P(GRP),
        P(GRP, None),
        P(GRP),
        P(REP, GRP, None),
    )
    out_specs = (
        P(REP, GRP, None),
        P(REP, GRP, None),
        P(GRP),
        P(GRP),
        P(GRP, None),
        P(GRP),
        P(GRP),
        P(GRP, None),
        P(GRP),
        P(GRP),
        P(GRP),
        P(GRP, None),
        P(GRP),
        P(GRP, None),
        P(GRP),
    )
    return jax.shard_map(
        per_device, mesh=fine, in_specs=in_specs, out_specs=out_specs, check_vma=False
    )
```

```python
import functools
import math

import jax
import jax.numpy as jnp
from jax import lax
from jax.experimental import pallas as pl
from jax.experimental.pallas import tpu as pltpu
from jax.sharding import PartitionSpec as P

HEADS = 25
HEAD_DIM = 64
SLOTS = 4
SLOT_WIDTH = SLOTS * HEAD_DIM
STRIDE = 3 * HEAD_DIM
BLOCK = 256

bf16 = jnp.bfloat16
f32 = jnp.float32


LAYOUT = (("x", 4), ("zl", 2), ("c", 2), ("y", 4), ("zh", 2))
REP = ("x", "zl", "c")
GRP = ("y", "zh")
TEAM = ("y", "c")
REPLICAS = ("zl", "x", "zh")
Z_RING = ("zl", "zh")
Z_PLACES = (0, 2, 1, 3)
ROLES = [(0, 0), (1, 2), (2, 1), (3, 3)]
OWNERS = [
    [(l * 4 + k * 2 + h, (h ^ i) * 4 + l * 2 + k) for l in range(2) for k in range(2) for h in range(2)]
    for i in range(2)
]


def ring(value, axis, step):
    index = Z_PLACES if axis == Z_RING else range(4)
    return lax.ppermute(value, axis, [(index[(i + step) % 4], index[i]) for i in range(4)])


def ring_all(values, axis):
    return [values[0]] + [ring(values[k], axis, k) for k in range(1, 4)]


def flipped(value, axis):
    return lax.ppermute(value, axis, [(0, 1), (1, 0)])


def swap_roles(value):
    return lax.ppermute(value, ("c", "zh"), ROLES)


def swap_selected(value, stays):
    return jnp.where(stays, value, lax.ppermute(value, ("c", "zh"), ROLES[1:3]))


def other_core(value):
    return lax.ppermute(value, "c", [(0, 1), (1, 0)])


def exchange(parts, axes):
    return lax.all_to_all(parts, axes, 0, 0)


def gather(block, axes):
    return lax.all_gather(block, axes, axis=0)


def team_sum(parts):
    return lax.psum_scatter(parts.astype(bf16), TEAM, scatter_dimension=0, tiled=True)


def windows(rows, count):
    tiles = rows // 8
    starts = [tiles * i // count for i in range(count)]
    size = max(b - a for a, b in zip(starts, starts[1:] + [tiles]))
    return size * 8, [8 * s for s in starts]


def joined(parts, starts, rows, axis):
    ends = starts[1:] + [rows]
    return jnp.concatenate(
        [lax.slice_in_dim(p, 0, e - s, axis=axis) for p, s, e in zip(parts, starts, ends)], axis
    )


def norm_parts(value, gain, shift):
    center = value - jnp.mean(value, axis=-1, keepdims=True)
    spread = jnp.mean(center * center, axis=-1, keepdims=True)
    factor = lax.rsqrt(spread + 1e-05)
    normed = center * factor
    return (normed * gain + shift, normed, factor)


def norm_back(grad_value, normed, factor, gain):
    grad_normed = grad_value * gain
    mean_first = jnp.mean(grad_normed, axis=-1, keepdims=True)
    mean_second = jnp.mean(grad_normed * normed, axis=-1, keepdims=True)
    return factor * (grad_normed - mean_first - normed * mean_second)


def dot(left, right):
    return jnp.dot(left, right, preferred_element_type=f32)


def dot_rows(left, right):
    return lax.dot_general(left, right, (((0,), (0,)), ((), ())), preferred_element_type=f32)


def dot_cols(left, right):
    return lax.dot_general(left, right, (((1,), (1,)), ((), ())), preferred_element_type=f32)


def call(kernel, name, out_shape, *operands, scratch=(), flops=0, light=False):
    specs = [
        pl.BlockSpec(memory_space=pltpu.SMEM if op.dtype == jnp.int32 else pltpu.VMEM)
        for op in operands
    ]
    out_specs = jax.tree.map(lambda _: pl.BlockSpec(memory_space=pltpu.VMEM), out_shape)
    moved = sum(op.size * op.dtype.itemsize for op in operands)
    moved += sum(o.size * o.dtype.itemsize for o in jax.tree.leaves(out_shape))
    return pl.pallas_call(
        kernel,
        out_shape=out_shape,
        in_specs=specs,
        out_specs=out_specs,
        scratch_shapes=list(scratch),
        compiler_params=pltpu.CompilerParams(vmem_limit_bytes=56 * 2**20),
        cost_estimate=pl.CostEstimate(
            flops=1 if light else int(flops),
            bytes_accessed=1 if light else int(moved),
            transcendentals=0,
        ),
        name=name,
    )(*operands)


def struct(shape, dtype):
    return jax.ShapeDtypeStruct(shape, dtype)


Y, C, RANK, ZH, Z, X, ZL, MINE = range(8)


def qkv_columns_kernel(place_ref, weight_ref, *refs):
    out_refs, held_ref = refs[:4], refs[4]
    c = place_ref[C]
    width = weight_ref.shape[1] // 3
    for part in range(3):
        lanes = slice(part * SLOT_WIDTH, (part + 1) * SLOT_WIDTH)
        for y in range(4):
            start = part * width + 2 * STRIDE * y
            even = weight_ref[:, start : start + SLOT_WIDTH]
            odd = weight_ref[:, start + STRIDE : start + STRIDE + SLOT_WIDTH]
            held_ref[y, :, lanes] = jnp.where(c == 0, even, odd)
    for k in range(4):
        out_refs[k][...] = held_ref[lax.rem(place_ref[Y] + 4 - k, 4)]


def fc_columns_kernel(place_ref, weight_ref, *refs):
    out_refs, held_ref = refs[:4], refs[4]
    c = place_ref[C]
    hidden = weight_ref.shape[1] // 8
    for y in range(4):
        start = 2 * hidden * y
        even = weight_ref[:, start : start + hidden]
        odd = weight_ref[:, start + hidden : start + 2 * hidden]
        held_ref[y] = jnp.where(c == 0, even, odd)
    for k in range(4):
        out_refs[k][...] = held_ref[lax.rem(place_ref[Y] + 4 - k, 4)]


def fc_whole_kernel(place_ref, *refs):
    out_ref = refs[8]
    zh = place_ref[ZH]
    for k in range(4):
        y = lax.rem(place_ref[Y] + k, 4)
        out_ref[2 * y + zh] = refs[k][...]
        out_ref[2 * y + 1 - zh] = refs[4 + k][...]


def branch_kernel(
    slots_ref, tokens_ref, norm_ref, rows_ref, middle_ref, second_ref, parts_ref, flat_ref
):
    shard = parts_ref.shape[2]
    for rank in range(8):
        wide = STRIDE if rank < 7 else SLOT_WIDTH
        flat_ref[:, STRIDE * rank : STRIDE * rank + wide] = slots_ref[rank, :, :wide]
    for rank in range(8):
        parts_ref[rank] = flat_ref[:, shard * rank : shard * (rank + 1)]
    total = tokens_ref[...].astype(f32) + norm_ref[4:5, :] + dot(flat_ref[...], rows_ref[...])
    middle_ref[...] = total
    second_ref[...] = norm_parts(total, norm_ref[5:6, :], norm_ref[6:7, :])[0].astype(bf16)


def branch_back_kernel(
    place_ref,
    grad_ref,
    middle_ref,
    cot_ref,
    norm_ref,
    rows_ref,
    grad_middle_ref,
    branch_ref,
    slots_ref,
    sums_ref,
    flat_ref,
):
    gain = norm_ref[5:6, :]
    _, normed, factor = norm_parts(middle_ref[...], gain, gain)
    grad = grad_ref[...].astype(f32)
    cot = cot_ref[...].astype(f32)
    grad_middle = cot + norm_back(grad, normed, factor, gain)
    branch = grad_middle.astype(bf16)
    grad_middle_ref[...] = grad_middle
    branch_ref[...] = branch
    flat_ref[...] = dot_cols(branch, rows_ref[...]).astype(bf16)
    for rank in range(8):
        slots_ref[rank] = flat_ref[:, STRIDE * rank : STRIDE * rank + SLOT_WIDTH]
    sums_ref[0:1, :] = jnp.sum(branch.astype(f32), axis=0, keepdims=True)
    sums_ref[1:2, :] = jnp.sum(grad * normed, axis=0, keepdims=True)
    sums_ref[2:3, :] = jnp.sum(grad, axis=0, keepdims=True)
    sums_ref[3:4, :] = jnp.sum(cot, axis=0, keepdims=True)


def column_ring_kernel(place_ref, left_ref, right_ref, *refs):
    out_refs, held_ref = refs[:4], refs[4]
    shard = left_ref.shape[1] // 8
    size, starts = windows(shard, 8)
    held_ref[...] = dot_rows(left_ref[...], right_ref[...])
    for k in range(4):
        x = lax.rem(place_ref[X] + 4 - k, 4)
        for z in range(4):
            for y in range(4):
                base = (2 * y + z // 2) * shard + starts[4 * (z % 2)]
                at = pl.multiple_of(base + starts[1] * x, 8)
                out_refs[k][z, y] = held_ref[pl.ds(at, size), :].astype(bf16)


def row_grad_kernel(place_ref, left_ref, right_ref, *refs):
    out_refs, held_ref = refs[:4], refs[4]
    rows = left_ref.shape[1]
    size = windows(rows, 16)[0]
    held_ref[...] = dot_rows(left_ref[...], right_ref[...])
    for k in range(4):
        z = lax.rem(place_ref[Z] + 4 - k, 4)
        for x in range(4):
            window = (lax.rem(z, 2) * 4 + x) * 2 + lax.div(z, 2)
            at = pl.multiple_of(lax.div(rows // 8 * window, 16) * 8, 8)
            out_refs[k][x] = held_ref[pl.ds(at, size), :].astype(bf16)


def last_grads_kernel(place_ref, first_ref, mixed_ref, attended_ref, branch_ref, out_ref, held_ref):
    shard = first_ref.shape[1] // 8
    slots = mixed_ref.shape[1]
    size, starts = windows(shard, 8)
    held_ref[...] = dot_rows(first_ref[...], mixed_ref[...])
    for y in range(4):
        for zh in range(2):
            base = (2 * y + zh) * shard
            for i, start in enumerate(starts):
                rows = slice(y % 2 * size, (y % 2 + 1) * size)
                lanes = slice(y // 2 * slots, (y // 2 + 1) * slots)
                block = held_ref[base + start : base + start + size, :]
                out_ref[2 * i + zh, rows, lanes] = block.astype(bf16)
    size_out, starts_out = windows(shard, 16)
    grad = dot_rows(attended_ref[...], branch_ref[...])
    rest = jnp.zeros((2 * size, out_ref.shape[2] - 2 * slots), bf16)
    for i, start in enumerate(starts_out):
        out_ref[i, : 2 * size, 2 * slots :] = rest
        out_ref[i, 2 * size :, :] = grad[start : start + size_out].astype(bf16)


def last_sum_kernel(parts_ref, qkv_ref, out_ref):
    size, slots = qkv_ref.shape[1:]
    total = parts_ref[0].astype(f32)
    for i in range(1, 16):
        total = total + parts_ref[i].astype(f32)
    total = total.astype(bf16)
    for y in range(4):
        rows = slice(y % 2 * size, (y % 2 + 1) * size)
        qkv_ref[y] = total[rows, y // 2 * slots : (y // 2 + 1) * slots]
    out_ref[...] = total[2 * size :, :]


def fold_kernel(which, place_ref, *refs):
    for k in range(4):
        at = lax.rem(place_ref[which] + 4 - k, 4)
        total = refs[0][at].astype(f32)
        for j in range(1, 4):
            total = total + refs[j][at].astype(f32)
        refs[4 + k][...] = total.astype(bf16)


def stack_kernel(*refs):
    for k, ref in enumerate(refs[:-1]):
        refs[-1][k] = ref[...]


def column_total_kernel(spans, ringed, place_ref, own_ref, other_ref, out_ref):
    _, starts = windows(out_ref.shape[0], 8)
    ends = starts[1:] + [out_ref.shape[0]]
    for rank in range(8):
        y = lax.rem(rank // 2 + 4 - place_ref[Y], 4) if ringed else rank // 2
        mine = place_ref[C] == rank % 2
        rows = [
            jnp.where(mine, own_ref[i, y], other_ref[i, y]).astype(f32)[: end - start]
            for i, (start, end) in enumerate(zip(starts, ends))
        ]
        block = jnp.concatenate(rows, axis=0)
        for source, target, wide in spans[rank]:
            out_ref[:, target : target + wide] = block[:, source : source + wide]


def proj_total_kernel(place_ref, own_ref, other_ref, out_ref):
    tiles = out_ref.shape[0] // 8
    small = tiles // 16 * 8
    for part, ref in enumerate((own_ref, other_ref)):
        zl = place_ref[C] if part == 0 else 1 - place_ref[C]
        for x in range(4):
            for i in range(2):
                zh = place_ref[ZL] if i == 0 else 1 - place_ref[ZL]
                window = (zl * 4 + x) * 2 + zh
                start = lax.div(tiles * window, 16)
                wide = lax.div(tiles * (window + 1), 16) - start > small // 8
                at = pl.multiple_of(start * 8, 8)
                block = ref[x, i].astype(f32)
                out_ref[pl.ds(at, small), :] = block[:small]

                @pl.when(wide)
                def _(at=at, block=block):
                    out_ref[pl.ds(pl.multiple_of(at + small, 8), 8), :] = block[small:]


def row_total_kernel(place_ref, own_ref, other_ref, out_ref):
    mine = place_ref[MINE]
    _, starts = windows(out_ref.shape[0], 16)
    ends = starts[1:] + [out_ref.shape[0]]
    for i, (start, end) in enumerate(zip(starts, ends)):
        block = jnp.where(mine == 1, own_ref[i], other_ref[i])
        out_ref[start:end, :] = block[: end - start].astype(f32)


def attend_kernel(place_ref, tokens_ref, norm_ref, bias_ref, *refs):
    pieces, (first_ref, qkv_ref, out_ref, top_ref, cols_ref) = refs[:8], refs[8:]
    length = tokens_ref.shape[0]
    shard = cols_ref.shape[1]
    zh = place_ref[ZH]
    for k in range(4):
        y = lax.rem(place_ref[Y] + k, 4)
        cols_ref[2 * y + zh] = pieces[k][...]
        cols_ref[2 * y + 1 - zh] = pieces[4 + k][...]
    gain = norm_ref[0:1, :]
    shift = norm_ref[1:2, :]
    for block in range(length // BLOCK):
        rows = slice(block * BLOCK, (block + 1) * BLOCK)
        first = norm_parts(tokens_ref[rows, :].astype(f32), gain, shift)[0].astype(bf16)
        first_ref[rows, :] = first
        mixed = bias_ref[...]
        for g in range(8):
            mixed = mixed + dot(first[:, g * shard : (g + 1) * shard], cols_ref[g])
        qkv_ref[rows, :] = mixed.astype(bf16)
    for head in range(SLOTS):
        lanes = slice(head * HEAD_DIM, (head + 1) * HEAD_DIM)
        keys = qkv_ref[:, SLOT_WIDTH + head * HEAD_DIM : SLOT_WIDTH + (head + 1) * HEAD_DIM]
        values = qkv_ref[
            :, 2 * SLOT_WIDTH + head * HEAD_DIM : 2 * SLOT_WIDTH + (head + 1) * HEAD_DIM
        ]
        for block in range(length // BLOCK):
            rows = slice(block * BLOCK, (block + 1) * BLOCK)
            width = (block + 1) * BLOCK
            query = qkv_ref[rows, lanes] * bf16(1.0 / math.sqrt(HEAD_DIM))
            scores = dot_cols(query, keys[:width])
            row = lax.broadcasted_iota(jnp.int32, (BLOCK, width), 0) + block * BLOCK
            col = lax.broadcasted_iota(jnp.int32, (BLOCK, width), 1)
            scores = jnp.where(col <= row, scores, -1e30)
            top = jnp.max(scores, axis=-1, keepdims=True)
            probs = jnp.exp(scores - top)
            total = jnp.sum(probs, axis=-1, keepdims=True)
            mixed = dot(probs.astype(bf16), values[:width])
            out_ref[rows, lanes] = (mixed / total).astype(bf16)
            top_ref[rows, head : head + 1] = top + jnp.log(total)


def hidden_kernel(
    place_ref, second_ref, cols_ref, bias_ref, grad_ref, active_ref, hidden_ref, sums_ref, out_ref
):
    length = second_ref.shape[0]
    sums = jnp.zeros(sums_ref.shape, f32)
    for block in range(length // BLOCK):
        rows = slice(block * BLOCK, (block + 1) * BLOCK)
        pre = dot(second_ref[rows, :], cols_ref[...]) + bias_ref[...]
        square = pre * pre
        bent = jnp.tanh(0.7978845608028654 * (pre + 0.044715 * square * pre))
        half = 0.5 * (1.0 + bent)
        active_ref[rows, :] = (pre * half).astype(bf16)
        slope = half + 0.5 * pre * (1.0 - bent * bent) * (
            0.7978845608028654 + (3.0 * 0.044715 * 0.7978845608028654) * square
        )
        grad = (grad_ref[rows, :] * slope).astype(bf16)
        hidden_ref[rows, :] = grad
        sums = sums + jnp.sum(grad.astype(f32), axis=0, keepdims=True)
        out_ref[rows, :] = dot_cols(grad, cols_ref[...]).astype(bf16)
    sums_ref[...] = sums


def down_kernel(active_ref, rows_ref, out_ref):
    for block in range(active_ref.shape[0] // BLOCK):
        rows = slice(block * BLOCK, (block + 1) * BLOCK)
        out_ref[rows, :] = dot(active_ref[rows, :], rows_ref[...]).astype(bf16)


def attend_back_kernel(
    place_ref,
    qkv_ref,
    grad_ref,
    out_ref,
    top_ref,
    cols_ref,
    down_ref,
    mixed_ref,
    parts_ref,
    sums_ref,
    query_ref,
):
    length = qkv_ref.shape[0]
    scale = 1.0 / math.sqrt(HEAD_DIM)
    ones = jnp.ones((8, HEAD_DIM), bf16)
    for head in range(SLOTS):
        base = head * HEAD_DIM
        lanes = slice(base, base + HEAD_DIM)
        key_lanes = slice(SLOT_WIDTH + base, SLOT_WIDTH + base + HEAD_DIM)
        value_lanes = slice(2 * SLOT_WIDTH + base, 2 * SLOT_WIDTH + base + HEAD_DIM)
        query = qkv_ref[:, lanes] * bf16(scale)
        grad = grad_ref[:, lanes]
        if head == SLOTS - 1:
            grad = jnp.where(place_ref[RANK] == 7, grad, jnp.zeros_like(grad))
        top = top_ref[head : head + 1, :]
        delta = dot_cols(ones, grad * out_ref[:, lanes])[0:1, :]
        for block in range(length // BLOCK):
            start = block * BLOCK
            rows = slice(start, start + BLOCK)
            width = length - start
            keys = qkv_ref[rows, key_lanes]
            values = qkv_ref[rows, value_lanes]
            scores = dot_cols(keys, query[start:])
            row = lax.broadcasted_iota(jnp.int32, (BLOCK, width), 0)
            col = lax.broadcasted_iota(jnp.int32, (BLOCK, width), 1)
            probs = jnp.where(row <= col, jnp.exp(scores - top[:, start:]), 0.0)
            grad_probs = dot_cols(values, grad[start:])
            grad_scores = (probs * (grad_probs - delta[:, start:])).astype(bf16)
            mixed_ref[rows, value_lanes] = dot(probs.astype(bf16), grad[start:]).astype(bf16)
            mixed_ref[rows, key_lanes] = dot(grad_scores, query[start:]).astype(bf16)
            term = dot_rows(grad_scores, keys)
            if block == 0:
                query_ref[...] = term
            else:
                query_ref[start:, :] += term
        mixed_ref[:, lanes] = (query_ref[...] * scale).astype(bf16)
    sums = jnp.zeros(sums_ref.shape, f32)
    for block in range(length // BLOCK):
        rows = slice(block * BLOCK, (block + 1) * BLOCK)
        mixed = mixed_ref[rows, :]
        sums = sums + jnp.sum(mixed.astype(f32), axis=0, keepdims=True)
        first = dot_cols(mixed, cols_ref[...]).astype(bf16)
        for half in range(2):
            rank = 2 * block + half
            parts_ref[rank, 0] = first[half * BLOCK // 2 : (half + 1) * BLOCK // 2]
            parts_ref[rank, 1] = down_ref[rank]
    sums_ref[...] = sums


def input_back_kernel(
    parts_ref, tokens_ref, middle_ref, grad_ref, norm_ref, out_ref, sums_ref
):
    gain = norm_ref[0:1, :]
    _, normed, factor = norm_parts(tokens_ref[...].astype(f32), gain, gain)
    grad = parts_ref[0].astype(f32)
    out_ref[0] = (grad_ref[...] + norm_back(grad, normed, factor, gain)).astype(bf16)
    down = parts_ref[1].astype(f32) + norm_ref[7:8, :]
    out_ref[1] = (middle_ref[...] + down).astype(bf16)
    sums_ref[0:1, :] = jnp.sum(grad * normed, axis=0, keepdims=True)
    sums_ref[1:2, :] = jnp.sum(grad, axis=0, keepdims=True)


def after(value, *others):
    return lax.optimization_barrier((value,) + others)[0]


def per_device(
    tokens,
    ln1_gain,
    ln1_bias,
    w_qkv,
    bias_q,
    bias_v,
    w_out,
    bias_out,
    ln2_gain,
    ln2_bias,
    w_fc,
    bias_fc,
    w_proj,
    bias_proj,
    cotangent,
):
    _, span, width = tokens.shape
    shard = width // 8
    hidden = w_fc.shape[1] // 8
    length = span * 8
    slots = 3 * SLOT_WIDTH
    x, zl, c, y, zh = [lax.axis_index(name) for name, _ in LAYOUT]
    rank = y * 2 + c
    place = jnp.stack(
        [y, c, rank, zh, zh * 2 + zl, x, zl, (c == zh).astype(jnp.int32)]
    ).astype(jnp.int32)

    stays = c == zh
    own_tokens = swap_roles(tokens.reshape(span, width))
    all_tokens = gather(own_tokens, TEAM).reshape(length, width)
    out_rows = swap_roles(w_out)
    qkv_parts = call(
        qkv_columns_kernel,
        "qkv_columns",
        [struct((shard, slots), bf16)] * 4,
        place,
        w_qkv,
        scratch=[pltpu.VMEM((4, shard, slots), bf16)],
    )
    qkv_own = ring_all(qkv_parts, "y")
    small = jnp.concatenate(
        [ln1_gain, ln1_bias, bias_q, bias_v, bias_out, ln2_gain, ln2_bias, bias_proj, bias_fc]
    ).reshape(3, hidden)
    small_all = exchange(
        after(jnp.broadcast_to(small, (8, 3, hidden)), qkv_parts[0]), GRP
    )
    qkv_other = [flipped(after(part, small_all), "zh") for part in qkv_own]
    place = after(place, small_all)
    fc_parts = call(
        fc_columns_kernel,
        "fc_columns",
        [struct((shard, hidden), bf16)] * 4,
        place,
        w_fc,
        scratch=[pltpu.VMEM((4, shard, hidden), bf16)],
    )
    own_cot = swap_roles(after(cotangent, *qkv_other).reshape(span, width))

    small_all = small_all.astype(f32)
    hidden_bias = lax.dynamic_index_in_dim(small_all, rank, 0, keepdims=False)[2:3]
    vectors = small_all[:, :2].reshape(8, 8, shard).transpose(1, 0, 2).reshape(8, width)
    bias_slots = jnp.concatenate(
        [
            lax.dynamic_slice_in_dim(vectors[2], STRIDE * rank, SLOT_WIDTH),
            jnp.zeros((SLOT_WIDTH,), f32),
            lax.dynamic_slice_in_dim(vectors[3], STRIDE * rank, SLOT_WIDTH),
        ]
    ).reshape(1, slots)

    out_all = gather(out_rows, TEAM).reshape(width, width)
    all_cot = gather(after(own_cot, out_rows), TEAM).reshape(length, width)
    proj_came = lax.ppermute(after(w_proj, *qkv_other), ("c", "zh"), ROLES[1:3])
    proj_rows = jnp.where(stays, w_proj, proj_came)
    fc_own = ring_all([after(part, *qkv_other) for part in fc_parts], "y")

    first, qkv, attended_slots, top, qkv_cols = call(
        attend_kernel,
        "attend",
        (
            struct((length, width), bf16),
            struct((length, slots), bf16),
            struct((length, SLOT_WIDTH), bf16),
            struct((length, SLOTS), f32),
            struct((8, shard, slots), bf16),
        ),
        after(place, bias_slots),
        all_tokens,
        vectors,
        bias_slots,
        *qkv_own,
        *qkv_other,
        flops=2 * length * width * slots,
    )
    qkv_cols = qkv_cols.reshape(width, slots)
    fc_other = [flipped(part, "zh") for part in fc_own]
    attended = exchange(
        after(attended_slots, *fc_own).reshape(8, span, SLOT_WIDTH), TEAM
    )
    middle, second, attended_parts = call(
        branch_kernel,
        "branch",
        (
            struct((span, width), f32),
            struct((span, width), bf16),
            struct((8, span, shard), bf16),
        ),
        after(attended, proj_came),
        own_tokens,
        vectors,
        out_all,
        scratch=[pltpu.VMEM((span, width), bf16)],
        flops=2 * span * width * width,
    )

    second_all = gather(second, TEAM).reshape(length, width)
    attended_own = exchange(after(attended_parts, second), TEAM)
    grad_active = dot_cols(after(all_cot, second), proj_rows)
    fc_cols = call(
        fc_whole_kernel,
        "fc_whole",
        struct((8, shard, hidden), bf16),
        place,
        after(fc_own[0], grad_active),
        *fc_own[1:],
        *fc_other,
    ).reshape(width, hidden)
    active, grad_hidden, hidden_sums, second_parts = call(
        hidden_kernel,
        "hidden",
        (
            struct((length, hidden), bf16),
            struct((length, hidden), bf16),
            struct((1, hidden), f32),
            struct((length, width), bf16),
        ),
        after(place, attended_own),
        second_all,
        fc_cols,
        hidden_bias,
        grad_active,
        flops=4 * length * width * hidden,
    )
    grad_second = team_sum(second_parts)
    window = windows(shard, 8)[0]
    fc_grad = call(
        column_ring_kernel,
        "fc_grad",
        [struct((4, 4, window, hidden), bf16)] * 4,
        place,
        second_all,
        grad_hidden,
        scratch=[pltpu.VMEM((width, hidden), f32)],
        flops=2 * length * width * hidden,
    )
    fc_grad = ring_all(fc_grad, "x")
    row_window = windows(hidden, 16)[0]
    proj_grad = call(
        row_grad_kernel,
        "proj_grad",
        [struct((4, row_window, width), bf16)] * 4,
        after(place, fc_grad[0]),
        active,
        all_cot,
        scratch=[pltpu.VMEM((hidden, width), f32)],
        flops=2 * length * width * hidden,
    )
    down_parts = call(
        down_kernel,
        "down",
        struct((length, width), bf16),
        after(active, proj_grad[0]),
        proj_rows,
        light=True,
    )
    proj_near = [ring(proj_grad[k], Z_RING, k) for k in (1, 3)]
    proj_far = ring(after(proj_grad[2], *proj_near), Z_RING, 2)
    proj_grad = [proj_grad[0], proj_near[0], proj_far, proj_near[1]]

    grad_middle, grad_branch, grad_slots, branch_sums = call(
        branch_back_kernel,
        "branch_back",
        (
            struct((span, width), f32),
            struct((span, width), bf16),
            struct((8, span, SLOT_WIDTH), bf16),
            struct((4, width), f32),
        ),
        after(place, fc_grad[0], *proj_near, down_parts),
        grad_second,
        middle,
        own_cot,
        vectors,
        out_all,
        scratch=[pltpu.VMEM((span, width), bf16)],
        light=True,
    )
    grad_heads = exchange(grad_slots, TEAM).reshape(length, SLOT_WIDTH)

    def fold(which, parts, name, *behind):
        parts = [after(parts[0], *behind)] + parts[1:]
        return call(
            functools.partial(fold_kernel, which),
            name,
            [struct(parts[0].shape[1:], bf16)] * 4,
            place,
            *parts,
            light=True,
        )

    fc_grad = ring_all(fold(Z, fc_grad, "fc_fold", grad_slots), Z_RING)
    branch_all = gather(grad_branch, TEAM).reshape(length, width)
    grad_mixed, last_parts, mixed_sums = call(
        attend_back_kernel,
        "attend_back",
        (
            struct((length, slots), bf16),
            struct((8, 2, span, width), bf16),
            struct((1, slots), f32),
        ),
        after(place, proj_far, *fc_grad),
        qkv,
        grad_heads,
        attended_slots,
        top.T,
        qkv_cols,
        down_parts.reshape(8, span, width),
        scratch=[pltpu.VMEM((length, HEAD_DIM), f32)],
        flops=20 * length * width * slots,
    )
    last = team_sum(last_parts.reshape(2 * length, width)).reshape(2, span, width)
    fc_grad = ring_all(fold(Y, fc_grad, "fc_fold_last", grad_mixed), "y")
    proj_grad = ring_all(fold(X, proj_grad, "proj_fold", grad_mixed), "x")
    last_grads = call(
        last_grads_kernel,
        "last_grads",
        struct((16, 2 * window + windows(shard, 16)[0], width), bf16),
        place,
        after(first, fc_grad[0], proj_grad[0]),
        grad_mixed,
        attended_own.reshape(length, shard),
        branch_all,
        scratch=[pltpu.VMEM((width, slots), f32)],
        flops=2 * length * width * (slots + shard),
    )
    place = after(place, last_grads)
    last_grads = exchange(after(last_grads, *fc_grad, *proj_grad), REPLICAS)

    def stacked(parts, name):
        return call(
            stack_kernel, name, struct((len(parts),) + parts[0].shape, bf16), *parts
        )

    def row_total(whole, rows, name, *behind):
        whole = after(whole, *behind)
        return call(
            row_total_kernel, name, struct((rows, width), f32), place, whole, other_core(whole)
        )

    proj_sum = sum(part.astype(f32) for part in [after(proj_grad[0], place)] + proj_grad[1:])
    proj_sum = proj_sum.astype(bf16)
    proj_both = [lax.ppermute(proj_sum, ("zl", "c", "zh"), owners) for owners in OWNERS]
    proj_whole = gather(stacked(proj_both, "proj_both"), "x")
    fc_near = stacked([after(fc_grad[0], place)] + fc_grad[1:], "fc_near")
    qkv_sum, out_sum = call(
        last_sum_kernel,
        "last_sum",
        (struct((4, window, slots), bf16), struct((windows(shard, 16)[0], width), bf16)),
        last_grads,
    )
    qkv_sum = exchange(after(qkv_sum, last), "y")
    qkv_whole = gather(qkv_sum, ("zl", "x"))
    results, first_sums = call(
        input_back_kernel,
        "input_back",
        (struct((2, span, width), bf16), struct((2, width), f32)),
        last,
        own_tokens,
        middle,
        grad_middle,
        after(vectors, qkv_sum),
    )
    results_home = swap_roles(results)

    blank = jnp.zeros((1, width), f32)
    at = (0, STRIDE * rank)
    small_terms = jnp.concatenate(
        [
            first_sums,
            lax.dynamic_update_slice(blank, mixed_sums[:, :SLOT_WIDTH], at),
            lax.dynamic_update_slice(blank, mixed_sums[:, 2 * SLOT_WIDTH :], at),
            branch_sums,
        ]
    )
    hidden_term = lax.dynamic_update_slice(
        jnp.zeros((8, hidden), f32), hidden_sums, (rank, 0)
    )
    small_terms = small_terms.reshape(8, 8, shard).transpose(1, 0, 2).reshape(8, 2, hidden)
    small_terms = jnp.concatenate([small_terms, hidden_term[:, None]], axis=1)
    small_sum = jnp.sum(exchange(after(small_terms, qkv_sum), GRP), axis=0)
    out_whole = exchange(
        after(jnp.broadcast_to(out_sum, (16,) + out_sum.shape), small_sum), REPLICAS
    )
    small_last = jnp.broadcast_to(after(small_sum, out_whole), (16, 3, hidden))
    small_last = jnp.sum(exchange(small_last, REP), axis=0)
    owned = small_last[:2].reshape(8, shard)

    qkv_spans = [
        [
            (p * SLOT_WIDTH, p * width + STRIDE * r, STRIDE if r < 7 else SLOT_WIDTH)
            for p in range(3)
        ]
        for r in range(8)
    ]
    proj_whole = after(proj_whole, qkv_sum)
    proj_total = call(
        proj_total_kernel,
        "proj_total",
        struct((hidden, width), f32),
        after(place, small_sum),
        proj_whole,
        other_core(proj_whole),
    )
    qkv_total = call(
        functools.partial(column_total_kernel, qkv_spans, False),
        "qkv_total",
        struct((shard, 3 * width), f32),
        after(place, results, small_last),
        qkv_whole,
        other_core(qkv_whole),
    )
    out_total = row_total(out_whole, shard, "out_total")
    fc_whole = gather(after(fc_near, qkv_whole, small_last), ("zl", "x"))
    fc_spans = [[(0, rank * hidden, hidden)] for rank in range(8)]
    fc_total = call(
        functools.partial(column_total_kernel, fc_spans, True),
        "fc_total",
        struct((shard, 8 * hidden), f32),
        after(place, qkv_total, out_total, proj_total),
        fc_whole,
        other_core(fc_whole),
    )
    return (
        results_home[1].reshape(1, span, width),
        results_home[0].astype(f32).reshape(1, span, width),
        owned[0],
        owned[1],
        qkv_total,
        owned[2],
        owned[3],
        out_total,
        owned[4],
        owned[5],
        owned[6],
        fc_total,
        small_last[2],
        proj_total,
        owned[7],
    )


def solution(mesh):
    names = tuple(name for name, _ in LAYOUT)
    fine = jax.sharding.Mesh(mesh.devices.reshape([size for _, size in LAYOUT]), names)
    in_specs = (
        P(REP, GRP, None),
        P(GRP),
        P(GRP),
        P(GRP, None),
        P(GRP),
        P(GRP),
        P(GRP, None),
        P(GRP),
        P(GRP),
        P(GRP),
        P(GRP, None),
        P(GRP),
        P(GRP, None),
        P(GRP),
        P(REP, GRP, None),
    )
    out_specs = (
        P(REP, GRP, None),
        P(REP, GRP, None),
        P(GRP),
        P(GRP),
        P(GRP, None),
        P(GRP),
        P(GRP),
        P(GRP, None),
        P(GRP),
        P(GRP),
        P(GRP),
        P(GRP, None),
        P(GRP),
        P(GRP, None),
        P(GRP),
    )
    return jax.shard_map(
        per_device, mesh=fine, in_specs=in_specs, out_specs=out_specs, check_vma=False
    )
```

```python
import functools
import math

import jax
import jax.numpy as jnp
from jax import lax
from jax.experimental import pallas as pl
from jax.experimental.pallas import tpu as pltpu
from jax.sharding import PartitionSpec as P

HEADS = 25
HEAD_DIM = 64
SLOTS = 4
SLOT_WIDTH = SLOTS * HEAD_DIM
STRIDE = 3 * HEAD_DIM
BLOCK = 256

bf16 = jnp.bfloat16
f32 = jnp.float32


LAYOUT = (("x", 4), ("zl", 2), ("c", 2), ("y", 4), ("zh", 2))
REP = ("x", "zl", "c")
GRP = ("y", "zh")
TEAM = ("y", "c")
REPLICAS = ("zl", "x", "zh")
Z_RING = ("zl", "zh")
Z_PLACES = (0, 2, 1, 3)
ROLES = [(0, 0), (1, 2), (2, 1), (3, 3)]
OWNERS = [
    [(l * 4 + k * 2 + h, (h ^ i) * 4 + l * 2 + k) for l in range(2) for k in range(2) for h in range(2)]
    for i in range(2)
]


def ring(value, axis, step):
    index = Z_PLACES if axis == Z_RING else range(4)
    return lax.ppermute(value, axis, [(index[(i + step) % 4], index[i]) for i in range(4)])


def ring_all(values, axis):
    return [values[0]] + [ring(values[k], axis, k) for k in range(1, 4)]


def flipped(value, axis):
    return lax.ppermute(value, axis, [(0, 1), (1, 0)])


def swap_roles(value):
    return lax.ppermute(value, ("c", "zh"), ROLES)


def swap_selected(value, stays):
    return jnp.where(stays, value, lax.ppermute(value, ("c", "zh"), ROLES[1:3]))


def other_core(value):
    return lax.ppermute(value, "c", [(0, 1), (1, 0)])


def exchange(parts, axes):
    return lax.all_to_all(parts, axes, 0, 0)


def gather(block, axes):
    return lax.all_gather(block, axes, axis=0)


def team_sum(parts):
    return lax.psum_scatter(parts.astype(bf16), TEAM, scatter_dimension=0, tiled=True)


def windows(rows, count):
    tiles = rows // 8
    starts = [tiles * i // count for i in range(count)]
    size = max(b - a for a, b in zip(starts, starts[1:] + [tiles]))
    return size * 8, [8 * s for s in starts]


def joined(parts, starts, rows, axis):
    ends = starts[1:] + [rows]
    return jnp.concatenate(
        [lax.slice_in_dim(p, 0, e - s, axis=axis) for p, s, e in zip(parts, starts, ends)], axis
    )


def norm_parts(value, gain, shift):
    center = value - jnp.mean(value, axis=-1, keepdims=True)
    spread = jnp.mean(center * center, axis=-1, keepdims=True)
    factor = lax.rsqrt(spread + 1e-05)
    normed = center * factor
    return (normed * gain + shift, normed, factor)


def norm_back(grad_value, normed, factor, gain):
    grad_normed = grad_value * gain
    mean_first = jnp.mean(grad_normed, axis=-1, keepdims=True)
    mean_second = jnp.mean(grad_normed * normed, axis=-1, keepdims=True)
    return factor * (grad_normed - mean_first - normed * mean_second)


def dot(left, right):
    return jnp.dot(left, right, preferred_element_type=f32)


def dot_rows(left, right):
    return lax.dot_general(left, right, (((0,), (0,)), ((), ())), preferred_element_type=f32)


def dot_cols(left, right):
    return lax.dot_general(left, right, (((1,), (1,)), ((), ())), preferred_element_type=f32)


def call(kernel, name, out_shape, *operands, scratch=(), flops=0, light=False):
    specs = [
        pl.BlockSpec(memory_space=pltpu.SMEM if op.dtype == jnp.int32 else pltpu.VMEM)
        for op in operands
    ]
    out_specs = jax.tree.map(lambda _: pl.BlockSpec(memory_space=pltpu.VMEM), out_shape)
    moved = sum(op.size * op.dtype.itemsize for op in operands)
    moved += sum(o.size * o.dtype.itemsize for o in jax.tree.leaves(out_shape))
    return pl.pallas_call(
        kernel,
        out_shape=out_shape,
        in_specs=specs,
        out_specs=out_specs,
        scratch_shapes=list(scratch),
        compiler_params=pltpu.CompilerParams(vmem_limit_bytes=56 * 2**20),
        cost_estimate=pl.CostEstimate(
            flops=1 if light else int(flops),
            bytes_accessed=1 if light else int(moved),
            transcendentals=0,
        ),
        name=name,
    )(*operands)


def struct(shape, dtype):
    return jax.ShapeDtypeStruct(shape, dtype)


Y, C, RANK, ZH, Z, X, ZL, MINE = range(8)


def qkv_columns_kernel(place_ref, weight_ref, *refs):
    out_refs, held_ref = refs[:4], refs[4]
    c = place_ref[C]
    width = weight_ref.shape[1] // 3
    for part in range(3):
        lanes = slice(part * SLOT_WIDTH, (part + 1) * SLOT_WIDTH)
        for y in range(4):
            start = part * width + 2 * STRIDE * y
            even = weight_ref[:, start : start + SLOT_WIDTH]
            odd = weight_ref[:, start + STRIDE : start + STRIDE + SLOT_WIDTH]
            held_ref[y, :, lanes] = jnp.where(c == 0, even, odd)
    for k in range(4):
        out_refs[k][...] = held_ref[lax.rem(place_ref[Y] + 4 - k, 4)]


def fc_columns_kernel(place_ref, weight_ref, *refs):
    out_refs, held_ref = refs[:4], refs[4]
    c = place_ref[C]
    hidden = weight_ref.shape[1] // 8
    for y in range(4):
        start = 2 * hidden * y
        even = weight_ref[:, start : start + hidden]
        odd = weight_ref[:, start + hidden : start + 2 * hidden]
        held_ref[y] = jnp.where(c == 0, even, odd)
    for k in range(4):
        out_refs[k][...] = held_ref[lax.rem(place_ref[Y] + 4 - k, 4)]


def fc_whole_kernel(place_ref, *refs):
    out_ref = refs[8]
    zh = place_ref[ZH]
    for k in range(4):
        y = lax.rem(place_ref[Y] + k, 4)
        out_ref[2 * y + zh] = refs[k][...]
        out_ref[2 * y + 1 - zh] = refs[4 + k][...]


def branch_kernel(
    slots_ref, tokens_ref, norm_ref, rows_ref, middle_ref, second_ref, parts_ref, flat_ref
):
    shard = parts_ref.shape[2]
    for rank in range(8):
        wide = STRIDE if rank < 7 else SLOT_WIDTH
        flat_ref[:, STRIDE * rank : STRIDE * rank + wide] = slots_ref[rank, :, :wide]
    for rank in range(8):
        parts_ref[rank] = flat_ref[:, shard * rank : shard * (rank + 1)]
    total = tokens_ref[...].astype(f32) + norm_ref[4:5, :] + dot(flat_ref[...], rows_ref[...])
    middle_ref[...] = total
    second_ref[...] = norm_parts(total, norm_ref[5:6, :], norm_ref[6:7, :])[0].astype(bf16)


def branch_back_kernel(
    place_ref,
    grad_ref,
    middle_ref,
    cot_ref,
    norm_ref,
    rows_ref,
    grad_middle_ref,
    branch_ref,
    slots_ref,
    sums_ref,
    flat_ref,
):
    gain = norm_ref[5:6, :]
    _, normed, factor = norm_parts(middle_ref[...], gain, gain)
    grad = grad_ref[...].astype(f32)
    cot = cot_ref[...].astype(f32)
    grad_middle = cot + norm_back(grad, normed, factor, gain)
    branch = grad_middle.astype(bf16)
    grad_middle_ref[...] = grad_middle
    branch_ref[...] = branch
    flat_ref[...] = dot_cols(branch, rows_ref[...]).astype(bf16)
    for rank in range(8):
        slots_ref[rank] = flat_ref[:, STRIDE * rank : STRIDE * rank + SLOT_WIDTH]
    sums_ref[0:1, :] = jnp.sum(branch.astype(f32), axis=0, keepdims=True)
    sums_ref[1:2, :] = jnp.sum(grad * normed, axis=0, keepdims=True)
    sums_ref[2:3, :] = jnp.sum(grad, axis=0, keepdims=True)
    sums_ref[3:4, :] = jnp.sum(cot, axis=0, keepdims=True)


def column_ring_kernel(place_ref, left_ref, right_ref, *refs):
    out_refs, held_ref = refs[:4], refs[4]
    shard = left_ref.shape[1] // 8
    size, starts = windows(shard, 8)
    held_ref[...] = dot_rows(left_ref[...], right_ref[...])
    for k in range(4):
        x = lax.rem(place_ref[X] + 4 - k, 4)
        for z in range(4):
            for y in range(4):
                base = (2 * y + z // 2) * shard + starts[4 * (z % 2)]
                at = pl.multiple_of(base + starts[1] * x, 8)
                out_refs[k][z, y] = held_ref[pl.ds(at, size), :].astype(bf16)


def row_grad_kernel(place_ref, left_ref, right_ref, *refs):
    out_refs, held_ref = refs[:4], refs[4]
    rows = left_ref.shape[1]
    size = windows(rows, 16)[0]
    held_ref[...] = dot_rows(left_ref[...], right_ref[...])
    for k in range(4):
        z = lax.rem(place_ref[Z] + 4 - k, 4)
        for x in range(4):
            window = (lax.rem(z, 2) * 4 + x) * 2 + lax.div(z, 2)
            at = pl.multiple_of(lax.div(rows // 8 * window, 16) * 8, 8)
            out_refs[k][x] = held_ref[pl.ds(at, size), :].astype(bf16)


def last_grads_kernel(place_ref, first_ref, mixed_ref, attended_ref, branch_ref, out_ref, held_ref):
    shard = first_ref.shape[1] // 8
    slots = mixed_ref.shape[1]
    size, starts = windows(shard, 8)
    held_ref[...] = dot_rows(first_ref[...], mixed_ref[...])
    for y in range(4):
        for zh in range(2):
            base = (2 * y + zh) * shard
            for i, start in enumerate(starts):
                rows = slice(y % 2 * size, (y % 2 + 1) * size)
                lanes = slice(y // 2 * slots, (y // 2 + 1) * slots)
                block = held_ref[base + start : base + start + size, :]
                out_ref[2 * i + zh, rows, lanes] = block.astype(bf16)
    size_out, starts_out = windows(shard, 16)
    grad = dot_rows(attended_ref[...], branch_ref[...])
    rest = jnp.zeros((2 * size, out_ref.shape[2] - 2 * slots), bf16)
    for i, start in enumerate(starts_out):
        out_ref[i, : 2 * size, 2 * slots :] = rest
        out_ref[i, 2 * size :, :] = grad[start : start + size_out].astype(bf16)


def last_sum_kernel(parts_ref, qkv_ref, out_ref):
    size, slots = qkv_ref.shape[1:]
    total = parts_ref[0].astype(f32)
    for i in range(1, 16):
        total = total + parts_ref[i].astype(f32)
    total = total.astype(bf16)
    for y in range(4):
        rows = slice(y % 2 * size, (y % 2 + 1) * size)
        qkv_ref[y] = total[rows, y // 2 * slots : (y // 2 + 1) * slots]
    out_ref[...] = total[2 * size :, :]


def fold_kernel(which, place_ref, *refs):
    for k in range(4):
        at = lax.rem(place_ref[which] + 4 - k, 4)
        total = refs[0][at].astype(f32)
        for j in range(1, 4):
            total = total + refs[j][at].astype(f32)
        refs[4 + k][...] = total.astype(bf16)


def stack_kernel(*refs):
    for k, ref in enumerate(refs[:-1]):
        refs[-1][k] = ref[...]


def column_total_kernel(spans, ringed, place_ref, own_ref, other_ref, out_ref):
    _, starts = windows(out_ref.shape[0], 8)
    ends = starts[1:] + [out_ref.shape[0]]
    for rank in range(8):
        y = lax.rem(rank // 2 + 4 - place_ref[Y], 4) if ringed else rank // 2
        mine = place_ref[C] == rank % 2
        rows = [
            jnp.where(mine, own_ref[i, y], other_ref[i, y]).astype(f32)[: end - start]
            for i, (start, end) in enumerate(zip(starts, ends))
        ]
        block = jnp.concatenate(rows, axis=0)
        for source, target, wide in spans[rank]:
            out_ref[:, target : target + wide] = block[:, source : source + wide]


def proj_total_kernel(place_ref, own_ref, other_ref, out_ref):
    tiles = out_ref.shape[0] // 8
    small = tiles // 16 * 8
    for part, ref in enumerate((own_ref, other_ref)):
        zl = place_ref[C] if part == 0 else 1 - place_ref[C]
        for x in range(4):
            for i in range(2):
                zh = place_ref[ZL] if i == 0 else 1 - place_ref[ZL]
                window = (zl * 4 + x) * 2 + zh
                start = lax.div(tiles * window, 16)
                wide = lax.div(tiles * (window + 1), 16) - start > small // 8
                at = pl.multiple_of(start * 8, 8)
                block = ref[x, i].astype(f32)
                out_ref[pl.ds(at, small), :] = block[:small]

                @pl.when(wide)
                def _(at=at, block=block):
                    out_ref[pl.ds(pl.multiple_of(at + small, 8), 8), :] = block[small:]


def row_total_kernel(place_ref, own_ref, other_ref, out_ref):
    mine = place_ref[MINE]
    _, starts = windows(out_ref.shape[0], 16)
    ends = starts[1:] + [out_ref.shape[0]]
    for i, (start, end) in enumerate(zip(starts, ends)):
        block = jnp.where(mine == 1, own_ref[i], other_ref[i])
        out_ref[start:end, :] = block[: end - start].astype(f32)


def attend_kernel(place_ref, tokens_ref, norm_ref, bias_ref, *refs):
    pieces, (first_ref, qkv_ref, out_ref, top_ref, cols_ref) = refs[:8], refs[8:]
    length = tokens_ref.shape[0]
    shard = cols_ref.shape[1]
    zh = place_ref[ZH]
    for k in range(4):
        y = lax.rem(place_ref[Y] + k, 4)
        cols_ref[2 * y + zh] = pieces[k][...]
        cols_ref[2 * y + 1 - zh] = pieces[4 + k][...]
    gain = norm_ref[0:1, :]
    shift = norm_ref[1:2, :]
    for block in range(length // BLOCK):
        rows = slice(block * BLOCK, (block + 1) * BLOCK)
        first = norm_parts(tokens_ref[rows, :].astype(f32), gain, shift)[0].astype(bf16)
        first_ref[rows, :] = first
        mixed = bias_ref[...]
        for g in range(8):
            mixed = mixed + dot(first[:, g * shard : (g + 1) * shard], cols_ref[g])
        qkv_ref[rows, :] = mixed.astype(bf16)
    for head in range(SLOTS):
        lanes = slice(head * HEAD_DIM, (head + 1) * HEAD_DIM)
        keys = qkv_ref[:, SLOT_WIDTH + head * HEAD_DIM : SLOT_WIDTH + (head + 1) * HEAD_DIM]
        values = qkv_ref[
            :, 2 * SLOT_WIDTH + head * HEAD_DIM : 2 * SLOT_WIDTH + (head + 1) * HEAD_DIM
        ]
        for block in range(length // BLOCK):
            rows = slice(block * BLOCK, (block + 1) * BLOCK)
            width = (block + 1) * BLOCK
            query = qkv_ref[rows, lanes] * bf16(1.0 / math.sqrt(HEAD_DIM))
            scores = dot_cols(query, keys[:width])
            row = lax.broadcasted_iota(jnp.int32, (BLOCK, width), 0) + block * BLOCK
            col = lax.broadcasted_iota(jnp.int32, (BLOCK, width), 1)
            scores = jnp.where(col <= row, scores, -1e30)
            top = jnp.max(scores, axis=-1, keepdims=True)
            probs = jnp.exp(scores - top)
            total = jnp.sum(probs, axis=-1, keepdims=True)
            mixed = dot(probs.astype(bf16), values[:width])
            out_ref[rows, lanes] = (mixed / total).astype(bf16)
            top_ref[rows, head : head + 1] = top + jnp.log(total)


def hidden_kernel(
    place_ref, second_ref, cols_ref, bias_ref, grad_ref, active_ref, hidden_ref, sums_ref, out_ref
):
    length = second_ref.shape[0]
    sums = jnp.zeros(sums_ref.shape, f32)
    for block in range(length // BLOCK):
        rows = slice(block * BLOCK, (block + 1) * BLOCK)
        pre = dot(second_ref[rows, :], cols_ref[...]) + bias_ref[...]
        square = pre * pre
        bent = jnp.tanh(0.7978845608028654 * (pre + 0.044715 * square * pre))
        half = 0.5 * (1.0 + bent)
        active_ref[rows, :] = (pre * half).astype(bf16)
        slope = half + 0.5 * pre * (1.0 - bent * bent) * (
            0.7978845608028654 + (3.0 * 0.044715 * 0.7978845608028654) * square
        )
        grad = (grad_ref[rows, :] * slope).astype(bf16)
        hidden_ref[rows, :] = grad
        sums = sums + jnp.sum(grad.astype(f32), axis=0, keepdims=True)
        out_ref[rows, :] = dot_cols(grad, cols_ref[...]).astype(bf16)
    sums_ref[...] = sums


def down_kernel(active_ref, rows_ref, out_ref):
    for block in range(active_ref.shape[0] // BLOCK):
        rows = slice(block * BLOCK, (block + 1) * BLOCK)
        out_ref[rows, :] = dot(active_ref[rows, :], rows_ref[...]).astype(bf16)


def attend_back_kernel(
    place_ref,
    qkv_ref,
    grad_ref,
    out_ref,
    top_ref,
    cols_ref,
    down_ref,
    mixed_ref,
    parts_ref,
    sums_ref,
    query_ref,
):
    length = qkv_ref.shape[0]
    scale = 1.0 / math.sqrt(HEAD_DIM)
    ones = jnp.ones((8, HEAD_DIM), bf16)
    for head in range(SLOTS):
        base = head * HEAD_DIM
        lanes = slice(base, base + HEAD_DIM)
        key_lanes = slice(SLOT_WIDTH + base, SLOT_WIDTH + base + HEAD_DIM)
        value_lanes = slice(2 * SLOT_WIDTH + base, 2 * SLOT_WIDTH + base + HEAD_DIM)
        query = qkv_ref[:, lanes] * bf16(scale)
        grad = grad_ref[:, lanes]
        if head == SLOTS - 1:
            grad = jnp.where(place_ref[RANK] == 7, grad, jnp.zeros_like(grad))
        top = top_ref[head : head + 1, :]
        delta = dot_cols(ones, grad * out_ref[:, lanes])[0:1, :]
        for block in range(length // BLOCK):
            start = block * BLOCK
            rows = slice(start, start + BLOCK)
            width = length - start
            keys = qkv_ref[rows, key_lanes]
            values = qkv_ref[rows, value_lanes]
            scores = dot_cols(keys, query[start:])
            row = lax.broadcasted_iota(jnp.int32, (BLOCK, width), 0)
            col = lax.broadcasted_iota(jnp.int32, (BLOCK, width), 1)
            probs = jnp.where(row <= col, jnp.exp(scores - top[:, start:]), 0.0)
            grad_probs = dot_cols(values, grad[start:])
            grad_scores = (probs * (grad_probs - delta[:, start:])).astype(bf16)
            mixed_ref[rows, value_lanes] = dot(probs.astype(bf16), grad[start:]).astype(bf16)
            mixed_ref[rows, key_lanes] = dot(grad_scores, query[start:]).astype(bf16)
            term = dot_rows(grad_scores, keys)
            if block == 0:
                query_ref[...] = term
            else:
                query_ref[start:, :] += term
        mixed_ref[:, lanes] = (query_ref[...] * scale).astype(bf16)
    sums = jnp.zeros(sums_ref.shape, f32)
    for block in range(length // BLOCK):
        rows = slice(block * BLOCK, (block + 1) * BLOCK)
        mixed = mixed_ref[rows, :]
        sums = sums + jnp.sum(mixed.astype(f32), axis=0, keepdims=True)
        first = dot_cols(mixed, cols_ref[...]).astype(bf16)
        for half in range(2):
            rank = 2 * block + half
            parts_ref[rank, 0] = first[half * BLOCK // 2 : (half + 1) * BLOCK // 2]
            parts_ref[rank, 1] = down_ref[rank]
    sums_ref[...] = sums


def input_back_kernel(
    parts_ref, tokens_ref, middle_ref, grad_ref, norm_ref, out_ref, sums_ref
):
    gain = norm_ref[0:1, :]
    _, normed, factor = norm_parts(tokens_ref[...].astype(f32), gain, gain)
    grad = parts_ref[0].astype(f32)
    out_ref[0] = (grad_ref[...] + norm_back(grad, normed, factor, gain)).astype(bf16)
    down = parts_ref[1].astype(f32) + norm_ref[7:8, :]
    out_ref[1] = (middle_ref[...] + down).astype(bf16)
    sums_ref[0:1, :] = jnp.sum(grad * normed, axis=0, keepdims=True)
    sums_ref[1:2, :] = jnp.sum(grad, axis=0, keepdims=True)


def after(value, *others):
    return lax.optimization_barrier((value,) + others)[0]


def per_device(
    tokens,
    ln1_gain,
    ln1_bias,
    w_qkv,
    bias_q,
    bias_v,
    w_out,
    bias_out,
    ln2_gain,
    ln2_bias,
    w_fc,
    bias_fc,
    w_proj,
    bias_proj,
    cotangent,
):
    _, span, width = tokens.shape
    shard = width // 8
    hidden = w_fc.shape[1] // 8
    length = span * 8
    slots = 3 * SLOT_WIDTH
    x, zl, c, y, zh = [lax.axis_index(name) for name, _ in LAYOUT]
    rank = y * 2 + c
    place = jnp.stack(
        [y, c, rank, zh, zh * 2 + zl, x, zl, (c == zh).astype(jnp.int32)]
    ).astype(jnp.int32)

    stays = c == zh
    own_tokens = swap_roles(tokens.reshape(span, width))
    qkv_parts = call(
        qkv_columns_kernel,
        "qkv_columns",
        [struct((shard, slots), bf16)] * 4,
        place,
        w_qkv,
        scratch=[pltpu.VMEM((4, shard, slots), bf16)],
    )
    all_tokens = gather(after(own_tokens, qkv_parts[0]), TEAM).reshape(length, width)
    qkv_own = ring_all(qkv_parts, "y")
    qkv_other = [flipped(part, "zh") for part in qkv_own]
    out_rows = swap_roles(after(w_out, *qkv_own))
    small = jnp.concatenate(
        [ln1_gain, ln1_bias, bias_q, bias_v, bias_out, ln2_gain, ln2_bias, bias_proj, bias_fc]
    ).reshape(3, hidden)
    small_all = exchange(
        after(jnp.broadcast_to(small, (8, 3, hidden)), qkv_other[0]), GRP
    )
    place = after(place, small_all)
    fc_parts = call(
        fc_columns_kernel,
        "fc_columns",
        [struct((shard, hidden), bf16)] * 4,
        place,
        w_fc,
        scratch=[pltpu.VMEM((4, shard, hidden), bf16)],
    )
    own_cot = swap_roles(after(cotangent, *qkv_other).reshape(span, width))

    small_all = small_all.astype(f32)
    hidden_bias = lax.dynamic_index_in_dim(small_all, rank, 0, keepdims=False)[2:3]
    vectors = small_all[:, :2].reshape(8, 8, shard).transpose(1, 0, 2).reshape(8, width)
    bias_slots = jnp.concatenate(
        [
            lax.dynamic_slice_in_dim(vectors[2], STRIDE * rank, SLOT_WIDTH),
            jnp.zeros((SLOT_WIDTH,), f32),
            lax.dynamic_slice_in_dim(vectors[3], STRIDE * rank, SLOT_WIDTH),
        ]
    ).reshape(1, slots)

    out_all = gather(out_rows, TEAM).reshape(width, width)
    all_cot = gather(after(own_cot, out_rows), TEAM).reshape(length, width)
    proj_came = lax.ppermute(after(w_proj, *qkv_other), ("c", "zh"), ROLES[1:3])
    proj_rows = jnp.where(stays, w_proj, proj_came)
    fc_own = ring_all([after(part, *qkv_other) for part in fc_parts], "y")

    first, qkv, attended_slots, top, qkv_cols = call(
        attend_kernel,
        "attend",
        (
            struct((length, width), bf16),
            struct((length, slots), bf16),
            struct((length, SLOT_WIDTH), bf16),
            struct((length, SLOTS), f32),
            struct((8, shard, slots), bf16),
        ),
        after(place, bias_slots),
        all_tokens,
        vectors,
        bias_slots,
        *qkv_own,
        *qkv_other,
        flops=2 * length * width * slots,
    )
    qkv_cols = qkv_cols.reshape(width, slots)
    fc_other = [flipped(part, "zh") for part in fc_own]
    attended = exchange(
        after(attended_slots, *fc_own).reshape(8, span, SLOT_WIDTH), TEAM
    )
    middle, second, attended_parts = call(
        branch_kernel,
        "branch",
        (
            struct((span, width), f32),
            struct((span, width), bf16),
            struct((8, span, shard), bf16),
        ),
        after(attended, proj_came),
        own_tokens,
        vectors,
        out_all,
        scratch=[pltpu.VMEM((span, width), bf16)],
        flops=2 * span * width * width,
    )

    second_all = gather(second, TEAM).reshape(length, width)
    attended_own = exchange(after(attended_parts, second), TEAM)
    grad_active = dot_cols(after(all_cot, second), proj_rows)
    fc_cols = call(
        fc_whole_kernel,
        "fc_whole",
        struct((8, shard, hidden), bf16),
        place,
        after(fc_own[0], grad_active),
        *fc_own[1:],
        *fc_other,
    ).reshape(width, hidden)
    active, grad_hidden, hidden_sums, second_parts = call(
        hidden_kernel,
        "hidden",
        (
            struct((length, hidden), bf16),
            struct((length, hidden), bf16),
            struct((1, hidden), f32),
            struct((length, width), bf16),
        ),
        after(place, attended_own),
        second_all,
        fc_cols,
        hidden_bias,
        grad_active,
        flops=4 * length * width * hidden,
    )
    grad_second = team_sum(second_parts)
    window = windows(shard, 8)[0]
    fc_grad = call(
        column_ring_kernel,
        "fc_grad",
        [struct((4, 4, window, hidden), bf16)] * 4,
        place,
        second_all,
        grad_hidden,
        scratch=[pltpu.VMEM((width, hidden), f32)],
        flops=2 * length * width * hidden,
    )
    fc_grad = ring_all(fc_grad, "x")
    row_window = windows(hidden, 16)[0]
    proj_grad = call(
        row_grad_kernel,
        "proj_grad",
        [struct((4, row_window, width), bf16)] * 4,
        after(place, fc_grad[0]),
        active,
        all_cot,
        scratch=[pltpu.VMEM((hidden, width), f32)],
        flops=2 * length * width * hidden,
    )
    down_parts = call(
        down_kernel,
        "down",
        struct((length, width), bf16),
        after(active, proj_grad[0]),
        proj_rows,
        light=True,
    )
    proj_near = [ring(proj_grad[k], Z_RING, k) for k in (1, 3)]
    proj_far = ring(after(proj_grad[2], *proj_near), Z_RING, 2)
    proj_grad = [proj_grad[0], proj_near[0], proj_far, proj_near[1]]

    grad_middle, grad_branch, grad_slots, branch_sums = call(
        branch_back_kernel,
        "branch_back",
        (
            struct((span, width), f32),
            struct((span, width), bf16),
            struct((8, span, SLOT_WIDTH), bf16),
            struct((4, width), f32),
        ),
        after(place, *fc_grad, *proj_near, down_parts),
        grad_second,
        middle,
        own_cot,
        vectors,
        out_all,
        scratch=[pltpu.VMEM((span, width), bf16)],
        light=True,
    )
    grad_heads = exchange(grad_slots, TEAM).reshape(length, SLOT_WIDTH)

    def fold(which, parts, name, *behind):
        parts = [after(parts[0], *behind)] + parts[1:]
        return call(
            functools.partial(fold_kernel, which),
            name,
            [struct(parts[0].shape[1:], bf16)] * 4,
            place,
            *parts,
            light=True,
        )

    fc_grad = ring_all(fold(Z, fc_grad, "fc_fold", grad_slots), Z_RING)
    branch_all = gather(grad_branch, TEAM).reshape(length, width)
    grad_mixed, last_parts, mixed_sums = call(
        attend_back_kernel,
        "attend_back",
        (
            struct((length, slots), bf16),
            struct((8, 2, span, width), bf16),
            struct((1, slots), f32),
        ),
        place,
        qkv,
        grad_heads,
        attended_slots,
        top.T,
        qkv_cols,
        down_parts.reshape(8, span, width),
        scratch=[pltpu.VMEM((length, HEAD_DIM), f32)],
        flops=20 * length * width * slots,
    )
    last = team_sum(last_parts.reshape(2 * length, width)).reshape(2, span, width)
    last_grads = call(
        last_grads_kernel,
        "last_grads",
        struct((16, 2 * window + windows(shard, 16)[0], width), bf16),
        place,
        first,
        grad_mixed,
        attended_own.reshape(length, shard),
        branch_all,
        scratch=[pltpu.VMEM((width, slots), f32)],
        flops=2 * length * width * (slots + shard),
    )
    place = after(place, last_grads)
    last_grads = exchange(last_grads, REPLICAS)

    def stacked(parts, name):
        return call(
            stack_kernel, name, struct((len(parts),) + parts[0].shape, bf16), *parts
        )

    def row_total(whole, rows, name, *behind):
        whole = after(whole, *behind)
        return call(
            row_total_kernel, name, struct((rows, width), f32), place, whole, other_core(whole)
        )

    qkv_sum, out_sum = call(
        last_sum_kernel,
        "last_sum",
        (struct((4, window, slots), bf16), struct((windows(shard, 16)[0], width), bf16)),
        after(last_grads, proj_far, *fc_grad),
    )
    qkv_sum = exchange(after(qkv_sum, last), "y")
    qkv_whole = gather(qkv_sum, ("zl", "x"))
    fc_grad = ring_all(fold(Y, fc_grad, "fc_fold_last", qkv_sum), "y")
    proj_grad = ring_all(fold(X, proj_grad, "proj_fold", qkv_sum), "x")
    proj_sum = sum(part.astype(f32) for part in proj_grad).astype(bf16)
    proj_both = [lax.ppermute(proj_sum, ("zl", "c", "zh"), owners) for owners in OWNERS]
    proj_whole = gather(stacked(proj_both, "proj_both"), "x")
    fc_near = stacked(fc_grad, "fc_near")
    results, first_sums = call(
        input_back_kernel,
        "input_back",
        (struct((2, span, width), bf16), struct((2, width), f32)),
        last,
        own_tokens,
        middle,
        grad_middle,
        after(vectors, qkv_sum),
    )
    results_home = swap_roles(results)

    blank = jnp.zeros((1, width), f32)
    at = (0, STRIDE * rank)
    small_terms = jnp.concatenate(
        [
            first_sums,
            lax.dynamic_update_slice(blank, mixed_sums[:, :SLOT_WIDTH], at),
            lax.dynamic_update_slice(blank, mixed_sums[:, 2 * SLOT_WIDTH :], at),
            branch_sums,
        ]
    )
    hidden_term = lax.dynamic_update_slice(
        jnp.zeros((8, hidden), f32), hidden_sums, (rank, 0)
    )
    small_terms = small_terms.reshape(8, 8, shard).transpose(1, 0, 2).reshape(8, 2, hidden)
    small_terms = jnp.concatenate([small_terms, hidden_term[:, None]], axis=1)
    small_sum = jnp.sum(exchange(after(small_terms, qkv_sum), GRP), axis=0)
    out_whole = exchange(
        after(jnp.broadcast_to(out_sum, (16,) + out_sum.shape), small_sum), REPLICAS
    )
    small_last = jnp.broadcast_to(after(small_sum, out_whole), (16, 3, hidden))
    small_last = jnp.sum(exchange(small_last, REP), axis=0)
    owned = small_last[:2].reshape(8, shard)

    qkv_spans = [
        [
            (p * SLOT_WIDTH, p * width + STRIDE * r, STRIDE if r < 7 else SLOT_WIDTH)
            for p in range(3)
        ]
        for r in range(8)
    ]
    fc_whole = gather(after(fc_near, qkv_whole), ("zl", "x"))
    qkv_whole, fc_whole, proj_whole, out_whole = [
        after(whole, small_last) for whole in (qkv_whole, fc_whole, proj_whole, out_whole)
    ]
    proj_total = call(
        proj_total_kernel,
        "proj_total",
        struct((hidden, width), f32),
        after(place, small_sum),
        proj_whole,
        other_core(proj_whole),
    )
    qkv_total = call(
        functools.partial(column_total_kernel, qkv_spans, False),
        "qkv_total",
        struct((shard, 3 * width), f32),
        after(place, results, small_last),
        qkv_whole,
        other_core(qkv_whole),
    )
    out_total = row_total(out_whole, shard, "out_total")
    fc_spans = [[(0, rank * hidden, hidden)] for rank in range(8)]
    fc_total = call(
        functools.partial(column_total_kernel, fc_spans, True),
        "fc_total",
        struct((shard, 8 * hidden), f32),
        after(place, qkv_total, out_total, proj_total),
        fc_whole,
        other_core(fc_whole),
    )
    return (
        results_home[1].reshape(1, span, width),
        results_home[0].astype(f32).reshape(1, span, width),
        owned[0],
        owned[1],
        qkv_total,
        owned[2],
        owned[3],
        out_total,
        owned[4],
        owned[5],
        owned[6],
        fc_total,
        small_last[2],
        proj_total,
        owned[7],
    )


def solution(mesh):
    names = tuple(name for name, _ in LAYOUT)
    fine = jax.sharding.Mesh(mesh.devices.reshape([size for _, size in LAYOUT]), names)
    in_specs = (
        P(REP, GRP, None),
        P(GRP),
        P(GRP),
        P(GRP, None),
        P(GRP),
        P(GRP),
        P(GRP, None),
        P(GRP),
        P(GRP),
        P(GRP),
        P(GRP, None),
        P(GRP),
        P(GRP, None),
        P(GRP),
        P(REP, GRP, None),
    )
    out_specs = (
        P(REP, GRP, None),
        P(REP, GRP, None),
        P(GRP),
        P(GRP),
        P(GRP, None),
        P(GRP),
        P(GRP),
        P(GRP, None),
        P(GRP),
        P(GRP),
        P(GRP),
        P(GRP, None),
        P(GRP),
        P(GRP, None),
        P(GRP),
    )
    return jax.shard_map(
        per_device, mesh=fine, in_specs=in_specs, out_specs=out_specs, check_vma=False
    )
```

```python
import functools
import math

import jax
import jax.numpy as jnp
from jax import lax
from jax.experimental import pallas as pl
from jax.experimental.pallas import tpu as pltpu
from jax.sharding import PartitionSpec as P

HEADS = 25
HEAD_DIM = 64
SLOTS = 4
SLOT_WIDTH = SLOTS * HEAD_DIM
STRIDE = 3 * HEAD_DIM
BLOCK = 256

bf16 = jnp.bfloat16
f32 = jnp.float32


LAYOUT = (("x", 4), ("zl", 2), ("c", 2), ("y", 4), ("zh", 2))
REP = ("x", "zl", "c")
GRP = ("y", "zh")
TEAM = ("y", "c")
REPLICAS = ("zl", "x", "zh")
Z_RING = ("zl", "zh")
Z_PLACES = (0, 2, 1, 3)
ROLES = [(0, 0), (1, 2), (2, 1), (3, 3)]
OWNERS = [
    [(l * 4 + k * 2 + h, (h ^ i) * 4 + l * 2 + k) for l in range(2) for k in range(2) for h in range(2)]
    for i in range(2)
]


def ring(value, axis, step):
    index = Z_PLACES if axis == Z_RING else range(4)
    return lax.ppermute(value, axis, [(index[(i + step) % 4], index[i]) for i in range(4)])


def ring_all(values, axis):
    return [values[0]] + [ring(values[k], axis, k) for k in range(1, 4)]


def flipped(value, axis):
    return lax.ppermute(value, axis, [(0, 1), (1, 0)])


def swap_roles(value):
    return lax.ppermute(value, ("c", "zh"), ROLES)


def swap_selected(value, stays):
    return jnp.where(stays, value, lax.ppermute(value, ("c", "zh"), ROLES[1:3]))


def other_core(value):
    return lax.ppermute(value, "c", [(0, 1), (1, 0)])


def exchange(parts, axes):
    return lax.all_to_all(parts, axes, 0, 0)


def gather(block, axes):
    return lax.all_gather(block, axes, axis=0)


def team_sum(parts):
    return lax.psum_scatter(parts.astype(bf16), TEAM, scatter_dimension=0, tiled=True)


def windows(rows, count):
    tiles = rows // 8
    starts = [tiles * i // count for i in range(count)]
    size = max(b - a for a, b in zip(starts, starts[1:] + [tiles]))
    return size * 8, [8 * s for s in starts]


def joined(parts, starts, rows, axis):
    ends = starts[1:] + [rows]
    return jnp.concatenate(
        [lax.slice_in_dim(p, 0, e - s, axis=axis) for p, s, e in zip(parts, starts, ends)], axis
    )


def norm_parts(value, gain, shift):
    center = value - jnp.mean(value, axis=-1, keepdims=True)
    spread = jnp.mean(center * center, axis=-1, keepdims=True)
    factor = lax.rsqrt(spread + 1e-05)
    normed = center * factor
    return (normed * gain + shift, normed, factor)


def norm_back(grad_value, normed, factor, gain):
    grad_normed = grad_value * gain
    mean_first = jnp.mean(grad_normed, axis=-1, keepdims=True)
    mean_second = jnp.mean(grad_normed * normed, axis=-1, keepdims=True)
    return factor * (grad_normed - mean_first - normed * mean_second)


def dot(left, right):
    return jnp.dot(left, right, preferred_element_type=f32)


def dot_rows(left, right):
    return lax.dot_general(left, right, (((0,), (0,)), ((), ())), preferred_element_type=f32)


def dot_cols(left, right):
    return lax.dot_general(left, right, (((1,), (1,)), ((), ())), preferred_element_type=f32)


def call(kernel, name, out_shape, *operands, scratch=(), flops=0, light=False):
    specs = [
        pl.BlockSpec(memory_space=pltpu.SMEM if op.dtype == jnp.int32 else pltpu.VMEM)
        for op in operands
    ]
    out_specs = jax.tree.map(lambda _: pl.BlockSpec(memory_space=pltpu.VMEM), out_shape)
    moved = sum(op.size * op.dtype.itemsize for op in operands)
    moved += sum(o.size * o.dtype.itemsize for o in jax.tree.leaves(out_shape))
    return pl.pallas_call(
        kernel,
        out_shape=out_shape,
        in_specs=specs,
        out_specs=out_specs,
        scratch_shapes=list(scratch),
        compiler_params=pltpu.CompilerParams(vmem_limit_bytes=56 * 2**20),
        cost_estimate=pl.CostEstimate(
            flops=1 if light else int(flops),
            bytes_accessed=1 if light else int(moved),
            transcendentals=0,
        ),
        name=name,
    )(*operands)


def struct(shape, dtype):
    return jax.ShapeDtypeStruct(shape, dtype)


Y, C, RANK, ZH, Z, X, ZL, MINE = range(8)


def qkv_columns_kernel(place_ref, weight_ref, *refs):
    out_refs, held_ref = refs[:4], refs[4]
    c = place_ref[C]
    width = weight_ref.shape[1] // 3
    for part in range(3):
        lanes = slice(part * SLOT_WIDTH, (part + 1) * SLOT_WIDTH)
        for y in range(4):
            start = part * width + 2 * STRIDE * y
            even = weight_ref[:, start : start + SLOT_WIDTH]
            odd = weight_ref[:, start + STRIDE : start + STRIDE + SLOT_WIDTH]
            held_ref[y, :, lanes] = jnp.where(c == 0, even, odd)
    for k in range(4):
        out_refs[k][...] = held_ref[lax.rem(place_ref[Y] + 4 - k, 4)]


def fc_columns_kernel(place_ref, weight_ref, *refs):
    out_refs, held_ref = refs[:4], refs[4]
    c = place_ref[C]
    hidden = weight_ref.shape[1] // 8
    for y in range(4):
        start = 2 * hidden * y
        even = weight_ref[:, start : start + hidden]
        odd = weight_ref[:, start + hidden : start + 2 * hidden]
        held_ref[y] = jnp.where(c == 0, even, odd)
    for k in range(4):
        out_refs[k][...] = held_ref[lax.rem(place_ref[Y] + 4 - k, 4)]


def fc_whole_kernel(place_ref, *refs):
    out_ref = refs[8]
    zh = place_ref[ZH]
    for k in range(4):
        y = lax.rem(place_ref[Y] + k, 4)
        out_ref[2 * y + zh] = refs[k][...]
        out_ref[2 * y + 1 - zh] = refs[4 + k][...]


def branch_kernel(
    slots_ref, tokens_ref, norm_ref, rows_ref, middle_ref, second_ref, parts_ref, flat_ref
):
    shard = parts_ref.shape[2]
    for rank in range(8):
        wide = STRIDE if rank < 7 else SLOT_WIDTH
        flat_ref[:, STRIDE * rank : STRIDE * rank + wide] = slots_ref[rank, :, :wide]
    for rank in range(8):
        parts_ref[rank] = flat_ref[:, shard * rank : shard * (rank + 1)]
    total = tokens_ref[...].astype(f32) + norm_ref[4:5, :] + dot(flat_ref[...], rows_ref[...])
    middle_ref[...] = total
    second_ref[...] = norm_parts(total, norm_ref[5:6, :], norm_ref[6:7, :])[0].astype(bf16)


def branch_back_kernel(
    place_ref,
    grad_ref,
    middle_ref,
    cot_ref,
    norm_ref,
    rows_ref,
    grad_middle_ref,
    branch_ref,
    slots_ref,
    sums_ref,
    flat_ref,
):
    gain = norm_ref[5:6, :]
    _, normed, factor = norm_parts(middle_ref[...], gain, gain)
    grad = grad_ref[...].astype(f32)
    cot = cot_ref[...].astype(f32)
    grad_middle = cot + norm_back(grad, normed, factor, gain)
    branch = grad_middle.astype(bf16)
    grad_middle_ref[...] = grad_middle
    branch_ref[...] = branch
    flat_ref[...] = dot_cols(branch, rows_ref[...]).astype(bf16)
    for rank in range(8):
        slots_ref[rank] = flat_ref[:, STRIDE * rank : STRIDE * rank + SLOT_WIDTH]
    sums_ref[0:1, :] = jnp.sum(branch.astype(f32), axis=0, keepdims=True)
    sums_ref[1:2, :] = jnp.sum(grad * normed, axis=0, keepdims=True)
    sums_ref[2:3, :] = jnp.sum(grad, axis=0, keepdims=True)
    sums_ref[3:4, :] = jnp.sum(cot, axis=0, keepdims=True)


def column_ring_kernel(place_ref, left_ref, right_ref, *refs):
    out_refs, held_ref = refs[:4], refs[4]
    shard = left_ref.shape[1] // 8
    size, starts = windows(shard, 8)
    held_ref[...] = dot_rows(left_ref[...], right_ref[...])
    for k in range(4):
        x = lax.rem(place_ref[X] + 4 - k, 4)
        for z in range(4):
            for y in range(4):
                base = (2 * y + z // 2) * shard + starts[4 * (z % 2)]
                at = pl.multiple_of(base + starts[1] * x, 8)
                out_refs[k][z, y] = held_ref[pl.ds(at, size), :].astype(bf16)


def row_grad_kernel(place_ref, left_ref, right_ref, *refs):
    out_refs, held_ref = refs[:4], refs[4]
    rows = left_ref.shape[1]
    size = windows(rows, 16)[0]
    held_ref[...] = dot_rows(left_ref[...], right_ref[...])
    for k in range(4):
        z = lax.rem(place_ref[Z] + 4 - k, 4)
        for x in range(4):
            window = (lax.rem(z, 2) * 4 + x) * 2 + lax.div(z, 2)
            at = pl.multiple_of(lax.div(rows // 8 * window, 16) * 8, 8)
            out_refs[k][x] = held_ref[pl.ds(at, size), :].astype(bf16)


def last_grads_kernel(place_ref, first_ref, mixed_ref, attended_ref, branch_ref, out_ref, held_ref):
    shard = first_ref.shape[1] // 8
    slots = mixed_ref.shape[1]
    size, starts = windows(shard, 8)
    held_ref[...] = dot_rows(first_ref[...], mixed_ref[...])
    for y in range(4):
        for zh in range(2):
            base = (2 * y + zh) * shard
            for i, start in enumerate(starts):
                rows = slice(y % 2 * size, (y % 2 + 1) * size)
                lanes = slice(y // 2 * slots, (y // 2 + 1) * slots)
                block = held_ref[base + start : base + start + size, :]
                out_ref[2 * i + zh, rows, lanes] = block.astype(bf16)
    size_out, starts_out = windows(shard, 16)
    grad = dot_rows(attended_ref[...], branch_ref[...])
    rest = jnp.zeros((2 * size, out_ref.shape[2] - 2 * slots), bf16)
    for i, start in enumerate(starts_out):
        out_ref[i, : 2 * size, 2 * slots :] = rest
        out_ref[i, 2 * size :, :] = grad[start : start + size_out].astype(bf16)


def last_sum_kernel(parts_ref, qkv_ref, out_ref):
    size, slots = qkv_ref.shape[1:]
    total = parts_ref[0].astype(f32)
    for i in range(1, 16):
        total = total + parts_ref[i].astype(f32)
    total = total.astype(bf16)
    for y in range(4):
        rows = slice(y % 2 * size, (y % 2 + 1) * size)
        qkv_ref[y] = total[rows, y // 2 * slots : (y // 2 + 1) * slots]
    out_ref[...] = total[2 * size :, :]


def fold_kernel(which, place_ref, *refs):
    for k in range(4):
        at = lax.rem(place_ref[which] + 4 - k, 4)
        total = refs[0][at].astype(f32)
        for j in range(1, 4):
            total = total + refs[j][at].astype(f32)
        refs[4 + k][...] = total.astype(bf16)


def stack_kernel(*refs):
    for k, ref in enumerate(refs[:-1]):
        refs[-1][k] = ref[...]


def column_ring_total_kernel(spans, place_ref, *refs):
    out_ref = refs[8]
    shard = out_ref.shape[0]
    _, starts = windows(shard, 8)
    step = starts[1]
    for j in range(4):
        x = lax.rem(place_ref[X] + j, 4)
        for flip in range(2):
            window = (place_ref[ZL] if flip == 0 else 1 - place_ref[ZL]) * 4 + x
            at = pl.multiple_of(window * step, 8)
            for rank in range(8):
                k = lax.rem(rank // 2 + 4 - place_ref[Y], 4)
                block = jnp.where(
                    place_ref[C] == rank % 2, refs[j][flip, k], refs[4 + j][flip, k]
                ).astype(f32)
                for source, target, wide in spans[rank]:
                    out_ref[pl.ds(at, step), target : target + wide] = block[
                        :step, source : source + wide
                    ]

                @pl.when(window == 7)
                def _(block=block, rank=rank):
                    for source, target, wide in spans[rank]:
                        out_ref[7 * step + step :, target : target + wide] = block[
                            step:, source : source + wide
                        ]


def column_total_kernel(spans, place_ref, own_ref, other_ref, out_ref):
    _, starts = windows(out_ref.shape[0], 8)
    ends = starts[1:] + [out_ref.shape[0]]
    for rank in range(8):
        y = rank // 2
        mine = place_ref[C] == rank % 2
        rows = [
            jnp.where(mine, own_ref[i, y], other_ref[i, y]).astype(f32)[: end - start]
            for i, (start, end) in enumerate(zip(starts, ends))
        ]
        block = jnp.concatenate(rows, axis=0)
        for source, target, wide in spans[rank]:
            out_ref[:, target : target + wide] = block[:, source : source + wide]


def proj_total_kernel(place_ref, own_ref, other_ref, out_ref):
    tiles = out_ref.shape[0] // 8
    small = tiles // 16 * 8
    for part, ref in enumerate((own_ref, other_ref)):
        zl = place_ref[C] if part == 0 else 1 - place_ref[C]
        for x in range(4):
            for i in range(2):
                zh = place_ref[ZL] if i == 0 else 1 - place_ref[ZL]
                window = (zl * 4 + x) * 2 + zh
                start = lax.div(tiles * window, 16)
                wide = lax.div(tiles * (window + 1), 16) - start > small // 8
                at = pl.multiple_of(start * 8, 8)
                block = ref[x, i].astype(f32)
                out_ref[pl.ds(at, small), :] = block[:small]

                @pl.when(wide)
                def _(at=at, block=block):
                    out_ref[pl.ds(pl.multiple_of(at + small, 8), 8), :] = block[small:]


def row_total_kernel(place_ref, own_ref, other_ref, out_ref):
    mine = place_ref[MINE]
    _, starts = windows(out_ref.shape[0], 16)
    ends = starts[1:] + [out_ref.shape[0]]
    for i, (start, end) in enumerate(zip(starts, ends)):
        block = jnp.where(mine == 1, own_ref[i], other_ref[i])
        out_ref[start:end, :] = block[: end - start].astype(f32)


def attend_kernel(place_ref, tokens_ref, norm_ref, bias_ref, *refs):
    pieces, (first_ref, qkv_ref, out_ref, top_ref, cols_ref) = refs[:8], refs[8:]
    length = tokens_ref.shape[0]
    shard = cols_ref.shape[1]
    zh = place_ref[ZH]
    for k in range(4):
        y = lax.rem(place_ref[Y] + k, 4)
        cols_ref[2 * y + zh] = pieces[k][...]
        cols_ref[2 * y + 1 - zh] = pieces[4 + k][...]
    gain = norm_ref[0:1, :]
    shift = norm_ref[1:2, :]
    for block in range(length // BLOCK):
        rows = slice(block * BLOCK, (block + 1) * BLOCK)
        first = norm_parts(tokens_ref[rows, :].astype(f32), gain, shift)[0].astype(bf16)
        first_ref[rows, :] = first
        mixed = bias_ref[...]
        for g in range(8):
            mixed = mixed + dot(first[:, g * shard : (g + 1) * shard], cols_ref[g])
        qkv_ref[rows, :] = mixed.astype(bf16)
    for head in range(SLOTS):
        lanes = slice(head * HEAD_DIM, (head + 1) * HEAD_DIM)
        keys = qkv_ref[:, SLOT_WIDTH + head * HEAD_DIM : SLOT_WIDTH + (head + 1) * HEAD_DIM]
        values = qkv_ref[
            :, 2 * SLOT_WIDTH + head * HEAD_DIM : 2 * SLOT_WIDTH + (head + 1) * HEAD_DIM
        ]
        for block in range(length // BLOCK):
            rows = slice(block * BLOCK, (block + 1) * BLOCK)
            width = (block + 1) * BLOCK
            query = qkv_ref[rows, lanes] * bf16(1.0 / math.sqrt(HEAD_DIM))
            scores = dot_cols(query, keys[:width])
            row = lax.broadcasted_iota(jnp.int32, (BLOCK, width), 0) + block * BLOCK
            col = lax.broadcasted_iota(jnp.int32, (BLOCK, width), 1)
            scores = jnp.where(col <= row, scores, -1e30)
            top = jnp.max(scores, axis=-1, keepdims=True)
            probs = jnp.exp(scores - top)
            total = jnp.sum(probs, axis=-1, keepdims=True)
            mixed = dot(probs.astype(bf16), values[:width])
            out_ref[rows, lanes] = (mixed / total).astype(bf16)
            top_ref[rows, head : head + 1] = top + jnp.log(total)


def hidden_kernel(
    place_ref, second_ref, cols_ref, bias_ref, grad_ref, active_ref, hidden_ref, sums_ref, out_ref
):
    length = second_ref.shape[0]
    sums = jnp.zeros(sums_ref.shape, f32)
    for block in range(length // BLOCK):
        rows = slice(block * BLOCK, (block + 1) * BLOCK)
        pre = dot(second_ref[rows, :], cols_ref[...]) + bias_ref[...]
        square = pre * pre
        bent = jnp.tanh(0.7978845608028654 * (pre + 0.044715 * square * pre))
        half = 0.5 * (1.0 + bent)
        active_ref[rows, :] = (pre * half).astype(bf16)
        slope = half + 0.5 * pre * (1.0 - bent * bent) * (
            0.7978845608028654 + (3.0 * 0.044715 * 0.7978845608028654) * square
        )
        grad = (grad_ref[rows, :] * slope).astype(bf16)
        hidden_ref[rows, :] = grad
        sums = sums + jnp.sum(grad.astype(f32), axis=0, keepdims=True)
        out_ref[rows, :] = dot_cols(grad, cols_ref[...]).astype(bf16)
    sums_ref[...] = sums


def down_kernel(active_ref, rows_ref, out_ref):
    for block in range(active_ref.shape[0] // BLOCK):
        rows = slice(block * BLOCK, (block + 1) * BLOCK)
        out_ref[rows, :] = dot(active_ref[rows, :], rows_ref[...]).astype(bf16)


def attend_back_kernel(
    place_ref,
    qkv_ref,
    grad_ref,
    out_ref,
    top_ref,
    cols_ref,
    down_ref,
    mixed_ref,
    parts_ref,
    sums_ref,
    query_ref,
):
    length = qkv_ref.shape[0]
    scale = 1.0 / math.sqrt(HEAD_DIM)
    ones = jnp.ones((8, HEAD_DIM), bf16)
    for head in range(SLOTS):
        base = head * HEAD_DIM
        lanes = slice(base, base + HEAD_DIM)
        key_lanes = slice(SLOT_WIDTH + base, SLOT_WIDTH + base + HEAD_DIM)
        value_lanes = slice(2 * SLOT_WIDTH + base, 2 * SLOT_WIDTH + base + HEAD_DIM)
        query = qkv_ref[:, lanes] * bf16(scale)
        grad = grad_ref[:, lanes]
        if head == SLOTS - 1:
            grad = jnp.where(place_ref[RANK] == 7, grad, jnp.zeros_like(grad))
        top = top_ref[head : head + 1, :]
        delta = dot_cols(ones, grad * out_ref[:, lanes])[0:1, :]
        for block in range(length // BLOCK):
            start = block * BLOCK
            rows = slice(start, start + BLOCK)
            width = length - start
            keys = qkv_ref[rows, key_lanes]
            values = qkv_ref[rows, value_lanes]
            scores = dot_cols(keys, query[start:])
            row = lax.broadcasted_iota(jnp.int32, (BLOCK, width), 0)
            col = lax.broadcasted_iota(jnp.int32, (BLOCK, width), 1)
            probs = jnp.where(row <= col, jnp.exp(scores - top[:, start:]), 0.0)
            grad_probs = dot_cols(values, grad[start:])
            grad_scores = (probs * (grad_probs - delta[:, start:])).astype(bf16)
            mixed_ref[rows, value_lanes] = dot(probs.astype(bf16), grad[start:]).astype(bf16)
            mixed_ref[rows, key_lanes] = dot(grad_scores, query[start:]).astype(bf16)
            term = dot_rows(grad_scores, keys)
            if block == 0:
                query_ref[...] = term
            else:
                query_ref[start:, :] += term
        mixed_ref[:, lanes] = (query_ref[...] * scale).astype(bf16)
    sums = jnp.zeros(sums_ref.shape, f32)
    for block in range(length // BLOCK):
        rows = slice(block * BLOCK, (block + 1) * BLOCK)
        mixed = mixed_ref[rows, :]
        sums = sums + jnp.sum(mixed.astype(f32), axis=0, keepdims=True)
        first = dot_cols(mixed, cols_ref[...]).astype(bf16)
        for half in range(2):
            rank = 2 * block + half
            parts_ref[rank, 0] = first[half * BLOCK // 2 : (half + 1) * BLOCK // 2]
            parts_ref[rank, 1] = down_ref[rank]
    sums_ref[...] = sums


def input_back_kernel(
    parts_ref, tokens_ref, middle_ref, grad_ref, norm_ref, out_ref, sums_ref
):
    gain = norm_ref[0:1, :]
    _, normed, factor = norm_parts(tokens_ref[...].astype(f32), gain, gain)
    grad = parts_ref[0].astype(f32)
    out_ref[0] = (grad_ref[...] + norm_back(grad, normed, factor, gain)).astype(bf16)
    down = parts_ref[1].astype(f32) + norm_ref[7:8, :]
    out_ref[1] = (middle_ref[...] + down).astype(bf16)
    sums_ref[0:1, :] = jnp.sum(grad * normed, axis=0, keepdims=True)
    sums_ref[1:2, :] = jnp.sum(grad, axis=0, keepdims=True)


def after(value, *others):
    return lax.optimization_barrier((value,) + others)[0]


def per_device(
    tokens,
    ln1_gain,
    ln1_bias,
    w_qkv,
    bias_q,
    bias_v,
    w_out,
    bias_out,
    ln2_gain,
    ln2_bias,
    w_fc,
    bias_fc,
    w_proj,
    bias_proj,
    cotangent,
):
    _, span, width = tokens.shape
    shard = width // 8
    hidden = w_fc.shape[1] // 8
    length = span * 8
    slots = 3 * SLOT_WIDTH
    x, zl, c, y, zh = [lax.axis_index(name) for name, _ in LAYOUT]
    rank = y * 2 + c
    place = jnp.stack(
        [y, c, rank, zh, zh * 2 + zl, x, zl, (c == zh).astype(jnp.int32)]
    ).astype(jnp.int32)

    stays = c == zh
    own_tokens = swap_roles(tokens.reshape(span, width))
    qkv_parts = call(
        qkv_columns_kernel,
        "qkv_columns",
        [struct((shard, slots), bf16)] * 4,
        place,
        w_qkv,
        scratch=[pltpu.VMEM((4, shard, slots), bf16)],
    )
    all_tokens = gather(after(own_tokens, qkv_parts[0]), TEAM).reshape(length, width)
    qkv_own = ring_all(qkv_parts, "y")
    qkv_other = [flipped(part, "zh") for part in qkv_own]
    out_rows = swap_roles(after(w_out, *qkv_own))
    small = jnp.concatenate(
        [ln1_gain, ln1_bias, bias_q, bias_v, bias_out, ln2_gain, ln2_bias, bias_proj, bias_fc]
    ).reshape(3, hidden)
    small_all = exchange(
        after(jnp.broadcast_to(small, (8, 3, hidden)), qkv_own[1]), GRP
    )
    place = after(place, small_all)
    fc_parts = call(
        fc_columns_kernel,
        "fc_columns",
        [struct((shard, hidden), bf16)] * 4,
        place,
        w_fc,
        scratch=[pltpu.VMEM((4, shard, hidden), bf16)],
    )
    own_cot = swap_roles(after(cotangent, *qkv_other).reshape(span, width))

    small_all = small_all.astype(f32)
    hidden_bias = lax.dynamic_index_in_dim(small_all, rank, 0, keepdims=False)[2:3]
    vectors = small_all[:, :2].reshape(8, 8, shard).transpose(1, 0, 2).reshape(8, width)
    bias_slots = jnp.concatenate(
        [
            lax.dynamic_slice_in_dim(vectors[2], STRIDE * rank, SLOT_WIDTH),
            jnp.zeros((SLOT_WIDTH,), f32),
            lax.dynamic_slice_in_dim(vectors[3], STRIDE * rank, SLOT_WIDTH),
        ]
    ).reshape(1, slots)

    out_all = gather(out_rows, TEAM).reshape(width, width)
    all_cot = gather(after(own_cot, out_rows), TEAM).reshape(length, width)
    proj_came = lax.ppermute(after(w_proj, *qkv_other), ("c", "zh"), ROLES[1:3])
    proj_rows = jnp.where(stays, w_proj, proj_came)
    fc_own = ring_all([after(part, *qkv_other) for part in fc_parts], "y")

    first, qkv, attended_slots, top, qkv_cols = call(
        attend_kernel,
        "attend",
        (
            struct((length, width), bf16),
            struct((length, slots), bf16),
            struct((length, SLOT_WIDTH), bf16),
            struct((length, SLOTS), f32),
            struct((8, shard, slots), bf16),
        ),
        after(place, bias_slots),
        all_tokens,
        vectors,
        bias_slots,
        *qkv_own,
        *qkv_other,
        flops=2 * length * width * slots,
    )
    qkv_cols = qkv_cols.reshape(width, slots)
    fc_other = [flipped(part, "zh") for part in fc_own]
    attended = exchange(
        after(attended_slots, *fc_own).reshape(8, span, SLOT_WIDTH), TEAM
    )
    middle, second, attended_parts = call(
        branch_kernel,
        "branch",
        (
            struct((span, width), f32),
            struct((span, width), bf16),
            struct((8, span, shard), bf16),
        ),
        after(attended, proj_came),
        own_tokens,
        vectors,
        out_all,
        scratch=[pltpu.VMEM((span, width), bf16)],
        flops=2 * span * width * width,
    )

    second_all = gather(second, TEAM).reshape(length, width)
    attended_own = exchange(after(attended_parts, second), TEAM)
    grad_active = dot_cols(after(all_cot, second), proj_rows)
    fc_cols = call(
        fc_whole_kernel,
        "fc_whole",
        struct((8, shard, hidden), bf16),
        place,
        after(fc_own[0], grad_active),
        *fc_own[1:],
        *fc_other,
    ).reshape(width, hidden)
    active, grad_hidden, hidden_sums, second_parts = call(
        hidden_kernel,
        "hidden",
        (
            struct((length, hidden), bf16),
            struct((length, hidden), bf16),
            struct((1, hidden), f32),
            struct((length, width), bf16),
        ),
        after(place, attended_own),
        second_all,
        fc_cols,
        hidden_bias,
        grad_active,
        flops=4 * length * width * hidden,
    )
    grad_second = team_sum(second_parts)
    window = windows(shard, 8)[0]
    fc_grad = call(
        column_ring_kernel,
        "fc_grad",
        [struct((4, 4, window, hidden), bf16)] * 4,
        place,
        second_all,
        grad_hidden,
        scratch=[pltpu.VMEM((width, hidden), f32)],
        flops=2 * length * width * hidden,
    )
    fc_grad = ring_all(fc_grad, "x")
    row_window = windows(hidden, 16)[0]
    proj_grad = call(
        row_grad_kernel,
        "proj_grad",
        [struct((4, row_window, width), bf16)] * 4,
        after(place, fc_grad[0]),
        active,
        all_cot,
        scratch=[pltpu.VMEM((hidden, width), f32)],
        flops=2 * length * width * hidden,
    )
    down_parts = call(
        down_kernel,
        "down",
        struct((length, width), bf16),
        after(active, proj_grad[0]),
        proj_rows,
        light=True,
    )
    proj_near = [ring(proj_grad[k], Z_RING, k) for k in (1, 3)]
    proj_far = ring(after(proj_grad[2], *proj_near), Z_RING, 2)
    proj_grad = [proj_grad[0], proj_near[0], proj_far, proj_near[1]]

    grad_middle, grad_branch, grad_slots, branch_sums = call(
        branch_back_kernel,
        "branch_back",
        (
            struct((span, width), f32),
            struct((span, width), bf16),
            struct((8, span, SLOT_WIDTH), bf16),
            struct((4, width), f32),
        ),
        after(place, *fc_grad, *proj_near, down_parts),
        grad_second,
        middle,
        own_cot,
        vectors,
        out_all,
        scratch=[pltpu.VMEM((span, width), bf16)],
        light=True,
    )
    grad_heads = exchange(grad_slots, TEAM).reshape(length, SLOT_WIDTH)

    def fold(which, parts, name, *behind):
        parts = [after(parts[0], *behind)] + parts[1:]
        return call(
            functools.partial(fold_kernel, which),
            name,
            [struct(parts[0].shape[1:], bf16)] * 4,
            place,
            *parts,
            light=True,
        )

    fc_grad = ring_all(fold(Z, fc_grad, "fc_fold", grad_slots), Z_RING)
    branch_all = gather(grad_branch, TEAM).reshape(length, width)
    grad_mixed, last_parts, mixed_sums = call(
        attend_back_kernel,
        "attend_back",
        (
            struct((length, slots), bf16),
            struct((8, 2, span, width), bf16),
            struct((1, slots), f32),
        ),
        after(place, proj_far, *fc_grad),
        qkv,
        grad_heads,
        attended_slots,
        top.T,
        qkv_cols,
        down_parts.reshape(8, span, width),
        scratch=[pltpu.VMEM((length, HEAD_DIM), f32)],
        flops=20 * length * width * slots,
    )
    last = team_sum(last_parts.reshape(2 * length, width)).reshape(2, span, width)
    last_grads = call(
        last_grads_kernel,
        "last_grads",
        struct((16, 2 * window + windows(shard, 16)[0], width), bf16),
        place,
        first,
        grad_mixed,
        attended_own.reshape(length, shard),
        branch_all,
        scratch=[pltpu.VMEM((width, slots), f32)],
        flops=2 * length * width * (slots + shard),
    )
    place = after(place, last_grads)
    last_grads = exchange(last_grads, REPLICAS)
    fc_grad = ring_all(fold(Y, fc_grad, "fc_fold_last", grad_mixed), "y")
    proj_grad = ring_all(fold(X, proj_grad, "proj_fold", grad_mixed), "x")

    def stacked(parts, name):
        return call(
            stack_kernel, name, struct((len(parts),) + parts[0].shape, bf16), *parts
        )

    def row_total(whole, rows, name, *behind):
        whole = after(whole, *behind)
        return call(
            row_total_kernel, name, struct((rows, width), f32), place, whole, other_core(whole)
        )

    proj_sum = sum(part.astype(f32) for part in proj_grad)
    proj_sum = proj_sum.astype(bf16)
    qkv_sum, out_sum = call(
        last_sum_kernel,
        "last_sum",
        (struct((4, window, slots), bf16), struct((windows(shard, 16)[0], width), bf16)),
        after(last_grads, proj_sum, *fc_grad),
    )
    qkv_sum = exchange(after(qkv_sum, last), "y")
    qkv_whole = gather(qkv_sum, ("zl", "x"))
    proj_sum = after(proj_sum, qkv_sum)
    proj_both = [lax.ppermute(proj_sum, ("zl", "c", "zh"), owners) for owners in OWNERS]
    proj_pair = stacked(proj_both, "proj_both")
    fc_near = stacked([after(fc_grad[0], qkv_sum)] + fc_grad[1:], "fc_near")
    fc_both = stacked([fc_near, flipped(fc_near, "zl")], "fc_both")
    fc_pieces = ring_all([fc_both] * 4, "x")
    fc_pieces = fc_pieces + [other_core(part) for part in fc_pieces]
    results, first_sums = call(
        input_back_kernel,
        "input_back",
        (struct((2, span, width), bf16), struct((2, width), f32)),
        last,
        own_tokens,
        middle,
        grad_middle,
        after(vectors, qkv_sum, fc_both),
    )
    results_home = swap_roles(results)

    blank = jnp.zeros((1, width), f32)
    at = (0, STRIDE * rank)
    small_terms = jnp.concatenate(
        [
            first_sums,
            lax.dynamic_update_slice(blank, mixed_sums[:, :SLOT_WIDTH], at),
            lax.dynamic_update_slice(blank, mixed_sums[:, 2 * SLOT_WIDTH :], at),
            branch_sums,
        ]
    )
    hidden_term = lax.dynamic_update_slice(
        jnp.zeros((8, hidden), f32), hidden_sums, (rank, 0)
    )
    small_terms = small_terms.reshape(8, 8, shard).transpose(1, 0, 2).reshape(8, 2, hidden)
    small_terms = jnp.concatenate([small_terms, hidden_term[:, None]], axis=1)
    small_sum = jnp.sum(exchange(after(small_terms, qkv_sum), GRP), axis=0)
    out_whole = exchange(
        after(jnp.broadcast_to(out_sum, (16,) + out_sum.shape), small_sum, *fc_pieces[:4]),
        REPLICAS,
    )
    small_last = jnp.broadcast_to(after(small_sum, out_whole), (16, 3, hidden))
    small_last = jnp.sum(exchange(small_last, REP), axis=0)
    owned = small_last[:2].reshape(8, shard)

    qkv_spans = [
        [
            (p * SLOT_WIDTH, p * width + STRIDE * r, STRIDE if r < 7 else SLOT_WIDTH)
            for p in range(3)
        ]
        for r in range(8)
    ]
    qkv_whole = after(qkv_whole, small_sum, *fc_pieces[:4])
    proj_whole = after(gather(after(proj_pair, qkv_whole), "x"), small_last)
    proj_total = call(
        proj_total_kernel,
        "proj_total",
        struct((hidden, width), f32),
        after(place, small_sum),
        proj_whole,
        other_core(proj_whole),
    )
    qkv_total = call(
        functools.partial(column_total_kernel, qkv_spans),
        "qkv_total",
        struct((shard, 3 * width), f32),
        after(place, results, small_last),
        qkv_whole,
        other_core(qkv_whole),
    )
    out_total = row_total(out_whole, shard, "out_total")
    fc_spans = [[(0, rank * hidden, hidden)] for rank in range(8)]
    fc_total = call(
        functools.partial(column_ring_total_kernel, fc_spans),
        "fc_total",
        struct((shard, 8 * hidden), f32),
        after(place, qkv_total, out_total, proj_total),
        *fc_pieces,
    )
    return (
        results_home[1].reshape(1, span, width),
        results_home[0].astype(f32).reshape(1, span, width),
        owned[0],
        owned[1],
        qkv_total,
        owned[2],
        owned[3],
        out_total,
        owned[4],
        owned[5],
        owned[6],
        fc_total,
        small_last[2],
        proj_total,
        owned[7],
    )


def solution(mesh):
    names = tuple(name for name, _ in LAYOUT)
    fine = jax.sharding.Mesh(mesh.devices.reshape([size for _, size in LAYOUT]), names)
    in_specs = (
        P(REP, GRP, None),
        P(GRP),
        P(GRP),
        P(GRP, None),
        P(GRP),
        P(GRP),
        P(GRP, None),
        P(GRP),
        P(GRP),
        P(GRP),
        P(GRP, None),
        P(GRP),
        P(GRP, None),
        P(GRP),
        P(REP, GRP, None),
    )
    out_specs = (
        P(REP, GRP, None),
        P(REP, GRP, None),
        P(GRP),
        P(GRP),
        P(GRP, None),
        P(GRP),
        P(GRP),
        P(GRP, None),
        P(GRP),
        P(GRP),
        P(GRP),
        P(GRP, None),
        P(GRP),
        P(GRP, None),
        P(GRP),
    )
    return jax.shard_map(
        per_device, mesh=fine, in_specs=in_specs, out_specs=out_specs, check_vma=False
    )
```

```python
import functools
import math

import jax
import jax.numpy as jnp
from jax import lax
from jax.experimental import pallas as pl
from jax.experimental.pallas import tpu as pltpu
from jax.sharding import PartitionSpec as P

HEADS = 25
HEAD_DIM = 64
SLOTS = 4
SLOT_WIDTH = SLOTS * HEAD_DIM
STRIDE = 3 * HEAD_DIM
BLOCK = 256

bf16 = jnp.bfloat16
f32 = jnp.float32


LAYOUT = (("x", 4), ("zl", 2), ("c", 2), ("y", 4), ("zh", 2))
REP = ("x", "zl", "c")
GRP = ("y", "zh")
TEAM = ("y", "c")
REPLICAS = ("zl", "x", "zh")
Z_RING = ("zl", "zh")
Z_PLACES = (0, 2, 1, 3)
ROLES = [(0, 0), (1, 2), (2, 1), (3, 3)]
OWNERS = [
    [(l * 4 + k * 2 + h, (h ^ i) * 4 + l * 2 + k) for l in range(2) for k in range(2) for h in range(2)]
    for i in range(2)
]


def ring(value, axis, step):
    index = Z_PLACES if axis == Z_RING else range(4)
    return lax.ppermute(value, axis, [(index[(i + step) % 4], index[i]) for i in range(4)])


def ring_all(values, axis):
    return [values[0]] + [ring(values[k], axis, k) for k in range(1, 4)]


def flipped(value, axis):
    return lax.ppermute(value, axis, [(0, 1), (1, 0)])


def swap_roles(value):
    return lax.ppermute(value, ("c", "zh"), ROLES)


def swap_selected(value, stays):
    return jnp.where(stays, value, lax.ppermute(value, ("c", "zh"), ROLES[1:3]))


def other_core(value):
    return lax.ppermute(value, "c", [(0, 1), (1, 0)])


def exchange(parts, axes):
    return lax.all_to_all(parts, axes, 0, 0)


def gather(block, axes):
    return lax.all_gather(block, axes, axis=0)


def team_sum(parts):
    return lax.psum_scatter(parts.astype(bf16), TEAM, scatter_dimension=0, tiled=True)


def windows(rows, count):
    tiles = rows // 8
    starts = [tiles * i // count for i in range(count)]
    size = max(b - a for a, b in zip(starts, starts[1:] + [tiles]))
    return size * 8, [8 * s for s in starts]


def joined(parts, starts, rows, axis):
    ends = starts[1:] + [rows]
    return jnp.concatenate(
        [lax.slice_in_dim(p, 0, e - s, axis=axis) for p, s, e in zip(parts, starts, ends)], axis
    )


def norm_parts(value, gain, shift):
    center = value - jnp.mean(value, axis=-1, keepdims=True)
    spread = jnp.mean(center * center, axis=-1, keepdims=True)
    factor = lax.rsqrt(spread + 1e-05)
    normed = center * factor
    return (normed * gain + shift, normed, factor)


def norm_back(grad_value, normed, factor, gain):
    grad_normed = grad_value * gain
    mean_first = jnp.mean(grad_normed, axis=-1, keepdims=True)
    mean_second = jnp.mean(grad_normed * normed, axis=-1, keepdims=True)
    return factor * (grad_normed - mean_first - normed * mean_second)


def dot(left, right):
    return jnp.dot(left, right, preferred_element_type=f32)


def dot_rows(left, right):
    return lax.dot_general(left, right, (((0,), (0,)), ((), ())), preferred_element_type=f32)


def dot_cols(left, right):
    return lax.dot_general(left, right, (((1,), (1,)), ((), ())), preferred_element_type=f32)


def call(kernel, name, out_shape, *operands, scratch=(), flops=0, light=False):
    specs = [
        pl.BlockSpec(memory_space=pltpu.SMEM if op.dtype == jnp.int32 else pltpu.VMEM)
        for op in operands
    ]
    out_specs = jax.tree.map(lambda _: pl.BlockSpec(memory_space=pltpu.VMEM), out_shape)
    moved = sum(op.size * op.dtype.itemsize for op in operands)
    moved += sum(o.size * o.dtype.itemsize for o in jax.tree.leaves(out_shape))
    return pl.pallas_call(
        kernel,
        out_shape=out_shape,
        in_specs=specs,
        out_specs=out_specs,
        scratch_shapes=list(scratch),
        compiler_params=pltpu.CompilerParams(vmem_limit_bytes=56 * 2**20),
        cost_estimate=pl.CostEstimate(
            flops=1 if light else int(flops),
            bytes_accessed=1 if light else int(moved),
            transcendentals=0,
        ),
        name=name,
    )(*operands)


def struct(shape, dtype):
    return jax.ShapeDtypeStruct(shape, dtype)


Y, C, RANK, ZH, Z, X, ZL, MINE = range(8)


def qkv_columns_kernel(place_ref, weight_ref, *refs):
    out_refs, held_ref = refs[:4], refs[4]
    c = place_ref[C]
    width = weight_ref.shape[1] // 3
    for part in range(3):
        lanes = slice(part * SLOT_WIDTH, (part + 1) * SLOT_WIDTH)
        for y in range(4):
            start = part * width + 2 * STRIDE * y
            even = weight_ref[:, start : start + SLOT_WIDTH]
            odd = weight_ref[:, start + STRIDE : start + STRIDE + SLOT_WIDTH]
            held_ref[y, :, lanes] = jnp.where(c == 0, even, odd)
    for k in range(4):
        out_refs[k][...] = held_ref[lax.rem(place_ref[Y] + 4 - k, 4)]


def fc_columns_kernel(place_ref, weight_ref, *refs):
    out_refs, held_ref = refs[:4], refs[4]
    c = place_ref[C]
    hidden = weight_ref.shape[1] // 8
    for y in range(4):
        start = 2 * hidden * y
        even = weight_ref[:, start : start + hidden]
        odd = weight_ref[:, start + hidden : start + 2 * hidden]
        held_ref[y] = jnp.where(c == 0, even, odd)
    for k in range(4):
        out_refs[k][...] = held_ref[lax.rem(place_ref[Y] + 4 - k, 4)]


def fc_whole_kernel(place_ref, *refs):
    out_ref = refs[8]
    zh = place_ref[ZH]
    for k in range(4):
        y = lax.rem(place_ref[Y] + k, 4)
        out_ref[2 * y + zh] = refs[k][...]
        out_ref[2 * y + 1 - zh] = refs[4 + k][...]


def branch_kernel(
    slots_ref, tokens_ref, norm_ref, rows_ref, middle_ref, second_ref, parts_ref, flat_ref
):
    shard = parts_ref.shape[2]
    for rank in range(8):
        wide = STRIDE if rank < 7 else SLOT_WIDTH
        flat_ref[:, STRIDE * rank : STRIDE * rank + wide] = slots_ref[rank, :, :wide]
    for rank in range(8):
        parts_ref[rank] = flat_ref[:, shard * rank : shard * (rank + 1)]
    total = tokens_ref[...].astype(f32) + norm_ref[4:5, :] + dot(flat_ref[...], rows_ref[...])
    middle_ref[...] = total
    second_ref[...] = norm_parts(total, norm_ref[5:6, :], norm_ref[6:7, :])[0].astype(bf16)


def branch_back_kernel(
    place_ref,
    grad_ref,
    middle_ref,
    cot_ref,
    norm_ref,
    rows_ref,
    grad_middle_ref,
    branch_ref,
    slots_ref,
    sums_ref,
    flat_ref,
):
    gain = norm_ref[5:6, :]
    _, normed, factor = norm_parts(middle_ref[...], gain, gain)
    grad = grad_ref[...].astype(f32)
    cot = cot_ref[...].astype(f32)
    grad_middle = cot + norm_back(grad, normed, factor, gain)
    branch = grad_middle.astype(bf16)
    grad_middle_ref[...] = grad_middle
    branch_ref[...] = branch
    flat_ref[...] = dot_cols(branch, rows_ref[...]).astype(bf16)
    for rank in range(8):
        slots_ref[rank] = flat_ref[:, STRIDE * rank : STRIDE * rank + SLOT_WIDTH]
    sums_ref[0:1, :] = jnp.sum(branch.astype(f32), axis=0, keepdims=True)
    sums_ref[1:2, :] = jnp.sum(grad * normed, axis=0, keepdims=True)
    sums_ref[2:3, :] = jnp.sum(grad, axis=0, keepdims=True)
    sums_ref[3:4, :] = jnp.sum(cot, axis=0, keepdims=True)


def column_ring_kernel(place_ref, left_ref, right_ref, *refs):
    out_refs, held_ref = refs[:4], refs[4]
    shard = left_ref.shape[1] // 8
    size, starts = windows(shard, 8)
    held_ref[...] = dot_rows(left_ref[...], right_ref[...])
    for k in range(4):
        x = lax.rem(place_ref[X] + 4 - k, 4)
        for z in range(4):
            for y in range(4):
                base = (2 * y + z // 2) * shard + starts[4 * (z % 2)]
                at = pl.multiple_of(base + starts[1] * x, 8)
                out_refs[k][z, y] = held_ref[pl.ds(at, size), :].astype(bf16)


def row_grad_kernel(place_ref, left_ref, right_ref, *refs):
    out_refs, held_ref = refs[:4], refs[4]
    rows = left_ref.shape[1]
    size = windows(rows, 16)[0]
    held_ref[...] = dot_rows(left_ref[...], right_ref[...])
    for k in range(4):
        z = lax.rem(place_ref[Z] + 4 - k, 4)
        for x in range(4):
            window = (lax.rem(z, 2) * 4 + x) * 2 + lax.div(z, 2)
            at = pl.multiple_of(lax.div(rows // 8 * window, 16) * 8, 8)
            out_refs[k][x] = held_ref[pl.ds(at, size), :].astype(bf16)


def last_grads_kernel(place_ref, first_ref, mixed_ref, attended_ref, branch_ref, out_ref, held_ref):
    shard = first_ref.shape[1] // 8
    slots = mixed_ref.shape[1]
    size, starts = windows(shard, 8)
    held_ref[...] = dot_rows(first_ref[...], mixed_ref[...])
    for y in range(4):
        for zh in range(2):
            base = (2 * y + zh) * shard
            for i, start in enumerate(starts):
                rows = slice(y % 2 * size, (y % 2 + 1) * size)
                lanes = slice(y // 2 * slots, (y // 2 + 1) * slots)
                block = held_ref[base + start : base + start + size, :]
                out_ref[2 * i + zh, rows, lanes] = block.astype(bf16)
    size_out, starts_out = windows(shard, 16)
    grad = dot_rows(attended_ref[...], branch_ref[...])
    rest = jnp.zeros((2 * size, out_ref.shape[2] - 2 * slots), bf16)
    for i, start in enumerate(starts_out):
        out_ref[i, : 2 * size, 2 * slots :] = rest
        out_ref[i, 2 * size :, :] = grad[start : start + size_out].astype(bf16)


def last_sum_kernel(parts_ref, qkv_ref, out_ref):
    size, slots = qkv_ref.shape[1:]
    total = parts_ref[0].astype(f32)
    for i in range(1, 16):
        total = total + parts_ref[i].astype(f32)
    total = total.astype(bf16)
    for y in range(4):
        rows = slice(y % 2 * size, (y % 2 + 1) * size)
        qkv_ref[y] = total[rows, y // 2 * slots : (y // 2 + 1) * slots]
    out_ref[...] = total[2 * size :, :]


def fold_kernel(which, place_ref, *refs):
    for k in range(4):
        at = lax.rem(place_ref[which] + 4 - k, 4)
        total = refs[0][at].astype(f32)
        for j in range(1, 4):
            total = total + refs[j][at].astype(f32)
        refs[4 + k][...] = total.astype(bf16)


def stack_kernel(*refs):
    for k, ref in enumerate(refs[:-1]):
        refs[-1][k] = ref[...]


def column_ring_total_kernel(spans, place_ref, *refs):
    out_ref = refs[8]
    shard = out_ref.shape[0]
    _, starts = windows(shard, 8)
    step = starts[1]
    for j in range(4):
        x = lax.rem(place_ref[X] + j, 4)
        for flip in range(2):
            window = (place_ref[ZL] if flip == 0 else 1 - place_ref[ZL]) * 4 + x
            at = pl.multiple_of(window * step, 8)
            for rank in range(8):
                k = lax.rem(rank // 2 + 4 - place_ref[Y], 4)
                block = jnp.where(
                    place_ref[C] == rank % 2, refs[j][flip, k], refs[4 + j][flip, k]
                ).astype(f32)
                for source, target, wide in spans[rank]:
                    out_ref[pl.ds(at, step), target : target + wide] = block[
                        :step, source : source + wide
                    ]

                @pl.when(window == 7)
                def _(block=block, rank=rank):
                    for source, target, wide in spans[rank]:
                        out_ref[7 * step + step :, target : target + wide] = block[
                            step:, source : source + wide
                        ]


def column_total_kernel(spans, place_ref, own_ref, other_ref, out_ref):
    _, starts = windows(out_ref.shape[0], 8)
    ends = starts[1:] + [out_ref.shape[0]]
    for rank in range(8):
        y = rank // 2
        mine = place_ref[C] == rank % 2
        rows = [
            jnp.where(mine, own_ref[i, y], other_ref[i, y]).astype(f32)[: end - start]
            for i, (start, end) in enumerate(zip(starts, ends))
        ]
        block = jnp.concatenate(rows, axis=0)
        for source, target, wide in spans[rank]:
            out_ref[:, target : target + wide] = block[:, source : source + wide]


def proj_total_kernel(place_ref, own_ref, other_ref, out_ref):
    tiles = out_ref.shape[0] // 8
    small = tiles // 16 * 8
    for part, ref in enumerate((own_ref, other_ref)):
        zl = place_ref[C] if part == 0 else 1 - place_ref[C]
        for x in range(4):
            for i in range(2):
                zh = place_ref[ZL] if i == 0 else 1 - place_ref[ZL]
                window = (zl * 4 + x) * 2 + zh
                start = lax.div(tiles * window, 16)
                wide = lax.div(tiles * (window + 1), 16) - start > small // 8
                at = pl.multiple_of(start * 8, 8)
                block = ref[x, i].astype(f32)
                out_ref[pl.ds(at, small), :] = block[:small]

                @pl.when(wide)
                def _(at=at, block=block):
                    out_ref[pl.ds(pl.multiple_of(at + small, 8), 8), :] = block[small:]


def row_total_kernel(place_ref, own_ref, other_ref, out_ref):
    mine = place_ref[MINE]
    _, starts = windows(out_ref.shape[0], 16)
    ends = starts[1:] + [out_ref.shape[0]]
    for i, (start, end) in enumerate(zip(starts, ends)):
        block = jnp.where(mine == 1, own_ref[i], other_ref[i])
        out_ref[start:end, :] = block[: end - start].astype(f32)


def attend_kernel(place_ref, tokens_ref, norm_ref, bias_ref, *refs):
    pieces, (first_ref, qkv_ref, out_ref, top_ref, cols_ref) = refs[:8], refs[8:]
    length = tokens_ref.shape[0]
    shard = cols_ref.shape[1]
    zh = place_ref[ZH]
    for k in range(4):
        y = lax.rem(place_ref[Y] + k, 4)
        cols_ref[2 * y + zh] = pieces[k][...]
        cols_ref[2 * y + 1 - zh] = pieces[4 + k][...]
    gain = norm_ref[0:1, :]
    shift = norm_ref[1:2, :]
    for block in range(length // BLOCK):
        rows = slice(block * BLOCK, (block + 1) * BLOCK)
        first = norm_parts(tokens_ref[rows, :].astype(f32), gain, shift)[0].astype(bf16)
        first_ref[rows, :] = first
        mixed = bias_ref[...]
        for g in range(8):
            mixed = mixed + dot(first[:, g * shard : (g + 1) * shard], cols_ref[g])
        qkv_ref[rows, :] = mixed.astype(bf16)
    for head in range(SLOTS):
        lanes = slice(head * HEAD_DIM, (head + 1) * HEAD_DIM)
        keys = qkv_ref[:, SLOT_WIDTH + head * HEAD_DIM : SLOT_WIDTH + (head + 1) * HEAD_DIM]
        values = qkv_ref[
            :, 2 * SLOT_WIDTH + head * HEAD_DIM : 2 * SLOT_WIDTH + (head + 1) * HEAD_DIM
        ]
        for block in range(length // BLOCK):
            rows = slice(block * BLOCK, (block + 1) * BLOCK)
            width = (block + 1) * BLOCK
            query = qkv_ref[rows, lanes] * bf16(1.0 / math.sqrt(HEAD_DIM))
            scores = dot_cols(query, keys[:width])
            row = lax.broadcasted_iota(jnp.int32, (BLOCK, width), 0) + block * BLOCK
            col = lax.broadcasted_iota(jnp.int32, (BLOCK, width), 1)
            scores = jnp.where(col <= row, scores, -1e30)
            top = jnp.max(scores, axis=-1, keepdims=True)
            probs = jnp.exp(scores - top)
            total = jnp.sum(probs, axis=-1, keepdims=True)
            mixed = dot(probs.astype(bf16), values[:width])
            out_ref[rows, lanes] = (mixed / total).astype(bf16)
            top_ref[rows, head : head + 1] = top + jnp.log(total)


def hidden_kernel(
    place_ref, second_ref, cols_ref, bias_ref, grad_ref, active_ref, hidden_ref, sums_ref, out_ref
):
    length = second_ref.shape[0]
    sums = jnp.zeros(sums_ref.shape, f32)
    for block in range(length // BLOCK):
        rows = slice(block * BLOCK, (block + 1) * BLOCK)
        pre = dot(second_ref[rows, :], cols_ref[...]) + bias_ref[...]
        square = pre * pre
        bent = jnp.tanh(0.7978845608028654 * (pre + 0.044715 * square * pre))
        half = 0.5 * (1.0 + bent)
        active_ref[rows, :] = (pre * half).astype(bf16)
        slope = half + 0.5 * pre * (1.0 - bent * bent) * (
            0.7978845608028654 + (3.0 * 0.044715 * 0.7978845608028654) * square
        )
        grad = (grad_ref[rows, :] * slope).astype(bf16)
        hidden_ref[rows, :] = grad
        sums = sums + jnp.sum(grad.astype(f32), axis=0, keepdims=True)
        out_ref[rows, :] = dot_cols(grad, cols_ref[...]).astype(bf16)
    sums_ref[...] = sums


def down_kernel(active_ref, rows_ref, out_ref):
    for block in range(active_ref.shape[0] // BLOCK):
        rows = slice(block * BLOCK, (block + 1) * BLOCK)
        out_ref[rows, :] = dot(active_ref[rows, :], rows_ref[...]).astype(bf16)


def attend_back_kernel(
    place_ref,
    qkv_ref,
    grad_ref,
    out_ref,
    top_ref,
    cols_ref,
    down_ref,
    mixed_ref,
    parts_ref,
    sums_ref,
    query_ref,
):
    length = qkv_ref.shape[0]
    scale = 1.0 / math.sqrt(HEAD_DIM)
    ones = jnp.ones((8, HEAD_DIM), bf16)
    for head in range(SLOTS):
        base = head * HEAD_DIM
        lanes = slice(base, base + HEAD_DIM)
        key_lanes = slice(SLOT_WIDTH + base, SLOT_WIDTH + base + HEAD_DIM)
        value_lanes = slice(2 * SLOT_WIDTH + base, 2 * SLOT_WIDTH + base + HEAD_DIM)
        query = qkv_ref[:, lanes] * bf16(scale)
        grad = grad_ref[:, lanes]
        if head == SLOTS - 1:
            grad = jnp.where(place_ref[RANK] == 7, grad, jnp.zeros_like(grad))
        top = top_ref[head : head + 1, :]
        delta = dot_cols(ones, grad * out_ref[:, lanes])[0:1, :]
        for block in range(length // BLOCK):
            start = block * BLOCK
            rows = slice(start, start + BLOCK)
            width = length - start
            keys = qkv_ref[rows, key_lanes]
            values = qkv_ref[rows, value_lanes]
            scores = dot_cols(keys, query[start:])
            row = lax.broadcasted_iota(jnp.int32, (BLOCK, width), 0)
            col = lax.broadcasted_iota(jnp.int32, (BLOCK, width), 1)
            probs = jnp.where(row <= col, jnp.exp(scores - top[:, start:]), 0.0)
            grad_probs = dot_cols(values, grad[start:])
            grad_scores = (probs * (grad_probs - delta[:, start:])).astype(bf16)
            mixed_ref[rows, value_lanes] = dot(probs.astype(bf16), grad[start:]).astype(bf16)
            mixed_ref[rows, key_lanes] = dot(grad_scores, query[start:]).astype(bf16)
            term = dot_rows(grad_scores, keys)
            if block == 0:
                query_ref[...] = term
            else:
                query_ref[start:, :] += term
        mixed_ref[:, lanes] = (query_ref[...] * scale).astype(bf16)
    sums = jnp.zeros(sums_ref.shape, f32)
    for block in range(length // BLOCK):
        rows = slice(block * BLOCK, (block + 1) * BLOCK)
        mixed = mixed_ref[rows, :]
        sums = sums + jnp.sum(mixed.astype(f32), axis=0, keepdims=True)
        first = dot_cols(mixed, cols_ref[...]).astype(bf16)
        for half in range(2):
            rank = 2 * block + half
            parts_ref[rank, 0] = first[half * BLOCK // 2 : (half + 1) * BLOCK // 2]
            parts_ref[rank, 1] = down_ref[rank]
    sums_ref[...] = sums


def input_back_kernel(
    parts_ref, tokens_ref, middle_ref, grad_ref, norm_ref, out_ref, sums_ref
):
    gain = norm_ref[0:1, :]
    _, normed, factor = norm_parts(tokens_ref[...].astype(f32), gain, gain)
    grad = parts_ref[0].astype(f32)
    out_ref[0] = (grad_ref[...] + norm_back(grad, normed, factor, gain)).astype(bf16)
    down = parts_ref[1].astype(f32) + norm_ref[7:8, :]
    out_ref[1] = (middle_ref[...] + down).astype(bf16)
    sums_ref[0:1, :] = jnp.sum(grad * normed, axis=0, keepdims=True)
    sums_ref[1:2, :] = jnp.sum(grad, axis=0, keepdims=True)


def after(value, *others):
    return lax.optimization_barrier((value,) + others)[0]


def per_device(
    tokens,
    ln1_gain,
    ln1_bias,
    w_qkv,
    bias_q,
    bias_v,
    w_out,
    bias_out,
    ln2_gain,
    ln2_bias,
    w_fc,
    bias_fc,
    w_proj,
    bias_proj,
    cotangent,
):
    _, span, width = tokens.shape
    shard = width // 8
    hidden = w_fc.shape[1] // 8
    length = span * 8
    slots = 3 * SLOT_WIDTH
    x, zl, c, y, zh = [lax.axis_index(name) for name, _ in LAYOUT]
    rank = y * 2 + c
    place = jnp.stack(
        [y, c, rank, zh, zh * 2 + zl, x, zl, (c == zh).astype(jnp.int32)]
    ).astype(jnp.int32)

    stays = c == zh
    own_tokens = swap_roles(tokens.reshape(span, width))
    qkv_parts = call(
        qkv_columns_kernel,
        "qkv_columns",
        [struct((shard, slots), bf16)] * 4,
        place,
        w_qkv,
        scratch=[pltpu.VMEM((4, shard, slots), bf16)],
    )
    all_tokens = gather(after(own_tokens, qkv_parts[0]), TEAM).reshape(length, width)
    qkv_own = ring_all(qkv_parts, "y")
    small = jnp.concatenate(
        [ln1_gain, ln1_bias, bias_q, bias_v, bias_out, ln2_gain, ln2_bias, bias_proj, bias_fc]
    ).reshape(3, hidden)
    small_all = exchange(
        after(jnp.broadcast_to(small, (8, 3, hidden)), qkv_parts[0]), GRP
    )
    qkv_other = [flipped(after(part, small_all), "zh") for part in qkv_own]
    out_rows = swap_roles(after(w_out, *qkv_own))
    place = after(place, small_all)
    fc_parts = call(
        fc_columns_kernel,
        "fc_columns",
        [struct((shard, hidden), bf16)] * 4,
        place,
        w_fc,
        scratch=[pltpu.VMEM((4, shard, hidden), bf16)],
    )
    own_cot = swap_roles(after(cotangent, *qkv_other).reshape(span, width))

    small_all = small_all.astype(f32)
    hidden_bias = lax.dynamic_index_in_dim(small_all, rank, 0, keepdims=False)[2:3]
    vectors = small_all[:, :2].reshape(8, 8, shard).transpose(1, 0, 2).reshape(8, width)
    bias_slots = jnp.concatenate(
        [
            lax.dynamic_slice_in_dim(vectors[2], STRIDE * rank, SLOT_WIDTH),
            jnp.zeros((SLOT_WIDTH,), f32),
            lax.dynamic_slice_in_dim(vectors[3], STRIDE * rank, SLOT_WIDTH),
        ]
    ).reshape(1, slots)

    out_all = gather(out_rows, TEAM).reshape(width, width)
    all_cot = gather(after(own_cot, out_rows), TEAM).reshape(length, width)
    proj_came = lax.ppermute(after(w_proj, *qkv_other), ("c", "zh"), ROLES[1:3])
    proj_rows = jnp.where(stays, w_proj, proj_came)
    fc_own = ring_all([after(part, *qkv_other) for part in fc_parts], "y")

    first, qkv, attended_slots, top, qkv_cols = call(
        attend_kernel,
        "attend",
        (
            struct((length, width), bf16),
            struct((length, slots), bf16),
            struct((length, SLOT_WIDTH), bf16),
            struct((length, SLOTS), f32),
            struct((8, shard, slots), bf16),
        ),
        after(place, bias_slots),
        all_tokens,
        vectors,
        bias_slots,
        *qkv_own,
        *qkv_other,
        flops=2 * length * width * slots,
    )
    qkv_cols = qkv_cols.reshape(width, slots)
    fc_other = [flipped(part, "zh") for part in fc_own]
    attended = exchange(
        after(attended_slots, *fc_own).reshape(8, span, SLOT_WIDTH), TEAM
    )
    middle, second, attended_parts = call(
        branch_kernel,
        "branch",
        (
            struct((span, width), f32),
            struct((span, width), bf16),
            struct((8, span, shard), bf16),
        ),
        after(attended, proj_came),
        own_tokens,
        vectors,
        out_all,
        scratch=[pltpu.VMEM((span, width), bf16)],
        flops=2 * span * width * width,
    )

    second_all = gather(second, TEAM).reshape(length, width)
    attended_own = exchange(after(attended_parts, second), TEAM)
    grad_active = dot_cols(after(all_cot, second), proj_rows)
    fc_cols = call(
        fc_whole_kernel,
        "fc_whole",
        struct((8, shard, hidden), bf16),
        place,
        after(fc_own[0], grad_active),
        *fc_own[1:],
        *fc_other,
    ).reshape(width, hidden)
    active, grad_hidden, hidden_sums, second_parts = call(
        hidden_kernel,
        "hidden",
        (
            struct((length, hidden), bf16),
            struct((length, hidden), bf16),
            struct((1, hidden), f32),
            struct((length, width), bf16),
        ),
        after(place, attended_own),
        second_all,
        fc_cols,
        hidden_bias,
        grad_active,
        flops=4 * length * width * hidden,
    )
    grad_second = team_sum(second_parts)
    window = windows(shard, 8)[0]
    fc_grad = call(
        column_ring_kernel,
        "fc_grad",
        [struct((4, 4, window, hidden), bf16)] * 4,
        place,
        second_all,
        grad_hidden,
        scratch=[pltpu.VMEM((width, hidden), f32)],
        flops=2 * length * width * hidden,
    )
    fc_grad = ring_all(fc_grad, "x")
    row_window = windows(hidden, 16)[0]
    proj_grad = call(
        row_grad_kernel,
        "proj_grad",
        [struct((4, row_window, width), bf16)] * 4,
        after(place, fc_grad[0]),
        active,
        all_cot,
        scratch=[pltpu.VMEM((hidden, width), f32)],
        flops=2 * length * width * hidden,
    )
    down_parts = call(
        down_kernel,
        "down",
        struct((length, width), bf16),
        after(active, proj_grad[0]),
        proj_rows,
        light=True,
    )
    proj_near = [ring(proj_grad[k], Z_RING, k) for k in (1, 3)]
    proj_far = ring(after(proj_grad[2], *proj_near), Z_RING, 2)
    proj_grad = [proj_grad[0], proj_near[0], proj_far, proj_near[1]]

    grad_middle, grad_branch, grad_slots, branch_sums = call(
        branch_back_kernel,
        "branch_back",
        (
            struct((span, width), f32),
            struct((span, width), bf16),
            struct((8, span, SLOT_WIDTH), bf16),
            struct((4, width), f32),
        ),
        after(place, *fc_grad, *proj_near, down_parts),
        grad_second,
        middle,
        own_cot,
        vectors,
        out_all,
        scratch=[pltpu.VMEM((span, width), bf16)],
        light=True,
    )
    grad_heads = exchange(grad_slots, TEAM).reshape(length, SLOT_WIDTH)

    def fold(which, parts, name, *behind):
        parts = [after(parts[0], *behind)] + parts[1:]
        return call(
            functools.partial(fold_kernel, which),
            name,
            [struct(parts[0].shape[1:], bf16)] * 4,
            place,
            *parts,
            light=True,
        )

    fc_grad = ring_all(fold(Z, fc_grad, "fc_fold", grad_slots), Z_RING)
    branch_all = gather(grad_branch, TEAM).reshape(length, width)
    grad_mixed, last_parts, mixed_sums = call(
        attend_back_kernel,
        "attend_back",
        (
            struct((length, slots), bf16),
            struct((8, 2, span, width), bf16),
            struct((1, slots), f32),
        ),
        after(place, proj_far, *fc_grad),
        qkv,
        grad_heads,
        attended_slots,
        top.T,
        qkv_cols,
        down_parts.reshape(8, span, width),
        scratch=[pltpu.VMEM((length, HEAD_DIM), f32)],
        flops=20 * length * width * slots,
    )
    last = team_sum(last_parts.reshape(2 * length, width)).reshape(2, span, width)
    fc_grad = ring_all(fold(Y, fc_grad, "fc_fold_last", grad_mixed), "y")
    proj_grad = ring_all(fold(X, proj_grad, "proj_fold", grad_mixed), "x")
    last_grads = call(
        last_grads_kernel,
        "last_grads",
        struct((16, 2 * window + windows(shard, 16)[0], width), bf16),
        place,
        after(first, fc_grad[0], proj_grad[0]),
        grad_mixed,
        attended_own.reshape(length, shard),
        branch_all,
        scratch=[pltpu.VMEM((width, slots), f32)],
        flops=2 * length * width * (slots + shard),
    )
    place = after(place, last_grads)
    last_grads = exchange(after(last_grads, *fc_grad, *proj_grad), REPLICAS)

    def stacked(parts, name):
        return call(
            stack_kernel, name, struct((len(parts),) + parts[0].shape, bf16), *parts
        )

    def row_total(whole, rows, name, *behind):
        whole = after(whole, *behind)
        return call(
            row_total_kernel, name, struct((rows, width), f32), place, whole, other_core(whole)
        )

    proj_sum = sum(part.astype(f32) for part in proj_grad)
    proj_sum = proj_sum.astype(bf16)
    qkv_sum, out_sum = call(
        last_sum_kernel,
        "last_sum",
        (struct((4, window, slots), bf16), struct((windows(shard, 16)[0], width), bf16)),
        last_grads,
    )
    qkv_sum = exchange(after(qkv_sum, last), "y")
    qkv_whole = gather(qkv_sum, ("zl", "x"))
    proj_sum = after(proj_sum, qkv_sum)
    proj_both = [lax.ppermute(proj_sum, ("zl", "c", "zh"), owners) for owners in OWNERS]
    proj_pair = stacked(proj_both, "proj_both")
    fc_near = stacked([after(fc_grad[0], qkv_sum)] + fc_grad[1:], "fc_near")
    fc_both = stacked([fc_near, flipped(fc_near, "zl")], "fc_both")
    fc_pieces = ring_all([fc_both] * 4, "x")
    fc_pieces = fc_pieces + [other_core(part) for part in fc_pieces]
    results, first_sums = call(
        input_back_kernel,
        "input_back",
        (struct((2, span, width), bf16), struct((2, width), f32)),
        last,
        own_tokens,
        middle,
        grad_middle,
        after(vectors, qkv_sum, fc_both),
    )
    results_home = swap_roles(results)

    blank = jnp.zeros((1, width), f32)
    at = (0, STRIDE * rank)
    small_terms = jnp.concatenate(
        [
            first_sums,
            lax.dynamic_update_slice(blank, mixed_sums[:, :SLOT_WIDTH], at),
            lax.dynamic_update_slice(blank, mixed_sums[:, 2 * SLOT_WIDTH :], at),
            branch_sums,
        ]
    )
    hidden_term = lax.dynamic_update_slice(
        jnp.zeros((8, hidden), f32), hidden_sums, (rank, 0)
    )
    small_terms = small_terms.reshape(8, 8, shard).transpose(1, 0, 2).reshape(8, 2, hidden)
    small_terms = jnp.concatenate([small_terms, hidden_term[:, None]], axis=1)
    small_sum = jnp.sum(exchange(after(small_terms, qkv_sum), GRP), axis=0)
    small_last = jnp.broadcast_to(small_sum, (16, 3, hidden))
    small_last = jnp.sum(exchange(small_last, REP), axis=0)
    out_whole = exchange(
        after(jnp.broadcast_to(out_sum, (16,) + out_sum.shape), small_last, *fc_pieces[:4]),
        REPLICAS,
    )
    owned = small_last[:2].reshape(8, shard)

    qkv_spans = [
        [
            (p * SLOT_WIDTH, p * width + STRIDE * r, STRIDE if r < 7 else SLOT_WIDTH)
            for p in range(3)
        ]
        for r in range(8)
    ]
    qkv_whole = after(qkv_whole, small_sum, *fc_pieces[:4])
    proj_whole = after(gather(after(proj_pair, qkv_whole), "x"), out_whole)
    fc_spans = [[(0, rank * hidden, hidden)] for rank in range(8)]
    fc_total = call(
        functools.partial(column_ring_total_kernel, fc_spans),
        "fc_total",
        struct((shard, 8 * hidden), f32),
        after(place, small_last),
        *fc_pieces,
    )
    proj_total = call(
        proj_total_kernel,
        "proj_total",
        struct((hidden, width), f32),
        after(place, fc_total),
        proj_whole,
        other_core(proj_whole),
    )
    qkv_total = call(
        functools.partial(column_total_kernel, qkv_spans),
        "qkv_total",
        struct((shard, 3 * width), f32),
        after(place, results, fc_total),
        qkv_whole,
        other_core(qkv_whole),
    )
    out_total = row_total(out_whole, shard, "out_total", fc_total)
    return (
        results_home[1].reshape(1, span, width),
        results_home[0].astype(f32).reshape(1, span, width),
        owned[0],
        owned[1],
        qkv_total,
        owned[2],
        owned[3],
        out_total,
        owned[4],
        owned[5],
        owned[6],
        fc_total,
        small_last[2],
        proj_total,
        owned[7],
    )


def solution(mesh):
    names = tuple(name for name, _ in LAYOUT)
    fine = jax.sharding.Mesh(mesh.devices.reshape([size for _, size in LAYOUT]), names)
    in_specs = (
        P(REP, GRP, None),
        P(GRP),
        P(GRP),
        P(GRP, None),
        P(GRP),
        P(GRP),
        P(GRP, None),
        P(GRP),
        P(GRP),
        P(GRP),
        P(GRP, None),
        P(GRP),
        P(GRP, None),
        P(GRP),
        P(REP, GRP, None),
    )
    out_specs = (
        P(REP, GRP, None),
        P(REP, GRP, None),
        P(GRP),
        P(GRP),
        P(GRP, None),
        P(GRP),
        P(GRP),
        P(GRP, None),
        P(GRP),
        P(GRP),
        P(GRP),
        P(GRP, None),
        P(GRP),
        P(GRP, None),
        P(GRP),
    )
    return jax.shard_map(
        per_device, mesh=fine, in_specs=in_specs, out_specs=out_specs, check_vma=False
    )
```

```python
import functools
import math

import jax
import jax.numpy as jnp
from jax import lax
from jax.experimental import pallas as pl
from jax.experimental.pallas import tpu as pltpu
from jax.sharding import PartitionSpec as P

HEADS = 25
HEAD_DIM = 64
SLOTS = 4
SLOT_WIDTH = SLOTS * HEAD_DIM
STRIDE = 3 * HEAD_DIM
BLOCK = 256

bf16 = jnp.bfloat16
f32 = jnp.float32


LAYOUT = (("x", 4), ("zl", 2), ("c", 2), ("y", 4), ("zh", 2))
REP = ("x", "zl", "c")
GRP = ("y", "zh")
TEAM = ("y", "c")
REPLICAS = ("zl", "x", "zh")
Z_RING = ("zl", "zh")
Z_PLACES = (0, 2, 1, 3)
ROLES = [(0, 0), (1, 2), (2, 1), (3, 3)]
OWNERS = [
    [(l * 4 + k * 2 + h, (h ^ i) * 4 + l * 2 + k) for l in range(2) for k in range(2) for h in range(2)]
    for i in range(2)
]


def ring(value, axis, step):
    index = Z_PLACES if axis == Z_RING else range(4)
    return lax.ppermute(value, axis, [(index[(i + step) % 4], index[i]) for i in range(4)])


def ring_all(values, axis):
    return [values[0]] + [ring(values[k], axis, k) for k in range(1, 4)]


def flipped(value, axis):
    return lax.ppermute(value, axis, [(0, 1), (1, 0)])


def swap_roles(value):
    return lax.ppermute(value, ("c", "zh"), ROLES)


def swap_selected(value, stays):
    return jnp.where(stays, value, lax.ppermute(value, ("c", "zh"), ROLES[1:3]))


def other_core(value):
    return lax.ppermute(value, "c", [(0, 1), (1, 0)])


def exchange(parts, axes):
    return lax.all_to_all(parts, axes, 0, 0)


def gather(block, axes):
    return lax.all_gather(block, axes, axis=0)


def team_sum(parts):
    return lax.psum_scatter(parts.astype(bf16), TEAM, scatter_dimension=0, tiled=True)


def windows(rows, count):
    tiles = rows // 8
    starts = [tiles * i // count for i in range(count)]
    size = max(b - a for a, b in zip(starts, starts[1:] + [tiles]))
    return size * 8, [8 * s for s in starts]


def joined(parts, starts, rows, axis):
    ends = starts[1:] + [rows]
    return jnp.concatenate(
        [lax.slice_in_dim(p, 0, e - s, axis=axis) for p, s, e in zip(parts, starts, ends)], axis
    )


def norm_parts(value, gain, shift):
    center = value - jnp.mean(value, axis=-1, keepdims=True)
    spread = jnp.mean(center * center, axis=-1, keepdims=True)
    factor = lax.rsqrt(spread + 1e-05)
    normed = center * factor
    return (normed * gain + shift, normed, factor)


def norm_back(grad_value, normed, factor, gain):
    grad_normed = grad_value * gain
    mean_first = jnp.mean(grad_normed, axis=-1, keepdims=True)
    mean_second = jnp.mean(grad_normed * normed, axis=-1, keepdims=True)
    return factor * (grad_normed - mean_first - normed * mean_second)


def dot(left, right):
    return jnp.dot(left, right, preferred_element_type=f32)


def dot_rows(left, right):
    return lax.dot_general(left, right, (((0,), (0,)), ((), ())), preferred_element_type=f32)


def dot_cols(left, right):
    return lax.dot_general(left, right, (((1,), (1,)), ((), ())), preferred_element_type=f32)


def call(kernel, name, out_shape, *operands, scratch=(), flops=0, light=False):
    specs = [
        pl.BlockSpec(memory_space=pltpu.SMEM if op.dtype == jnp.int32 else pltpu.VMEM)
        for op in operands
    ]
    out_specs = jax.tree.map(lambda _: pl.BlockSpec(memory_space=pltpu.VMEM), out_shape)
    moved = sum(op.size * op.dtype.itemsize for op in operands)
    moved += sum(o.size * o.dtype.itemsize for o in jax.tree.leaves(out_shape))
    return pl.pallas_call(
        kernel,
        out_shape=out_shape,
        in_specs=specs,
        out_specs=out_specs,
        scratch_shapes=list(scratch),
        compiler_params=pltpu.CompilerParams(vmem_limit_bytes=56 * 2**20),
        cost_estimate=pl.CostEstimate(
            flops=1 if light else int(flops),
            bytes_accessed=1 if light else int(moved),
            transcendentals=0,
        ),
        name=name,
    )(*operands)


def struct(shape, dtype):
    return jax.ShapeDtypeStruct(shape, dtype)


Y, C, RANK, ZH, Z, X, ZL, MINE = range(8)


def qkv_columns_kernel(place_ref, weight_ref, *refs):
    out_refs, held_ref = refs[:4], refs[4]
    c = place_ref[C]
    width = weight_ref.shape[1] // 3
    for part in range(3):
        lanes = slice(part * SLOT_WIDTH, (part + 1) * SLOT_WIDTH)
        for y in range(4):
            start = part * width + 2 * STRIDE * y
            even = weight_ref[:, start : start + SLOT_WIDTH]
            odd = weight_ref[:, start + STRIDE : start + STRIDE + SLOT_WIDTH]
            held_ref[y, :, lanes] = jnp.where(c == 0, even, odd)
    for k in range(4):
        out_refs[k][...] = held_ref[lax.rem(place_ref[Y] + 4 - k, 4)]


def fc_columns_kernel(place_ref, weight_ref, *refs):
    out_refs, held_ref = refs[:4], refs[4]
    c = place_ref[C]
    hidden = weight_ref.shape[1] // 8
    for y in range(4):
        start = 2 * hidden * y
        even = weight_ref[:, start : start + hidden]
        odd = weight_ref[:, start + hidden : start + 2 * hidden]
        held_ref[y] = jnp.where(c == 0, even, odd)
    for k in range(4):
        out_refs[k][...] = held_ref[lax.rem(place_ref[Y] + 4 - k, 4)]


def fc_whole_kernel(place_ref, *refs):
    out_ref = refs[8]
    zh = place_ref[ZH]
    for k in range(4):
        y = lax.rem(place_ref[Y] + k, 4)
        out_ref[2 * y + zh] = refs[k][...]
        out_ref[2 * y + 1 - zh] = refs[4 + k][...]


def branch_kernel(
    slots_ref, tokens_ref, norm_ref, rows_ref, middle_ref, second_ref, parts_ref, flat_ref
):
    shard = parts_ref.shape[2]
    for rank in range(8):
        wide = STRIDE if rank < 7 else SLOT_WIDTH
        flat_ref[:, STRIDE * rank : STRIDE * rank + wide] = slots_ref[rank, :, :wide]
    for rank in range(8):
        parts_ref[rank] = flat_ref[:, shard * rank : shard * (rank + 1)]
    total = tokens_ref[...].astype(f32) + norm_ref[4:5, :] + dot(flat_ref[...], rows_ref[...])
    middle_ref[...] = total
    second_ref[...] = norm_parts(total, norm_ref[5:6, :], norm_ref[6:7, :])[0].astype(bf16)


def branch_back_kernel(
    place_ref,
    grad_ref,
    middle_ref,
    cot_ref,
    norm_ref,
    rows_ref,
    grad_middle_ref,
    branch_ref,
    slots_ref,
    sums_ref,
    flat_ref,
):
    gain = norm_ref[5:6, :]
    _, normed, factor = norm_parts(middle_ref[...], gain, gain)
    grad = grad_ref[...].astype(f32)
    cot = cot_ref[...].astype(f32)
    grad_middle = cot + norm_back(grad, normed, factor, gain)
    branch = grad_middle.astype(bf16)
    grad_middle_ref[...] = grad_middle
    branch_ref[...] = branch
    flat_ref[...] = dot_cols(branch, rows_ref[...]).astype(bf16)
    for rank in range(8):
        slots_ref[rank] = flat_ref[:, STRIDE * rank : STRIDE * rank + SLOT_WIDTH]
    sums_ref[0:1, :] = jnp.sum(branch.astype(f32), axis=0, keepdims=True)
    sums_ref[1:2, :] = jnp.sum(grad * normed, axis=0, keepdims=True)
    sums_ref[2:3, :] = jnp.sum(grad, axis=0, keepdims=True)
    sums_ref[3:4, :] = jnp.sum(cot, axis=0, keepdims=True)


def column_ring_kernel(place_ref, left_ref, right_ref, *refs):
    out_refs, held_ref = refs[:4], refs[4]
    shard = left_ref.shape[1] // 8
    size, starts = windows(shard, 8)
    held_ref[...] = dot_rows(left_ref[...], right_ref[...])
    for k in range(4):
        x = lax.rem(place_ref[X] + 4 - k, 4)
        for z in range(4):
            for y in range(4):
                base = (2 * y + z // 2) * shard + starts[4 * (z % 2)]
                at = pl.multiple_of(base + starts[1] * x, 8)
                out_refs[k][z, y] = held_ref[pl.ds(at, size), :].astype(bf16)


def row_grad_kernel(place_ref, left_ref, right_ref, *refs):
    out_refs, held_ref = refs[:4], refs[4]
    rows = left_ref.shape[1]
    size = windows(rows, 16)[0]
    held_ref[...] = dot_rows(left_ref[...], right_ref[...])
    for k in range(4):
        z = lax.rem(place_ref[Z] + 4 - k, 4)
        for x in range(4):
            window = (lax.rem(z, 2) * 4 + x) * 2 + lax.div(z, 2)
            at = pl.multiple_of(lax.div(rows // 8 * window, 16) * 8, 8)
            out_refs[k][x] = held_ref[pl.ds(at, size), :].astype(bf16)


def last_grads_kernel(place_ref, first_ref, mixed_ref, attended_ref, branch_ref, out_ref, held_ref):
    shard = first_ref.shape[1] // 8
    slots = mixed_ref.shape[1]
    size, starts = windows(shard, 8)
    held_ref[...] = dot_rows(first_ref[...], mixed_ref[...])
    for y in range(4):
        for zh in range(2):
            base = (2 * y + zh) * shard
            for i, start in enumerate(starts):
                rows = slice(y % 2 * size, (y % 2 + 1) * size)
                lanes = slice(y // 2 * slots, (y // 2 + 1) * slots)
                block = held_ref[base + start : base + start + size, :]
                out_ref[2 * i + zh, rows, lanes] = block.astype(bf16)
    size_out, starts_out = windows(shard, 16)
    grad = dot_rows(attended_ref[...], branch_ref[...])
    rest = jnp.zeros((2 * size, out_ref.shape[2] - 2 * slots), bf16)
    for i, start in enumerate(starts_out):
        out_ref[i, : 2 * size, 2 * slots :] = rest
        out_ref[i, 2 * size :, :] = grad[start : start + size_out].astype(bf16)


def last_sum_kernel(parts_ref, qkv_ref, out_ref):
    size, slots = qkv_ref.shape[1:]
    total = parts_ref[0].astype(f32)
    for i in range(1, 16):
        total = total + parts_ref[i].astype(f32)
    total = total.astype(bf16)
    for y in range(4):
        rows = slice(y % 2 * size, (y % 2 + 1) * size)
        qkv_ref[y] = total[rows, y // 2 * slots : (y // 2 + 1) * slots]
    out_ref[...] = total[2 * size :, :]


def fold_kernel(which, place_ref, *refs):
    for k in range(4):
        at = lax.rem(place_ref[which] + 4 - k, 4)
        total = refs[0][at].astype(f32)
        for j in range(1, 4):
            total = total + refs[j][at].astype(f32)
        refs[4 + k][...] = total.astype(bf16)


def stack_kernel(*refs):
    for k, ref in enumerate(refs[:-1]):
        refs[-1][k] = ref[...]


def column_ring_total_kernel(spans, place_ref, *refs):
    out_ref = refs[8]
    shard = out_ref.shape[0]
    _, starts = windows(shard, 8)
    step = starts[1]
    for j in range(4):
        x = lax.rem(place_ref[X] + j, 4)
        for flip in range(2):
            window = (place_ref[ZL] if flip == 0 else 1 - place_ref[ZL]) * 4 + x
            at = pl.multiple_of(window * step, 8)
            for rank in range(8):
                k = lax.rem(rank // 2 + 4 - place_ref[Y], 4)
                block = jnp.where(
                    place_ref[C] == rank % 2, refs[j][flip, k], refs[4 + j][flip, k]
                ).astype(f32)
                for source, target, wide in spans[rank]:
                    out_ref[pl.ds(at, step), target : target + wide] = block[
                        :step, source : source + wide
                    ]

                @pl.when(window == 7)
                def _(block=block, rank=rank):
                    for source, target, wide in spans[rank]:
                        out_ref[7 * step + step :, target : target + wide] = block[
                            step:, source : source + wide
                        ]


def column_total_kernel(spans, place_ref, own_ref, other_ref, out_ref):
    _, starts = windows(out_ref.shape[0], 8)
    ends = starts[1:] + [out_ref.shape[0]]
    for rank in range(8):
        y = rank // 2
        mine = place_ref[C] == rank % 2
        rows = [
            jnp.where(mine, own_ref[i, y], other_ref[i, y]).astype(f32)[: end - start]
            for i, (start, end) in enumerate(zip(starts, ends))
        ]
        block = jnp.concatenate(rows, axis=0)
        for source, target, wide in spans[rank]:
            out_ref[:, target : target + wide] = block[:, source : source + wide]


def proj_total_kernel(place_ref, own_ref, other_ref, out_ref):
    tiles = out_ref.shape[0] // 8
    small = tiles // 16 * 8
    for part, ref in enumerate((own_ref, other_ref)):
        zl = place_ref[C] if part == 0 else 1 - place_ref[C]
        for x in range(4):
            for i in range(2):
                zh = place_ref[ZL] if i == 0 else 1 - place_ref[ZL]
                window = (zl * 4 + x) * 2 + zh
                start = lax.div(tiles * window, 16)
                wide = lax.div(tiles * (window + 1), 16) - start > small // 8
                at = pl.multiple_of(start * 8, 8)
                block = ref[x, i].astype(f32)
                out_ref[pl.ds(at, small), :] = block[:small]

                @pl.when(wide)
                def _(at=at, block=block):
                    out_ref[pl.ds(pl.multiple_of(at + small, 8), 8), :] = block[small:]


def row_total_kernel(place_ref, own_ref, other_ref, out_ref):
    mine = place_ref[MINE]
    _, starts = windows(out_ref.shape[0], 16)
    ends = starts[1:] + [out_ref.shape[0]]
    for i, (start, end) in enumerate(zip(starts, ends)):
        block = jnp.where(mine == 1, own_ref[i], other_ref[i])
        out_ref[start:end, :] = block[: end - start].astype(f32)


def attend_kernel(place_ref, tokens_ref, norm_ref, bias_ref, *refs):
    pieces, (first_ref, qkv_ref, out_ref, top_ref, cols_ref) = refs[:8], refs[8:]
    length = tokens_ref.shape[0]
    shard = cols_ref.shape[1]
    zh = place_ref[ZH]
    for k in range(4):
        y = lax.rem(place_ref[Y] + k, 4)
        cols_ref[2 * y + zh] = pieces[k][...]
        cols_ref[2 * y + 1 - zh] = pieces[4 + k][...]
    gain = norm_ref[0:1, :]
    shift = norm_ref[1:2, :]
    for block in range(length // BLOCK):
        rows = slice(block * BLOCK, (block + 1) * BLOCK)
        first = norm_parts(tokens_ref[rows, :].astype(f32), gain, shift)[0].astype(bf16)
        first_ref[rows, :] = first
        mixed = bias_ref[...]
        for g in range(8):
            mixed = mixed + dot(first[:, g * shard : (g + 1) * shard], cols_ref[g])
        qkv_ref[rows, :] = mixed.astype(bf16)
    for head in range(SLOTS):
        lanes = slice(head * HEAD_DIM, (head + 1) * HEAD_DIM)
        keys = qkv_ref[:, SLOT_WIDTH + head * HEAD_DIM : SLOT_WIDTH + (head + 1) * HEAD_DIM]
        values = qkv_ref[
            :, 2 * SLOT_WIDTH + head * HEAD_DIM : 2 * SLOT_WIDTH + (head + 1) * HEAD_DIM
        ]
        for block in range(length // BLOCK):
            rows = slice(block * BLOCK, (block + 1) * BLOCK)
            width = (block + 1) * BLOCK
            query = qkv_ref[rows, lanes] * bf16(1.0 / math.sqrt(HEAD_DIM))
            scores = dot_cols(query, keys[:width])
            row = lax.broadcasted_iota(jnp.int32, (BLOCK, width), 0) + block * BLOCK
            col = lax.broadcasted_iota(jnp.int32, (BLOCK, width), 1)
            scores = jnp.where(col <= row, scores, -1e30)
            top = jnp.max(scores, axis=-1, keepdims=True)
            probs = jnp.exp(scores - top)
            total = jnp.sum(probs, axis=-1, keepdims=True)
            mixed = dot(probs.astype(bf16), values[:width])
            out_ref[rows, lanes] = (mixed / total).astype(bf16)
            top_ref[rows, head : head + 1] = top + jnp.log(total)


def hidden_kernel(
    place_ref, second_ref, cols_ref, bias_ref, grad_ref, active_ref, hidden_ref, sums_ref, out_ref
):
    length = second_ref.shape[0]
    sums = jnp.zeros(sums_ref.shape, f32)
    for block in range(length // BLOCK):
        rows = slice(block * BLOCK, (block + 1) * BLOCK)
        pre = dot(second_ref[rows, :], cols_ref[...]) + bias_ref[...]
        square = pre * pre
        bent = jnp.tanh(0.7978845608028654 * (pre + 0.044715 * square * pre))
        half = 0.5 * (1.0 + bent)
        active_ref[rows, :] = (pre * half).astype(bf16)
        slope = half + 0.5 * pre * (1.0 - bent * bent) * (
            0.7978845608028654 + (3.0 * 0.044715 * 0.7978845608028654) * square
        )
        grad = (grad_ref[rows, :] * slope).astype(bf16)
        hidden_ref[rows, :] = grad
        sums = sums + jnp.sum(grad.astype(f32), axis=0, keepdims=True)
        out_ref[rows, :] = dot_cols(grad, cols_ref[...]).astype(bf16)
    sums_ref[...] = sums


def down_kernel(active_ref, rows_ref, out_ref):
    for block in range(active_ref.shape[0] // BLOCK):
        rows = slice(block * BLOCK, (block + 1) * BLOCK)
        out_ref[rows, :] = dot(active_ref[rows, :], rows_ref[...]).astype(bf16)


def attend_back_kernel(
    place_ref,
    qkv_ref,
    grad_ref,
    out_ref,
    top_ref,
    cols_ref,
    down_ref,
    mixed_ref,
    parts_ref,
    sums_ref,
    query_ref,
):
    length = qkv_ref.shape[0]
    scale = 1.0 / math.sqrt(HEAD_DIM)
    ones = jnp.ones((8, HEAD_DIM), bf16)
    for head in range(SLOTS):
        base = head * HEAD_DIM
        lanes = slice(base, base + HEAD_DIM)
        key_lanes = slice(SLOT_WIDTH + base, SLOT_WIDTH + base + HEAD_DIM)
        value_lanes = slice(2 * SLOT_WIDTH + base, 2 * SLOT_WIDTH + base + HEAD_DIM)
        query = qkv_ref[:, lanes] * bf16(scale)
        grad = grad_ref[:, lanes]
        if head == SLOTS - 1:
            grad = jnp.where(place_ref[RANK] == 7, grad, jnp.zeros_like(grad))
        top = top_ref[head : head + 1, :]
        delta = dot_cols(ones, grad * out_ref[:, lanes])[0:1, :]
        for block in range(length // BLOCK):
            start = block * BLOCK
            rows = slice(start, start + BLOCK)
            width = length - start
            keys = qkv_ref[rows, key_lanes]
            values = qkv_ref[rows, value_lanes]
            scores = dot_cols(keys, query[start:])
            row = lax.broadcasted_iota(jnp.int32, (BLOCK, width), 0)
            col = lax.broadcasted_iota(jnp.int32, (BLOCK, width), 1)
            probs = jnp.where(row <= col, jnp.exp(scores - top[:, start:]), 0.0)
            grad_probs = dot_cols(values, grad[start:])
            grad_scores = (probs * (grad_probs - delta[:, start:])).astype(bf16)
            mixed_ref[rows, value_lanes] = dot(probs.astype(bf16), grad[start:]).astype(bf16)
            mixed_ref[rows, key_lanes] = dot(grad_scores, query[start:]).astype(bf16)
            term = dot_rows(grad_scores, keys)
            if block == 0:
                query_ref[...] = term
            else:
                query_ref[start:, :] += term
        mixed_ref[:, lanes] = (query_ref[...] * scale).astype(bf16)
    sums = jnp.zeros(sums_ref.shape, f32)
    for block in range(length // BLOCK):
        rows = slice(block * BLOCK, (block + 1) * BLOCK)
        mixed = mixed_ref[rows, :]
        sums = sums + jnp.sum(mixed.astype(f32), axis=0, keepdims=True)
        first = dot_cols(mixed, cols_ref[...]).astype(bf16)
        for half in range(2):
            rank = 2 * block + half
            parts_ref[rank, 0] = first[half * BLOCK // 2 : (half + 1) * BLOCK // 2]
            parts_ref[rank, 1] = down_ref[rank]
    sums_ref[...] = sums


def input_back_kernel(
    parts_ref, tokens_ref, middle_ref, grad_ref, norm_ref, out_ref, sums_ref
):
    gain = norm_ref[0:1, :]
    _, normed, factor = norm_parts(tokens_ref[...].astype(f32), gain, gain)
    grad = parts_ref[0].astype(f32)
    out_ref[0] = (grad_ref[...] + norm_back(grad, normed, factor, gain)).astype(bf16)
    down = parts_ref[1].astype(f32) + norm_ref[7:8, :]
    out_ref[1] = (middle_ref[...] + down).astype(bf16)
    sums_ref[0:1, :] = jnp.sum(grad * normed, axis=0, keepdims=True)
    sums_ref[1:2, :] = jnp.sum(grad, axis=0, keepdims=True)


def after(value, *others):
    return lax.optimization_barrier((value,) + others)[0]


def per_device(
    tokens,
    ln1_gain,
    ln1_bias,
    w_qkv,
    bias_q,
    bias_v,
    w_out,
    bias_out,
    ln2_gain,
    ln2_bias,
    w_fc,
    bias_fc,
    w_proj,
    bias_proj,
    cotangent,
):
    _, span, width = tokens.shape
    shard = width // 8
    hidden = w_fc.shape[1] // 8
    length = span * 8
    slots = 3 * SLOT_WIDTH
    x, zl, c, y, zh = [lax.axis_index(name) for name, _ in LAYOUT]
    rank = y * 2 + c
    place = jnp.stack(
        [y, c, rank, zh, zh * 2 + zl, x, zl, (c == zh).astype(jnp.int32)]
    ).astype(jnp.int32)

    stays = c == zh
    own_tokens = swap_roles(tokens.reshape(span, width))
    qkv_parts = call(
        qkv_columns_kernel,
        "qkv_columns",
        [struct((shard, slots), bf16)] * 4,
        place,
        w_qkv,
        scratch=[pltpu.VMEM((4, shard, slots), bf16)],
    )
    all_tokens = gather(after(own_tokens, qkv_parts[0]), TEAM).reshape(length, width)
    qkv_own = ring_all(qkv_parts, "y")
    small = jnp.concatenate(
        [ln1_gain, ln1_bias, bias_q, bias_v, bias_out, ln2_gain, ln2_bias, bias_proj, bias_fc]
    ).reshape(3, hidden)
    small_all = exchange(
        after(jnp.broadcast_to(small, (8, 3, hidden)), qkv_parts[0]), GRP
    )
    qkv_other = [flipped(after(part, small_all), "zh") for part in qkv_own]
    out_rows = swap_roles(after(w_out, *qkv_own))
    place = after(place, small_all)
    fc_parts = call(
        fc_columns_kernel,
        "fc_columns",
        [struct((shard, hidden), bf16)] * 4,
        place,
        w_fc,
        scratch=[pltpu.VMEM((4, shard, hidden), bf16)],
    )
    own_cot = swap_roles(after(cotangent, *qkv_other).reshape(span, width))

    small_all = small_all.astype(f32)
    hidden_bias = lax.dynamic_index_in_dim(small_all, rank, 0, keepdims=False)[2:3]
    vectors = small_all[:, :2].reshape(8, 8, shard).transpose(1, 0, 2).reshape(8, width)
    bias_slots = jnp.concatenate(
        [
            lax.dynamic_slice_in_dim(vectors[2], STRIDE * rank, SLOT_WIDTH),
            jnp.zeros((SLOT_WIDTH,), f32),
            lax.dynamic_slice_in_dim(vectors[3], STRIDE * rank, SLOT_WIDTH),
        ]
    ).reshape(1, slots)

    out_all = gather(out_rows, TEAM).reshape(width, width)
    all_cot = gather(after(own_cot, out_rows), TEAM).reshape(length, width)
    proj_came = lax.ppermute(after(w_proj, *qkv_other), ("c", "zh"), ROLES[1:3])
    proj_rows = jnp.where(stays, w_proj, proj_came)
    fc_own = ring_all([after(part, *qkv_other) for part in fc_parts], "y")

    first, qkv, attended_slots, top, qkv_cols = call(
        attend_kernel,
        "attend",
        (
            struct((length, width), bf16),
            struct((length, slots), bf16),
            struct((length, SLOT_WIDTH), bf16),
            struct((length, SLOTS), f32),
            struct((8, shard, slots), bf16),
        ),
        after(place, bias_slots),
        all_tokens,
        vectors,
        bias_slots,
        *qkv_own,
        *qkv_other,
        flops=2 * length * width * slots,
    )
    qkv_cols = qkv_cols.reshape(width, slots)
    fc_other = [flipped(part, "zh") for part in fc_own]
    attended = exchange(
        after(attended_slots, *fc_own).reshape(8, span, SLOT_WIDTH), TEAM
    )
    middle, second, attended_parts = call(
        branch_kernel,
        "branch",
        (
            struct((span, width), f32),
            struct((span, width), bf16),
            struct((8, span, shard), bf16),
        ),
        after(attended, proj_came),
        own_tokens,
        vectors,
        out_all,
        scratch=[pltpu.VMEM((span, width), bf16)],
        flops=2 * span * width * width,
    )

    second_all = gather(second, TEAM).reshape(length, width)
    attended_own = exchange(after(attended_parts, second), TEAM)
    grad_active = dot_cols(after(all_cot, second), proj_rows)
    fc_cols = call(
        fc_whole_kernel,
        "fc_whole",
        struct((8, shard, hidden), bf16),
        place,
        after(fc_own[0], grad_active),
        *fc_own[1:],
        *fc_other,
    ).reshape(width, hidden)
    active, grad_hidden, hidden_sums, second_parts = call(
        hidden_kernel,
        "hidden",
        (
            struct((length, hidden), bf16),
            struct((length, hidden), bf16),
            struct((1, hidden), f32),
            struct((length, width), bf16),
        ),
        after(place, attended_own),
        second_all,
        fc_cols,
        hidden_bias,
        grad_active,
        flops=4 * length * width * hidden,
    )
    grad_second = team_sum(second_parts)
    window = windows(shard, 8)[0]
    fc_grad = call(
        column_ring_kernel,
        "fc_grad",
        [struct((4, 4, window, hidden), bf16)] * 4,
        place,
        second_all,
        grad_hidden,
        scratch=[pltpu.VMEM((width, hidden), f32)],
        flops=2 * length * width * hidden,
    )
    fc_grad = ring_all(fc_grad, "x")
    row_window = windows(hidden, 16)[0]
    proj_grad = call(
        row_grad_kernel,
        "proj_grad",
        [struct((4, row_window, width), bf16)] * 4,
        after(place, fc_grad[0]),
        active,
        all_cot,
        scratch=[pltpu.VMEM((hidden, width), f32)],
        flops=2 * length * width * hidden,
    )
    down_parts = call(
        down_kernel,
        "down",
        struct((length, width), bf16),
        after(active, proj_grad[0]),
        proj_rows,
        light=True,
    )
    proj_near = [ring(proj_grad[k], Z_RING, k) for k in (1, 3)]
    proj_far = ring(after(proj_grad[2], *proj_near), Z_RING, 2)
    proj_grad = [proj_grad[0], proj_near[0], proj_far, proj_near[1]]

    grad_middle, grad_branch, grad_slots, branch_sums = call(
        branch_back_kernel,
        "branch_back",
        (
            struct((span, width), f32),
            struct((span, width), bf16),
            struct((8, span, SLOT_WIDTH), bf16),
            struct((4, width), f32),
        ),
        after(place, *fc_grad, *proj_near, down_parts),
        grad_second,
        middle,
        own_cot,
        vectors,
        out_all,
        scratch=[pltpu.VMEM((span, width), bf16)],
        light=True,
    )
    grad_heads = exchange(grad_slots, TEAM).reshape(length, SLOT_WIDTH)

    def fold(which, parts, name, *behind):
        parts = [after(parts[0], *behind)] + parts[1:]
        return call(
            functools.partial(fold_kernel, which),
            name,
            [struct(parts[0].shape[1:], bf16)] * 4,
            place,
            *parts,
            light=True,
        )

    fc_grad = ring_all(fold(Z, fc_grad, "fc_fold", grad_slots), Z_RING)
    branch_all = gather(grad_branch, TEAM).reshape(length, width)
    grad_mixed, last_parts, mixed_sums = call(
        attend_back_kernel,
        "attend_back",
        (
            struct((length, slots), bf16),
            struct((8, 2, span, width), bf16),
            struct((1, slots), f32),
        ),
        after(place, proj_far, *fc_grad),
        qkv,
        grad_heads,
        attended_slots,
        top.T,
        qkv_cols,
        down_parts.reshape(8, span, width),
        scratch=[pltpu.VMEM((length, HEAD_DIM), f32)],
        flops=20 * length * width * slots,
    )
    last = team_sum(last_parts.reshape(2 * length, width)).reshape(2, span, width)
    fc_grad = ring_all(fold(Y, fc_grad, "fc_fold_last", grad_mixed), "y")
    proj_grad = ring_all(fold(X, proj_grad, "proj_fold", grad_mixed), "x")
    last_grads = call(
        last_grads_kernel,
        "last_grads",
        struct((16, 2 * window + windows(shard, 16)[0], width), bf16),
        place,
        after(first, fc_grad[0], proj_grad[0]),
        grad_mixed,
        attended_own.reshape(length, shard),
        branch_all,
        scratch=[pltpu.VMEM((width, slots), f32)],
        flops=2 * length * width * (slots + shard),
    )
    place = after(place, last_grads)
    last_grads = exchange(after(last_grads, *fc_grad, *proj_grad), REPLICAS)

    def stacked(parts, name):
        return call(
            stack_kernel, name, struct((len(parts),) + parts[0].shape, bf16), *parts
        )

    def row_total(whole, rows, name, *behind):
        whole = after(whole, *behind)
        return call(
            row_total_kernel, name, struct((rows, width), f32), place, whole, other_core(whole)
        )

    proj_sum = sum(part.astype(f32) for part in proj_grad)
    proj_sum = proj_sum.astype(bf16)
    qkv_sum, out_sum = call(
        last_sum_kernel,
        "last_sum",
        (struct((4, window, slots), bf16), struct((windows(shard, 16)[0], width), bf16)),
        last_grads,
    )
    qkv_sum = exchange(after(qkv_sum, last), "y")
    qkv_whole = gather(qkv_sum, ("zl", "x"))
    proj_sum = after(proj_sum, qkv_sum)
    proj_both = [lax.ppermute(proj_sum, ("zl", "c", "zh"), owners) for owners in OWNERS]
    proj_pair = stacked(proj_both, "proj_both")
    fc_near = stacked([after(fc_grad[0], qkv_sum)] + fc_grad[1:], "fc_near")
    fc_both = stacked([fc_near, flipped(fc_near, "zl")], "fc_both")
    fc_pieces = ring_all([fc_both] * 4, "x")
    fc_pieces = fc_pieces + [other_core(part) for part in fc_pieces]
    results, first_sums = call(
        input_back_kernel,
        "input_back",
        (struct((2, span, width), bf16), struct((2, width), f32)),
        last,
        own_tokens,
        middle,
        grad_middle,
        after(vectors, qkv_sum, fc_both, proj_pair),
    )
    results_home = swap_selected(results, stays)

    blank = jnp.zeros((1, width), f32)
    at = (0, STRIDE * rank)
    small_terms = jnp.concatenate(
        [
            first_sums,
            lax.dynamic_update_slice(blank, mixed_sums[:, :SLOT_WIDTH], at),
            lax.dynamic_update_slice(blank, mixed_sums[:, 2 * SLOT_WIDTH :], at),
            branch_sums,
        ]
    )
    hidden_term = lax.dynamic_update_slice(
        jnp.zeros((8, hidden), f32), hidden_sums, (rank, 0)
    )
    small_terms = small_terms.reshape(8, 8, shard).transpose(1, 0, 2).reshape(8, 2, hidden)
    small_terms = jnp.concatenate([small_terms, hidden_term[:, None]], axis=1)
    small_sum = jnp.sum(exchange(after(small_terms, qkv_sum), GRP), axis=0)
    small_last = jnp.broadcast_to(small_sum, (16, 3, hidden))
    small_last = jnp.sum(exchange(small_last, REP), axis=0)
    out_whole = exchange(
        after(jnp.broadcast_to(out_sum, (16,) + out_sum.shape), small_last, *fc_pieces[:4]),
        REPLICAS,
    )
    owned = small_last[:2].reshape(8, shard)

    qkv_spans = [
        [
            (p * SLOT_WIDTH, p * width + STRIDE * r, STRIDE if r < 7 else SLOT_WIDTH)
            for p in range(3)
        ]
        for r in range(8)
    ]
    qkv_whole = after(qkv_whole, small_sum, *fc_pieces[:4])
    proj_whole = gather(after(proj_pair, qkv_whole), "x")
    fc_spans = [[(0, rank * hidden, hidden)] for rank in range(8)]
    fc_total = call(
        functools.partial(column_ring_total_kernel, fc_spans),
        "fc_total",
        struct((shard, 8 * hidden), f32),
        after(place, small_last),
        *fc_pieces,
        light=True,
    )
    qkv_total = call(
        functools.partial(column_total_kernel, qkv_spans),
        "qkv_total",
        struct((shard, 3 * width), f32),
        after(place, results, fc_total),
        qkv_whole,
        other_core(qkv_whole),
        light=True,
    )
    proj_whole = after(proj_whole, qkv_total)
    proj_total = call(
        proj_total_kernel,
        "proj_total",
        struct((hidden, width), f32),
        after(place, qkv_total),
        proj_whole,
        other_core(proj_whole),
    )
    out_total = row_total(out_whole, shard, "out_total", fc_total, qkv_total)
    return (
        results_home[1].reshape(1, span, width),
        results_home[0].astype(f32).reshape(1, span, width),
        owned[0],
        owned[1],
        qkv_total,
        owned[2],
        owned[3],
        out_total,
        owned[4],
        owned[5],
        owned[6],
        fc_total,
        small_last[2],
        proj_total,
        owned[7],
    )


def solution(mesh):
    names = tuple(name for name, _ in LAYOUT)
    fine = jax.sharding.Mesh(mesh.devices.reshape([size for _, size in LAYOUT]), names)
    in_specs = (
        P(REP, GRP, None),
        P(GRP),
        P(GRP),
        P(GRP, None),
        P(GRP),
        P(GRP),
        P(GRP, None),
        P(GRP),
        P(GRP),
        P(GRP),
        P(GRP, None),
        P(GRP),
        P(GRP, None),
        P(GRP),
        P(REP, GRP, None),
    )
    out_specs = (
        P(REP, GRP, None),
        P(REP, GRP, None),
        P(GRP),
        P(GRP),
        P(GRP, None),
        P(GRP),
        P(GRP),
        P(GRP, None),
        P(GRP),
        P(GRP),
        P(GRP),
        P(GRP, None),
        P(GRP),
        P(GRP, None),
        P(GRP),
    )
    return jax.shard_map(
        per_device, mesh=fine, in_specs=in_specs, out_specs=out_specs, check_vma=False
    )
```
